32 devices in a mesh: gx: 4 (over z), gy: 4 (over x, core), gz: 2 (over y).
Axes of the slice: x: 2, y: 2, z: 4, core: 2. Of those that a mesh axis runs over, the one named last changes fastest.
Arguments:
- schur: float32 [4, 4, 2, 1536, 1536], P('gx', 'gy', 'gz'), as said below
- start_block: float32 [4, 4, 2, 6, 256, 32], P('gx', 'gy', 'gz'), may hold values from -6 to 6
- resid: float32 [4, 4, 2, 1536, 128], P('gx', 'gy', 'gz'), may hold values from -6 to 6
- group_of: int32 [8], replicated, may hold values from 0 to 1, as said below
Outputs:
- correction: float32 [4, 4, 2, 1536, 128], P('gx', 'gy', 'gz')
The draws below stay inside these ranges and needn't reach their ends.
Inputs may be any that keep to these rules, and one draw needn't show every extreme that they name: Each subdomain's schur is symmetric positive definite. `group_of`: each of the 2 groups has exactly 4 subdomains.
All inputs are finite; a program needn't handle non-finite values.
Results may differ from the reference program's by a relative error of at most 0.00022.
Values sent between devices are 32-bit elements; how exact they have to be, the bound alone decides.
No kernel may reach another device: no remote copies, remote signals or barrier semaphores. Data moves between devices by JAX's collectives and lax.ppermute only.
A program may use at most 128 MiB of HBM per device.

```python
import jax
import jax.numpy as jnp
from jax import lax

FACE = 256
NCON = 32
COLS = 128
NS_ITERS = 3
SUB_ITERS = 2
GROUP_SIZE = 4
ORDER = 1536
COARSE = 192
NSX = 4
NSY = 4
NSZ = 2
PLANE = 8
GROUPS = 2


def draw_schur(key, part):
    count = NSX * NSY * NSZ

    def single(index):
        sub_key = jax.random.fold_in(key, index)
        key_one, key_two = jax.random.split(sub_key, 2)
        normal_mat = jax.random.normal(key_one, (ORDER, ORDER), jnp.float32)
        diag_add = jax.random.uniform(key_two, (ORDER,), jnp.float32, 0.5, 1.5)
        matrix = 2.0 * jnp.dot(normal_mat, normal_mat.T, precision=lax.Precision.HIGHEST) / ORDER + jnp.diag(diag_add)
        return matrix
    return lax.map(single, jnp.arange(count)).reshape(NSX, NSY, NSZ, ORDER, ORDER)


def draw_group_of(key, part):
    shuffled = jax.random.permutation(jax.random.fold_in(key, 17), PLANE)
    return (shuffled // GROUP_SIZE).astype(jnp.int32)


def block_levels(stream_key, extent, pieces, least, largest):
    def one(position, parts):
        steps = jax.random.uniform(jax.random.fold_in(jax.random.fold_in(stream_key, 6), position), (parts,), jnp.float32, least / len(pieces), largest / len(pieces))
        return jnp.repeat(jnp.exp(steps), extent[position] // parts).reshape((-1,) + (1,) * (len(extent) - position - 1))

    loudness = one(*pieces[0])
    for cut in pieces[1:]:
        loudness = loudness * one(*cut)
    return loudness


def centred(rng, dims, deviation, most, pieces=(), kind=jnp.bfloat16):
    array = deviation * jax.random.normal(rng, dims, jnp.float32)
    if pieces:
        array = array * block_levels(rng, dims, pieces, -0.22, 0.18)
    return jnp.clip(array, -most, most).astype(kind)


def setup_inputs(seed: int = 0) -> dict:
    splits = jax.random.split(jax.random.key(seed), 5)
    schur = draw_schur(jax.random.fold_in(splits[4], 71), 0)
    start_block = centred(splits[1], (NSX, NSY, NSZ, 6, FACE, NCON), 1.0, 6.0, ((0, 4), (1, 4), (2, 2)), jnp.float32)
    resid = centred(splits[2], (NSX, NSY, NSZ, ORDER, COLS), 1.0, 6.0, ((0, 4), (1, 4), (2, 2)), jnp.float32)
    group_of = draw_group_of(jax.random.fold_in(splits[4], 71), 0)
    return {"schur": schur, "start_block": start_block, "resid": resid, "group_of": group_of}


precise = lax.Precision.HIGHEST

def neighbour_faces(stack):
    lower_x = jnp.roll(stack[:, :, :, 1], 1, axis=0)
    upper_x = jnp.roll(stack[:, :, :, 0], -1, axis=0)
    lower_y = jnp.roll(stack[:, :, :, 3], 1, axis=1)
    upper_y = jnp.roll(stack[:, :, :, 2], -1, axis=1)
    lower_z = jnp.roll(stack[:, :, :, 5], 1, axis=2)
    upper_z = jnp.roll(stack[:, :, :, 4], -1, axis=2)
    return jnp.stack([lower_x, upper_x, lower_y, upper_y, lower_z, upper_z], axis=3)

def newton_inverse(matrices):
    diag_vals = jnp.diagonal(matrices, axis1=1, axis2=2)
    identity = jnp.eye(matrices.shape[1], dtype=jnp.float32)
    inverse = identity[None] / diag_vals[:, None, :]
    for sweep in range(NS_ITERS):
        product = jnp.einsum('fij,fjk->fik', matrices, inverse, precision=precise)
        inverse = 2.0 * inverse - jnp.einsum('fij,fjk->fik', inverse, product, precision=precise)
    return inverse

def right_factor(factor, image):
    return jax.scipy.linalg.solve_triangular(factor, image.T, lower=True).T

def subspace(own, partner, inverse, starts):
    basis = starts
    for sweep in range(SUB_ITERS):
        image = jnp.einsum('fij,fjc->fic', partner, basis, precision=precise)
        image = jnp.einsum('fij,fjc->fic', inverse, image, precision=precise)
        image = jnp.einsum('fij,fjc->fic', own, image, precision=precise)
        gram = jnp.einsum('fic,fid->fcd', image, image, precision=precise)
        factor = jnp.linalg.cholesky(gram)
        basis = jax.vmap(right_factor)(factor, image)
    return basis

def local_phase(items):
    schur_one, own, partner, starts, resid_one = items
    inverse = newton_inverse(own + partner)
    basis = subspace(own, partner, inverse, starts)
    order = schur_one.shape[0]
    rows_grouped = schur_one.reshape(order, 6, FACE)
    side = jnp.einsum('igj,gjc->igc', rows_grouped, basis, precision=precise)
    side = side.reshape(6, FACE, 6, NCON)
    coarse_local = jnp.einsum('fic,figd->fcgd', basis, side, precision=precise).reshape(COARSE, COARSE)
    rhs_local = jnp.einsum('fic,fin->fcn', basis, resid_one.reshape(6, FACE, COLS), precision=precise).reshape(COARSE, COLS)
    return (inverse, basis, coarse_local, rhs_local)

def solve_one(matrix, rhs):
    factor = jnp.linalg.cholesky(matrix)
    return jax.scipy.linalg.cho_solve((factor, True), rhs)

def reference(schur, start_block, resid, group_of):
    count = NSX * NSY * NSZ
    own_all = jnp.stack([schur[:, :, :, f * FACE:(f + 1) * FACE, f * FACE:(f + 1) * FACE] for f in range(6)], axis=3)
    partner_all = neighbour_faces(own_all)
    flat = (schur.reshape(count, ORDER, ORDER), own_all.reshape(count, 6, FACE, FACE), partner_all.reshape(count, 6, FACE, FACE), start_block.reshape(count, 6, FACE, NCON), resid.reshape(count, ORDER, COLS))
    inverse, basis, coarse_local, rhs_local = lax.map(local_phase, flat)
    onehot = (group_of[:, None] == jnp.arange(GROUPS, dtype=jnp.int32)[None, :]).astype(jnp.float32)
    coarse_total = jnp.einsum('xpab,pg->xgab', coarse_local.reshape(NSX, PLANE, COARSE, COARSE), onehot, precision=precise)
    rhs_total = jnp.einsum('xpab,pg->xgab', rhs_local.reshape(NSX, PLANE, COARSE, COLS), onehot, precision=precise)
    member_matrix = coarse_total[:, group_of].reshape(count, COARSE, COARSE)
    member_rhs = rhs_total[:, group_of].reshape(count, COARSE, COLS)
    answer = jax.vmap(solve_one)(member_matrix, member_rhs)
    w_faces = jnp.einsum('dfic,dfcn->dfin', basis, answer.reshape(count, 6, NCON, COLS), precision=precise)
    own_flat = own_all.reshape(count, 6, FACE, FACE)
    products = jnp.einsum('dfij,dfjn->dfin', own_flat, w_faces, precision=precise)
    partner_y = neighbour_faces(products.reshape(NSX, NSY, NSZ, 6, FACE, COLS)).reshape(count, 6, FACE, COLS)
    correction = jnp.einsum('dfij,dfjn->dfin', inverse, products + partner_y, precision=precise)
    return correction.reshape(NSX, NSY, NSZ, ORDER, COLS)
```

```python
import functools

import jax
import jax.numpy as jnp
from jax import lax
from jax.experimental import pallas as pl
from jax.experimental.pallas import tpu as pltpu
from jax.sharding import PartitionSpec as P

NS_ITERS = 3
SUB_ITERS = 2
GROUP_SIZE = 4
FACES = 6
AXES = ("gx", "gy", "gz")
LIMIT = 50 * 1024 * 1024

precise = lax.Precision.HIGHEST


def dot(left, right, dims=((1,), (0,))):
    return lax.dot_general(
        left, right, (dims, ((), ())), precision=precise, preferred_element_type=jnp.float32
    )


def iota(shape, dim):
    return lax.broadcasted_iota(jnp.int32, shape, dim)


def ring(axis):
    count = lax.axis_size(axis)
    forward = [(i, (i + 1) % count) for i in range(count)]
    backward = [(target, source) for source, target in forward]
    return forward, backward


def flipped(axis, bit):
    return [(i, i ^ bit) for i in range(lax.axis_size(axis))]


def face_slots(counts):
    slots = []
    arrays = 0
    for count in counts:
        if count == 2:
            slots += [(arrays, 0), (arrays, 1)]
            arrays += 1
        else:
            slots += [(arrays, None), (arrays + 1, None)]
            arrays += 2
    return slots, arrays


def swap(arrays, counts):
    slots, _ = face_slots(counts)
    got = []
    where = []
    for position, axis in enumerate(AXES):
        forward, backward = ring(axis)
        even, odd = slots[2 * position], slots[2 * position + 1]
        if counts[position] == 2:
            where += [(len(got), 1), (len(got), 0)]
            got.append(lax.ppermute(arrays[even[0]], axis, forward))
        else:
            where += [(len(got), None), (len(got) + 1, None)]
            got.append(lax.ppermute(arrays[odd[0]], axis, forward))
            got.append(lax.ppermute(arrays[even[0]], axis, backward))
    return got, where


def pick(refs, slot):
    array, part = slot
    return refs[array][...] if part is None else refs[array][part]


def put(refs, slot, value):
    array, part = slot
    if part is None:
        refs[array][...] = value
    else:
        refs[array][part] = value


def slot_shapes(counts, shape):
    shapes = []
    for count in counts:
        if count == 2:
            shapes.append(jax.ShapeDtypeStruct((2,) + shape, jnp.float32))
        else:
            shapes += [jax.ShapeDtypeStruct(shape, jnp.float32)] * 2
    return shapes


def vmem_specs(count):
    return [pl.BlockSpec(memory_space=pltpu.VMEM)] * count


def pack_kernel(slots, width, schur_ref, *refs):
    outs, blocks, sems = refs[:-2], refs[-2], refs[-1]
    half = width // 2
    copies = []
    for f in range(FACES):
        place = pl.ds(f * width, width)
        copy = pltpu.make_async_copy(schur_ref.at[place, place], blocks.at[f], sems.at[f])
        copy.start()
        copies.append(copy)
    row, col = iota((half, half), 0), iota((half, half), 1)
    for f in range(FACES):
        copies[f].wait()
        first = blocks[f, 0:half, 0:half]
        second = blocks[f, half:width, half:width]
        diag = jnp.sum(jnp.where(row == col, second, 0.0), axis=0, keepdims=True)
        mixed = jnp.where(row >= col, first, second)
        tail = jnp.broadcast_to(diag, (8, half))
        put(outs, slots[f], jnp.concatenate([blocks[f, half:width, 0:half], mixed, tail], axis=0))


def unpack(packed):
    half = packed.shape[1]
    row, col = iota((half, half), 0), iota((half, half), 1)
    low = packed[0:half]
    mixed = packed[half : 2 * half]
    flip = mixed.T
    first = jnp.where(row >= col, mixed, flip)
    second = jnp.where(row < col, mixed, flip)
    second = jnp.where(row == col, packed[2 * half : 2 * half + 1], second)
    return jnp.concatenate(
        [jnp.concatenate([first, low.T], axis=1), jnp.concatenate([low, second], axis=1)], axis=0
    )


def factor_inverses(grams):
    size = grams[0].shape[0]
    strips = size // 8
    state = []
    for gram in grams:
        whole = jnp.concatenate(
            [gram, jnp.where(iota((size, size), 0) == iota((size, size), 1), 1.0, 0.0)], axis=1
        )
        state.append([whole[8 * s : 8 * s + 8] for s in range(strips)])
    below = iota((8, 1), 0)
    for k in range(size):
        strip, line = k // 8, k % 8
        for work in state:
            row = work[strip][line : line + 1]
            scaled = row * (1.0 / row[:, k : k + 1])
            for s in range(strip, strips):
                column = work[s][:, k : k + 1]
                if s == strip:
                    if line == 7:
                        continue
                    column = jnp.where(below > line, column, 0.0)
                work[s] = work[s] - column * scaled
    results = []
    for work in state:
        parts = []
        for s in range(strips):
            place = iota((8, size), 0) + 8 * s == iota((8, size), 1)
            pivot = jnp.sum(jnp.where(place, work[s][:, :size], 0.0), axis=1, keepdims=True)
            parts.append(work[s][:, size:] * lax.rsqrt(pivot))
        results.append(jnp.concatenate(parts, axis=0))
    return results


def main_kernel(where, slots, arrays, width, schur_ref, *refs):
    inputs = refs[:arrays]
    starts_ref, resid_ref = refs[arrays : arrays + 2]
    inverse_ref, payload_ref = refs[arrays + 2 : arrays + 4]
    products = refs[arrays + 4 : -5]
    own_ref, upper_ref, partner_ref, own_sems, upper_sems = refs[-5:]
    ncon = starts_ref.shape[2]
    columns = resid_ref.shape[1]
    copies = []
    for f in range(FACES):
        place = pl.ds(f * width, width)
        copy = pltpu.make_async_copy(schur_ref.at[place, place], own_ref.at[f], own_sems.at[f])
        copy.start()
        copies.append(copy)
    strips = []
    for f in range(FACES - 1):
        rest = (FACES - 1 - f) * width
        copy = pltpu.make_async_copy(
            schur_ref.at[pl.ds(f * width, width), pl.ds((f + 1) * width, rest)],
            upper_ref.at[f, :, pl.ds((f + 1) * width, rest)],
            upper_sems.at[f],
        )
        copy.start()
        strips.append(copy)
    eye = iota((width, width), 0) == iota((width, width), 1)
    for f in range(FACES):
        partner_ref[f] = unpack(pick(inputs, where[f]))
    sums = []
    for f in range(FACES):
        copies[f].wait()
        total = own_ref[f] + partner_ref[f]
        diagonal = jnp.where(eye, total, 0.0)
        across = 1.0 / jnp.sum(diagonal, axis=0, keepdims=True)
        down = 1.0 / jnp.sum(diagonal, axis=1, keepdims=True)
        inverse_ref[f] = jnp.where(eye, 2.0 * across, 0.0) - down * total * across
        sums.append(total)
    for sweep in range(NS_ITERS - 1):
        for f in range(FACES):
            guess = inverse_ref[f]
            inverse_ref[f] = 2.0 * guess - dot(guess, dot(sums[f], guess))
    basis = [starts_ref[f] for f in range(FACES)]
    for sweep in range(SUB_ITERS):
        for f in range(FACES):
            image = dot(own_ref[f], dot(inverse_ref[f], dot(partner_ref[f], basis[f])))
            if sweep < SUB_ITERS - 1:
                image = image * lax.rsqrt(jnp.sum(image * image, axis=0, keepdims=True))
            basis[f] = image
    factors = factor_inverses([dot(b, b, ((0,), (0,))) for b in basis])
    basis = [dot(basis[f], factors[f], ((1,), (1,))) for f in range(FACES)]
    for f in range(FACES - 1):
        strips[f].wait()
    rows = []
    for f in range(FACES):
        product = dot(own_ref[f], basis[f])
        put(products, slots[f], product.T)
        side = [product]
        for g in range(f + 1, FACES):
            side.append(dot(upper_ref[f, :, g * width : (g + 1) * width], basis[g]))
        rows.append(dot(basis[f], jnp.concatenate(side, axis=1), ((0,), (0,))))
    half = FACES * ncon // 2
    gap = jnp.zeros((ncon, ncon), jnp.float32)
    for f in range(FACES // 2):
        payload_ref[f * ncon : (f + 1) * ncon] = jnp.concatenate(
            [rows[f], rows[FACES - 1 - f], gap], axis=1
        )
    for f in range(FACES):
        right = dot(basis[f], resid_ref[f * width : (f + 1) * width], ((0,), (0,)))
        side, place = divmod(f, FACES // 2)
        payload_ref[
            half + place * ncon : half + (place + 1) * ncon, side * columns : (side + 1) * columns
        ] = right


def spread_kernel(where, slots, arrays, *refs):
    mine, theirs = refs[:arrays], refs[arrays : 2 * arrays]
    inverse_ref, out_ref = refs[2 * arrays :]
    for f in range(FACES):
        both = jnp.concatenate([pick(mine, slots[f]), pick(theirs, where[f])], axis=0)
        out_ref[f] = dot(both, inverse_ref[f], ((1,), (1,)))


def solve_kernel(slots, ncon, total_ref, answer_ref, *outs):
    half = FACES * ncon // 2
    columns = answer_ref.shape[1]
    matrix = []
    right = []
    for f in range(FACES):
        if f < FACES // 2:
            line = total_ref[f * ncon : (f + 1) * ncon, 0 : (FACES - f) * ncon]
        else:
            other = FACES - 1 - f
            start = (FACES - other) * ncon
            line = total_ref[other * ncon : (other + 1) * ncon, start : start + (FACES - f) * ncon]
        side, place = divmod(f, FACES // 2)
        matrix.append(line)
        right.append(
            total_ref[
                half + place * ncon : half + (place + 1) * ncon,
                side * columns : (side + 1) * columns,
            ]
        )
    for b in range(FACES):
        (factor,) = factor_inverses([matrix[b][:, 0:ncon]])
        line = dot(factor, matrix[b])
        rhs = dot(factor, right[b])
        for i in range(b + 1, FACES):
            begin = (i - b) * ncon
            lead = line[:, begin : begin + ncon]
            matrix[i] = matrix[i] - dot(lead, line[:, begin:], ((0,), (0,)))
            right[i] = right[i] - dot(lead, rhs, ((0,), (0,)))
        line = dot(factor, line, ((0,), (0,)))
        rhs = dot(factor, rhs, ((0,), (0,)))
        matrix[b], right[b] = line, rhs
        for i in range(b):
            lead = matrix[i][:, (b - i) * ncon : (b - i + 1) * ncon]
            right[i] = right[i] - dot(lead, rhs)
            if b < FACES - 1:
                tail = matrix[i][:, (b - i + 1) * ncon :] - dot(lead, line[:, ncon:])
                matrix[i] = jnp.concatenate([matrix[i][:, : (b - i + 1) * ncon], tail], axis=1)
    for f in range(FACES):
        answer_ref[f * ncon : (f + 1) * ncon] = right[f]
        put(outs, slots[f], right[f])


def last_kernel(where, arrays, ncon, spread_ref, answer_ref, *refs):
    theirs, out_ref = refs[:arrays], refs[arrays]
    width = spread_ref.shape[2]
    for f in range(FACES):
        both = jnp.concatenate(
            [answer_ref[f * ncon : (f + 1) * ncon], pick(theirs, where[f])], axis=0
        )
        out_ref[f * width : (f + 1) * width] = dot(spread_ref[f], both, ((0,), (0,)))


def group_total(payload, group_of):
    rows, planes = lax.axis_size("gy"), lax.axis_size("gz")
    groups = group_of.shape[0] // GROUP_SIZE
    y, z = lax.axis_index("gy"), lax.axis_index("gz")
    mine = group_of[y * planes + z]
    if groups != 2 or rows & (rows - 1) or planes & (planes - 1):
        chosen = jnp.arange(groups, dtype=jnp.int32) == mine
        total = lax.psum(jnp.where(chosen[:, None, None], payload[None], 0.0), ("gy", "gz"))
        return lax.dynamic_index_in_dim(total, mine, 0, keepdims=False)
    core = y & 1
    theirs = group_of[(y ^ 1) * planes + z]
    other = lax.ppermute(payload, "gy", flipped("gy", 1))
    part = jnp.where(mine == core, payload, 0.0) + jnp.where(theirs == core, other, 0.0)
    bit = 2
    while bit < rows:
        part = part + lax.ppermute(part, "gy", flipped("gy", bit))
        bit *= 2
    bit = 1
    while bit < planes:
        part = part + lax.ppermute(part, "gz", flipped("gz", bit))
        bit *= 2
    swapped = lax.ppermute(part, "gy", flipped("gy", 1))
    return jnp.where(mine == core, part, swapped)


def per_device(schur, start_block, resid, group_of):
    matrix = schur[0, 0, 0]
    starts = start_block[0, 0, 0]
    right = resid[0, 0, 0]
    order, columns = right.shape
    width, ncon = starts.shape[1:]
    counts = [lax.axis_size(axis) for axis in AXES]
    slots, arrays = face_slots(counts)
    coarse = FACES * ncon
    params = pltpu.CompilerParams(vmem_limit_bytes=LIMIT)
    anywhere = pl.BlockSpec(memory_space=pl.ANY)

    packed = pl.pallas_call(
        functools.partial(pack_kernel, slots, width),
        out_shape=slot_shapes(counts, (width + 8, width // 2)),
        in_specs=[anywhere],
        out_specs=vmem_specs(arrays),
        scratch_shapes=[
            pltpu.VMEM((FACES, width, width), jnp.float32),
            pltpu.SemaphoreType.DMA((FACES,)),
        ],
        compiler_params=params,
    )(matrix)
    got, where = swap(packed, counts)

    inverse, payload, *products = pl.pallas_call(
        functools.partial(main_kernel, where, slots, arrays, width),
        out_shape=[
            jax.ShapeDtypeStruct((FACES, width, width), jnp.float32),
            jax.ShapeDtypeStruct((coarse, 2 * columns), jnp.float32),
        ]
        + slot_shapes(counts, (ncon, width)),
        in_specs=[anywhere] + vmem_specs(arrays + 2),
        out_specs=vmem_specs(arrays + 2),
        scratch_shapes=[
            pltpu.VMEM((FACES, width, width), jnp.float32),
            pltpu.VMEM((FACES - 1, width, order), jnp.float32),
            pltpu.VMEM((FACES, width, width), jnp.float32),
            pltpu.SemaphoreType.DMA((FACES,)),
            pltpu.SemaphoreType.DMA((FACES - 1,)),
        ],
        compiler_params=params,
    )(matrix, *got, starts, right)

    total = group_total(payload, group_of)
    their_products, _ = swap(products, counts)
    spread = pl.pallas_call(
        functools.partial(spread_kernel, where, slots, arrays),
        out_shape=jax.ShapeDtypeStruct((FACES, 2 * ncon, width), jnp.float32),
        in_specs=vmem_specs(2 * arrays + 1),
        out_specs=pl.BlockSpec(memory_space=pltpu.VMEM),
        compiler_params=params,
    )(*products, *their_products, inverse)

    answer, *answers = pl.pallas_call(
        functools.partial(solve_kernel, slots, ncon),
        out_shape=[jax.ShapeDtypeStruct((coarse, columns), jnp.float32)]
        + slot_shapes(counts, (ncon, columns)),
        in_specs=vmem_specs(1),
        out_specs=vmem_specs(arrays + 1),
        compiler_params=params,
    )(total)
    their_answers, _ = swap(answers, counts)

    correction = pl.pallas_call(
        functools.partial(last_kernel, where, arrays, ncon),
        out_shape=jax.ShapeDtypeStruct((order, columns), jnp.float32),
        in_specs=vmem_specs(2 + arrays),
        out_specs=pl.BlockSpec(memory_space=pltpu.VMEM),
        compiler_params=params,
    )(spread, answer, *their_answers)
    return correction[None, None, None]


def solution(mesh):
    in_specs = (
        P("gx", "gy", "gz", None, None),
        P("gx", "gy", "gz", None, None, None),
        P("gx", "gy", "gz", None, None),
        P(),
    )
    out_specs = P("gx", "gy", "gz", None, None)
    return jax.shard_map(
        per_device, mesh=mesh, in_specs=in_specs, out_specs=out_specs, check_vma=False
    )
```

```python
import functools

import jax
import jax.numpy as jnp
from jax import lax
from jax.experimental import pallas as pl
from jax.experimental.pallas import tpu as pltpu
from jax.sharding import PartitionSpec as P

NS_ITERS = 3
SUB_ITERS = 2
GROUP_SIZE = 4
FACES = 6
BLOCKS = FACES // 2
AXES = ("gx", "gy", "gz")
LIMIT = 56 * 1024 * 1024

precise = lax.Precision.HIGHEST


def dot(left, right, dims=((1,), (0,))):
    return lax.dot_general(
        left, right, (dims, ((), ())), precision=precise, preferred_element_type=jnp.float32
    )


def split(value):
    high = value.astype(jnp.bfloat16)
    return high, (value - high.astype(jnp.float32)).astype(jnp.bfloat16)


def wide(left, right):
    return lax.dot_general(
        jnp.concatenate([left[0], left[0], left[1]], axis=1),
        jnp.concatenate([right[0], right[1], right[0]], axis=0),
        (((1,), (0,)), ((), ())),
        preferred_element_type=jnp.float32,
    )


def stacked(value):
    return jnp.concatenate(split(value), axis=0)


def thin(rows, matrix):
    out = lax.dot_general(
        jnp.concatenate([rows, rows], axis=1),
        jnp.concatenate(matrix, axis=0),
        (((1,), (0,)), ((), ())),
        preferred_element_type=jnp.float32,
    )
    half = rows.shape[0] // 2
    return out[:half] + out[half:]


def iota(shape, dim):
    return lax.broadcasted_iota(jnp.int32, shape, dim)


def ring(axis):
    count = lax.axis_size(axis)
    forward = [(i, (i + 1) % count) for i in range(count)]
    backward = [(target, source) for source, target in forward]
    return forward, backward


def flipped(axis, bit):
    return [(i, i ^ bit) for i in range(lax.axis_size(axis))]


def face_slots(counts):
    slots = []
    arrays = 0
    for count in counts:
        if count == 2:
            slots += [(arrays, 0), (arrays, 1)]
            arrays += 1
        else:
            slots += [(arrays, None), (arrays + 1, None)]
            arrays += 2
    return slots, arrays


def swap(arrays, counts):
    slots, _ = face_slots(counts)
    got = []
    where = []
    for position, axis in enumerate(AXES):
        forward, backward = ring(axis)
        even, odd = slots[2 * position], slots[2 * position + 1]
        if counts[position] == 2:
            where += [(len(got), 1), (len(got), 0)]
            got.append(lax.ppermute(arrays[even[0]], axis, forward))
        else:
            where += [(len(got), None), (len(got) + 1, None)]
            got.append(lax.ppermute(arrays[odd[0]], axis, forward))
            got.append(lax.ppermute(arrays[even[0]], axis, backward))
    return got, where


def pick(refs, slot):
    array, part = slot
    return refs[array][...] if part is None else refs[array][part]


def put(refs, slot, value):
    array, part = slot
    if part is None:
        refs[array][...] = value
    else:
        refs[array][part] = value


def slot_shapes(counts, shape):
    shapes = []
    for count in counts:
        if count == 2:
            shapes.append(jax.ShapeDtypeStruct((2,) + shape, jnp.float32))
        else:
            shapes += [jax.ShapeDtypeStruct(shape, jnp.float32)] * 2
    return shapes


def vmem_specs(count):
    return [pl.BlockSpec(memory_space=pltpu.VMEM)] * count


def pack_kernel(slots, width, schur_ref, starts_ref, *refs):
    outs, blocks, sems = refs[:-2], refs[-2], refs[-1]
    half = width // 2
    copies = []
    for f in range(FACES):
        place = pl.ds(f * width, width)
        copy = pltpu.make_async_copy(schur_ref.at[place, place], blocks.at[f], sems.at[f])
        copy.start()
        copies.append(copy)
    row, col = iota((half, half), 0), iota((half, half), 1)
    for f in range(FACES):
        copies[f].wait()
        first = blocks[f, 0:half, 0:half]
        second = blocks[f, half:width, half:width]
        diag = jnp.sum(jnp.where(row == col, second, 0.0), axis=0, keepdims=True)
        mixed = jnp.where(row >= col, first, second)
        tail = jnp.broadcast_to(diag, (8, half))
        starts = starts_ref[f]
        put(
            outs,
            slots[f],
            jnp.concatenate(
                [blocks[f, half:width, 0:half], mixed, tail, starts[:, :half], starts[:, half:]],
                axis=0,
            ),
        )


def unpack(packed):
    half = packed.shape[1]
    row, col = iota((half, half), 0), iota((half, half), 1)
    low = packed[0:half]
    mixed = packed[half : 2 * half]
    flip = mixed.T
    first = jnp.where(row >= col, mixed, flip)
    second = jnp.where(row < col, mixed, flip)
    second = jnp.where(row == col, packed[2 * half : 2 * half + 1], second)
    return jnp.concatenate(
        [jnp.concatenate([first, low.T], axis=1), jnp.concatenate([low, second], axis=1)], axis=0
    )


def unpack_starts(packed, ncon):
    half = packed.shape[1]
    rows = packed[2 * half + 8 :]
    return jnp.concatenate([rows[:ncon], rows[ncon:]], axis=1)


def factor_inverses(grams, block=8):
    size = grams[0].shape[0]
    strips = size // 8
    lanes = 128
    full = (8, lanes)
    state = []
    for gram in grams:
        parts = [gram, jnp.where(iota((size, size), 0) == iota((size, size), 1), 1.0, 0.0)]
        if 2 * size < lanes:
            parts.append(jnp.zeros((size, lanes - 2 * size), jnp.float32))
        whole = jnp.concatenate(parts, axis=1)
        state.append([whole[8 * s : 8 * s + 8] for s in range(strips)])
    below = iota(full, 0)

    def line_of(strip, line):
        return jnp.broadcast_to(strip[line : line + 1], full)

    for start in range(0, size, block):
        strip, first = start // 8, start % 8
        active = range(strip, strips)
        for work in state:
            cols = [
                {s: jnp.broadcast_to(work[s][:, start + j : start + j + 1], full) for s in active}
                for j in range(block)
            ]
            factors = []

            def eliminate(j, scale, stop):
                line = first + j
                factor = {s: cols[j][s] * scale for s in active}
                factor[strip] = jnp.where(below > line, factor[strip], 0.0)
                for later in range(j + 1, stop):
                    head = line_of(cols[later][strip], line)
                    for s in active:
                        cols[later][s] = cols[later][s] - factor[s] * head
                factors.append(factor)

            for j in range(0, block, 2):
                line = first + j
                corner = line_of(cols[j][strip], line)
                side = line_of(cols[j][strip], line + 1)
                last = line_of(cols[j + 1][strip], line + 1)
                inverse = 1.0 / (corner * last - side * side)
                eliminate(j, 1.0 / corner, block)
                eliminate(j + 1, corner * inverse, block)
            for j in range(block):
                row = line_of(work[strip], first + j)
                for s in active:
                    if s == strip and first + j == 7:
                        continue
                    work[s] = work[s] - factors[j][s] * row
    results = []
    for work in state:
        parts = []
        for s in range(strips):
            place = iota((8, size), 0) + 8 * s == iota((8, size), 1)
            pivot = jnp.sum(jnp.where(place, work[s][:, :size], 0.0), axis=1, keepdims=True)
            parts.append(work[s][:, size : 2 * size] * lax.rsqrt(pivot))
        results.append(jnp.concatenate(parts, axis=0))
    return results


def subspace(before, inverse, after, starts):
    basis = starts
    for sweep in range(SUB_ITERS):
        for matrices in (before, inverse, after):
            for f in range(FACES):
                basis[f] = thin(stacked(basis[f]), (matrices[f, 0], matrices[f, 1]))
        for f in range(FACES):
            norm = jnp.sum(basis[f] * basis[f], axis=1, keepdims=True)
            basis[f] = basis[f] * lax.rsqrt(norm)
    return basis


def main_kernel(where, arrays, width, schur_ref, *refs):
    inputs = refs[:arrays]
    starts_ref, resid_ref = refs[arrays : arrays + 2]
    payload_ref, product_ref, own_out, partner_out, inverse_out = refs[arrays + 2 : arrays + 7]
    own_ref, upper_ref, guess_ref, sum_ref, own_sems, upper_sems = refs[arrays + 7 :]
    ncon = starts_ref.shape[1]
    columns = resid_ref.shape[1]
    copies = []
    for f in range(FACES):
        place = pl.ds(f * width, width)
        copy = pltpu.make_async_copy(schur_ref.at[place, place], own_ref.at[f], own_sems.at[f])
        copy.start()
        copies.append(copy)
    strips = []
    for f in range(FACES - 1):
        rest = (FACES - 1 - f) * width
        copy = pltpu.make_async_copy(
            schur_ref.at[pl.ds(f * width, width), pl.ds((f + 1) * width, rest)],
            upper_ref.at[f, :, pl.ds((f + 1) * width, rest)],
            upper_sems.at[f],
        )
        copy.start()
        strips.append(copy)
    eye = iota((width, width), 0) == iota((width, width), 1)

    def store(ref, f, value):
        ref[f, 0], ref[f, 1] = split(value)

    for f in range(FACES):
        partner = unpack(pick(inputs, where[f]))
        copies[f].wait()
        own = own_ref[f]
        total = own + partner
        store(own_out, f, own)
        store(partner_out, f, partner)
        store(sum_ref, f, total)
        diagonal = jnp.where(eye, total, 0.0)
        across = 1.0 / jnp.sum(diagonal, axis=0, keepdims=True)
        down = 1.0 / jnp.sum(diagonal, axis=1, keepdims=True)
        guess_ref[f] = jnp.where(eye, 2.0 * across, 0.0) - down * total * across
    for sweep in range(NS_ITERS - 1):
        for f in range(FACES):
            guess = guess_ref[f]
            halves = split(guess)
            product = split(wide((sum_ref[f, 0], sum_ref[f, 1]), halves))
            guess = 2.0 * guess - wide(halves, product)
            if sweep < NS_ITERS - 2:
                guess_ref[f] = guess
            else:
                store(inverse_out, f, guess)
    basis = subspace(
        partner_out, inverse_out, own_out, [starts_ref[f] for f in range(FACES)]
    )
    grams = [dot(b, b, ((1,), (1,))) for b in basis]
    for f in range(FACES - 1):
        strips[f].wait()
    sides = []
    rights = []
    for f in range(FACES):
        rows = stacked(basis[f])
        side = {f: thin(rows, (own_out[f, 0], own_out[f, 1]))}
        for g in range(f + 1, FACES):
            side[g] = thin(rows, split(upper_ref[f, :, g * width : (g + 1) * width]))
        sides.append(side)
        rights.append(thin(rows, split(resid_ref[f * width : (f + 1) * width])))
    factors = factor_inverses(grams)
    basis = [dot(factors[f], basis[f]) for f in range(FACES)]
    blocks = []
    for g in range(FACES):
        tall = jnp.concatenate([sides[f][g] for f in range(g + 1)], axis=0)
        blocks.append(dot(tall, basis[g], ((1,), (1,))))
    even, odd, right = [], [], []
    lows = None
    for f in range(FACES):
        product_ref[f] = dot(factors[f], sides[f][f])
        line = [blocks[g][f * ncon : (f + 1) * ncon] for g in range(f, FACES)]
        line = dot(factors[f], jnp.concatenate([rights[f]] + line, axis=1))
        right.append(line[:, :columns])
        line = line[:, columns:]
        if f % 2 == 0:
            even.append(line)
            lows = line[:, ncon : 2 * ncon].T
        else:
            odd += [lows, line]
    payload_ref[...] = jnp.concatenate(
        [
            jnp.concatenate(even + right[0::2], axis=1),
            jnp.concatenate(odd + right[1::2], axis=1),
        ],
        axis=0,
    )


def spread_kernel(where, arrays, *refs):
    inputs = refs[:arrays]
    product_ref, own_ref, partner_ref, inverse_ref, out_ref = refs[arrays:]
    ncon = product_ref.shape[1]
    starts = [unpack_starts(pick(inputs, where[f]), ncon) for f in range(FACES)]
    basis = subspace(own_ref, inverse_ref, partner_ref, starts)
    factors = factor_inverses([dot(b, b, ((1,), (1,))) for b in basis])
    for f in range(FACES):
        theirs = thin(stacked(basis[f]), (partner_ref[f, 0], partner_ref[f, 1]))
        both = jnp.concatenate([product_ref[f], dot(factors[f], theirs)], axis=0)
        high, low = split(thin(stacked(both), (inverse_ref[f, 0], inverse_ref[f, 1])).T)
        out_ref[f] = jnp.concatenate([high, high, low], axis=1)


def factor_kernel(size, terms, *refs):
    total = refs[0][...]
    for term in range(1, terms):
        total = total + refs[term][...]
    scale_ref, out_ref = refs[terms:]
    rows = []
    offset = 0
    for b in range(BLOCKS):
        rows.append(total[:, offset : offset + (BLOCKS - b) * size])
        offset += (BLOCKS - b) * size
    eye = iota((size, size), 0) == iota((size, size), 1)
    downs, acrosses = [], []
    for b in range(BLOCKS):
        diagonal = jnp.where(eye, rows[b][:, :size], 0.0)
        downs.append(lax.rsqrt(jnp.sum(diagonal, axis=1, keepdims=True)))
        acrosses.append(lax.rsqrt(jnp.sum(diagonal, axis=0, keepdims=True)))
    blocks = {}
    for b in range(BLOCKS):
        for c in range(b, BLOCKS):
            block = rows[b][:, (c - b) * size : (c - b + 1) * size]
            blocks[b, c] = downs[b] * block * acrosses[c]
    lower = {}
    for b in range(BLOCKS):
        (inverse,) = factor_inverses([blocks[b, b]])
        upper = {}
        for c in range(b + 1, BLOCKS):
            upper[c] = dot(inverse, blocks[b, c])
        for c in range(b + 1, BLOCKS):
            for d in range(c, BLOCKS):
                blocks[c, d] = blocks[c, d] - dot(upper[c], upper[d], ((0,), (0,)))
        lower[b, b] = inverse
        for c in range(b):
            lower[b, c] = dot(inverse, lower[b, c])
        for later in range(b + 1, BLOCKS):
            for c in range(b + 1):
                term = dot(upper[later], lower[b, c], ((0,), (0,)))
                lower[later, c] = lower[later, c] - term if c < b else -term
    for b in range(BLOCKS):
        line = [lower[b, c] if c <= b else jnp.zeros((size, size), jnp.float32) for c in range(BLOCKS)]
        out_ref[b * size : (b + 1) * size] = jnp.concatenate(line, axis=1)
        scale_ref[b * size : (b + 1) * size] = jnp.broadcast_to(downs[b], (size, 128))


def solve_kernel(size, ncon, terms, scale_ref, factor_ref, *refs):
    total = refs[0][...]
    for term in range(1, terms):
        total = total + refs[term][...]
    answer_ref, even_ref, odd_ref = refs[terms:]
    columns = answer_ref.shape[1]
    right = jnp.concatenate(
        [total[:, b * columns : (b + 1) * columns] for b in range(BLOCKS)], axis=0
    )
    scale = scale_ref[:, 0:1]
    factor = factor_ref[...]
    answer = scale * dot(factor, dot(factor, scale * right), ((0,), (0,)))
    answer_ref[...] = answer
    even_ref[...] = answer[:ncon]
    odd_ref[...] = answer[ncon : 2 * ncon]


def last_product(spread, mine, theirs):
    high, low = split(jnp.concatenate([mine, theirs], axis=0))
    return lax.dot_general(
        spread,
        jnp.concatenate([high, low, high], axis=0),
        (((1,), (0,)), ((), ())),
        preferred_element_type=jnp.float32,
    )


def last_kernel(where, arrays, ncon, spread_ref, answer_ref, *refs):
    theirs, out_ref = refs[:arrays], refs[arrays]
    width = spread_ref.shape[1]
    for f in range(FACES):
        mine = answer_ref[f * ncon : (f + 1) * ncon]
        out_ref[f * width : (f + 1) * width] = last_product(
            spread_ref[f], mine, pick(theirs, where[f])
        )


def last_pair_kernel(
    ncon, flag_ref, spread_ref, here_ref, there_ref, low_ref, high_ref, other_ref, out_ref
):
    width = spread_ref.shape[1]

    def answer(flag, f):
        place = slice(f * ncon, (f + 1) * ncon)
        return jnp.where(flag == 1, here_ref[place], there_ref[place])

    own = flag_ref[0]
    for f in range(FACES):
        if f < 2:
            near = (low_ref, high_ref)[f][...]
            theirs = jnp.where(own == 1, near, other_ref[f * ncon : (f + 1) * ncon])
        else:
            theirs = answer(flag_ref[f], f ^ 1)
        out_ref[f * width : (f + 1) * width] = last_product(spread_ref[f], answer(own, f), theirs)


def pair_sum(value, rows, planes):
    rounds = [("gy", bit) for bit in (2**i for i in range(1, rows.bit_length() - 1))]
    rounds += [("gz", bit) for bit in (2**i for i in range(planes.bit_length() - 1))]
    for axis, bit in rounds[:-1]:
        value = value + lax.ppermute(value, axis, flipped(axis, bit))
    axis, bit = rounds[-1]
    return [value, lax.ppermute(value, axis, flipped(axis, bit))]


def per_device(schur, start_block, resid, group_of):
    matrix = schur[0, 0, 0]
    starts = start_block[0, 0, 0].transpose(0, 2, 1)
    right = resid[0, 0, 0]
    order, columns = right.shape
    ncon, width = starts.shape[1:]
    counts = [lax.axis_size(axis) for axis in AXES]
    slots, arrays = face_slots(counts)
    coarse = FACES * ncon
    size = 2 * ncon
    coarse_lanes = size * BLOCKS * (BLOCKS + 1) // 2
    params = pltpu.CompilerParams(vmem_limit_bytes=LIMIT)
    anywhere = pl.BlockSpec(memory_space=pl.ANY)
    halves = jax.ShapeDtypeStruct((FACES, 2, width, width), jnp.bfloat16)

    def shape(*dims):
        return jax.ShapeDtypeStruct(dims, jnp.float32)

    packed = pl.pallas_call(
        functools.partial(pack_kernel, slots, width),
        out_shape=slot_shapes(counts, (width + 8 + 2 * ncon, width // 2)),
        in_specs=[anywhere] + vmem_specs(1),
        out_specs=vmem_specs(arrays),
        scratch_shapes=[
            pltpu.VMEM((FACES, width, width), jnp.float32),
            pltpu.SemaphoreType.DMA((FACES,)),
        ],
        compiler_params=params,
    )(matrix, starts)
    got, where = swap(packed, counts)

    payload, product, own, partner, inverse = pl.pallas_call(
        functools.partial(main_kernel, where, arrays, width),
        out_shape=[
            shape(size, coarse_lanes + BLOCKS * columns),
            shape(FACES, ncon, width),
            halves,
            halves,
            halves,
        ],
        in_specs=[anywhere] + vmem_specs(arrays + 2),
        out_specs=vmem_specs(5),
        scratch_shapes=[
            pltpu.VMEM((FACES, width, width), jnp.float32),
            pltpu.VMEM((FACES - 1, width, order), jnp.float32),
            pltpu.VMEM((FACES, width, width), jnp.float32),
            pltpu.VMEM((FACES, 2, width, width), jnp.bfloat16),
            pltpu.SemaphoreType.DMA((FACES,)),
            pltpu.SemaphoreType.DMA((FACES - 1,)),
        ],
        compiler_params=params,
    )(matrix, *got, starts, right)

    spread = pl.pallas_call(
        functools.partial(spread_kernel, where, arrays),
        out_shape=jax.ShapeDtypeStruct((FACES, width, 3 * size), jnp.bfloat16),
        in_specs=vmem_specs(arrays + 4),
        out_specs=pl.BlockSpec(memory_space=pltpu.VMEM),
        compiler_params=params,
        cost_estimate=pl.CostEstimate(
            flops=4 * 10**9, bytes_accessed=10 * 2**20, transcendentals=0
        ),
    )(*got, product, own, partner, inverse)

    rows, planes = counts[1], counts[2]
    groups = group_of.shape[0] // GROUP_SIZE
    y, z = lax.axis_index("gy"), lax.axis_index("gz")
    mine = group_of[y * planes + z]
    paired = groups == 2 and rows > 1 and not (rows & (rows - 1) or planes & (planes - 1))
    if paired:
        core = y & 1
        neighbour = group_of[(y ^ 1) * planes + z]
        other = lax.ppermute(payload, "gy", flipped("gy", 1))
        part = jnp.where(mine == core, payload, 0.0) + jnp.where(neighbour == core, other, 0.0)
        matrices = pair_sum(part[:, :coarse_lanes], rows, planes)
        rights = pair_sum(part[:, coarse_lanes:], rows, planes)
    else:
        chosen = jnp.arange(groups, dtype=jnp.int32) == mine
        total = lax.psum(jnp.where(chosen[:, None, None], payload[None], 0.0), ("gy", "gz"))
        total = lax.dynamic_index_in_dim(total, mine, 0, keepdims=False)
        matrices, rights = [total[:, :coarse_lanes]], [total[:, coarse_lanes:]]

    scale, factor = pl.pallas_call(
        functools.partial(factor_kernel, size, len(matrices)),
        out_shape=[shape(coarse, 128), shape(coarse, coarse)],
        in_specs=vmem_specs(len(matrices)),
        out_specs=vmem_specs(2),
        compiler_params=params,
    )(*matrices)
    answer, even, odd = pl.pallas_call(
        functools.partial(solve_kernel, size, ncon, len(rights)),
        out_shape=[shape(coarse, columns), shape(ncon, columns), shape(ncon, columns)],
        in_specs=vmem_specs(2 + len(rights)),
        out_specs=vmem_specs(3),
        compiler_params=params,
    )(scale, factor, *rights)

    result = shape(order, columns)
    out_spec = pl.BlockSpec(memory_space=pltpu.VMEM)
    if paired:
        places = [
            y * planes + z,
            y * planes + z,
            (y + rows - 1) % rows * planes + z,
            (y + 1) % rows * planes + z,
            y * planes + (z + planes - 1) % planes,
            y * planes + (z + 1) % planes,
        ]
        flags = (group_of[jnp.stack(places)] == core).astype(jnp.int32)
        forward, backward = ring("gx")
        low = lax.ppermute(odd, "gx", forward)
        high = lax.ppermute(even, "gx", backward)
        there = lax.ppermute(answer, "gy", flipped("gy", 1))
        others = lax.ppermute(jnp.concatenate([low, high], axis=0), "gy", flipped("gy", 1))
        correction = pl.pallas_call(
            functools.partial(last_pair_kernel, ncon),
            out_shape=result,
            in_specs=[pl.BlockSpec(memory_space=pltpu.SMEM)] + vmem_specs(6),
            out_specs=out_spec,
            compiler_params=params,
        )(flags, spread, answer, there, low, high, others)
    else:
        faces = answer.reshape(FACES, ncon, columns)
        sent = []
        for position, count in enumerate(counts):
            pair = faces[2 * position : 2 * position + 2]
            sent += [pair] if count == 2 else [pair[0], pair[1]]
        their_answers, _ = swap(sent, counts)
        correction = pl.pallas_call(
            functools.partial(last_kernel, where, arrays, ncon),
            out_shape=result,
            in_specs=vmem_specs(2 + arrays),
            out_specs=out_spec,
            compiler_params=params,
        )(spread, answer, *their_answers)
    return correction[None, None, None]


def solution(mesh):
    in_specs = (
        P("gx", "gy", "gz", None, None),
        P("gx", "gy", "gz", None, None, None),
        P("gx", "gy", "gz", None, None),
        P(),
    )
    out_specs = P("gx", "gy", "gz", None, None)
    return jax.shard_map(
        per_device, mesh=mesh, in_specs=in_specs, out_specs=out_specs, check_vma=False
    )
```

```python
import functools

import jax
import jax.numpy as jnp
from jax import lax
from jax.experimental import pallas as pl
from jax.experimental.pallas import tpu as pltpu
from jax.sharding import PartitionSpec as P

NS_ITERS = 3
SUB_ITERS = 2
GROUP_SIZE = 4
FACES = 6
BLOCKS = FACES // 2
AXES = ("gx", "gy", "gz")
MIB = 1024 * 1024

precise = lax.Precision.HIGHEST


def dot(left, right, dims=((1,), (0,))):
    return lax.dot_general(
        left, right, (dims, ((), ())), precision=precise, preferred_element_type=jnp.float32
    )


def split(value):
    high = value.astype(jnp.bfloat16)
    return high, (value - high.astype(jnp.float32)).astype(jnp.bfloat16)


def wide(left, right):
    return lax.dot_general(
        jnp.concatenate([left[0], left[0], left[1]], axis=1),
        jnp.concatenate([right[0], right[1], right[0]], axis=0),
        (((1,), (0,)), ((), ())),
        preferred_element_type=jnp.float32,
    )


def stacked(value):
    return jnp.concatenate(split(value), axis=0)


def thin(rows, matrix):
    out = lax.dot_general(
        jnp.concatenate([rows, rows], axis=1),
        jnp.concatenate(matrix, axis=0),
        (((1,), (0,)), ((), ())),
        preferred_element_type=jnp.float32,
    )
    half = rows.shape[0] // 2
    return out[:half] + out[half:]


def iota(shape, dim):
    return lax.broadcasted_iota(jnp.int32, shape, dim)


def ring(axis):
    count = lax.axis_size(axis)
    forward = [(i, (i + 1) % count) for i in range(count)]
    backward = [(target, source) for source, target in forward]
    return forward, backward


def flipped(axis, bit):
    return [(i, i ^ bit) for i in range(lax.axis_size(axis))]


def face_slots(counts):
    slots = []
    arrays = 0
    for count in counts:
        if count == 2:
            slots += [(arrays, 0), (arrays, 1)]
            arrays += 1
        else:
            slots += [(arrays, None), (arrays + 1, None)]
            arrays += 2
    return slots, arrays


def swap(arrays, counts):
    slots, _ = face_slots(counts)
    got = []
    where = []
    for position, axis in enumerate(AXES):
        forward, backward = ring(axis)
        even, odd = slots[2 * position], slots[2 * position + 1]
        if counts[position] == 2:
            where += [(len(got), 1), (len(got), 0)]
            got.append(lax.ppermute(arrays[even[0]], axis, forward))
        else:
            where += [(len(got), None), (len(got) + 1, None)]
            got.append(lax.ppermute(arrays[odd[0]], axis, forward))
            got.append(lax.ppermute(arrays[even[0]], axis, backward))
    return got, where


def pick(refs, slot):
    array, part = slot
    return refs[array][...] if part is None else refs[array][part]


def put(refs, slot, value):
    array, part = slot
    if part is None:
        refs[array][...] = value
    else:
        refs[array][part] = value


def slot_shapes(counts, shape):
    shapes = []
    for count in counts:
        if count == 2:
            shapes.append(jax.ShapeDtypeStruct((2,) + shape, jnp.float32))
        else:
            shapes += [jax.ShapeDtypeStruct(shape, jnp.float32)] * 2
    return shapes


def vmem_specs(count):
    return [pl.BlockSpec(memory_space=pltpu.VMEM)] * count


def pack_kernel(slots, width, schur_ref, starts_ref, *refs):
    outs, blocks, starts, sems, start_sem = refs[:-4], refs[-4], refs[-3], refs[-2], refs[-1]
    half = width // 2
    copies = []
    for f in range(FACES):
        place = pl.ds(f * width, width)
        copy = pltpu.make_async_copy(schur_ref.at[place, place], blocks.at[f], sems.at[f])
        copy.start()
        copies.append(copy)
    start_copy = pltpu.make_async_copy(starts_ref, starts, start_sem)
    start_copy.start()
    row, col = iota((half, half), 0), iota((half, half), 1)
    start_copy.wait()
    for f in range(FACES):
        copies[f].wait()
        first = blocks[f, 0:half, 0:half]
        second = blocks[f, half:width, half:width]
        diag = jnp.sum(jnp.where(row == col, second, 0.0), axis=0, keepdims=True)
        mixed = jnp.where(row >= col, first, second)
        tail = jnp.broadcast_to(diag, (8, half))
        start = starts[f]
        put(
            outs,
            slots[f],
            jnp.concatenate(
                [blocks[f, half:width, 0:half], mixed, tail, start[:, :half], start[:, half:]],
                axis=0,
            ),
        )


def unpack(packed):
    half = packed.shape[1]
    row, col = iota((half, half), 0), iota((half, half), 1)
    low = packed[0:half]
    mixed = packed[half : 2 * half]
    flip = mixed.T
    first = jnp.where(row >= col, mixed, flip)
    second = jnp.where(row < col, mixed, flip)
    second = jnp.where(row == col, packed[2 * half : 2 * half + 1], second)
    return jnp.concatenate(
        [jnp.concatenate([first, low.T], axis=1), jnp.concatenate([low, second], axis=1)], axis=0
    )


def unpack_starts(packed, ncon):
    half = packed.shape[1]
    rows = packed[2 * half + 8 :]
    return jnp.concatenate([rows[:ncon], rows[ncon:]], axis=1)


def factor_inverses(grams, block=8):
    size = grams[0].shape[0]
    strips = size // 8
    lanes = 128
    full = (8, lanes)
    state = []
    for gram in grams:
        parts = [gram, jnp.where(iota((size, size), 0) == iota((size, size), 1), 1.0, 0.0)]
        if 2 * size < lanes:
            parts.append(jnp.zeros((size, lanes - 2 * size), jnp.float32))
        whole = jnp.concatenate(parts, axis=1)
        state.append([whole[8 * s : 8 * s + 8] for s in range(strips)])
    below = iota(full, 0)

    def line_of(strip, line):
        return jnp.broadcast_to(strip[line : line + 1], full)

    for start in range(0, size, block):
        strip, first = start // 8, start % 8
        active = range(strip, strips)
        for work in state:
            cols = [
                {s: jnp.broadcast_to(work[s][:, start + j : start + j + 1], full) for s in active}
                for j in range(block)
            ]
            factors = []

            def eliminate(j, scale, stop):
                line = first + j
                factor = {s: cols[j][s] * scale for s in active}
                factor[strip] = jnp.where(below > line, factor[strip], 0.0)
                for later in range(j + 1, stop):
                    head = line_of(cols[later][strip], line)
                    for s in active:
                        cols[later][s] = cols[later][s] - factor[s] * head
                factors.append(factor)

            for j in range(0, block, 2):
                line = first + j
                corner = line_of(cols[j][strip], line)
                side = line_of(cols[j][strip], line + 1)
                last = line_of(cols[j + 1][strip], line + 1)
                inverse = 1.0 / (corner * last - side * side)
                eliminate(j, 1.0 / corner, block)
                eliminate(j + 1, corner * inverse, block)
            for j in range(block):
                row = line_of(work[strip], first + j)
                for s in active:
                    if s == strip and first + j == 7:
                        continue
                    work[s] = work[s] - factors[j][s] * row
    results = []
    for work in state:
        parts = []
        for s in range(strips):
            place = iota((8, size), 0) + 8 * s == iota((8, size), 1)
            pivot = jnp.sum(jnp.where(place, work[s][:, :size], 0.0), axis=1, keepdims=True)
            parts.append(work[s][:, size : 2 * size] * lax.rsqrt(pivot))
        results.append(jnp.concatenate(parts, axis=0))
    return results


def store(ref, f, value):
    ref[f, 0], ref[f, 1] = split(value)


def load(ref, f):
    return ref[f, 0], ref[f, 1]


def begin(packed, copies, own_ref, own_out, partner_out, sum_ref):
    width = own_ref.shape[1]
    eye = iota((width, width), 0) == iota((width, width), 1)
    guesses = []
    for f in range(len(packed)):
        partner = unpack(packed[f])
        copies[f].wait()
        own = own_ref[f]
        total = own + partner
        store(own_out, f, own)
        store(partner_out, f, partner)
        store(sum_ref, f, total)
        diagonal = jnp.where(eye, total, 0.0)
        across = 1.0 / jnp.sum(diagonal, axis=0, keepdims=True)
        down = 1.0 / jnp.sum(diagonal, axis=1, keepdims=True)
        guesses.append(jnp.where(eye, 2.0 * across, 0.0) - down * total * across)
    return guesses


def newton(guesses, sum_ref):
    results = []
    for f, guess in enumerate(guesses):
        halves = split(guess)
        product = split(wide(load(sum_ref, f), halves))
        results.append(2.0 * guess - wide(halves, product))
    return results


def unit_rows(basis):
    return [b * lax.rsqrt(jnp.sum(b * b, axis=1, keepdims=True)) for b in basis]


def sweep_basis(before, inverse, after, basis):
    for matrices in (before, inverse, after):
        basis = [thin(stacked(b), matrix) for b, matrix in zip(basis, matrices)]
    return unit_rows(basis)


def copy_own(schur_ref, faces, width, own_ref, sems):
    copies = []
    for i, f in enumerate(faces):
        place = pl.ds(f * width, width)
        copy = pltpu.make_async_copy(schur_ref.at[place, place], own_ref.at[i], sems.at[i])
        copy.start()
        copies.append(copy)
    return copies


def early_kernel(faces, where, arrays, width, schur_ref, *refs):
    inputs = refs[:arrays]
    starts_ref = refs[arrays]
    basis_out, own_out, partner_out, inverse_out = refs[arrays + 1 : arrays + 5]
    own_ref, sum_ref, own_sems = refs[arrays + 5 :]
    count = len(faces)
    copies = copy_own(schur_ref, faces, width, own_ref, own_sems)
    packed = [pick(inputs, slot) for slot in where]
    guesses = begin(packed, copies, own_ref, own_out, partner_out, sum_ref)
    for sweep in range(NS_ITERS - 1):
        guesses = newton(guesses, sum_ref)
    for i in range(count):
        store(inverse_out, i, guesses[i])
    basis = [starts_ref[f] for f in faces]
    matrices = [[load(ref, i) for i in range(count)] for ref in (partner_out, inverse_out, own_out)]
    for sweep in range(SUB_ITERS):
        basis = sweep_basis(*matrices, basis)
    for i in range(count):
        basis_out[i] = basis[i]


def main_kernel(early, late, where, arrays, width, schur_ref, *refs):
    inputs = refs[:arrays]
    starts_ref, resid_ref, early_basis, early_own = refs[arrays : arrays + 4]
    payload_ref, product_ref, own_out, partner_out, inverse_out = refs[arrays + 4 : arrays + 9]
    own_ref, upper_ref, sum_ref, own_sems, upper_sems = refs[arrays + 9 :]
    ncon = starts_ref.shape[1]
    columns = resid_ref.shape[1]
    copies = copy_own(schur_ref, late, width, own_ref, own_sems)
    strips = {}
    for f in [*early, *late]:
        rest = (FACES - 1 - f) * width
        if not rest:
            continue
        strips[f] = pltpu.make_async_copy(
            schur_ref.at[pl.ds(f * width, width), pl.ds((f + 1) * width, rest)],
            upper_ref.at[f, :, pl.ds((f + 1) * width, rest)],
            upper_sems.at[f],
        )
        strips[f].start()
    sides = {}
    rights = {}
    grams = {}

    def project(f, basis, own):
        rows = stacked(basis)
        grams[f] = dot(basis, basis, ((1,), (1,)))
        side = {f: thin(rows, own)}
        for g in range(f + 1, FACES):
            side[g] = thin(rows, split(upper_ref[f, :, g * width : (g + 1) * width]))
        sides[f] = side
        rights[f] = thin(rows, split(resid_ref[f * width : (f + 1) * width]))

    packed = [pick(inputs, slot) for slot in where]
    guesses = begin(packed, copies, own_ref, own_out, partner_out, sum_ref)
    for f in early:
        if f in strips:
            strips[f].wait()
    vectors = {f: early_basis[i] for i, f in enumerate(early)}
    pending = [(f, vectors[f], load(early_own, i)) for i, f in enumerate(early)]
    for sweep in range(NS_ITERS - 1):
        guesses = newton(guesses, sum_ref)
        if pending:
            project(*pending.pop(0))
    for i in range(len(late)):
        store(inverse_out, i, guesses[i])
    basis = [starts_ref[f] for f in late]
    matrices = [
        [load(ref, i) for i in range(len(late))] for ref in (partner_out, inverse_out, own_out)
    ]
    for sweep in range(SUB_ITERS):
        basis = sweep_basis(*matrices, basis)
        if pending:
            project(*pending.pop(0))
    for item in pending:
        project(*item)
    for f in late:
        if f in strips:
            strips[f].wait()
    for i, f in enumerate(late):
        vectors[f] = basis[i]
        project(f, basis[i], load(own_out, i))
    factors = factor_inverses([grams[f] for f in range(FACES)])
    basis = [dot(factors[f], vectors[f]) for f in range(FACES)]
    blocks = []
    for g in range(FACES):
        tall = jnp.concatenate([sides[f][g] for f in range(g + 1)], axis=0)
        blocks.append(dot(tall, basis[g], ((1,), (1,))))
    even, odd, right = [], [], []
    lows = None
    for f in range(FACES):
        product_ref[f] = dot(factors[f], sides[f][f])
        line = [blocks[g][f * ncon : (f + 1) * ncon] for g in range(f, FACES)]
        line = dot(factors[f], jnp.concatenate([rights[f]] + line, axis=1))
        right.append(line[:, :columns])
        line = line[:, columns:]
        if f % 2 == 0:
            even.append(line)
            lows = line[:, ncon : 2 * ncon].T
        else:
            odd += [lows, line]
    payload_ref[...] = jnp.concatenate(
        [
            jnp.concatenate(even + right[0::2], axis=1),
            jnp.concatenate(odd + right[1::2], axis=1),
        ],
        axis=0,
    )


def find(faces, refs, f):
    for group, ref in zip(faces, refs):
        if f in group:
            return load(ref, list(group).index(f))


def theirs_kernel(faces, where, arrays, ncon, *refs):
    inputs = refs[:arrays]
    own_refs, partner_refs, inverse_refs = (refs[arrays + i : arrays + i + 2] for i in (0, 2, 4))
    basis_out = refs[arrays + 6]
    basis = [unpack_starts(pick(inputs, where[f]), ncon) for f in range(FACES)]
    matrices = [
        [find(faces, group, f) for f in range(FACES)]
        for group in (own_refs, inverse_refs, partner_refs)
    ]
    for sweep in range(SUB_ITERS):
        basis = sweep_basis(*matrices, basis)
    for f in range(FACES):
        basis_out[f] = basis[f]


def spread_kernel(faces, unread, basis_ref, product_ref, *refs):
    partner_refs, inverse_refs, out_ref = refs[0:2], refs[2:4], refs[4]
    basis = [basis_ref[f] for f in range(FACES)]
    factors = factor_inverses([dot(b, b, ((1,), (1,))) for b in basis])
    for f in range(FACES):
        product = thin(stacked(basis[f]), find(faces, partner_refs, f))
        both = jnp.concatenate([product_ref[f], dot(factors[f], product)], axis=0)
        high, low = split(thin(stacked(both), find(faces, inverse_refs, f)).T)
        out_ref[f] = jnp.concatenate([high, high, low], axis=1)


def member(group_ref, planes, dy=0, dz=0):
    y, z = lax.axis_index("gy"), lax.axis_index("gz")
    rows = lax.axis_size("gy")
    return group_ref[lax.rem(y + dy + rows, rows) * planes + lax.rem(z + dz + planes, planes)]


def choose_kernel(planes, group_ref, here_ref, there_ref, out_ref):
    core = lax.rem(lax.axis_index("gy"), 2)
    mine = member(group_ref, planes) == core
    other = member(group_ref, planes, dy=1 - 2 * core) == core
    out_ref[...] = jnp.where(mine, here_ref[...], 0.0) + jnp.where(other, there_ref[...], 0.0)


def add_kernel(first_ref, second_ref, unread, out_ref):
    out_ref[...] = first_ref[...] + second_ref[...]


def solve_kernel(size, ncon, terms, *refs):
    total = refs[0][...]
    for term in range(1, terms):
        total = total + refs[term][...]
    answer_ref, even_ref, odd_ref = refs[-3:]
    columns = answer_ref.shape[1]
    lines = []
    offset = 0
    for b in range(BLOCKS):
        lines.append(total[:, offset : offset + (BLOCKS - b) * size])
        offset += (BLOCKS - b) * size
    eye = iota((size, size), 0) == iota((size, size), 1)
    downs, acrosses = [], []
    for b in range(BLOCKS):
        diagonal = jnp.where(eye, lines[b][:, :size], 0.0)
        downs.append(lax.rsqrt(jnp.sum(diagonal, axis=1, keepdims=True)))
        acrosses.append(lax.rsqrt(jnp.sum(diagonal, axis=0, keepdims=True)))
    blocks = {}
    rights = []
    for b in range(BLOCKS):
        for c in range(b, BLOCKS):
            block = lines[b][:, (c - b) * size : (c - b + 1) * size]
            blocks[b, c] = downs[b] * block * acrosses[c]
        start = offset + b * columns
        rights.append(downs[b] * total[:, start : start + columns])
    for b in range(BLOCKS):
        (inverse,) = factor_inverses([blocks[b, b]])
        later = range(b + 1, BLOCKS)
        row = dot(inverse, jnp.concatenate([rights[b]] + [blocks[b, c] for c in later], axis=1))
        upper = {c: row[:, columns + (c - b - 1) * size : columns + (c - b) * size] for c in later}
        for c in later:
            for d in range(c, BLOCKS):
                blocks[c, d] = blocks[c, d] - dot(upper[c], upper[d], ((0,), (0,)))
            rights[c] = rights[c] - dot(upper[c], row[:, :columns], ((0,), (0,)))
        row = dot(inverse, row, ((0,), (0,)))
        rights[b] = row[:, :columns]
        for c in later:
            blocks[b, c] = row[:, columns + (c - b - 1) * size : columns + (c - b) * size]
        for i in range(b):
            for c in later:
                blocks[i, c] = blocks[i, c] - dot(blocks[i, b], blocks[b, c])
            rights[i] = rights[i] - dot(blocks[i, b], rights[b])
    answer = [downs[b] * rights[b] for b in range(BLOCKS)]
    answer_ref[...] = jnp.concatenate(answer, axis=0)
    even_ref[...] = answer[0][:ncon]
    odd_ref[...] = answer[0][ncon : 2 * ncon]


def last_product(spread, mine, theirs):
    high, low = split(jnp.concatenate([mine, theirs], axis=0))
    return lax.dot_general(
        spread,
        jnp.concatenate([high, low, high], axis=0),
        (((1,), (0,)), ((), ())),
        preferred_element_type=jnp.float32,
    )


def last_faces(spread_ref, pairs, out_ref, result, sems):
    width = spread_ref.shape[1]
    copies = []
    for f, (mine, theirs) in enumerate(pairs):
        place = pl.ds(f * width, width)
        result[f * width : (f + 1) * width] = last_product(spread_ref[f], mine, theirs)
        copy = pltpu.make_async_copy(result.at[place], out_ref.at[place], sems.at[f])
        copy.start()
        copies.append(copy)
    for copy in copies:
        copy.wait()


def last_kernel(where, arrays, ncon, spread_ref, answer_ref, *refs):
    theirs = refs[:arrays]
    pairs = [
        (answer_ref[f * ncon : (f + 1) * ncon], pick(theirs, where[f])) for f in range(FACES)
    ]
    last_faces(spread_ref, pairs, *refs[arrays:])


def last_pair_kernel(
    ncon, planes, group_ref, spread_ref, here_ref, there_ref, low_ref, high_ref, other_ref, *refs
):
    core = lax.rem(lax.axis_index("gy"), 2)

    def answer(group, f):
        place = slice(f * ncon, (f + 1) * ncon)
        return jnp.where(group == core, here_ref[place], there_ref[place])

    own = member(group_ref, planes)
    shifts = [(0, 0), (0, 0), (-1, 0), (1, 0), (0, -1), (0, 1)]
    pairs = []
    for f, (dy, dz) in enumerate(shifts):
        if f < 2:
            near = (low_ref, high_ref)[f][...]
            theirs = jnp.where(own == core, near, other_ref[f * ncon : (f + 1) * ncon])
        else:
            theirs = answer(member(group_ref, planes, dy, dz), f ^ 1)
        pairs.append((answer(own, f), theirs))
    last_faces(spread_ref, pairs, *refs)


def sum_rounds(rows, planes):
    rounds = [("gy", 2**i) for i in range(1, rows.bit_length() - 1)]
    return rounds + [("gz", 2**i) for i in range(planes.bit_length() - 1)]


def per_device(schur, start_block, resid, group_of):
    matrix = schur[0, 0, 0]
    starts = start_block[0, 0, 0].transpose(0, 2, 1)
    right = resid[0, 0, 0]
    order, columns = right.shape
    ncon, width = starts.shape[1:]
    counts = [lax.axis_size(axis) for axis in AXES]
    slots, arrays = face_slots(counts)
    coarse = FACES * ncon
    size = 2 * ncon
    lanes = size * BLOCKS * (BLOCKS + 1) // 2 + BLOCKS * columns
    anywhere = pl.BlockSpec(memory_space=pl.ANY)
    scalars = pl.BlockSpec(memory_space=pltpu.SMEM)
    early, late = (2, 3, 4, 5), (0, 1)
    faces = (early, late)

    def shape(*dims):
        return jax.ShapeDtypeStruct(dims, jnp.float32)

    def halves(count):
        return jax.ShapeDtypeStruct((count, 2, width, width), jnp.bfloat16)

    def params(mib):
        return pltpu.CompilerParams(vmem_limit_bytes=mib * MIB)

    packed = pl.pallas_call(
        functools.partial(pack_kernel, slots, width),
        out_shape=slot_shapes(counts, (width + 8 + 2 * ncon, width // 2)),
        in_specs=[anywhere, anywhere],
        out_specs=vmem_specs(arrays),
        scratch_shapes=[
            pltpu.VMEM((FACES, width, width), jnp.float32),
            pltpu.VMEM((FACES, ncon, width), jnp.float32),
            pltpu.SemaphoreType.DMA((FACES,)),
            pltpu.SemaphoreType.DMA,
        ],
        compiler_params=params(12),
    )(matrix, starts)
    got, where = swap(packed, counts)
    ahead = slots[2][0]
    got_late, got_early = got[:ahead], got[ahead:]
    where_early = [(where[f][0] - ahead, where[f][1]) for f in early]
    where_late = [where[f] for f in late]

    early_basis, early_own, early_partner, early_inverse = pl.pallas_call(
        functools.partial(early_kernel, early, where_early, len(got_early), width),
        out_shape=[shape(len(early), ncon, width)] + [halves(len(early))] * 3,
        in_specs=[anywhere] + vmem_specs(len(got_early) + 1),
        out_specs=vmem_specs(4),
        scratch_shapes=[
            pltpu.VMEM((len(early), width, width), jnp.float32),
            pltpu.VMEM((len(early), 2, width, width), jnp.bfloat16),
            pltpu.SemaphoreType.DMA((len(early),)),
        ],
        compiler_params=params(24),
    )(matrix, *got_early, starts)

    payload, product, late_own, late_partner, late_inverse = pl.pallas_call(
        functools.partial(main_kernel, early, late, where_late, len(got_late), width),
        out_shape=[shape(size, lanes), shape(FACES, ncon, width)] + [halves(len(late))] * 3,
        in_specs=[anywhere] + vmem_specs(len(got_late) + 4),
        out_specs=vmem_specs(5),
        scratch_shapes=[
            pltpu.VMEM((len(late), width, width), jnp.float32),
            pltpu.VMEM((FACES - 1, width, order), jnp.float32),
            pltpu.VMEM((len(late), 2, width, width), jnp.bfloat16),
            pltpu.SemaphoreType.DMA((len(late),)),
            pltpu.SemaphoreType.DMA((FACES - 1,)),
        ],
        compiler_params=params(32),
    )(matrix, *got_late, starts, right, early_basis, early_own)

    owns = [early_own, late_own]
    partners = [early_partner, late_partner]
    inverses = [early_inverse, late_inverse]
    theirs = pl.pallas_call(
        functools.partial(theirs_kernel, faces, where, arrays, ncon),
        out_shape=shape(FACES, ncon, width),
        in_specs=vmem_specs(arrays + 6),
        out_specs=vmem_specs(1)[0],
        compiler_params=params(20),
        cost_estimate=pl.CostEstimate(
            flops=4 * 10**9, bytes_accessed=10 * 2**20, transcendentals=0
        ),
    )(*got, *owns, *partners, *inverses)

    def spread_of(token):
        return pl.pallas_call(
            functools.partial(spread_kernel, faces),
            out_shape=jax.ShapeDtypeStruct((FACES, width, 3 * size), jnp.bfloat16),
            in_specs=[anywhere] + vmem_specs(6),
            out_specs=vmem_specs(1)[0],
            compiler_params=params(20),
            cost_estimate=pl.CostEstimate(
                flops=4 * 10**9, bytes_accessed=10 * 2**20, transcendentals=0
            ),
        )(token, theirs, product, *partners, *inverses)

    def solve(terms, unread):
        return pl.pallas_call(
            functools.partial(solve_kernel, size, ncon, len(terms)),
            out_shape=[shape(coarse, columns), shape(ncon, columns), shape(ncon, columns)],
            in_specs=vmem_specs(len(terms)) + [anywhere] * len(unread),
            out_specs=vmem_specs(3),
            compiler_params=params(12),
        )(*terms, *unread)

    rows, planes = counts[1], counts[2]
    groups = group_of.shape[0] // GROUP_SIZE
    result_scratch = [
        pltpu.VMEM((order, columns), jnp.float32),
        pltpu.SemaphoreType.DMA((FACES,)),
    ]
    if groups == 2 and rows > 1 and not (rows & (rows - 1) or planes & (planes - 1)):
        other = lax.ppermute(payload, "gy", flipped("gy", 1))
        part = pl.pallas_call(
            functools.partial(choose_kernel, planes),
            out_shape=shape(size, lanes),
            in_specs=[scalars] + vmem_specs(2),
            out_specs=vmem_specs(1)[0],
            compiler_params=params(8),
        )(group_of, payload, other)
        rounds = sum_rounds(rows, planes)
        spread = None
        for axis, bit in rounds[:-1]:
            moved = lax.ppermute(part, axis, flipped(axis, bit))
            part = pl.pallas_call(
                add_kernel,
                out_shape=shape(size, lanes),
                in_specs=vmem_specs(2) + [anywhere],
                out_specs=vmem_specs(1)[0],
                compiler_params=params(8),
            )(part, moved, theirs)
        axis, bit = rounds[-1]
        moved = lax.ppermute(part, axis, flipped(axis, bit))
        spread = spread_of(part)
        answer, even, odd = solve([part, moved], [spread])
        there = lax.ppermute(answer, "gy", flipped("gy", 1))
        forward, backward = ring("gx")
        low = lax.ppermute(odd, "gx", forward)
        high = lax.ppermute(even, "gx", backward)
        others = lax.ppermute(jnp.concatenate([low, high], axis=0), "gy", flipped("gy", 1))
        correction = pl.pallas_call(
            functools.partial(last_pair_kernel, ncon, planes),
            out_shape=shape(order, columns),
            in_specs=[scalars] + vmem_specs(6),
            out_specs=anywhere,
            scratch_shapes=result_scratch,
            compiler_params=params(8),
        )(group_of, spread, answer, there, low, high, others)
    else:
        y, z = lax.axis_index("gy"), lax.axis_index("gz")
        mine = group_of[y * planes + z]
        chosen = jnp.arange(groups, dtype=jnp.int32) == mine
        total = lax.psum(jnp.where(chosen[:, None, None], payload[None], 0.0), ("gy", "gz"))
        total = lax.dynamic_index_in_dim(total, mine, 0, keepdims=False)
        spread = spread_of(payload)
        answer, _, _ = solve([total], [])
        blocks = answer.reshape(FACES, ncon, columns)
        sent = []
        for position, count in enumerate(counts):
            pair = blocks[2 * position : 2 * position + 2]
            sent += [pair] if count == 2 else [pair[0], pair[1]]
        their_answers, _ = swap(sent, counts)
        correction = pl.pallas_call(
            functools.partial(last_kernel, where, arrays, ncon),
            out_shape=shape(order, columns),
            in_specs=vmem_specs(2 + arrays),
            out_specs=anywhere,
            scratch_shapes=result_scratch,
            compiler_params=params(8),
        )(spread, answer, *their_answers)
    return correction[None, None, None]


def solution(mesh):
    in_specs = (
        P("gx", "gy", "gz", None, None),
        P("gx", "gy", "gz", None, None, None),
        P("gx", "gy", "gz", None, None),
        P(),
    )
    out_specs = P("gx", "gy", "gz", None, None)
    return jax.shard_map(
        per_device, mesh=mesh, in_specs=in_specs, out_specs=out_specs, check_vma=False
    )
```

```python
import functools

import jax
import jax.numpy as jnp
from jax import lax
from jax.experimental import pallas as pl
from jax.experimental.pallas import tpu as pltpu
from jax.sharding import PartitionSpec as P

NS_ITERS = 3
SUB_ITERS = 2
GROUP_SIZE = 4
FACES = 6
BLOCKS = FACES // 2
AXES = ("gx", "gy", "gz")
MIB = 1024 * 1024

precise = lax.Precision.HIGHEST


def dot(left, right, dims=((1,), (0,))):
    return lax.dot_general(
        left, right, (dims, ((), ())), precision=precise, preferred_element_type=jnp.float32
    )


def split(value):
    high = value.astype(jnp.bfloat16)
    return high, (value - high.astype(jnp.float32)).astype(jnp.bfloat16)


def wide(left, right):
    return lax.dot_general(
        jnp.concatenate([left[0], left[0], left[1]], axis=1),
        jnp.concatenate([right[0], right[1], right[0]], axis=0),
        (((1,), (0,)), ((), ())),
        preferred_element_type=jnp.float32,
    )


def stacked(value):
    return jnp.concatenate(split(value), axis=0)


def thin(rows, matrix):
    out = lax.dot_general(
        jnp.concatenate([rows, rows], axis=1),
        jnp.concatenate(matrix, axis=0),
        (((1,), (0,)), ((), ())),
        preferred_element_type=jnp.float32,
    )
    half = rows.shape[0] // 2
    return out[:half] + out[half:]


def iota(shape, dim):
    return lax.broadcasted_iota(jnp.int32, shape, dim)


def flipped(axis, bit):
    return [(i, i ^ bit) for i in range(lax.axis_size(axis))]


def outer_pairs(axis):
    count = lax.axis_size(axis)
    return [(i, (i + 1 if i % 2 else i - 1) % count) for i in range(count)]


def face_arrays(count):
    return 1 if count == 2 else 2


def exchange(arrays, axis):
    if lax.axis_size(axis) == 2:
        return [lax.ppermute(arrays[0], axis, flipped(axis, 1))]
    return [
        lax.ppermute(arrays[0], axis, flipped(axis, 1)),
        lax.ppermute(arrays[1], axis, outer_pairs(axis)),
    ]


def is_even(axis):
    return lax.rem(lax.axis_index(axis), 2) == 0


def send(refs, axis, even, odd):
    if lax.axis_size(axis) == 2:
        refs[0][0] = even
        refs[0][1] = odd
    else:
        upward = is_even(axis)
        refs[0][...] = jnp.where(upward, odd, even)
        refs[1][...] = jnp.where(upward, even, odd)


def receive(refs, axis):
    if lax.axis_size(axis) == 2:
        return refs[0][1], refs[0][0]
    upward = is_even(axis)
    first, second = refs[0][...], refs[1][...]
    return jnp.where(upward, second, first), jnp.where(upward, first, second)


def face_shapes(count, shape):
    if count == 2:
        return [jax.ShapeDtypeStruct((2,) + shape, jnp.float32)]
    return [jax.ShapeDtypeStruct(shape, jnp.float32)] * 2


def vmem_specs(count):
    return [pl.BlockSpec(memory_space=pltpu.VMEM)] * count


def pack_kernel(counts, width, schur_ref, starts_ref, *refs):
    outs, blocks = refs[:-4], refs[-4]
    starts, sems, start_sem = refs[-3:]
    half = width // 2
    copies = []
    for f in range(FACES):
        place = pl.ds(f * width, width)
        copy = pltpu.make_async_copy(schur_ref.at[place, place], blocks.at[f], sems.at[f])
        copy.start()
        copies.append(copy)
    start_copy = pltpu.make_async_copy(starts_ref, starts, start_sem)
    start_copy.start()
    row, col = iota((half, half), 0), iota((half, half), 1)
    start_copy.wait()

    def pack(f):
        copies[f].wait()
        first = blocks[f, 0:half, 0:half]
        second = blocks[f, half:width, half:width]
        diag = jnp.sum(jnp.where(row == col, second, 0.0), axis=0, keepdims=True)
        mixed = jnp.where(row >= col, first, second)
        tail = jnp.broadcast_to(diag, (8, half))
        start = starts[f]
        return jnp.concatenate(
            [blocks[f, half:width, 0:half], mixed, tail, start[:, :half], start[:, half:]], axis=0
        )

    done = 0
    for position, axis in enumerate(AXES):
        number = face_arrays(counts[position])
        send(outs[done : done + number], axis, pack(2 * position), pack(2 * position + 1))
        done += number


def unpack(packed):
    half = packed.shape[1]
    row, col = iota((half, half), 0), iota((half, half), 1)
    low = packed[0:half]
    mixed = packed[half : 2 * half]
    flip = mixed.T
    first = jnp.where(row >= col, mixed, flip)
    second = jnp.where(row < col, mixed, flip)
    second = jnp.where(row == col, packed[2 * half : 2 * half + 1], second)
    return jnp.concatenate(
        [jnp.concatenate([first, low.T], axis=1), jnp.concatenate([low, second], axis=1)], axis=0
    )


def unpack_starts(packed, ncon):
    half = packed.shape[1]
    rows = packed[2 * half + 8 :]
    return jnp.concatenate([rows[:ncon], rows[ncon:]], axis=1)


def factor_inverses(grams, block=8, invert=False):
    size = grams[0].shape[0]
    strips = size // 8
    lanes = 128
    full = (8, lanes)
    state = []
    for gram in grams:
        parts = [gram, jnp.where(iota((size, size), 0) == iota((size, size), 1), 1.0, 0.0)]
        if 2 * size < lanes:
            parts.append(jnp.zeros((size, lanes - 2 * size), jnp.float32))
        whole = jnp.concatenate(parts, axis=1)
        state.append([whole[8 * s : 8 * s + 8] for s in range(strips)])
    below = iota(full, 0)

    def line_of(strip, line):
        return jnp.broadcast_to(strip[line : line + 1], full)

    for start in range(0, size, block):
        strip, first = start // 8, start % 8
        active = range(0 if invert else strip, strips)
        for work in state:
            cols = [
                {s: jnp.broadcast_to(work[s][:, start + j : start + j + 1], full) for s in active}
                for j in range(block)
            ]
            factors = []

            def eliminate(j, scale, stop):
                line = first + j
                factor = {s: cols[j][s] * scale for s in active}
                hit = below != line if invert else below > line
                factor[strip] = jnp.where(hit, factor[strip], 0.0)
                for later in range(j + 1, stop):
                    head = line_of(cols[later][strip], line)
                    for s in active:
                        cols[later][s] = cols[later][s] - factor[s] * head
                factors.append(factor)

            for j in range(0, block, 2):
                line = first + j
                corner = line_of(cols[j][strip], line)
                side = line_of(cols[j][strip], line + 1)
                last = line_of(cols[j + 1][strip], line + 1)
                inverse = 1.0 / (corner * last - side * side)
                eliminate(j, 1.0 / corner, block)
                eliminate(j + 1, corner * inverse, block)
            for j in range(block):
                row = line_of(work[strip], first + j)
                for s in active:
                    if s == strip and first + j == 7 and not invert:
                        continue
                    work[s] = work[s] - factors[j][s] * row
    results = []
    for work in state:
        parts = []
        for s in range(strips):
            place = iota((8, size), 0) + 8 * s == iota((8, size), 1)
            pivot = jnp.sum(jnp.where(place, work[s][:, :size], 0.0), axis=1, keepdims=True)
            scale = 1.0 / pivot if invert else lax.rsqrt(pivot)
            parts.append(work[s][:, size : 2 * size] * scale)
        results.append(jnp.concatenate(parts, axis=0))
    return results


def member(group_ref, planes, dy=0, dz=0):
    y, z = lax.axis_index("gy"), lax.axis_index("gz")
    rows = lax.axis_size("gy")
    return group_ref[lax.rem(y + dy + rows, rows) * planes + lax.rem(z + dz + planes, planes)]


def store(ref, f, value):
    ref[f, 0], ref[f, 1] = split(value)


def load(ref, f):
    return ref[f, 0], ref[f, 1]


def upper_index(f, g):
    return sum(FACES - 1 - i for i in range(f)) + g - f - 1


def halves_kernel(planes, schur_ref, group_ref, own_ref, own_out, upper_out, flag_out, *scratch):
    upper_ref, sems = scratch
    width = own_ref.shape[1]
    strips = []
    for f in range(FACES - 1):
        rest = (FACES - 1 - f) * width
        copy = pltpu.make_async_copy(
            schur_ref.at[pl.ds(f * width, width), pl.ds((f + 1) * width, rest)],
            upper_ref.at[f, :, pl.ds((f + 1) * width, rest)],
            sems.at[f],
        )
        copy.start()
        strips.append(copy)
    core = lax.rem(lax.axis_index("gy"), 2)
    near = [(0, 0), (1 - 2 * core, 0), (-1, 0), (1, 0), (0, -1), (0, 1)]
    row = iota(flag_out.shape, 0)
    flags = jnp.zeros(flag_out.shape, jnp.float32)
    for i, (dy, dz) in enumerate(near):
        hit = member(group_ref, planes, dy, dz) == core
        flags = jnp.where(row == i, jnp.where(hit, 1.0, 0.0), flags)
    flag_out[...] = flags
    for f in range(FACES):
        store(own_out, f, own_ref[f])
    for f in range(FACES - 1):
        strips[f].wait()
        for g in range(f + 1, FACES):
            store(upper_out, upper_index(f, g), upper_ref[f, :, g * width : (g + 1) * width])


def begin(packed, owns, partner_out, sum_ref):
    width = owns[0].shape[1]
    eye = iota((width, width), 0) == iota((width, width), 1)
    guesses = []
    for f in range(len(packed)):
        partner = unpack(packed[f])
        total = owns[f] + partner
        store(partner_out, f, partner)
        store(sum_ref, f, total)
        diagonal = jnp.where(eye, total, 0.0)
        across = 1.0 / jnp.sum(diagonal, axis=0, keepdims=True)
        down = 1.0 / jnp.sum(diagonal, axis=1, keepdims=True)
        guesses.append(jnp.where(eye, 2.0 * across, 0.0) - down * total * across)
    return guesses


def newton(guesses, sum_ref):
    results = []
    for f, guess in enumerate(guesses):
        halves = split(guess)
        product = split(wide(load(sum_ref, f), halves))
        results.append(2.0 * guess - wide(halves, product))
    return results


def unit_rows(basis):
    return [b * lax.rsqrt(jnp.sum(b * b, axis=1, keepdims=True)) for b in basis]


def sweep_basis(before, inverse, after, basis):
    for matrices in (before, inverse, after):
        basis = [thin(stacked(b), matrix) for b, matrix in zip(basis, matrices)]
    return unit_rows(basis)


def early_kernel(axes, faces, *refs):
    arrays = len(refs) - 7
    inputs = refs[:arrays]
    own_ref, halves_ref, starts_ref, basis_out, partner_out, inverse_out, sum_ref = refs[arrays:]
    count = len(faces)
    packed = []
    done = 0
    for axis in axes:
        number = face_arrays(lax.axis_size(axis))
        packed += receive(inputs[done : done + number], axis)
        done += number
    guesses = begin(packed, [own_ref[f] for f in faces], partner_out, sum_ref)
    for sweep in range(NS_ITERS - 1):
        guesses = newton(guesses, sum_ref)
    for i in range(count):
        store(inverse_out, i, guesses[i])
    basis = [starts_ref[f] for f in faces]
    matrices = [
        [load(partner_out, i) for i in range(count)],
        [load(inverse_out, i) for i in range(count)],
        [load(halves_ref, f) for f in faces],
    ]
    for sweep in range(SUB_ITERS):
        basis = sweep_basis(*matrices, basis)
    for i in range(count):
        basis_out[i] = basis[i]


def main_kernel(axes, early, late, *refs):
    arrays = len(refs) - 11
    inputs = refs[:arrays]
    own_ref, halves_ref, upper_ref, starts_ref, resid_ref, early_basis = refs[arrays : arrays + 6]
    payload_ref, product_ref, partner_out, inverse_out, sum_ref = refs[arrays + 6 :]
    ncon, width = starts_ref.shape[1:]
    columns = resid_ref.shape[1]
    sides = {}
    rights = {}
    grams = {}
    vectors = {}
    count = len(late)

    def project(f, basis):
        vectors[f] = basis
        rows = stacked(basis)
        grams[f] = dot(basis, basis, ((1,), (1,)))
        side = {f: thin(rows, load(halves_ref, f))}
        for g in range(f + 1, FACES):
            side[g] = thin(rows, load(upper_ref, upper_index(f, g)))
        sides[f] = side
        rights[f] = thin(rows, split(resid_ref[f * width : (f + 1) * width]))

    packed = []
    done = 0
    for axis in axes:
        number = face_arrays(lax.axis_size(axis))
        packed += receive(inputs[done : done + number], axis)
        done += number
    guesses = begin(packed, [own_ref[f] for f in late], partner_out, sum_ref)
    pending = [(f, early_basis[i]) for i, f in enumerate(early)]
    for sweep in range(NS_ITERS - 1):
        guesses = newton(guesses, sum_ref)
        if pending:
            project(*pending.pop(0))
    for i in range(count):
        store(inverse_out, i, guesses[i])
    basis = [starts_ref[f] for f in late]
    matrices = [
        [load(partner_out, i) for i in range(count)],
        [load(inverse_out, i) for i in range(count)],
        [load(halves_ref, f) for f in late],
    ]
    for sweep in range(SUB_ITERS):
        basis = sweep_basis(*matrices, basis)
        if pending:
            project(*pending.pop(0))
    for item in pending:
        project(*item)
    for i, f in enumerate(late):
        project(f, basis[i])
    factors = factor_inverses([grams[f] for f in range(FACES)])
    blocks = []
    for g in range(FACES):
        tall = jnp.concatenate([sides[f][g] for f in range(g + 1)], axis=0)
        blocks.append(dot(dot(tall, vectors[g], ((1,), (1,))), factors[g], ((1,), (1,))))
    even, odd, right = [], [], []
    lows = None
    for f in range(FACES):
        product_ref[f] = dot(factors[f], sides[f][f])
        line = [blocks[g][f * ncon : (f + 1) * ncon] for g in range(f, FACES)]
        line = dot(factors[f], jnp.concatenate([rights[f]] + line, axis=1))
        right.append(line[:, :columns])
        line = line[:, columns:]
        if f % 2 == 0:
            even.append(line)
            lows = line[:, ncon : 2 * ncon].T
        else:
            odd += [lows, line]
    payload_ref[...] = jnp.concatenate(
        [
            jnp.concatenate(even + right[0::2], axis=1),
            jnp.concatenate(odd + right[1::2], axis=1),
        ],
        axis=0,
    )


def find(faces, refs, f):
    for group, ref in zip(faces, refs):
        if f in group:
            return load(ref, list(group).index(f))


def theirs_kernel(faces, ncon, *refs):
    arrays = len(refs) - 7
    inputs = refs[:arrays]
    own_ref, partner_refs, inverse_refs = refs[arrays], refs[-6:-4], refs[-4:-2]
    basis_out, product_out = refs[-2:]
    basis = []
    done = 0
    for axis in AXES:
        number = face_arrays(lax.axis_size(axis))
        packed = receive(inputs[done : done + number], axis)
        basis += [unpack_starts(part, ncon) for part in packed]
        done += number
    matrices = [
        [load(own_ref, f) for f in range(FACES)],
        [find(faces, inverse_refs, f) for f in range(FACES)],
        [find(faces, partner_refs, f) for f in range(FACES)],
    ]
    for sweep in range(SUB_ITERS):
        basis = sweep_basis(*matrices, basis)
    for f in range(FACES):
        basis_out[f] = basis[f]
        product_out[f] = thin(stacked(basis[f]), matrices[2][f])


def spread_kernel(faces, unread, basis_ref, theirs_ref, product_ref, *refs):
    inverse_refs, out_ref = refs[0:2], refs[2]
    basis = [basis_ref[f] for f in range(FACES)]
    factors = factor_inverses([dot(b, b, ((1,), (1,))) for b in basis])
    for f in range(FACES):
        both = jnp.concatenate([product_ref[f], dot(factors[f], theirs_ref[f])], axis=0)
        high, low = split(thin(stacked(both), find(faces, inverse_refs, f)).T)
        out_ref[f] = jnp.concatenate([high, high, low], axis=1)


def choose_kernel(flag_ref, here_ref, there_ref, matrix_ref, right_ref):
    mine = flag_ref[0:1, 0:1] > 0.5
    other = flag_ref[1:2, 0:1] > 0.5
    total = jnp.where(mine, here_ref[...], 0.0) + jnp.where(other, there_ref[...], 0.0)
    lanes = matrix_ref.shape[1]
    matrix_ref[...] = total[:, :lanes]
    right_ref[...] = total[:, lanes:]


def add_kernel(first_ref, second_ref, third_ref, fourth_ref, unread, matrix_ref, right_ref):
    matrix_ref[...] = first_ref[...] + second_ref[...]
    right_ref[...] = third_ref[...] + fourth_ref[...]


def solve_kernel(size, ncon, terms, *refs):
    matrix, right = refs[0][...], refs[terms][...]
    for term in range(1, terms):
        matrix = matrix + refs[term][...]
        right = right + refs[terms + term][...]
    answer_ref, sent = refs[2 * terms + 1], refs[2 * terms + 2 :]
    columns = answer_ref.shape[1]
    lines = []
    offset = 0
    for b in range(BLOCKS):
        lines.append(matrix[:, offset : offset + (BLOCKS - b) * size])
        offset += (BLOCKS - b) * size
    eye = iota((size, size), 0) == iota((size, size), 1)
    downs, acrosses = [], []
    for b in range(BLOCKS):
        diagonal = jnp.where(eye, lines[b][:, :size], 0.0)
        downs.append(lax.rsqrt(jnp.sum(diagonal, axis=1, keepdims=True)))
        acrosses.append(lax.rsqrt(jnp.sum(diagonal, axis=0, keepdims=True)))
    blocks = {}
    rights = []
    for b in range(BLOCKS):
        for c in range(b, BLOCKS):
            block = lines[b][:, (c - b) * size : (c - b + 1) * size]
            blocks[b, c] = downs[b] * block * acrosses[c]
            if c > b:
                blocks[c, b] = blocks[b, c].T
        rights.append(downs[b] * right[:, b * columns : (b + 1) * columns])
    for b in range(BLOCKS):
        (inverse,) = factor_inverses([blocks[b, b]], invert=True)
        later = range(b + 1, BLOCKS)
        row = dot(inverse, jnp.concatenate([rights[b]] + [blocks[b, c] for c in later], axis=1))
        rights[b] = row[:, :columns]
        for c in later:
            start = columns + (c - b - 1) * size
            blocks[b, c] = row[:, start : start + size]
        for i in range(BLOCKS):
            if i == b:
                continue
            change = dot(blocks[i, b], row)
            rights[i] = rights[i] - change[:, :columns]
            for c in later:
                start = columns + (c - b - 1) * size
                blocks[i, c] = blocks[i, c] - change[:, start : start + size]
    answer = [downs[b] * rights[b] for b in range(BLOCKS)]
    answer_ref[...] = jnp.concatenate(answer, axis=0)
    if sent:
        send(sent, AXES[0], answer[0][:ncon], answer[0][ncon : 2 * ncon])


def last_product(spread, mine, theirs):
    high, low = split(jnp.concatenate([mine, theirs], axis=0))
    return lax.dot_general(
        spread,
        jnp.concatenate([high, low, high], axis=0),
        (((1,), (0,)), ((), ())),
        preferred_element_type=jnp.float32,
    )


def last_faces(spread_ref, pairs, out_ref, result, sems):
    width = spread_ref.shape[1]
    copies = []
    for f, (mine, theirs) in pairs.items():
        place = pl.ds(f * width, width)
        result[f * width : (f + 1) * width] = last_product(spread_ref[f], mine, theirs)
        copy = pltpu.make_async_copy(result.at[place], out_ref.at[place], sems.at[f])
        copy.start()
        copies.append(copy)
    for copy in copies:
        copy.wait()


def last_kernel(ncon, spread_ref, answer_ref, *refs):
    inputs, rest = refs[:-3], refs[-3:]
    pairs = {}
    done = 0
    for position, axis in enumerate(AXES):
        number = face_arrays(lax.axis_size(axis))
        near = receive(inputs[done : done + number], axis)
        done += number
        for f, theirs in zip((2 * position, 2 * position + 1), near):
            pairs[f] = (answer_ref[f * ncon : (f + 1) * ncon], theirs)
    last_faces(spread_ref, pairs, *rest)


def last_near_kernel(ncon, flag_ref, spread_ref, here_ref, there_ref, *refs):
    def answer(flag, f):
        place = slice(f * ncon, (f + 1) * ncon)
        hit = flag_ref[flag : flag + 1, 0:1] > 0.5
        return jnp.where(hit, here_ref[place], there_ref[place])

    pairs = {f: (answer(0, f), answer(f, f ^ 1)) for f in range(2, FACES)}
    last_faces(spread_ref, pairs, *refs)


def last_far_kernel(ncon, flag_ref, spread_ref, here_ref, there_ref, *refs):
    arrays = (len(refs) - 4) // 2
    same, other = refs[:arrays], refs[arrays : 2 * arrays]
    hit = flag_ref[0:1, 0:1] > 0.5
    pairs = {}
    for f, near, far in zip((0, 1), receive(same, AXES[0]), receive(other, AXES[0])):
        place = slice(f * ncon, (f + 1) * ncon)
        mine = jnp.where(hit, here_ref[place], there_ref[place])
        pairs[f] = (mine, jnp.where(hit, near, far))
    last_faces(spread_ref, pairs, *refs[2 * arrays + 1 :])


def sum_rounds(rows, planes):
    rounds = [("gy", 2**i) for i in range(1, rows.bit_length() - 1)]
    return rounds + [("gz", 2**i) for i in range(planes.bit_length() - 1)]


def per_device(schur, start_block, resid, group_of):
    matrix = schur[0, 0, 0]
    matrix = pltpu.with_memory_space_constraint(matrix, pltpu.HBM)
    starts = start_block[0, 0, 0].transpose(0, 2, 1)
    right = resid[0, 0, 0]
    order, columns = right.shape
    ncon, width = starts.shape[1:]
    counts = [lax.axis_size(axis) for axis in AXES]
    arrays = sum(face_arrays(count) for count in counts)
    coarse = FACES * ncon
    size = 2 * ncon
    lanes = size * BLOCKS * (BLOCKS + 1) // 2
    uppers = FACES * (FACES - 1) // 2
    anywhere = pl.BlockSpec(memory_space=pl.ANY)
    main_memory = pl.BlockSpec(memory_space=pltpu.HBM)
    scalars = pl.BlockSpec(memory_space=pltpu.SMEM)
    early, late = (2, 3), (0, 1, 4, 5)
    faces = (early, late)
    planes = counts[2]

    def shape(*dims):
        return jax.ShapeDtypeStruct(dims, jnp.float32)

    def halves(count):
        return jax.ShapeDtypeStruct((count, 2, width, width), jnp.bfloat16)

    def params(mib):
        return pltpu.CompilerParams(vmem_limit_bytes=mib * MIB)

    def cost(us):
        return pl.CostEstimate(flops=us * 10**9, bytes_accessed=2**20, transcendentals=0)

    *packed, own = pl.pallas_call(
        functools.partial(pack_kernel, counts, width),
        out_shape=[
            part
            for count in counts
            for part in face_shapes(count, (width + 8 + 2 * ncon, width // 2))
        ]
        + [shape(FACES, width, width)],
        in_specs=[main_memory, main_memory],
        out_specs=vmem_specs(arrays + 1),
        scratch_shapes=[
            pltpu.VMEM((FACES, ncon, width), jnp.float32),
            pltpu.SemaphoreType.DMA((FACES,)),
            pltpu.SemaphoreType.DMA,
        ],
        compiler_params=params(12),
    )(matrix, pltpu.with_memory_space_constraint(starts, pltpu.HBM))
    got = []
    for axis in AXES:
        number = face_arrays(lax.axis_size(axis))
        got.append(exchange(packed[:number], axis))
        packed = packed[number:]

    own_halves, upper_halves, flags = pl.pallas_call(
        functools.partial(halves_kernel, planes),
        out_shape=[halves(FACES), halves(uppers), shape(8, 128)],
        in_specs=[main_memory, scalars] + vmem_specs(1),
        out_specs=vmem_specs(3),
        scratch_shapes=[
            pltpu.VMEM((FACES - 1, width, order), jnp.float32),
            pltpu.SemaphoreType.DMA((FACES - 1,)),
        ],
        compiler_params=params(24),
        cost_estimate=cost(2),
    )(matrix, group_of, own)

    early_basis, early_partner, early_inverse = pl.pallas_call(
        functools.partial(early_kernel, AXES[1:2], early),
        out_shape=[shape(len(early), ncon, width)] + [halves(len(early))] * 2,
        in_specs=vmem_specs(len(got[1]) + 3),
        out_specs=vmem_specs(3),
        scratch_shapes=[pltpu.VMEM((len(early), 2, width, width), jnp.bfloat16)],
        compiler_params=params(16),
        cost_estimate=cost(2),
    )(*got[1], own, own_halves, starts)

    payload, product, late_partner, late_inverse = pl.pallas_call(
        functools.partial(main_kernel, (AXES[0], AXES[2]), early, late),
        out_shape=[shape(size, lanes + BLOCKS * columns), shape(FACES, ncon, width)]
        + [halves(len(late))] * 2,
        in_specs=vmem_specs(len(got[0]) + len(got[2]) + 6),
        out_specs=vmem_specs(4),
        scratch_shapes=[pltpu.VMEM((len(late), 2, width, width), jnp.bfloat16)],
        compiler_params=params(24),
        cost_estimate=cost(8),
    )(*got[0], *got[2], own, own_halves, upper_halves, starts, right, early_basis)

    partners = [early_partner, late_partner]
    inverses = [early_inverse, late_inverse]
    their_basis, their_product = pl.pallas_call(
        functools.partial(theirs_kernel, faces, ncon),
        out_shape=[shape(FACES, ncon, width)] * 2,
        in_specs=vmem_specs(arrays + 5),
        out_specs=vmem_specs(2),
        compiler_params=params(16),
        cost_estimate=cost(2),
    )(*got[0], *got[1], *got[2], own_halves, *partners, *inverses)

    def spread_of(token):
        return pl.pallas_call(
            functools.partial(spread_kernel, faces),
            out_shape=jax.ShapeDtypeStruct((FACES, width, 3 * size), jnp.bfloat16),
            in_specs=[anywhere] + vmem_specs(5),
            out_specs=vmem_specs(1)[0],
            compiler_params=params(16),
            cost_estimate=cost(3),
        )(token, their_basis, their_product, product, *inverses)

    def solve(matrices, rights, token, sent):
        return pl.pallas_call(
            functools.partial(solve_kernel, size, ncon, len(matrices)),
            out_shape=[shape(coarse, columns)] + sent,
            in_specs=vmem_specs(2 * len(matrices)) + [anywhere],
            out_specs=vmem_specs(1 + len(sent)),
            compiler_params=params(12),
            cost_estimate=cost(7),
        )(*matrices, *rights, token)

    result = dict(
        out_shape=shape(order, columns),
        out_specs=main_memory,
        scratch_shapes=[
            pltpu.VMEM((order, columns), jnp.float32),
            pltpu.SemaphoreType.DMA((FACES,)),
        ],
        compiler_params=params(8),
        cost_estimate=cost(1),
    )
    rows = counts[1]
    groups = group_of.shape[0] // GROUP_SIZE
    if groups == 2 and rows > 1 and not (rows & (rows - 1) or planes & (planes - 1)):
        other = lax.ppermute(payload, "gy", flipped("gy", 1))
        pair_shape = [shape(size, lanes), shape(size, BLOCKS * columns)]
        left, rest = pl.pallas_call(
            choose_kernel,
            out_shape=pair_shape,
            in_specs=vmem_specs(3),
            out_specs=vmem_specs(2),
            compiler_params=params(8),
        )(flags, payload, other)
        rounds = sum_rounds(rows, planes)
        for step in range(len(rounds)):
            axis, bit = rounds[step]
            left_moved = lax.ppermute(left, axis, flipped(axis, bit))
            axis, bit = rounds[-1 - step]
            rest_moved = lax.ppermute(rest, axis, flipped(axis, bit))
            if step == len(rounds) - 1:
                break
            left, rest = pl.pallas_call(
                add_kernel,
                out_shape=pair_shape,
                in_specs=vmem_specs(4) + [anywhere],
                out_specs=vmem_specs(2),
                compiler_params=params(8),
            )(left, left_moved, rest, rest_moved, their_basis)
        spread = spread_of(left)
        answer, *sent = solve(
            [left, left_moved],
            [rest, rest_moved],
            spread,
            face_shapes(counts[0], (ncon, columns)),
        )
        there = lax.ppermute(answer, "gy", flipped("gy", 1))
        same = exchange(sent, AXES[0])
        across = lax.ppermute(jnp.concatenate(same, axis=0), "gy", flipped("gy", 1))
        cut = across.shape[0] // len(same)
        across = [across[i * cut : (i + 1) * cut] for i in range(len(same))]
        correction = pl.pallas_call(
            functools.partial(last_near_kernel, ncon),
            in_specs=vmem_specs(4),
            **result,
        )(flags, spread, answer, there)
        correction = pl.pallas_call(
            functools.partial(last_far_kernel, ncon),
            in_specs=vmem_specs(4 + 2 * len(same)) + [main_memory],
            input_output_aliases={4 + 2 * len(same): 0},
            **result,
        )(flags, spread, answer, there, *same, *across, correction)
    else:
        y, z = lax.axis_index("gy"), lax.axis_index("gz")
        mine = group_of[y * planes + z]
        chosen = jnp.arange(groups, dtype=jnp.int32) == mine
        total = lax.psum(jnp.where(chosen[:, None, None], payload[None], 0.0), ("gy", "gz"))
        total = lax.dynamic_index_in_dim(total, mine, 0, keepdims=False)
        spread = spread_of(payload)
        (answer,) = solve([total[:, :lanes]], [total[:, lanes:]], spread, [])
        blocks = answer.reshape(FACES, ncon, columns)
        near = []
        for position, axis in enumerate(AXES):
            even, odd = blocks[2 * position], blocks[2 * position + 1]
            if counts[position] == 2:
                sent = [jnp.stack([even, odd])]
            else:
                upward = is_even(axis)
                sent = [jnp.where(upward, odd, even), jnp.where(upward, even, odd)]
            near += exchange(sent, axis)
        correction = pl.pallas_call(
            functools.partial(last_kernel, ncon),
            in_specs=vmem_specs(2 + arrays),
            **result,
        )(spread, answer, *near)
    return correction[None, None, None]


def solution(mesh):
    in_specs = (
        P("gx", "gy", "gz", None, None),
        P("gx", "gy", "gz", None, None, None),
        P("gx", "gy", "gz", None, None),
        P(),
    )
    out_specs = P("gx", "gy", "gz", None, None)
    return jax.shard_map(
        per_device, mesh=mesh, in_specs=in_specs, out_specs=out_specs, check_vma=False
    )
```

```python
import functools

import jax
import jax.numpy as jnp
from jax import lax
from jax.experimental import pallas as pl
from jax.experimental.pallas import tpu as pltpu
from jax.sharding import PartitionSpec as P

NS_ITERS = 3
SUB_ITERS = 2
GROUP_SIZE = 4
FACES = 6
BLOCKS = FACES // 2
AXES = ("gx", "gy", "gz")
MIB = 1024 * 1024

precise = lax.Precision.HIGHEST


def dot(left, right, dims=((1,), (0,))):
    return lax.dot_general(
        left, right, (dims, ((), ())), precision=precise, preferred_element_type=jnp.float32
    )


def split(value):
    high = value.astype(jnp.bfloat16)
    return high, (value - high.astype(jnp.float32)).astype(jnp.bfloat16)


def wide(left, right):
    return lax.dot_general(
        jnp.concatenate([left[0], left[0], left[1]], axis=1),
        jnp.concatenate([right[0], right[1], right[0]], axis=0),
        (((1,), (0,)), ((), ())),
        preferred_element_type=jnp.float32,
    )


def stacked(value):
    return jnp.concatenate(split(value), axis=0)


def thin(rows, matrix):
    out = lax.dot_general(
        jnp.concatenate([rows, rows], axis=1),
        jnp.concatenate(matrix, axis=0),
        (((1,), (0,)), ((), ())),
        preferred_element_type=jnp.float32,
    )
    half = rows.shape[0] // 2
    return out[:half] + out[half:]


def iota(shape, dim):
    return lax.broadcasted_iota(jnp.int32, shape, dim)


def flipped(axis, bit):
    return [(i, i ^ bit) for i in range(lax.axis_size(axis))]


def outer_pairs(axis):
    count = lax.axis_size(axis)
    return [(i, (i + 1 if i % 2 else i - 1) % count) for i in range(count)]


def face_arrays(count):
    return 1 if count == 2 else 2


def exchange(arrays, axis):
    if lax.axis_size(axis) == 2:
        return [lax.ppermute(arrays[0], axis, flipped(axis, 1))]
    return [
        lax.ppermute(arrays[0], axis, outer_pairs(axis)),
        lax.ppermute(arrays[1], axis, flipped(axis, 1)),
    ]


def is_even(axis):
    return lax.rem(lax.axis_index(axis), 2) == 0


def send(refs, axis, even, odd):
    if lax.axis_size(axis) == 2:
        refs[0][0] = even
        refs[0][1] = odd
    else:
        upward = is_even(axis)
        refs[0][...] = jnp.where(upward, even, odd)
        refs[1][...] = jnp.where(upward, odd, even)


def receive(refs, axis):
    if lax.axis_size(axis) == 2:
        return refs[0][1], refs[0][0]
    upward = is_even(axis)
    first, second = refs[0][...], refs[1][...]
    return jnp.where(upward, first, second), jnp.where(upward, second, first)


def face_shapes(count, shape):
    if count == 2:
        return [jax.ShapeDtypeStruct((2,) + shape, jnp.float32)]
    return [jax.ShapeDtypeStruct(shape, jnp.float32)] * 2


def vmem_specs(count):
    return [pl.BlockSpec(memory_space=pltpu.VMEM)] * count


def pack_kernel(counts, width, schur_ref, starts_ref, *refs):
    outs, blocks = refs[:-4], refs[-4]
    starts, sems, start_sem = refs[-3:]
    half = width // 2
    copies = []
    for f in range(FACES):
        place = pl.ds(f * width, width)
        copy = pltpu.make_async_copy(schur_ref.at[place, place], blocks.at[f], sems.at[f])
        copy.start()
        copies.append(copy)
    start_copy = pltpu.make_async_copy(starts_ref, starts, start_sem)
    start_copy.start()
    row, col = iota((half, half), 0), iota((half, half), 1)
    start_copy.wait()

    def pack(f):
        copies[f].wait()
        first = blocks[f, 0:half, 0:half]
        second = blocks[f, half:width, half:width]
        diag = jnp.sum(jnp.where(row == col, second, 0.0), axis=0, keepdims=True)
        mixed = jnp.where(row >= col, first, second)
        tail = jnp.broadcast_to(diag, (8, half))
        start = starts[f]
        return jnp.concatenate(
            [blocks[f, half:width, 0:half], mixed, tail, start[:, :half], start[:, half:]], axis=0
        )

    done = 0
    for position, axis in enumerate(AXES):
        number = face_arrays(counts[position])
        send(outs[done : done + number], axis, pack(2 * position), pack(2 * position + 1))
        done += number


def unpack(packed):
    half = packed.shape[1]
    row, col = iota((half, half), 0), iota((half, half), 1)
    low = packed[0:half]
    mixed = packed[half : 2 * half]
    flip = mixed.T
    first = jnp.where(row >= col, mixed, flip)
    second = jnp.where(row < col, mixed, flip)
    second = jnp.where(row == col, packed[2 * half : 2 * half + 1], second)
    return jnp.concatenate(
        [jnp.concatenate([first, low.T], axis=1), jnp.concatenate([low, second], axis=1)], axis=0
    )


def unpack_starts(packed, ncon):
    half = packed.shape[1]
    rows = packed[2 * half + 8 :]
    return jnp.concatenate([rows[:ncon], rows[ncon:]], axis=1)


def factor_inverses(grams, block=8):
    size = grams[0].shape[0]
    strips = size // 8
    lanes = 128
    full = (8, lanes)
    state = []
    for gram in grams:
        parts = [gram, jnp.where(iota((size, size), 0) == iota((size, size), 1), 1.0, 0.0)]
        if 2 * size < lanes:
            parts.append(jnp.zeros((size, lanes - 2 * size), jnp.float32))
        whole = jnp.concatenate(parts, axis=1)
        state.append([whole[8 * s : 8 * s + 8] for s in range(strips)])
    below = iota(full, 0)

    def line_of(strip, line):
        return jnp.broadcast_to(strip[line : line + 1], full)

    for start in range(0, size, block):
        strip, first = start // 8, start % 8
        active = range(strip, strips)
        for work in state:
            cols = [
                {s: jnp.broadcast_to(work[s][:, start + j : start + j + 1], full) for s in active}
                for j in range(block)
            ]
            factors = []

            def eliminate(j, scale, stop):
                line = first + j
                factor = {s: cols[j][s] * scale for s in active}
                factor[strip] = jnp.where(below > line, factor[strip], 0.0)
                for later in range(j + 1, stop):
                    head = line_of(cols[later][strip], line)
                    for s in active:
                        cols[later][s] = cols[later][s] - factor[s] * head
                factors.append(factor)

            for j in range(0, block, 2):
                line = first + j
                corner = line_of(cols[j][strip], line)
                side = line_of(cols[j][strip], line + 1)
                last = line_of(cols[j + 1][strip], line + 1)
                inverse = 1.0 / (corner * last - side * side)
                eliminate(j, 1.0 / corner, block)
                eliminate(j + 1, corner * inverse, block)
            for j in range(block):
                row = line_of(work[strip], first + j)
                for s in active:
                    if s == strip and first + j == 7:
                        continue
                    work[s] = work[s] - factors[j][s] * row
    results = []
    for work in state:
        parts = []
        for s in range(strips):
            place = iota((8, size), 0) + 8 * s == iota((8, size), 1)
            pivot = jnp.sum(jnp.where(place, work[s][:, :size], 0.0), axis=1, keepdims=True)
            parts.append(work[s][:, size : 2 * size] * lax.rsqrt(pivot))
        results.append(jnp.concatenate(parts, axis=0))
    return results


def member(group_ref, planes, dy=0, dz=0):
    y, z = lax.axis_index("gy"), lax.axis_index("gz")
    rows = lax.axis_size("gy")
    return group_ref[lax.rem(y + dy + rows, rows) * planes + lax.rem(z + dz + planes, planes)]


def store(ref, f, value):
    ref[f, 0], ref[f, 1] = split(value)


def load(ref, f):
    return ref[f, 0], ref[f, 1]


def upper_index(f, g):
    return sum(FACES - 1 - i for i in range(f)) + g - f - 1


def halves_kernel(planes, schur_ref, group_ref, own_ref, own_out, upper_out, flag_out, *scratch):
    upper_ref, sems = scratch
    width = own_ref.shape[1]
    strips = []
    for f in range(FACES - 1):
        rest = (FACES - 1 - f) * width
        copy = pltpu.make_async_copy(
            schur_ref.at[pl.ds(f * width, width), pl.ds((f + 1) * width, rest)],
            upper_ref.at[f, :, pl.ds((f + 1) * width, rest)],
            sems.at[f],
        )
        copy.start()
        strips.append(copy)
    core = lax.rem(lax.axis_index("gy"), 2)
    near = [(0, 0), (1 - 2 * core, 0), (-1, 0), (1, 0), (0, -1), (0, 1)]
    row = iota(flag_out.shape, 0)
    flags = jnp.zeros(flag_out.shape, jnp.float32)
    for i, (dy, dz) in enumerate(near):
        hit = member(group_ref, planes, dy, dz) == core
        flags = jnp.where(row == i, jnp.where(hit, 1.0, 0.0), flags)
    flag_out[...] = flags
    for f in range(FACES):
        store(own_out, f, own_ref[f])
    for f in range(FACES - 1):
        strips[f].wait()
        for g in range(f + 1, FACES):
            store(upper_out, upper_index(f, g), upper_ref[f, :, g * width : (g + 1) * width])


def begin(packed, owns, partner_out, sum_ref):
    width = owns[0].shape[1]
    eye = iota((width, width), 0) == iota((width, width), 1)
    guesses = []
    for f in range(len(packed)):
        partner = unpack(packed[f])
        total = owns[f] + partner
        store(partner_out, f, partner)
        store(sum_ref, f, total)
        diagonal = jnp.where(eye, total, 0.0)
        across = 1.0 / jnp.sum(diagonal, axis=0, keepdims=True)
        down = 1.0 / jnp.sum(diagonal, axis=1, keepdims=True)
        guesses.append(jnp.where(eye, 2.0 * across, 0.0) - down * total * across)
    return guesses


def newton(guesses, sum_ref):
    results = []
    for f, guess in enumerate(guesses):
        halves = split(guess)
        product = split(wide(load(sum_ref, f), halves))
        results.append(2.0 * guess - wide(halves, product))
    return results


def unit_rows(basis):
    return [b * lax.rsqrt(jnp.sum(b * b, axis=1, keepdims=True)) for b in basis]


def sweep_basis(before, inverse, after, basis):
    for matrices in (before, inverse, after):
        basis = [thin(stacked(b), matrix) for b, matrix in zip(basis, matrices)]
    return unit_rows(basis)


def early_kernel(axes, faces, *refs):
    arrays = len(refs) - 7
    inputs = refs[:arrays]
    own_ref, halves_ref, starts_ref, basis_out, partner_out, inverse_out, sum_ref = refs[arrays:]
    count = len(faces)
    packed = []
    done = 0
    for axis in axes:
        number = face_arrays(lax.axis_size(axis))
        packed += receive(inputs[done : done + number], axis)
        done += number
    guesses = begin(packed, [own_ref[f] for f in faces], partner_out, sum_ref)
    for sweep in range(NS_ITERS - 1):
        guesses = newton(guesses, sum_ref)
    for i in range(count):
        store(inverse_out, i, guesses[i])
    basis = [starts_ref[f] for f in faces]
    matrices = [
        [load(partner_out, i) for i in range(count)],
        [load(inverse_out, i) for i in range(count)],
        [load(halves_ref, f) for f in faces],
    ]
    for sweep in range(SUB_ITERS):
        basis = sweep_basis(*matrices, basis)
    for i in range(count):
        basis_out[i] = basis[i]


def main_kernel(axes, early, late, *refs):
    arrays = len(refs) - 11
    inputs = refs[:arrays]
    own_ref, halves_ref, upper_ref, starts_ref, resid_ref, early_basis = refs[arrays : arrays + 6]
    payload_ref, product_ref, partner_out, inverse_out, sum_ref = refs[arrays + 6 :]
    ncon, width = starts_ref.shape[1:]
    columns = resid_ref.shape[1]
    sides = {}
    rights = {}
    grams = {}
    vectors = {}
    count = len(late)

    def project(f, basis):
        vectors[f] = basis
        rows = stacked(basis)
        grams[f] = dot(basis, basis, ((1,), (1,)))
        side = {f: thin(rows, load(halves_ref, f))}
        for g in range(f + 1, FACES):
            side[g] = thin(rows, load(upper_ref, upper_index(f, g)))
        sides[f] = side
        rights[f] = thin(rows, split(resid_ref[f * width : (f + 1) * width]))

    packed = []
    done = 0
    for axis in axes:
        number = face_arrays(lax.axis_size(axis))
        packed += receive(inputs[done : done + number], axis)
        done += number
    guesses = begin(packed, [own_ref[f] for f in late], partner_out, sum_ref)
    pending = [(f, early_basis[i]) for i, f in enumerate(early)]
    for sweep in range(NS_ITERS - 1):
        guesses = newton(guesses, sum_ref)
        if pending:
            project(*pending.pop(0))
    for i in range(count):
        store(inverse_out, i, guesses[i])
    basis = [starts_ref[f] for f in late]
    matrices = [
        [load(partner_out, i) for i in range(count)],
        [load(inverse_out, i) for i in range(count)],
        [load(halves_ref, f) for f in late],
    ]
    for sweep in range(SUB_ITERS):
        basis = sweep_basis(*matrices, basis)
        if pending:
            project(*pending.pop(0))
    for item in pending:
        project(*item)
    for i, f in enumerate(late):
        project(f, basis[i])
    factors = factor_inverses([grams[f] for f in range(FACES)])
    blocks = []
    for g in range(FACES):
        tall = jnp.concatenate([sides[f][g] for f in range(g + 1)], axis=0)
        blocks.append(dot(dot(tall, vectors[g], ((1,), (1,))), factors[g], ((1,), (1,))))
    even, odd, right = [], [], []
    lows = None
    for f in range(FACES):
        product_ref[f] = dot(factors[f], sides[f][f])
        line = [blocks[g][f * ncon : (f + 1) * ncon] for g in range(f, FACES)]
        line = dot(factors[f], jnp.concatenate([rights[f]] + line, axis=1))
        right.append(line[:, :columns])
        line = line[:, columns:]
        if f % 2 == 0:
            even.append(line)
            lows = line[:, ncon : 2 * ncon].T
        else:
            odd += [lows, line]
    payload_ref[...] = jnp.concatenate(
        [
            jnp.concatenate(even + right[0::2], axis=1),
            jnp.concatenate(odd + right[1::2], axis=1),
        ],
        axis=0,
    )


def find(faces, refs, f):
    for group, ref in zip(faces, refs):
        if f in group:
            return load(ref, list(group).index(f))


def theirs_kernel(faces, ncon, *refs):
    arrays = len(refs) - 7
    inputs = refs[:arrays]
    own_ref, partner_refs, inverse_refs = refs[arrays], refs[-6:-4], refs[-4:-2]
    basis_out, product_out = refs[-2:]
    basis = []
    done = 0
    for axis in AXES:
        number = face_arrays(lax.axis_size(axis))
        packed = receive(inputs[done : done + number], axis)
        basis += [unpack_starts(part, ncon) for part in packed]
        done += number
    matrices = [
        [load(own_ref, f) for f in range(FACES)],
        [find(faces, inverse_refs, f) for f in range(FACES)],
        [find(faces, partner_refs, f) for f in range(FACES)],
    ]
    for sweep in range(SUB_ITERS):
        basis = sweep_basis(*matrices, basis)
    for f in range(FACES):
        basis_out[f] = basis[f]
        product_out[f] = thin(stacked(basis[f]), matrices[2][f])


def spread_kernel(faces, unread, basis_ref, theirs_ref, product_ref, *refs):
    inverse_refs, out_ref = refs[0:2], refs[2]
    basis = [basis_ref[f] for f in range(FACES)]
    factors = factor_inverses([dot(b, b, ((1,), (1,))) for b in basis])
    for f in range(FACES):
        both = jnp.concatenate([product_ref[f], dot(factors[f], theirs_ref[f])], axis=0)
        high, low = split(thin(stacked(both), find(faces, inverse_refs, f)).T)
        out_ref[f] = jnp.concatenate([high, high, low], axis=1)


def choose_kernel(flag_ref, here_ref, there_ref, matrix_ref, right_ref):
    mine = flag_ref[0:1, 0:1] > 0.5
    other = flag_ref[1:2, 0:1] > 0.5
    total = jnp.where(mine, here_ref[...], 0.0) + jnp.where(other, there_ref[...], 0.0)
    lanes = matrix_ref.shape[1]
    matrix_ref[...] = total[:, :lanes]
    right_ref[...] = total[:, lanes:]


def add_kernel(first_ref, second_ref, third_ref, fourth_ref, unread, matrix_ref, right_ref):
    matrix_ref[...] = first_ref[...] + second_ref[...]
    right_ref[...] = third_ref[...] + fourth_ref[...]


def solve_kernel(size, terms, *refs):
    matrix, right = refs[0][...], refs[terms][...]
    for term in range(1, terms):
        matrix = matrix + refs[term][...]
        right = right + refs[terms + term][...]
    answer_ref = refs[2 * terms + 1]
    columns = answer_ref.shape[1]
    lines = []
    offset = 0
    for b in range(BLOCKS):
        lines.append(matrix[:, offset : offset + (BLOCKS - b) * size])
        offset += (BLOCKS - b) * size
    eye = iota((size, size), 0) == iota((size, size), 1)
    downs, acrosses = [], []
    for b in range(BLOCKS):
        diagonal = jnp.where(eye, lines[b][:, :size], 0.0)
        downs.append(lax.rsqrt(jnp.sum(diagonal, axis=1, keepdims=True)))
        acrosses.append(lax.rsqrt(jnp.sum(diagonal, axis=0, keepdims=True)))
    blocks = {}
    rights = []
    for b in range(BLOCKS):
        for c in range(b, BLOCKS):
            block = lines[b][:, (c - b) * size : (c - b + 1) * size]
            blocks[b, c] = downs[b] * block * acrosses[c]
        rights.append(downs[b] * right[:, b * columns : (b + 1) * columns])
    for b in range(BLOCKS):
        (inverse,) = factor_inverses([blocks[b, b]])
        later = range(b + 1, BLOCKS)
        row = dot(inverse, jnp.concatenate([rights[b]] + [blocks[b, c] for c in later], axis=1))
        upper = {c: row[:, columns + (c - b - 1) * size : columns + (c - b) * size] for c in later}
        for c in later:
            for d in range(c, BLOCKS):
                blocks[c, d] = blocks[c, d] - dot(upper[c], upper[d], ((0,), (0,)))
            rights[c] = rights[c] - dot(upper[c], row[:, :columns], ((0,), (0,)))
        row = dot(inverse, row, ((0,), (0,)))
        rights[b] = row[:, :columns]
        for c in later:
            blocks[b, c] = row[:, columns + (c - b - 1) * size : columns + (c - b) * size]
        for i in range(b):
            for c in later:
                blocks[i, c] = blocks[i, c] - dot(blocks[i, b], blocks[b, c])
            rights[i] = rights[i] - dot(blocks[i, b], rights[b])
    answer = [downs[b] * rights[b] for b in range(BLOCKS)]
    answer_ref[...] = jnp.concatenate(answer, axis=0)


def rows_kernel(ncon, flag_ref, here_ref, there_ref, *refs):
    hit = flag_ref[0:1, 0:1] > 0.5
    rows = jnp.where(hit, here_ref[: 2 * ncon], there_ref[: 2 * ncon])
    refs[-1][...] = rows
    send(refs[:-1], AXES[0], rows[:ncon], rows[ncon:])


def last_product(spread, mine, theirs):
    high, low = split(jnp.concatenate([mine, theirs], axis=0))
    return lax.dot_general(
        spread,
        jnp.concatenate([high, low, high], axis=0),
        (((1,), (0,)), ((), ())),
        preferred_element_type=jnp.float32,
    )


def last_faces(spread_ref, pairs, out_ref, result, sems):
    width = spread_ref.shape[1]
    copies = []
    for f, (mine, theirs) in pairs.items():
        place = pl.ds(f * width, width)
        result[f * width : (f + 1) * width] = last_product(spread_ref[f], mine, theirs)
        copy = pltpu.make_async_copy(result.at[place], out_ref.at[place], sems.at[f])
        copy.start()
        copies.append(copy)
    for copy in copies:
        copy.wait()


def last_kernel(ncon, spread_ref, answer_ref, *refs):
    inputs, rest = refs[:-3], refs[-3:]
    pairs = {}
    done = 0
    for position, axis in enumerate(AXES):
        number = face_arrays(lax.axis_size(axis))
        near = receive(inputs[done : done + number], axis)
        done += number
        for f, theirs in zip((2 * position, 2 * position + 1), near):
            pairs[f] = (answer_ref[f * ncon : (f + 1) * ncon], theirs)
    last_faces(spread_ref, pairs, *rest)


def last_near_kernel(ncon, flag_ref, spread_ref, here_ref, there_ref, *refs):
    def answer(flag, f):
        place = slice(f * ncon, (f + 1) * ncon)
        hit = flag_ref[flag : flag + 1, 0:1] > 0.5
        return jnp.where(hit, here_ref[place], there_ref[place])

    pairs = {f: (answer(0, f), answer(f, f ^ 1)) for f in range(2, FACES)}
    last_faces(spread_ref, pairs, *refs)


def last_far_kernel(ncon, spread_ref, rows_ref, *refs):
    theirs = receive(refs[:-4], AXES[0])
    pairs = {f: (rows_ref[f * ncon : (f + 1) * ncon], theirs[f]) for f in (0, 1)}
    last_faces(spread_ref, pairs, *refs[-3:])


def sum_rounds(rows, planes):
    rounds = [("gy", 2**i) for i in range(1, rows.bit_length() - 1)]
    return rounds + [("gz", 2**i) for i in range(planes.bit_length() - 1)]


def per_device(schur, start_block, resid, group_of):
    matrix = schur[0, 0, 0]
    matrix = pltpu.with_memory_space_constraint(matrix, pltpu.HBM)
    starts = start_block[0, 0, 0].transpose(0, 2, 1)
    right = resid[0, 0, 0]
    order, columns = right.shape
    ncon, width = starts.shape[1:]
    counts = [lax.axis_size(axis) for axis in AXES]
    arrays = sum(face_arrays(count) for count in counts)
    coarse = FACES * ncon
    size = 2 * ncon
    lanes = size * BLOCKS * (BLOCKS + 1) // 2
    uppers = FACES * (FACES - 1) // 2
    anywhere = pl.BlockSpec(memory_space=pl.ANY)
    main_memory = pl.BlockSpec(memory_space=pltpu.HBM)
    scalars = pl.BlockSpec(memory_space=pltpu.SMEM)
    early, late = (4, 5), (0, 1, 2, 3)
    faces = (early, late)
    planes = counts[2]

    def shape(*dims):
        return jax.ShapeDtypeStruct(dims, jnp.float32)

    def halves(count):
        return jax.ShapeDtypeStruct((count, 2, width, width), jnp.bfloat16)

    def params(mib):
        return pltpu.CompilerParams(vmem_limit_bytes=mib * MIB)

    def cost(us):
        return pl.CostEstimate(flops=us * 10**9, bytes_accessed=2**20, transcendentals=0)

    *packed, own = pl.pallas_call(
        functools.partial(pack_kernel, counts, width),
        out_shape=[
            part
            for count in counts
            for part in face_shapes(count, (width + 8 + 2 * ncon, width // 2))
        ]
        + [shape(FACES, width, width)],
        in_specs=[main_memory, main_memory],
        out_specs=vmem_specs(arrays + 1),
        scratch_shapes=[
            pltpu.VMEM((FACES, ncon, width), jnp.float32),
            pltpu.SemaphoreType.DMA((FACES,)),
            pltpu.SemaphoreType.DMA,
        ],
        compiler_params=params(12),
    )(matrix, pltpu.with_memory_space_constraint(starts, pltpu.HBM))
    ends = [sum(face_arrays(count) for count in counts[:position]) for position in range(4)]
    got = {}
    for position in (2, 0, 1):
        got[position] = exchange(packed[ends[position] : ends[position + 1]], AXES[position])

    own_halves, upper_halves, flags = pl.pallas_call(
        functools.partial(halves_kernel, planes),
        out_shape=[halves(FACES), halves(uppers), shape(8, 128)],
        in_specs=[main_memory, scalars] + vmem_specs(1),
        out_specs=vmem_specs(3),
        scratch_shapes=[
            pltpu.VMEM((FACES - 1, width, order), jnp.float32),
            pltpu.SemaphoreType.DMA((FACES - 1,)),
        ],
        compiler_params=params(24),
        cost_estimate=cost(2),
    )(matrix, group_of, own)

    early_basis, early_partner, early_inverse = pl.pallas_call(
        functools.partial(early_kernel, AXES[2:3], early),
        out_shape=[shape(len(early), ncon, width)] + [halves(len(early))] * 2,
        in_specs=vmem_specs(len(got[2]) + 3),
        out_specs=vmem_specs(3),
        scratch_shapes=[pltpu.VMEM((len(early), 2, width, width), jnp.bfloat16)],
        compiler_params=params(16),
        cost_estimate=cost(2),
    )(*got[2], own, own_halves, starts)

    payload, product, late_partner, late_inverse = pl.pallas_call(
        functools.partial(main_kernel, (AXES[0], AXES[1]), early, late),
        out_shape=[shape(size, lanes + BLOCKS * columns), shape(FACES, ncon, width)]
        + [halves(len(late))] * 2,
        in_specs=vmem_specs(len(got[0]) + len(got[1]) + 6),
        out_specs=vmem_specs(4),
        scratch_shapes=[pltpu.VMEM((len(late), 2, width, width), jnp.bfloat16)],
        compiler_params=params(24),
        cost_estimate=cost(8),
    )(*got[0], *got[1], own, own_halves, upper_halves, starts, right, early_basis)

    partners = [early_partner, late_partner]
    inverses = [early_inverse, late_inverse]
    their_basis, their_product = pl.pallas_call(
        functools.partial(theirs_kernel, faces, ncon),
        out_shape=[shape(FACES, ncon, width)] * 2,
        in_specs=vmem_specs(arrays + 5),
        out_specs=vmem_specs(2),
        compiler_params=params(16),
        cost_estimate=cost(2),
    )(*got[0], *got[1], *got[2], own_halves, *partners, *inverses)

    def spread_of(token):
        return pl.pallas_call(
            functools.partial(spread_kernel, faces),
            out_shape=jax.ShapeDtypeStruct((FACES, width, 3 * size), jnp.bfloat16),
            in_specs=[anywhere] + vmem_specs(5),
            out_specs=vmem_specs(1)[0],
            compiler_params=params(16),
            cost_estimate=cost(3),
        )(token, their_basis, their_product, product, *inverses)

    def solve(matrices, rights, token):
        return pl.pallas_call(
            functools.partial(solve_kernel, size, len(matrices)),
            out_shape=shape(coarse, columns),
            in_specs=vmem_specs(2 * len(matrices)) + [anywhere],
            out_specs=vmem_specs(1)[0],
            compiler_params=params(12),
            cost_estimate=cost(7),
        )(*matrices, *rights, token)

    result = dict(
        out_shape=shape(order, columns),
        out_specs=main_memory,
        scratch_shapes=[
            pltpu.VMEM((order, columns), jnp.float32),
            pltpu.SemaphoreType.DMA((FACES,)),
        ],
        compiler_params=params(8),
        cost_estimate=cost(1),
    )
    rows = counts[1]
    groups = group_of.shape[0] // GROUP_SIZE
    if groups == 2 and rows > 1 and not (rows & (rows - 1) or planes & (planes - 1)):
        other = lax.ppermute(payload, "gy", flipped("gy", 1))
        pair_shape = [shape(size, lanes), shape(size, BLOCKS * columns)]
        left, rest = pl.pallas_call(
            choose_kernel,
            out_shape=pair_shape,
            in_specs=vmem_specs(3),
            out_specs=vmem_specs(2),
            compiler_params=params(8),
        )(flags, payload, other)
        rounds = sum_rounds(rows, planes)
        for step in range(len(rounds)):
            axis, bit = rounds[step]
            left_moved = lax.ppermute(left, axis, flipped(axis, bit))
            axis, bit = rounds[-1 - step]
            rest_moved = lax.ppermute(rest, axis, flipped(axis, bit))
            if step == len(rounds) - 1:
                break
            left, rest = pl.pallas_call(
                add_kernel,
                out_shape=pair_shape,
                in_specs=vmem_specs(4) + [anywhere],
                out_specs=vmem_specs(2),
                compiler_params=params(8),
            )(left, left_moved, rest, rest_moved, their_basis)
        spread = spread_of(left)
        answer = solve([left, left_moved], [rest, rest_moved], spread)
        there = lax.ppermute(answer, "gy", flipped("gy", 1))
        *sent, mine = pl.pallas_call(
            functools.partial(rows_kernel, ncon),
            out_shape=face_shapes(counts[0], (ncon, columns)) + [shape(size, columns)],
            in_specs=vmem_specs(3),
            out_specs=vmem_specs(face_arrays(counts[0]) + 1),
            compiler_params=params(8),
        )(flags, answer, there)
        across = exchange(sent, AXES[0])
        correction = pl.pallas_call(
            functools.partial(last_near_kernel, ncon),
            in_specs=vmem_specs(4),
            **result,
        )(flags, spread, answer, there)
        correction = pl.pallas_call(
            functools.partial(last_far_kernel, ncon),
            in_specs=vmem_specs(2 + len(across)) + [main_memory],
            input_output_aliases={2 + len(across): 0},
            **result,
        )(spread, mine, *across, correction)
    else:
        y, z = lax.axis_index("gy"), lax.axis_index("gz")
        mine = group_of[y * planes + z]
        chosen = jnp.arange(groups, dtype=jnp.int32) == mine
        total = lax.psum(jnp.where(chosen[:, None, None], payload[None], 0.0), ("gy", "gz"))
        total = lax.dynamic_index_in_dim(total, mine, 0, keepdims=False)
        spread = spread_of(payload)
        answer = solve([total[:, :lanes]], [total[:, lanes:]], spread)
        blocks = answer.reshape(FACES, ncon, columns)
        near = []
        for position, axis in enumerate(AXES):
            even, odd = blocks[2 * position], blocks[2 * position + 1]
            if counts[position] == 2:
                sent = [jnp.stack([even, odd])]
            else:
                upward = is_even(axis)
                sent = [jnp.where(upward, even, odd), jnp.where(upward, odd, even)]
            near += exchange(sent, axis)
        correction = pl.pallas_call(
            functools.partial(last_kernel, ncon),
            in_specs=vmem_specs(2 + arrays),
            **result,
        )(spread, answer, *near)
    return correction[None, None, None]


def solution(mesh):
    in_specs = (
        P("gx", "gy", "gz", None, None),
        P("gx", "gy", "gz", None, None, None),
        P("gx", "gy", "gz", None, None),
        P(),
    )
    out_specs = P("gx", "gy", "gz", None, None)
    return jax.shard_map(
        per_device, mesh=mesh, in_specs=in_specs, out_specs=out_specs, check_vma=False
    )
```

```python
import functools

import jax
import jax.numpy as jnp
from jax import lax
from jax.experimental import pallas as pl
from jax.experimental.pallas import tpu as pltpu
from jax.sharding import PartitionSpec as P

NS_ITERS = 3
SUB_ITERS = 2
GROUP_SIZE = 4
FACES = 6
BLOCKS = FACES // 2
AXES = ("gx", "gy", "gz")
MIB = 1024 * 1024

precise = lax.Precision.HIGHEST


def dot(left, right, dims=((1,), (0,))):
    return lax.dot_general(
        left, right, (dims, ((), ())), precision=precise, preferred_element_type=jnp.float32
    )


def split(value):
    high = value.astype(jnp.bfloat16)
    return high, (value - high.astype(jnp.float32)).astype(jnp.bfloat16)


def wide(left, right):
    return lax.dot_general(
        jnp.concatenate([left[0], left[0], left[1]], axis=1),
        jnp.concatenate([right[0], right[1], right[0]], axis=0),
        (((1,), (0,)), ((), ())),
        preferred_element_type=jnp.float32,
    )


def stacked(value):
    return jnp.concatenate(split(value), axis=0)


def thin(rows, matrix):
    out = lax.dot_general(
        jnp.concatenate([rows, rows], axis=1),
        jnp.concatenate(matrix, axis=0),
        (((1,), (0,)), ((), ())),
        preferred_element_type=jnp.float32,
    )
    half = rows.shape[0] // 2
    return out[:half] + out[half:]


def iota(shape, dim):
    return lax.broadcasted_iota(jnp.int32, shape, dim)


def flipped(axis, bit):
    return [(i, i ^ bit) for i in range(lax.axis_size(axis))]


def outer_pairs(axis):
    count = lax.axis_size(axis)
    return [(i, (i + 1 if i % 2 else i - 1) % count) for i in range(count)]


def face_arrays(count):
    return 1 if count == 2 else 2


def exchange(arrays, axis):
    if lax.axis_size(axis) == 2:
        return [lax.ppermute(arrays[0], axis, flipped(axis, 1))]
    return [
        lax.ppermute(arrays[0], axis, outer_pairs(axis)),
        lax.ppermute(arrays[1], axis, flipped(axis, 1)),
    ]


def is_even(axis):
    return lax.rem(lax.axis_index(axis), 2) == 0


def send(refs, axis, even, odd):
    if lax.axis_size(axis) == 2:
        refs[0][0] = even
        refs[0][1] = odd
    else:
        upward = is_even(axis)
        refs[0][...] = jnp.where(upward, even, odd)
        refs[1][...] = jnp.where(upward, odd, even)


def receive(refs, axis):
    if lax.axis_size(axis) == 2:
        return refs[0][1], refs[0][0]
    upward = is_even(axis)
    first, second = refs[0][...], refs[1][...]
    return jnp.where(upward, first, second), jnp.where(upward, second, first)


def face_shapes(count, shape):
    if count == 2:
        return [jax.ShapeDtypeStruct((2,) + shape, jnp.float32)]
    return [jax.ShapeDtypeStruct(shape, jnp.float32)] * 2


def vmem_specs(count):
    return [pl.BlockSpec(memory_space=pltpu.VMEM)] * count


def pack_kernel(counts, width, schur_ref, starts_ref, *refs):
    outs, blocks = refs[:-4], refs[-4]
    starts, sems, start_sem = refs[-3:]
    half = width // 2
    copies = []
    for f in range(FACES):
        place = pl.ds(f * width, width)
        copy = pltpu.make_async_copy(schur_ref.at[place, place], blocks.at[f], sems.at[f])
        copy.start()
        copies.append(copy)
    start_copy = pltpu.make_async_copy(starts_ref.at[pl.ds(0, 4)], starts, start_sem)
    start_copy.start()
    row, col = iota((half, half), 0), iota((half, half), 1)
    start_copy.wait()

    def pack(f):
        copies[f].wait()
        first = blocks[f, 0:half, 0:half]
        second = blocks[f, half:width, half:width]
        diag = jnp.sum(jnp.where(row == col, second, 0.0), axis=0, keepdims=True)
        mixed = jnp.where(row >= col, first, second)
        tail = jnp.broadcast_to(diag, (8, half))
        parts = [blocks[f, half:width, 0:half], mixed, tail]
        if f < 4:
            parts += [starts[f, :, :half], starts[f, :, half:]]
        return jnp.concatenate(parts, axis=0)

    done = 0
    for position, axis in enumerate(AXES):
        number = face_arrays(counts[position])
        send(outs[done : done + number], axis, pack(2 * position), pack(2 * position + 1))
        done += number


def unpack(packed):
    half = packed.shape[1]
    row, col = iota((half, half), 0), iota((half, half), 1)
    low = packed[0:half]
    mixed = packed[half : 2 * half]
    flip = mixed.T
    first = jnp.where(row >= col, mixed, flip)
    second = jnp.where(row < col, mixed, flip)
    second = jnp.where(row == col, packed[2 * half : 2 * half + 1], second)
    return jnp.concatenate(
        [jnp.concatenate([first, low.T], axis=1), jnp.concatenate([low, second], axis=1)], axis=0
    )


def unpack_starts(packed, ncon):
    half = packed.shape[1]
    rows = packed[2 * half + 8 :]
    return jnp.concatenate([rows[:ncon], rows[ncon:]], axis=1)


def factor_inverses(grams, block=8):
    size = grams[0].shape[0]
    strips = size // 8
    lanes = 128
    full = (8, lanes)
    state = []
    for gram in grams:
        parts = [gram, jnp.where(iota((size, size), 0) == iota((size, size), 1), 1.0, 0.0)]
        if 2 * size < lanes:
            parts.append(jnp.zeros((size, lanes - 2 * size), jnp.float32))
        whole = jnp.concatenate(parts, axis=1)
        state.append([whole[8 * s : 8 * s + 8] for s in range(strips)])
    below = iota(full, 0)

    def line_of(strip, line):
        return jnp.broadcast_to(strip[line : line + 1], full)

    for start in range(0, size, block):
        strip, first = start // 8, start % 8
        active = range(strip, strips)
        for work in state:
            cols = [
                {s: jnp.broadcast_to(work[s][:, start + j : start + j + 1], full) for s in active}
                for j in range(block)
            ]
            factors = []

            def eliminate(j, scale, stop):
                line = first + j
                factor = {s: cols[j][s] * scale for s in active}
                factor[strip] = jnp.where(below > line, factor[strip], 0.0)
                for later in range(j + 1, stop):
                    head = line_of(cols[later][strip], line)
                    for s in active:
                        cols[later][s] = cols[later][s] - factor[s] * head
                factors.append(factor)

            for j in range(0, block, 2):
                line = first + j
                corner = line_of(cols[j][strip], line)
                side = line_of(cols[j][strip], line + 1)
                last = line_of(cols[j + 1][strip], line + 1)
                inverse = 1.0 / (corner * last - side * side)
                eliminate(j, 1.0 / corner, block)
                eliminate(j + 1, corner * inverse, block)
            for j in range(block):
                row = line_of(work[strip], first + j)
                for s in active:
                    if s == strip and first + j == 7:
                        continue
                    work[s] = work[s] - factors[j][s] * row
    results = []
    for work in state:
        parts = []
        for s in range(strips):
            place = iota((8, size), 0) + 8 * s == iota((8, size), 1)
            pivot = jnp.sum(jnp.where(place, work[s][:, :size], 0.0), axis=1, keepdims=True)
            parts.append(work[s][:, size : 2 * size] * lax.rsqrt(pivot))
        results.append(jnp.concatenate(parts, axis=0))
    return results


def member(group_ref, planes, dy=0, dz=0):
    y, z = lax.axis_index("gy"), lax.axis_index("gz")
    rows = lax.axis_size("gy")
    return group_ref[lax.rem(y + dy + rows, rows) * planes + lax.rem(z + dz + planes, planes)]


def store(ref, f, value):
    ref[f, 0], ref[f, 1] = split(value)


def load(ref, f):
    return ref[f, 0], ref[f, 1]


def upper_index(f, g):
    return sum(FACES - 1 - i for i in range(f)) + g - f - 1


def halves_kernel(planes, schur_ref, group_ref, own_ref, own_out, upper_out, flag_out, *scratch):
    upper_ref, sems = scratch
    width = own_ref.shape[1]
    strips = []
    for f in range(FACES - 1):
        rest = (FACES - 1 - f) * width
        copy = pltpu.make_async_copy(
            schur_ref.at[pl.ds(f * width, width), pl.ds((f + 1) * width, rest)],
            upper_ref.at[f, :, pl.ds((f + 1) * width, rest)],
            sems.at[f],
        )
        copy.start()
        strips.append(copy)
    core = lax.rem(lax.axis_index("gy"), 2)
    near = [(0, 0), (1 - 2 * core, 0), (-1, 0), (1, 0), (0, -1), (0, 1)]
    row = iota(flag_out.shape, 0)
    flags = jnp.zeros(flag_out.shape, jnp.float32)
    for i, (dy, dz) in enumerate(near):
        hit = member(group_ref, planes, dy, dz) == core
        flags = jnp.where(row == i, jnp.where(hit, 1.0, 0.0), flags)
    flag_out[...] = flags
    for f in range(FACES):
        store(own_out, f, own_ref[f])
    for f in range(FACES - 1):
        strips[f].wait()
        for g in range(f + 1, FACES):
            store(upper_out, upper_index(f, g), upper_ref[f, :, g * width : (g + 1) * width])


def begin(packed, owns, partner_out, sum_ref):
    width = owns[0].shape[1]
    eye = iota((width, width), 0) == iota((width, width), 1)
    guesses = []
    for f in range(len(packed)):
        partner = unpack(packed[f])
        total = owns[f] + partner
        store(partner_out, f, partner)
        store(sum_ref, f, total)
        diagonal = jnp.where(eye, total, 0.0)
        across = 1.0 / jnp.sum(diagonal, axis=0, keepdims=True)
        down = 1.0 / jnp.sum(diagonal, axis=1, keepdims=True)
        guesses.append(jnp.where(eye, 2.0 * across, 0.0) - down * total * across)
    return guesses


def newton(guesses, sum_ref):
    results = []
    for f, guess in enumerate(guesses):
        halves = split(guess)
        product = split(wide(load(sum_ref, f), halves))
        results.append(2.0 * guess - wide(halves, product))
    return results


def unit_rows(basis):
    return [b * lax.rsqrt(jnp.sum(b * b, axis=1, keepdims=True)) for b in basis]


def sweep_basis(before, inverse, after, basis):
    for matrices in (before, inverse, after):
        basis = [thin(stacked(b), matrix) for b, matrix in zip(basis, matrices)]
    return unit_rows(basis)


def early_kernel(axes, faces, *refs):
    arrays = len(refs) - 7
    inputs = refs[:arrays]
    own_ref, halves_ref, starts_ref, basis_out, partner_out, inverse_out, sum_ref = refs[arrays:]
    count = len(faces)
    packed = []
    done = 0
    for axis in axes:
        number = face_arrays(lax.axis_size(axis))
        packed += receive(inputs[done : done + number], axis)
        done += number
    guesses = begin(packed, [own_ref[f] for f in faces], partner_out, sum_ref)
    for sweep in range(NS_ITERS - 1):
        guesses = newton(guesses, sum_ref)
    for i in range(count):
        store(inverse_out, i, guesses[i])
    basis = [starts_ref[f] for f in faces]
    matrices = [
        [load(partner_out, i) for i in range(count)],
        [load(inverse_out, i) for i in range(count)],
        [load(halves_ref, f) for f in faces],
    ]
    for sweep in range(SUB_ITERS):
        basis = sweep_basis(*matrices, basis)
    for i in range(count):
        basis_out[i] = basis[i]


def main_kernel(axes, early, late, *refs):
    arrays = len(refs) - 11
    inputs = refs[:arrays]
    own_ref, halves_ref, upper_ref, starts_ref, resid_ref, early_basis = refs[arrays : arrays + 6]
    payload_ref, product_ref, partner_out, inverse_out, sum_ref = refs[arrays + 6 :]
    ncon, width = starts_ref.shape[1:]
    columns = resid_ref.shape[1]
    sides = {}
    rights = {}
    grams = {}
    vectors = {}
    count = len(late)

    def project(f, basis):
        vectors[f] = basis
        rows = stacked(basis)
        grams[f] = dot(basis, basis, ((1,), (1,)))
        side = {f: thin(rows, load(halves_ref, f))}
        for g in range(f + 1, FACES):
            side[g] = thin(rows, load(upper_ref, upper_index(f, g)))
        sides[f] = side
        rights[f] = thin(rows, split(resid_ref[f * width : (f + 1) * width]))

    packed = []
    done = 0
    for axis in axes:
        number = face_arrays(lax.axis_size(axis))
        packed += receive(inputs[done : done + number], axis)
        done += number
    guesses = begin(packed, [own_ref[f] for f in late], partner_out, sum_ref)
    pending = [(f, early_basis[i]) for i, f in enumerate(early)]
    for sweep in range(NS_ITERS - 1):
        guesses = newton(guesses, sum_ref)
        if pending:
            project(*pending.pop(0))
    for i in range(count):
        store(inverse_out, i, guesses[i])
    basis = [starts_ref[f] for f in late]
    matrices = [
        [load(partner_out, i) for i in range(count)],
        [load(inverse_out, i) for i in range(count)],
        [load(halves_ref, f) for f in late],
    ]
    for sweep in range(SUB_ITERS):
        basis = sweep_basis(*matrices, basis)
        if pending:
            project(*pending.pop(0))
    for item in pending:
        project(*item)
    for i, f in enumerate(late):
        project(f, basis[i])
    factors = factor_inverses([grams[f] for f in range(FACES)])
    blocks = []
    for g in range(FACES):
        tall = jnp.concatenate([sides[f][g] for f in range(g + 1)], axis=0)
        blocks.append(dot(dot(tall, vectors[g], ((1,), (1,))), factors[g], ((1,), (1,))))
    even, odd, right, products = [], [], [], []
    lows = None
    for f in range(FACES):
        products.append(dot(factors[f], sides[f][f]))
        product_ref[f] = products[f]
        line = [blocks[g][f * ncon : (f + 1) * ncon] for g in range(f, FACES)]
        line = dot(factors[f], jnp.concatenate([rights[f]] + line, axis=1))
        right.append(line[:, :columns])
        line = line[:, columns:]
        if f % 2 == 0:
            even.append(line)
            lows = line[:, ncon : 2 * ncon].T
        else:
            odd += [lows, line]
    upward = is_even("gy")
    inner = jnp.where(upward, products[3], products[2])
    outer = jnp.where(upward, products[2], products[3])
    whole = [
        jnp.concatenate(even + right[0::2], axis=1),
        jnp.concatenate(odd + right[1::2], axis=1),
    ]
    payload_ref[...] = jnp.concatenate(
        [jnp.concatenate(whole, axis=0), fold(inner), fold(outer)], axis=1
    )


def fold(product):
    half = product.shape[1] // 2
    return jnp.concatenate([product[:, :half], product[:, half:]], axis=0)


def unfold(rows):
    half = rows.shape[0] // 2
    return jnp.concatenate([rows[:half], rows[half:]], axis=1)


def find(faces, refs, f):
    for group, ref in zip(faces, refs):
        if f in group:
            return load(ref, list(group).index(f))


def spread_kernel(faces, ncon, unread, *refs):
    packed = receive(refs[:-7], AXES[0])
    own_ref, product_ref = refs[-7:-5]
    partner_refs, inverse_refs, out_ref = refs[-5:-3], refs[-3:-1], refs[-1]
    basis = [unpack_starts(part, ncon) for part in packed]
    matrices = [
        [load(own_ref, f) for f in range(2)],
        [find(faces, inverse_refs, f) for f in range(2)],
        [find(faces, partner_refs, f) for f in range(2)],
    ]
    for sweep in range(SUB_ITERS):
        basis = sweep_basis(*matrices, basis)
    factors = factor_inverses([dot(b, b, ((1,), (1,))) for b in basis])
    for f in range(2):
        theirs = dot(factors[f], thin(stacked(basis[f]), matrices[2][f]))
        both = jnp.concatenate([product_ref[f], theirs], axis=0)
        high, low = split(thin(stacked(both), matrices[1][f]).T)
        out_ref[f] = jnp.concatenate([high, high, low], axis=1)


def choose_kernel(flag_ref, here_ref, there_ref, product_ref, matrix_ref, right_ref):
    mine = flag_ref[0:1, 0:1] > 0.5
    other = flag_ref[1:2, 0:1] > 0.5
    half = product_ref.shape[2] // 2
    lanes, wide_lanes = matrix_ref.shape[1] - half, here_ref.shape[1] - 2 * half
    here, there = here_ref[:, :wide_lanes], there_ref[:, :wide_lanes]
    total = jnp.where(mine, here, 0.0) + jnp.where(other, there, 0.0)
    outer = there_ref[:, wide_lanes + half :]
    matrix_ref[...] = jnp.concatenate([total[:, :lanes], outer], axis=1)
    right_ref[...] = jnp.concatenate([total[:, lanes:], fold(product_ref[4])], axis=1)


def add_kernel(first_ref, second_ref, third_ref, fourth_ref, product_ref, unread, *refs):
    matrix_ref, right_ref = refs
    half = product_ref.shape[2] // 2
    lanes, right_lanes = matrix_ref.shape[1] - half, right_ref.shape[1]
    total = first_ref[:, :lanes] + second_ref[:, :lanes]
    matrix_ref[...] = jnp.concatenate([total, fold(product_ref[5])], axis=1)
    right_ref[...] = third_ref[:, :right_lanes] + fourth_ref[:, :right_lanes]


def solve_kernel(size, terms, columns, *refs):
    lanes = size * BLOCKS * (BLOCKS + 1) // 2
    matrix, right = refs[0][:, :lanes], refs[terms][...]
    for term in range(1, terms):
        matrix = matrix + refs[term][:, :lanes]
        right = right + refs[terms + term][...]
    answer_ref = refs[-1]
    lines = []
    offset = 0
    for b in range(BLOCKS):
        lines.append(matrix[:, offset : offset + (BLOCKS - b) * size])
        offset += (BLOCKS - b) * size
    eye = iota((size, size), 0) == iota((size, size), 1)
    downs, acrosses = [], []
    for b in range(BLOCKS):
        diagonal = jnp.where(eye, lines[b][:, :size], 0.0)
        downs.append(lax.rsqrt(jnp.sum(diagonal, axis=1, keepdims=True)))
        acrosses.append(lax.rsqrt(jnp.sum(diagonal, axis=0, keepdims=True)))
    blocks = {}
    rights = []
    for b in range(BLOCKS):
        for c in range(b, BLOCKS):
            block = lines[b][:, (c - b) * size : (c - b + 1) * size]
            blocks[b, c] = downs[b] * block * acrosses[c]
            if c > b:
                blocks[c, b] = blocks[b, c].T
        rights.append(downs[b] * right[:, b * columns : (b + 1) * columns])
    for b in range(BLOCKS):
        (inverse,) = factor_inverses([blocks[b, b]])
        later = range(b + 1, BLOCKS)
        row = dot(inverse, jnp.concatenate([rights[b]] + [blocks[b, c] for c in later], axis=1))
        if later:
            column = jnp.concatenate([blocks[c, b] for c in later], axis=0)
            change = dot(dot(column, inverse, ((1,), (1,))), row)
        for i, c in enumerate(later):
            part = change[i * size : (i + 1) * size]
            rights[c] = rights[c] - part[:, :columns]
            for j, d in enumerate(later):
                start = columns + j * size
                blocks[c, d] = blocks[c, d] - part[:, start : start + size]
        row = dot(inverse, row, ((0,), (0,)))
        rights[b] = row[:, :columns]
        for c in later:
            blocks[b, c] = row[:, columns + (c - b - 1) * size : columns + (c - b) * size]
        for i in range(b):
            for c in later:
                blocks[i, c] = blocks[i, c] - dot(blocks[i, b], blocks[b, c])
            rights[i] = rights[i] - dot(blocks[i, b], rights[b])
    answer = [downs[b] * rights[b] for b in range(BLOCKS)]
    answer_ref[...] = jnp.concatenate(answer, axis=0)


def rows_kernel(ncon, flag_ref, here_ref, there_ref, *refs):
    hit = flag_ref[0:1, 0:1] > 0.5
    rows = jnp.where(hit, here_ref[: 2 * ncon], there_ref[: 2 * ncon])
    refs[-1][...] = rows
    send(refs[:-1], AXES[0], rows[:ncon], rows[ncon:])


def last_product(spread, mine, theirs):
    high, low = split(jnp.concatenate([mine, theirs], axis=0))
    return lax.dot_general(
        spread,
        jnp.concatenate([high, low, high], axis=0),
        (((1,), (0,)), ((), ())),
        preferred_element_type=jnp.float32,
    )


def through(inverse, mine, theirs, my_answer, their_answer):
    high, low = split(jnp.concatenate([mine, theirs], axis=0).T)
    spread = jnp.concatenate([high, high, low], axis=1)
    return wide(inverse, split(last_product(spread, my_answer, their_answer)))


def last_faces(values, width, out_ref, result, sems):
    copies = []
    for f, value in values.items():
        place = pl.ds(f * width, width)
        result[f * width : (f + 1) * width] = value()
        copy = pltpu.make_async_copy(result.at[place], out_ref.at[place], sems.at[f])
        copy.start()
        copies.append(copy)
    for copy in copies:
        copy.wait()


def last_plain_kernel(faces, product_ref, early_inverse, late_inverse, answer_ref, *refs):
    inputs, rest = refs[:-3], refs[-3:]
    ncon, width = product_ref.shape[1:]
    values = {}
    done = 0
    near = []
    for axis in AXES[1:] * 2:
        number = face_arrays(lax.axis_size(axis))
        near += receive(inputs[done : done + number], axis)
        done += number
    for f in range(2, FACES):
        values[f] = functools.partial(
            through,
            find(faces, (early_inverse, late_inverse), f),
            product_ref[f],
            near[f - 2],
            answer_ref[f * ncon : (f + 1) * ncon],
            near[f + 2],
        )
    last_faces(values, width, *rest)


def last_near_kernel(
    faces,
    columns,
    flag_ref,
    product_ref,
    early_inverse,
    late_inverse,
    there_ref,
    matrix_ref,
    right_ref,
    matrix_last,
    here_answer,
    there_answer,
    *refs,
):
    ncon, width = product_ref.shape[1:]
    half = width // 2
    lanes = matrix_ref.shape[1] - half
    inner = unfold(there_ref[:, lanes + BLOCKS * columns : lanes + BLOCKS * columns + half])
    outer = unfold(matrix_ref[:, lanes:])
    upward = is_even("gy")
    theirs = {
        2: jnp.where(upward, outer, inner),
        3: jnp.where(upward, inner, outer),
        4: unfold(matrix_last[:, lanes:]),
        5: unfold(right_ref[:, BLOCKS * columns :]),
    }

    def answer(flag, f):
        place = slice(f * ncon, (f + 1) * ncon)
        hit = flag_ref[flag : flag + 1, 0:1] > 0.5
        return jnp.where(hit, here_answer[place], there_answer[place])

    values = {}
    for f in range(2, FACES):
        values[f] = functools.partial(
            through,
            find(faces, (early_inverse, late_inverse), f),
            product_ref[f],
            theirs[f],
            answer(0, f),
            answer(f, f ^ 1),
        )
    last_faces(values, width, *refs)


def last_far_kernel(ncon, spread_ref, rows_ref, *refs):
    theirs = receive(refs[:-4], AXES[0])
    values = {}
    for f in range(2):
        mine = rows_ref[f * ncon : (f + 1) * ncon]
        values[f] = functools.partial(last_product, spread_ref[f], mine, theirs[f])
    last_faces(values, spread_ref.shape[1], *refs[-3:])


def per_device(schur, start_block, resid, group_of):
    matrix = schur[0, 0, 0]
    matrix = pltpu.with_memory_space_constraint(matrix, pltpu.HBM)
    starts = start_block[0, 0, 0].transpose(0, 2, 1)
    right = resid[0, 0, 0]
    order, columns = right.shape
    ncon, width = starts.shape[1:]
    counts = [lax.axis_size(axis) for axis in AXES]
    arrays = sum(face_arrays(count) for count in counts)
    coarse = FACES * ncon
    size = 2 * ncon
    half = width // 2
    lanes = size * BLOCKS * (BLOCKS + 1) // 2
    right_lanes = BLOCKS * columns
    uppers = FACES * (FACES - 1) // 2
    anywhere = pl.BlockSpec(memory_space=pl.ANY)
    main_memory = pl.BlockSpec(memory_space=pltpu.HBM)
    scalars = pl.BlockSpec(memory_space=pltpu.SMEM)
    early, late = (4, 5), (0, 1, 2, 3)
    faces = (early, late)
    planes = counts[2]

    def shape(*dims):
        return jax.ShapeDtypeStruct(dims, jnp.float32)

    def halves(count):
        return jax.ShapeDtypeStruct((count, 2, width, width), jnp.bfloat16)

    def params(mib):
        return pltpu.CompilerParams(vmem_limit_bytes=mib * MIB)

    def cost(us):
        return pl.CostEstimate(flops=us * 10**9, bytes_accessed=2**20, transcendentals=0)

    *packed, own = pl.pallas_call(
        functools.partial(pack_kernel, counts, width),
        out_shape=face_shapes(counts[0], (width + 8 + 2 * ncon, half))
        + face_shapes(counts[1], (width + 8 + 2 * ncon, half))
        + face_shapes(counts[2], (width + 8, half))
        + [shape(FACES, width, width)],
        in_specs=[main_memory, main_memory],
        out_specs=vmem_specs(arrays + 1),
        scratch_shapes=[
            pltpu.VMEM((4, ncon, width), jnp.float32),
            pltpu.SemaphoreType.DMA((FACES,)),
            pltpu.SemaphoreType.DMA,
        ],
        compiler_params=params(12),
    )(matrix, pltpu.with_memory_space_constraint(starts, pltpu.HBM))
    ends = [sum(face_arrays(count) for count in counts[:position]) for position in range(4)]
    got = {}
    for position in (2, 0, 1):
        got[position] = exchange(packed[ends[position] : ends[position + 1]], AXES[position])

    own_halves, upper_halves, flags = pl.pallas_call(
        functools.partial(halves_kernel, planes),
        out_shape=[halves(FACES), halves(uppers), shape(8, 128)],
        in_specs=[main_memory, scalars] + vmem_specs(1),
        out_specs=vmem_specs(3),
        scratch_shapes=[
            pltpu.VMEM((FACES - 1, width, order), jnp.float32),
            pltpu.SemaphoreType.DMA((FACES - 1,)),
        ],
        compiler_params=params(24),
        cost_estimate=cost(2),
    )(matrix, group_of, own)

    early_basis, early_partner, early_inverse = pl.pallas_call(
        functools.partial(early_kernel, AXES[2:3], early),
        out_shape=[shape(len(early), ncon, width)] + [halves(len(early))] * 2,
        in_specs=vmem_specs(len(got[2]) + 3),
        out_specs=vmem_specs(3),
        scratch_shapes=[pltpu.VMEM((len(early), 2, width, width), jnp.bfloat16)],
        compiler_params=params(16),
        cost_estimate=cost(2),
    )(*got[2], own, own_halves, starts)

    payload, product, late_partner, late_inverse = pl.pallas_call(
        functools.partial(main_kernel, (AXES[0], AXES[1]), early, late),
        out_shape=[shape(size, lanes + right_lanes + 2 * half), shape(FACES, ncon, width)]
        + [halves(len(late))] * 2,
        in_specs=vmem_specs(len(got[0]) + len(got[1]) + 6),
        out_specs=vmem_specs(4),
        scratch_shapes=[pltpu.VMEM((len(late), 2, width, width), jnp.bfloat16)],
        compiler_params=params(24),
        cost_estimate=cost(8),
    )(*got[0], *got[1], own, own_halves, upper_halves, starts, right, early_basis)

    partners = [early_partner, late_partner]
    inverses = [early_inverse, late_inverse]
    def spread_of(token):
        return pl.pallas_call(
            functools.partial(spread_kernel, faces, ncon),
            out_shape=jax.ShapeDtypeStruct((2, width, 3 * size), jnp.bfloat16),
            in_specs=[anywhere] + vmem_specs(len(got[0]) + 6),
            out_specs=vmem_specs(1)[0],
            compiler_params=params(16),
            cost_estimate=cost(3),
        )(token, *got[0], own_halves, product, *partners, *inverses)

    def solve(matrices, rights):
        return pl.pallas_call(
            functools.partial(solve_kernel, size, len(matrices), columns),
            out_shape=shape(coarse, columns),
            in_specs=vmem_specs(2 * len(matrices)),
            out_specs=vmem_specs(1)[0],
            compiler_params=params(12),
            cost_estimate=cost(7),
        )(*matrices, *rights)

    result = dict(
        out_shape=shape(order, columns),
        out_specs=main_memory,
        scratch_shapes=[
            pltpu.VMEM((order, columns), jnp.float32),
            pltpu.SemaphoreType.DMA((FACES,)),
        ],
        compiler_params=params(12),
        cost_estimate=cost(1),
    )
    groups = group_of.shape[0] // GROUP_SIZE
    if groups == 2 and counts[1] == 4 and planes == 2:
        core_swap, chip_x, chip_y = flipped("gy", 1), flipped("gy", 2), flipped("gz", 1)
        other = lax.ppermute(payload, "gy", core_swap)
        left, rest = pl.pallas_call(
            choose_kernel,
            out_shape=[shape(size, lanes + half), shape(size, right_lanes + half)],
            in_specs=vmem_specs(4),
            out_specs=vmem_specs(2),
            compiler_params=params(8),
        )(flags, payload, other, product)
        left_moved = lax.ppermute(left, "gy", chip_x)
        rest_moved = lax.ppermute(rest, "gz", chip_y)
        spread = spread_of(left)
        left_last, rest_last = pl.pallas_call(
            add_kernel,
            out_shape=[shape(size, lanes + half), shape(size, right_lanes)],
            in_specs=vmem_specs(5) + [anywhere],
            out_specs=vmem_specs(2),
            compiler_params=params(8),
        )(left, left_moved, rest, rest_moved, product, spread)
        left_other = lax.ppermute(left_last, "gz", chip_y)
        rest_other = lax.ppermute(rest_last, "gy", chip_x)
        answer = solve([left_last, left_other], [rest_last, rest_other])
        there = lax.ppermute(answer, "gy", core_swap)
        *sent, mine = pl.pallas_call(
            functools.partial(rows_kernel, ncon),
            out_shape=face_shapes(counts[0], (ncon, columns)) + [shape(size, columns)],
            in_specs=vmem_specs(3),
            out_specs=vmem_specs(face_arrays(counts[0]) + 1),
            compiler_params=params(8),
        )(flags, answer, there)
        across = exchange(sent, AXES[0])
        correction = pl.pallas_call(
            functools.partial(last_near_kernel, faces, columns),
            in_specs=vmem_specs(10),
            **result,
        )(
            flags, product, *inverses, other, left_moved, rest_moved, left_other, answer, there
        )
    else:
        y, z = lax.axis_index("gy"), lax.axis_index("gz")
        member_of = group_of[y * planes + z]
        chosen = jnp.arange(groups, dtype=jnp.int32) == member_of
        part = payload[:, : lanes + right_lanes]
        total = lax.psum(jnp.where(chosen[:, None, None], part[None], 0.0), ("gy", "gz"))
        total = lax.dynamic_index_in_dim(total, member_of, 0, keepdims=False)
        spread = spread_of(payload)
        answer = solve([total[:, :lanes]], [total[:, lanes:]])

        def from_near(faces_of, axis):
            even, odd = faces_of
            if lax.axis_size(axis) == 2:
                return exchange([jnp.stack([even, odd])], axis)
            upward = is_even(axis)
            return exchange([jnp.where(upward, even, odd), jnp.where(upward, odd, even)], axis)

        blocks = answer.reshape(FACES, ncon, columns)
        near = []
        for parts in (product, blocks):
            near += from_near(parts[2:4], AXES[1]) + from_near(parts[4:6], AXES[2])
        mine = answer[:size]
        across = from_near(blocks[:2], AXES[0])
        correction = pl.pallas_call(
            functools.partial(last_plain_kernel, faces),
            in_specs=vmem_specs(4 + len(near)),
            **result,
        )(product, *inverses, answer, *near)
    correction = pl.pallas_call(
        functools.partial(last_far_kernel, ncon),
        in_specs=vmem_specs(2 + len(across)) + [main_memory],
        input_output_aliases={2 + len(across): 0},
        **result,
    )(spread, mine, *across, correction)
    return correction[None, None, None]


def solution(mesh):
    in_specs = (
        P("gx", "gy", "gz", None, None),
        P("gx", "gy", "gz", None, None, None),
        P("gx", "gy", "gz", None, None),
        P(),
    )
    out_specs = P("gx", "gy", "gz", None, None)
    return jax.shard_map(
        per_device, mesh=mesh, in_specs=in_specs, out_specs=out_specs, check_vma=False
    )
```

```python
import functools

import jax
import jax.numpy as jnp
from jax import lax
from jax.experimental import pallas as pl
from jax.experimental.pallas import tpu as pltpu
from jax.sharding import PartitionSpec as P

NS_ITERS = 3
SUB_ITERS = 2
GROUP_SIZE = 4
FACES = 6
BLOCKS = FACES // 2
AXES = ("gx", "gy", "gz")
MIB = 1024 * 1024

precise = lax.Precision.HIGHEST


def dot(left, right, dims=((1,), (0,))):
    return lax.dot_general(
        left, right, (dims, ((), ())), precision=precise, preferred_element_type=jnp.float32
    )


def split(value):
    high = value.astype(jnp.bfloat16)
    return high, (value - high.astype(jnp.float32)).astype(jnp.bfloat16)


def wide(left, right):
    return lax.dot_general(
        jnp.concatenate([left[0], left[0], left[1]], axis=1),
        jnp.concatenate([right[0], right[1], right[0]], axis=0),
        (((1,), (0,)), ((), ())),
        preferred_element_type=jnp.float32,
    )


def stacked(value):
    return jnp.concatenate(split(value), axis=0)


def thin(rows, matrix):
    out = lax.dot_general(
        jnp.concatenate([rows, rows], axis=1),
        jnp.concatenate(matrix, axis=0),
        (((1,), (0,)), ((), ())),
        preferred_element_type=jnp.float32,
    )
    half = rows.shape[0] // 2
    return out[:half] + out[half:]


def iota(shape, dim):
    return lax.broadcasted_iota(jnp.int32, shape, dim)


def flipped(axis, bit):
    return [(i, i ^ bit) for i in range(lax.axis_size(axis))]


def outer_pairs(axis):
    count = lax.axis_size(axis)
    return [(i, (i + 1 if i % 2 else i - 1) % count) for i in range(count)]


def face_arrays(count):
    return 1 if count == 2 else 2


def exchange(arrays, axis):
    if lax.axis_size(axis) == 2:
        return [lax.ppermute(arrays[0], axis, flipped(axis, 1))]
    return [
        lax.ppermute(arrays[0], axis, outer_pairs(axis)),
        lax.ppermute(arrays[1], axis, flipped(axis, 1)),
    ]


def is_even(axis):
    return lax.rem(lax.axis_index(axis), 2) == 0


def send(refs, axis, even, odd):
    if lax.axis_size(axis) == 2:
        refs[0][0] = even
        refs[0][1] = odd
    else:
        upward = is_even(axis)
        refs[0][...] = jnp.where(upward, even, odd)
        refs[1][...] = jnp.where(upward, odd, even)


def receive(refs, axis):
    if lax.axis_size(axis) == 2:
        return refs[0][1], refs[0][0]
    upward = is_even(axis)
    first, second = refs[0][...], refs[1][...]
    return jnp.where(upward, first, second), jnp.where(upward, second, first)


def face_shapes(count, shape):
    if count == 2:
        return [jax.ShapeDtypeStruct((2,) + shape, jnp.float32)]
    return [jax.ShapeDtypeStruct(shape, jnp.float32)] * 2


def vmem_specs(count):
    return [pl.BlockSpec(memory_space=pltpu.VMEM)] * count


def pack_kernel(counts, width, schur_ref, *refs):
    outs, blocks, sems = refs[:-2], refs[-2], refs[-1]
    half = width // 2
    copies = []
    for f in range(FACES):
        place = pl.ds(f * width, width)
        copy = pltpu.make_async_copy(schur_ref.at[place, place], blocks.at[f], sems.at[f])
        copy.start()
        copies.append(copy)
    row, col = iota((half, half), 0), iota((half, half), 1)

    def pack(f):
        copies[f].wait()
        first = blocks[f, 0:half, 0:half]
        second = blocks[f, half:width, half:width]
        diag = jnp.sum(jnp.where(row == col, second, 0.0), axis=0, keepdims=True)
        mixed = jnp.where(row >= col, first, second)
        tail = jnp.broadcast_to(diag, (8, half))
        return jnp.concatenate([blocks[f, half:width, 0:half], mixed, tail], axis=0)

    done = 0
    for position, axis in enumerate(AXES):
        number = face_arrays(counts[position])
        send(outs[done : done + number], axis, pack(2 * position), pack(2 * position + 1))
        done += number


def unpack(packed):
    half = packed.shape[1]
    row, col = iota((half, half), 0), iota((half, half), 1)
    low = packed[0:half]
    mixed = packed[half : 2 * half]
    flip = mixed.T
    first = jnp.where(row >= col, mixed, flip)
    second = jnp.where(row < col, mixed, flip)
    second = jnp.where(row == col, packed[2 * half : 2 * half + 1], second)
    return jnp.concatenate(
        [jnp.concatenate([first, low.T], axis=1), jnp.concatenate([low, second], axis=1)], axis=0
    )


def factor_inverses(grams, block=8):
    size = grams[0].shape[0]
    strips = size // 8
    lanes = 128
    full = (8, lanes)
    state = []
    for gram in grams:
        parts = [gram, jnp.where(iota((size, size), 0) == iota((size, size), 1), 1.0, 0.0)]
        if 2 * size < lanes:
            parts.append(jnp.zeros((size, lanes - 2 * size), jnp.float32))
        whole = jnp.concatenate(parts, axis=1)
        state.append([whole[8 * s : 8 * s + 8] for s in range(strips)])
    below = iota(full, 0)

    def line_of(strip, line):
        return jnp.broadcast_to(strip[line : line + 1], full)

    for start in range(0, size, block):
        strip, first = start // 8, start % 8
        active = range(strip, strips)
        for work in state:
            cols = [
                {s: jnp.broadcast_to(work[s][:, start + j : start + j + 1], full) for s in active}
                for j in range(block)
            ]
            factors = []

            def eliminate(j, scale, stop):
                line = first + j
                factor = {s: cols[j][s] * scale for s in active}
                factor[strip] = jnp.where(below > line, factor[strip], 0.0)
                for later in range(j + 1, stop):
                    head = line_of(cols[later][strip], line)
                    for s in active:
                        cols[later][s] = cols[later][s] - factor[s] * head
                factors.append(factor)

            for j in range(0, block, 2):
                line = first + j
                corner = line_of(cols[j][strip], line)
                side = line_of(cols[j][strip], line + 1)
                last = line_of(cols[j + 1][strip], line + 1)
                inverse = 1.0 / (corner * last - side * side)
                eliminate(j, 1.0 / corner, block)
                eliminate(j + 1, corner * inverse, block)
            for j in range(block):
                row = line_of(work[strip], first + j)
                for s in active:
                    if s == strip and first + j == 7:
                        continue
                    work[s] = work[s] - factors[j][s] * row
    results = []
    for work in state:
        parts = []
        for s in range(strips):
            place = iota((8, size), 0) + 8 * s == iota((8, size), 1)
            pivot = jnp.sum(jnp.where(place, work[s][:, :size], 0.0), axis=1, keepdims=True)
            parts.append(work[s][:, size : 2 * size] * lax.rsqrt(pivot))
        results.append(jnp.concatenate(parts, axis=0))
    return results


def member(group_ref, planes, dy=0, dz=0):
    y, z = lax.axis_index("gy"), lax.axis_index("gz")
    rows = lax.axis_size("gy")
    return group_ref[lax.rem(y + dy + rows, rows) * planes + lax.rem(z + dz + planes, planes)]


def store(ref, f, value):
    ref[f, 0], ref[f, 1] = split(value)


def load(ref, f):
    return ref[f, 0], ref[f, 1]


def upper_index(f, g):
    return sum(FACES - 1 - i for i in range(f)) + g - f - 1


def halves_kernel(planes, schur_ref, group_ref, own_ref, own_out, upper_out, flag_out, *scratch):
    upper_ref, sems = scratch
    width = own_ref.shape[1]
    strips = []
    for f in range(FACES - 1):
        rest = (FACES - 1 - f) * width
        copy = pltpu.make_async_copy(
            schur_ref.at[pl.ds(f * width, width), pl.ds((f + 1) * width, rest)],
            upper_ref.at[f, :, pl.ds((f + 1) * width, rest)],
            sems.at[f],
        )
        copy.start()
        strips.append(copy)
    core = lax.rem(lax.axis_index("gy"), 2)
    near = [(0, 0), (1 - 2 * core, 0), (-1, 0), (1, 0), (0, -1), (0, 1)]
    row = iota(flag_out.shape, 0)
    flags = jnp.zeros(flag_out.shape, jnp.float32)
    for i, (dy, dz) in enumerate(near):
        hit = member(group_ref, planes, dy, dz) == core
        flags = jnp.where(row == i, jnp.where(hit, 1.0, 0.0), flags)
    flag_out[...] = flags
    for f in range(FACES):
        store(own_out, f, own_ref[f])
    for f in range(FACES - 1):
        strips[f].wait()
        for g in range(f + 1, FACES):
            store(upper_out, upper_index(f, g), upper_ref[f, :, g * width : (g + 1) * width])


def begin(packed, owns, partner_out, sum_ref):
    width = owns[0].shape[1]
    eye = iota((width, width), 0) == iota((width, width), 1)
    guesses = []
    for f in range(len(packed)):
        partner = unpack(packed[f])
        total = owns[f] + partner
        store(partner_out, f, partner)
        store(sum_ref, f, total)
        diagonal = jnp.where(eye, total, 0.0)
        across = 1.0 / jnp.sum(diagonal, axis=0, keepdims=True)
        down = 1.0 / jnp.sum(diagonal, axis=1, keepdims=True)
        guesses.append(jnp.where(eye, 2.0 * across, 0.0) - down * total * across)
    return guesses


def newton(guesses, sum_ref):
    results = []
    for f, guess in enumerate(guesses):
        halves = split(guess)
        product = split(wide(load(sum_ref, f), halves))
        results.append(2.0 * guess - wide(halves, product))
    return results


def unit_rows(basis):
    return [b * lax.rsqrt(jnp.sum(b * b, axis=1, keepdims=True)) for b in basis]


def sweep_basis(before, inverse, after, basis):
    for matrices in (before, inverse, after):
        basis = [thin(stacked(b), matrix) for b, matrix in zip(basis, matrices)]
    return unit_rows(basis)


def early_kernel(axes, faces, *refs):
    arrays = len(refs) - 7
    inputs = refs[:arrays]
    own_ref, halves_ref, starts_ref, basis_out, partner_out, inverse_out, sum_ref = refs[arrays:]
    count = len(faces)
    packed = []
    done = 0
    for axis in axes:
        number = face_arrays(lax.axis_size(axis))
        packed += receive(inputs[done : done + number], axis)
        done += number
    guesses = begin(packed, [own_ref[f] for f in faces], partner_out, sum_ref)
    for sweep in range(NS_ITERS - 1):
        guesses = newton(guesses, sum_ref)
    for i in range(count):
        store(inverse_out, i, guesses[i])
    basis = [starts_ref[f] for f in faces]
    matrices = [
        [load(partner_out, i) for i in range(count)],
        [load(inverse_out, i) for i in range(count)],
        [load(halves_ref, f) for f in faces],
    ]
    for sweep in range(SUB_ITERS):
        basis = sweep_basis(*matrices, basis)
    for i in range(count):
        basis_out[i] = basis[i]


def main_kernel(axes, early, late, *refs):
    arrays = len(refs) - 11
    inputs = refs[:arrays]
    own_ref, halves_ref, upper_ref, starts_ref, resid_ref, early_basis = refs[arrays : arrays + 6]
    payload_ref, product_ref, partner_out, inverse_out, sum_ref = refs[arrays + 6 :]
    ncon, width = starts_ref.shape[1:]
    columns = resid_ref.shape[1]
    sides = {}
    rights = {}
    grams = {}
    vectors = {}
    count = len(late)

    def project(f, basis):
        vectors[f] = basis
        rows = stacked(basis)
        grams[f] = dot(basis, basis, ((1,), (1,)))
        side = {f: thin(rows, load(halves_ref, f))}
        for g in range(f + 1, FACES):
            side[g] = thin(rows, load(upper_ref, upper_index(f, g)))
        sides[f] = side
        rights[f] = thin(rows, split(resid_ref[f * width : (f + 1) * width]))

    packed = []
    done = 0
    for axis in axes:
        number = face_arrays(lax.axis_size(axis))
        packed += receive(inputs[done : done + number], axis)
        done += number
    guesses = begin(packed, [own_ref[f] for f in late], partner_out, sum_ref)
    pending = [(f, early_basis[i]) for i, f in enumerate(early)]
    for sweep in range(NS_ITERS - 1):
        guesses = newton(guesses, sum_ref)
        if pending:
            project(*pending.pop(0))
    for i in range(count):
        store(inverse_out, i, guesses[i])
    basis = [starts_ref[f] for f in late]
    matrices = [
        [load(partner_out, i) for i in range(count)],
        [load(inverse_out, i) for i in range(count)],
        [load(halves_ref, f) for f in late],
    ]
    for sweep in range(SUB_ITERS):
        basis = sweep_basis(*matrices, basis)
        if pending:
            project(*pending.pop(0))
    for item in pending:
        project(*item)
    for i, f in enumerate(late):
        project(f, basis[i])
    factors = factor_inverses([grams[f] for f in range(FACES)])
    blocks = []
    for g in range(FACES):
        tall = jnp.concatenate([sides[f][g] for f in range(g + 1)], axis=0)
        blocks.append(dot(dot(tall, vectors[g], ((1,), (1,))), factors[g], ((1,), (1,))))
    even, odd, right, products = [], [], [], []
    lows = None
    for f in range(FACES):
        products.append(dot(factors[f], sides[f][f]))
        product_ref[f] = products[f]
        line = [blocks[g][f * ncon : (f + 1) * ncon] for g in range(f, FACES)]
        line = dot(factors[f], jnp.concatenate([rights[f]] + line, axis=1))
        right.append(line[:, :columns])
        line = line[:, columns:]
        if f % 2 == 0:
            even.append(line)
            lows = line[:, ncon : 2 * ncon].T
        else:
            odd += [lows, line]
    upward = is_even("gy")
    inner = jnp.where(upward, products[3], products[2])
    outer = jnp.where(upward, products[2], products[3])
    whole = [
        jnp.concatenate(even + right[0::2], axis=1),
        jnp.concatenate(odd + right[1::2], axis=1),
    ]
    payload_ref[...] = jnp.concatenate(
        [jnp.concatenate(whole, axis=0), fold(inner), fold(outer)], axis=1
    )


def fold(product):
    half = product.shape[1] // 2
    return jnp.concatenate([product[:, :half], product[:, half:]], axis=0)


def unfold(rows):
    half = rows.shape[0] // 2
    return jnp.concatenate([rows[:half], rows[half:]], axis=1)


def find(faces, refs, f):
    for group, ref in zip(faces, refs):
        if f in group:
            return load(ref, list(group).index(f))


def spread_pair(mine, theirs, inverse):
    high, low = split(thin(stacked(jnp.concatenate([mine, theirs], axis=0)), inverse).T)
    return jnp.concatenate([high, high, low], axis=1)


def their_y_products(there_ref, matrix_ref, start):
    half = (there_ref.shape[1] - start) // 2
    inner = unfold(there_ref[:, start : start + half])
    outer = unfold(matrix_ref[:, matrix_ref.shape[1] - half :])
    upward = is_even("gy")
    return jnp.where(upward, outer, inner), jnp.where(upward, inner, outer)


def spread_kernel(faces, start, unread, product_ref, early_inverse, late_inverse, *refs):
    out_ref = refs[-1]
    inverses = (early_inverse, late_inverse)
    ready = refs[:-1]
    if start:
        ready, (there_ref, matrix_ref, right_ref) = refs[:-4], refs[-4:-1]
    theirs = list(receive(ready, AXES[0]))
    if start:
        theirs += their_y_products(there_ref, matrix_ref, start)
        half = product_ref.shape[2] // 2
        theirs.append(unfold(right_ref[:, right_ref.shape[1] - half :]))
    for i, product in enumerate(theirs):
        f = i if i < 4 else FACES - 1
        out_ref[i] = spread_pair(product_ref[f], product, find(faces, inverses, f))


def choose_kernel(flag_ref, here_ref, there_ref, product_ref, matrix_ref, right_ref, *sent):
    mine = flag_ref[0:1, 0:1] > 0.5
    other = flag_ref[1:2, 0:1] > 0.5
    half = product_ref.shape[2] // 2
    lanes, wide_lanes = matrix_ref.shape[1] - half, here_ref.shape[1] - 2 * half
    here, there = here_ref[:, :wide_lanes], there_ref[:, :wide_lanes]
    total = jnp.where(mine, here, 0.0) + jnp.where(other, there, 0.0)
    outer = there_ref[:, wide_lanes + half :]
    matrix_ref[...] = jnp.concatenate([total[:, :lanes], outer], axis=1)
    right_ref[...] = jnp.concatenate([total[:, lanes:], fold(product_ref[4])], axis=1)
    send(sent, AXES[0], product_ref[0], product_ref[1])


def add_kernel(first_ref, second_ref, third_ref, fourth_ref, product_ref, *refs):
    matrix_ref, right_ref = refs[-2:]
    half = product_ref.shape[2] // 2
    lanes, right_lanes = matrix_ref.shape[1] - half, right_ref.shape[1]
    total = first_ref[:, :lanes] + second_ref[:, :lanes]
    matrix_ref[...] = jnp.concatenate([total, fold(product_ref[5])], axis=1)
    right_ref[...] = third_ref[:, :right_lanes] + fourth_ref[:, :right_lanes]


def solve_kernel(size, terms, columns, *refs):
    lanes = size * BLOCKS * (BLOCKS + 1) // 2
    matrix, right = refs[0][:, :lanes], refs[terms][...]
    for term in range(1, terms):
        matrix = matrix + refs[term][:, :lanes]
        right = right + refs[terms + term][...]
    answer_ref = refs[-1]
    lines = []
    offset = 0
    for b in range(BLOCKS):
        lines.append(matrix[:, offset : offset + (BLOCKS - b) * size])
        offset += (BLOCKS - b) * size
    eye = iota((size, size), 0) == iota((size, size), 1)
    downs, acrosses = [], []
    for b in range(BLOCKS):
        diagonal = jnp.where(eye, lines[b][:, :size], 0.0)
        downs.append(lax.rsqrt(jnp.sum(diagonal, axis=1, keepdims=True)))
        acrosses.append(lax.rsqrt(jnp.sum(diagonal, axis=0, keepdims=True)))
    blocks = {}
    rights = []
    for b in range(BLOCKS):
        for c in range(b, BLOCKS):
            block = lines[b][:, (c - b) * size : (c - b + 1) * size]
            blocks[b, c] = downs[b] * block * acrosses[c]
            if c > b:
                blocks[c, b] = blocks[b, c].T
        rights.append(downs[b] * right[:, b * columns : (b + 1) * columns])
    for b in range(BLOCKS):
        (inverse,) = factor_inverses([blocks[b, b]])
        later = range(b + 1, BLOCKS)
        row = dot(inverse, jnp.concatenate([rights[b]] + [blocks[b, c] for c in later], axis=1))
        if later:
            column = jnp.concatenate([blocks[c, b] for c in later], axis=0)
            change = dot(dot(column, inverse, ((1,), (1,))), row)
        for i, c in enumerate(later):
            part = change[i * size : (i + 1) * size]
            rights[c] = rights[c] - part[:, :columns]
            for j, d in enumerate(later):
                start = columns + j * size
                blocks[c, d] = blocks[c, d] - part[:, start : start + size]
        row = dot(inverse, row, ((0,), (0,)))
        rights[b] = row[:, :columns]
        for c in later:
            blocks[b, c] = row[:, columns + (c - b - 1) * size : columns + (c - b) * size]
        for i in range(b):
            for c in later:
                blocks[i, c] = blocks[i, c] - dot(blocks[i, b], blocks[b, c])
            rights[i] = rights[i] - dot(blocks[i, b], rights[b])
    answer = [downs[b] * rights[b] for b in range(BLOCKS)]
    answer_ref[...] = jnp.concatenate(answer, axis=0)


def rows_kernel(ncon, flag_ref, here_ref, there_ref, *refs):
    hit = flag_ref[0:1, 0:1] > 0.5
    rows = jnp.where(hit, here_ref[: 2 * ncon], there_ref[: 2 * ncon])
    refs[-1][...] = rows
    send(refs[:-1], AXES[0], rows[:ncon], rows[ncon:])


def last_product(spread, mine, theirs):
    high, low = split(jnp.concatenate([mine, theirs], axis=0))
    return lax.dot_general(
        spread,
        jnp.concatenate([high, low, high], axis=0),
        (((1,), (0,)), ((), ())),
        preferred_element_type=jnp.float32,
    )


def through(inverse, mine, theirs, my_answer, their_answer):
    high, low = split(jnp.concatenate([mine, theirs], axis=0).T)
    spread = jnp.concatenate([high, high, low], axis=1)
    return wide(inverse, split(last_product(spread, my_answer, their_answer)))


def last_faces(values, width, out_ref, result, sems):
    copies = []
    for f, value in values.items():
        place = pl.ds(f * width, width)
        result[f * width : (f + 1) * width] = value()
        copy = pltpu.make_async_copy(result.at[place], out_ref.at[place], sems.at[f])
        copy.start()
        copies.append(copy)
    for copy in copies:
        copy.wait()


def last_plain_kernel(faces, product_ref, early_inverse, late_inverse, answer_ref, *refs):
    inputs, rest = refs[:-3], refs[-3:]
    ncon, width = product_ref.shape[1:]
    values = {}
    done = 0
    near = []
    for axis in AXES[1:] * 2:
        number = face_arrays(lax.axis_size(axis))
        near += receive(inputs[done : done + number], axis)
        done += number
    for f in range(2, FACES):
        values[f] = functools.partial(
            through,
            find(faces, (early_inverse, late_inverse), f),
            product_ref[f],
            near[f - 2],
            answer_ref[f * ncon : (f + 1) * ncon],
            near[f + 2],
        )
    last_faces(values, width, *rest)


def last_near_kernel(
    faces, flag_ref, product_ref, early_inverse, late_inverse, matrix_ref, spread_ref, *refs
):
    here_answer, there_answer = refs[:2]
    ncon, width = product_ref.shape[1:]
    half = width // 2

    def answer(flag, f):
        place = slice(f * ncon, (f + 1) * ncon)
        hit = flag_ref[flag : flag + 1, 0:1] > 0.5
        return jnp.where(hit, here_answer[place], there_answer[place])

    values = {}
    for f in (2, 3, 5):
        values[f] = functools.partial(
            last_product, spread_ref[min(f, 4)], answer(0, f), answer(f, f ^ 1)
        )
    values[4] = functools.partial(
        through,
        find(faces, (early_inverse, late_inverse), 4),
        product_ref[4],
        unfold(matrix_ref[:, matrix_ref.shape[1] - half :]),
        answer(0, 4),
        answer(4, 5),
    )
    last_faces(values, width, *refs[2:])


def last_far_kernel(ncon, spread_ref, rows_ref, *refs):
    theirs = receive(refs[:-4], AXES[0])
    values = {}
    for f in range(2):
        mine = rows_ref[f * ncon : (f + 1) * ncon]
        values[f] = functools.partial(last_product, spread_ref[f], mine, theirs[f])
    last_faces(values, spread_ref.shape[1], *refs[-3:])


def per_device(schur, start_block, resid, group_of):
    matrix = schur[0, 0, 0]
    matrix = pltpu.with_memory_space_constraint(matrix, pltpu.HBM)
    starts = start_block[0, 0, 0].transpose(0, 2, 1)
    right = resid[0, 0, 0]
    order, columns = right.shape
    ncon, width = starts.shape[1:]
    counts = [lax.axis_size(axis) for axis in AXES]
    arrays = sum(face_arrays(count) for count in counts)
    coarse = FACES * ncon
    size = 2 * ncon
    half = width // 2
    lanes = size * BLOCKS * (BLOCKS + 1) // 2
    right_lanes = BLOCKS * columns
    uppers = FACES * (FACES - 1) // 2
    anywhere = pl.BlockSpec(memory_space=pl.ANY)
    main_memory = pl.BlockSpec(memory_space=pltpu.HBM)
    scalars = pl.BlockSpec(memory_space=pltpu.SMEM)
    early, late = (2, 3), (0, 1, 4, 5)
    faces = (early, late)
    planes = counts[2]

    def shape(*dims):
        return jax.ShapeDtypeStruct(dims, jnp.float32)

    def halves(count):
        return jax.ShapeDtypeStruct((count, 2, width, width), jnp.bfloat16)

    def params(mib):
        return pltpu.CompilerParams(vmem_limit_bytes=mib * MIB)

    def cost(us):
        return pl.CostEstimate(flops=us * 10**9, bytes_accessed=2**20, transcendentals=0)

    *packed, own = pl.pallas_call(
        functools.partial(pack_kernel, counts, width),
        out_shape=[part for count in counts for part in face_shapes(count, (width + 8, half))]
        + [shape(FACES, width, width)],
        in_specs=[main_memory],
        out_specs=vmem_specs(arrays + 1),
        scratch_shapes=[pltpu.SemaphoreType.DMA((FACES,))],
        compiler_params=params(12),
    )(matrix)
    ends = [sum(face_arrays(count) for count in counts[:position]) for position in range(4)]
    got = {}
    for position in (2, 0, 1):
        got[position] = exchange(packed[ends[position] : ends[position + 1]], AXES[position])

    own_halves, upper_halves, flags = pl.pallas_call(
        functools.partial(halves_kernel, planes),
        out_shape=[halves(FACES), halves(uppers), shape(8, 128)],
        in_specs=[main_memory, scalars] + vmem_specs(1),
        out_specs=vmem_specs(3),
        scratch_shapes=[
            pltpu.VMEM((FACES - 1, width, order), jnp.float32),
            pltpu.SemaphoreType.DMA((FACES - 1,)),
        ],
        compiler_params=params(24),
        cost_estimate=cost(2),
    )(matrix, group_of, own)

    early_basis, early_partner, early_inverse = pl.pallas_call(
        functools.partial(early_kernel, AXES[1:2], early),
        out_shape=[shape(len(early), ncon, width)] + [halves(len(early))] * 2,
        in_specs=vmem_specs(len(got[1]) + 3),
        out_specs=vmem_specs(3),
        scratch_shapes=[pltpu.VMEM((len(early), 2, width, width), jnp.bfloat16)],
        compiler_params=params(16),
        cost_estimate=cost(2),
    )(*got[1], own, own_halves, starts)

    payload, product, late_partner, late_inverse = pl.pallas_call(
        functools.partial(main_kernel, (AXES[0], AXES[2]), early, late),
        out_shape=[shape(size, lanes + right_lanes + 2 * half), shape(FACES, ncon, width)]
        + [halves(len(late))] * 2,
        in_specs=vmem_specs(len(got[0]) + len(got[2]) + 6),
        out_specs=vmem_specs(4),
        scratch_shapes=[pltpu.VMEM((len(late), 2, width, width), jnp.bfloat16)],
        compiler_params=params(24),
        cost_estimate=cost(8),
    )(*got[0], *got[2], own, own_halves, upper_halves, starts, right, early_basis)

    inverses = [early_inverse, late_inverse]
    def spread_of(token, theirs, start, *more):
        return pl.pallas_call(
            functools.partial(spread_kernel, faces, start),
            out_shape=jax.ShapeDtypeStruct((5 if start else 2, width, 3 * size), jnp.bfloat16),
            in_specs=[anywhere] + vmem_specs(3 + len(theirs) + len(more)),
            out_specs=vmem_specs(1)[0],
            compiler_params=params(16),
            cost_estimate=cost(3),
        )(token, product, *inverses, *theirs, *more)

    def solve(matrices, rights, unread):
        return pl.pallas_call(
            functools.partial(solve_kernel, size, len(matrices), columns),
            out_shape=shape(coarse, columns),
            in_specs=vmem_specs(2 * len(matrices)) + [anywhere],
            out_specs=vmem_specs(1)[0],
            compiler_params=params(12),
            cost_estimate=cost(7),
        )(*matrices, *rights, unread)

    result = dict(
        out_shape=shape(order, columns),
        out_specs=main_memory,
        scratch_shapes=[
            pltpu.VMEM((order, columns), jnp.float32),
            pltpu.SemaphoreType.DMA((FACES,)),
        ],
        compiler_params=params(12),
        cost_estimate=cost(1),
    )
    groups = group_of.shape[0] // GROUP_SIZE
    if groups == 2 and counts[1] == 4 and planes == 2:
        core_swap, chip_x, chip_y = flipped("gy", 1), flipped("gy", 2), flipped("gz", 1)
        other = lax.ppermute(payload, "gy", core_swap)
        left, rest, *sent = pl.pallas_call(
            choose_kernel,
            out_shape=[shape(size, lanes + half), shape(size, right_lanes + half)]
            + face_shapes(counts[0], (ncon, width)),
            in_specs=vmem_specs(4),
            out_specs=vmem_specs(2 + face_arrays(counts[0])),
            compiler_params=params(8),
        )(flags, payload, other, product)
        left_moved = lax.ppermute(left, "gy", chip_x)
        rest_moved = lax.ppermute(rest, "gz", chip_y)
        theirs = exchange(sent, AXES[0])
        left_last, rest_last = pl.pallas_call(
            add_kernel,
            out_shape=[shape(size, lanes + half), shape(size, right_lanes)],
            in_specs=vmem_specs(5) + [anywhere] * len(theirs),
            out_specs=vmem_specs(2),
            compiler_params=params(8),
        )(left, left_moved, rest, rest_moved, product, *theirs)
        left_other = lax.ppermute(left_last, "gz", chip_y)
        rest_other = lax.ppermute(rest_last, "gy", chip_x)
        spread = spread_of(
            left_last, theirs, lanes + right_lanes, other, left_moved, rest_moved
        )
        answer = solve([left_last, left_other], [rest_last, rest_other], spread)
        there = lax.ppermute(answer, "gy", core_swap)
        *sent, mine = pl.pallas_call(
            functools.partial(rows_kernel, ncon),
            out_shape=face_shapes(counts[0], (ncon, columns)) + [shape(size, columns)],
            in_specs=vmem_specs(3),
            out_specs=vmem_specs(face_arrays(counts[0]) + 1),
            compiler_params=params(8),
        )(flags, answer, there)
        across = exchange(sent, AXES[0])
        correction = pl.pallas_call(
            functools.partial(last_near_kernel, faces),
            in_specs=vmem_specs(8),
            **result,
        )(flags, product, *inverses, left_other, spread, answer, there)
    else:
        y, z = lax.axis_index("gy"), lax.axis_index("gz")
        member_of = group_of[y * planes + z]
        chosen = jnp.arange(groups, dtype=jnp.int32) == member_of
        part = payload[:, : lanes + right_lanes]
        total = lax.psum(jnp.where(chosen[:, None, None], part[None], 0.0), ("gy", "gz"))
        total = lax.dynamic_index_in_dim(total, member_of, 0, keepdims=False)
        answer = solve([total[:, :lanes]], [total[:, lanes:]], product)

        def from_near(faces_of, axis):
            even, odd = faces_of
            if lax.axis_size(axis) == 2:
                return exchange([jnp.stack([even, odd])], axis)
            upward = is_even(axis)
            return exchange([jnp.where(upward, even, odd), jnp.where(upward, odd, even)], axis)

        blocks = answer.reshape(FACES, ncon, columns)
        near = []
        for parts in (product, blocks):
            near += from_near(parts[2:4], AXES[1]) + from_near(parts[4:6], AXES[2])
        mine = answer[:size]
        across = from_near(blocks[:2], AXES[0])
        spread = spread_of(payload, from_near(product[:2], AXES[0]), 0)
        correction = pl.pallas_call(
            functools.partial(last_plain_kernel, faces),
            in_specs=vmem_specs(4 + len(near)),
            **result,
        )(product, *inverses, answer, *near)
    correction = pl.pallas_call(
        functools.partial(last_far_kernel, ncon),
        in_specs=vmem_specs(2 + len(across)) + [main_memory],
        input_output_aliases={2 + len(across): 0},
        **result,
    )(spread, mine, *across, correction)
    return correction[None, None, None]


def solution(mesh):
    in_specs = (
        P("gx", "gy", "gz", None, None),
        P("gx", "gy", "gz", None, None, None),
        P("gx", "gy", "gz", None, None),
        P(),
    )
    out_specs = P("gx", "gy", "gz", None, None)
    return jax.shard_map(
        per_device, mesh=mesh, in_specs=in_specs, out_specs=out_specs, check_vma=False
    )
```

```python
import functools

import jax
import jax.numpy as jnp
from jax import lax
from jax.experimental import pallas as pl
from jax.experimental.pallas import tpu as pltpu
from jax.sharding import PartitionSpec as P

NS_ITERS = 3
SUB_ITERS = 2
GROUP_SIZE = 4
FACES = 6
BLOCKS = FACES // 2
AXES = ("gx", "gy", "gz")
MIB = 1024 * 1024

precise = lax.Precision.HIGHEST


def dot(left, right, dims=((1,), (0,))):
    return lax.dot_general(
        left, right, (dims, ((), ())), precision=precise, preferred_element_type=jnp.float32
    )


def split(value):
    high = value.astype(jnp.bfloat16)
    return high, (value - high.astype(jnp.float32)).astype(jnp.bfloat16)


def wide(left, right):
    return lax.dot_general(
        jnp.concatenate([left[0], left[0], left[1]], axis=1),
        jnp.concatenate([right[0], right[1], right[0]], axis=0),
        (((1,), (0,)), ((), ())),
        preferred_element_type=jnp.float32,
    )


def stacked(value):
    return jnp.concatenate(split(value), axis=0)


def thin(rows, matrix):
    out = lax.dot_general(
        jnp.concatenate([rows, rows], axis=1),
        jnp.concatenate(matrix, axis=0),
        (((1,), (0,)), ((), ())),
        preferred_element_type=jnp.float32,
    )
    half = rows.shape[0] // 2
    return out[:half] + out[half:]


def iota(shape, dim):
    return lax.broadcasted_iota(jnp.int32, shape, dim)


def flipped(axis, bit):
    return [(i, i ^ bit) for i in range(lax.axis_size(axis))]


def outer_pairs(axis):
    count = lax.axis_size(axis)
    return [(i, (i + 1 if i % 2 else i - 1) % count) for i in range(count)]


def face_arrays(count):
    return 1 if count == 2 else 2


def exchange(arrays, axis):
    if lax.axis_size(axis) == 2:
        return [lax.ppermute(arrays[0], axis, flipped(axis, 1))]
    return [
        lax.ppermute(arrays[0], axis, flipped(axis, 1)),
        lax.ppermute(arrays[1], axis, outer_pairs(axis)),
    ]


def is_even(axis):
    return lax.rem(lax.axis_index(axis), 2) == 0


def send(refs, axis, even, odd):
    if lax.axis_size(axis) == 2:
        refs[0][0] = even
        refs[0][1] = odd
    else:
        upward = is_even(axis)
        refs[0][...] = jnp.where(upward, odd, even)
        refs[1][...] = jnp.where(upward, even, odd)


def receive(refs, axis):
    if lax.axis_size(axis) == 2:
        return refs[0][1], refs[0][0]
    upward = is_even(axis)
    first, second = refs[0][...], refs[1][...]
    return jnp.where(upward, second, first), jnp.where(upward, first, second)


def face_shapes(count, shape):
    if count == 2:
        return [jax.ShapeDtypeStruct((2,) + shape, jnp.float32)]
    return [jax.ShapeDtypeStruct(shape, jnp.float32)] * 2


def vmem_specs(count):
    return [pl.BlockSpec(memory_space=pltpu.VMEM)] * count


def pack_kernel(counts, width, schur_ref, *refs):
    outs, blocks, sems = refs[:-2], refs[-2], refs[-1]
    half = width // 2
    copies = []
    for f in range(FACES):
        place = pl.ds(f * width, width)
        copy = pltpu.make_async_copy(schur_ref.at[place, place], blocks.at[f], sems.at[f])
        copy.start()
        copies.append(copy)
    row, col = iota((half, half), 0), iota((half, half), 1)

    def pack(f):
        copies[f].wait()
        first = blocks[f, 0:half, 0:half]
        second = blocks[f, half:width, half:width]
        diag = jnp.sum(jnp.where(row == col, second, 0.0), axis=0, keepdims=True)
        mixed = jnp.where(row >= col, first, second)
        tail = jnp.broadcast_to(diag, (8, half))
        return jnp.concatenate([blocks[f, half:width, 0:half], mixed, tail], axis=0)

    done = 0
    for position, axis in enumerate(AXES):
        number = face_arrays(counts[position])
        send(outs[done : done + number], axis, pack(2 * position), pack(2 * position + 1))
        done += number


def unpack(packed):
    half = packed.shape[1]
    row, col = iota((half, half), 0), iota((half, half), 1)
    low = packed[0:half]
    mixed = packed[half : 2 * half]
    flip = mixed.T
    first = jnp.where(row >= col, mixed, flip)
    second = jnp.where(row < col, mixed, flip)
    second = jnp.where(row == col, packed[2 * half : 2 * half + 1], second)
    return jnp.concatenate(
        [jnp.concatenate([first, low.T], axis=1), jnp.concatenate([low, second], axis=1)], axis=0
    )


def factor_inverses(grams, block=8):
    size = grams[0].shape[0]
    strips = size // 8
    lanes = 128
    full = (8, lanes)
    state = []
    for gram in grams:
        parts = [gram, jnp.where(iota((size, size), 0) == iota((size, size), 1), 1.0, 0.0)]
        if 2 * size < lanes:
            parts.append(jnp.zeros((size, lanes - 2 * size), jnp.float32))
        whole = jnp.concatenate(parts, axis=1)
        state.append([whole[8 * s : 8 * s + 8] for s in range(strips)])
    below = iota(full, 0)

    def line_of(strip, line):
        return jnp.broadcast_to(strip[line : line + 1], full)

    for start in range(0, size, block):
        strip, first = start // 8, start % 8
        active = range(strip, strips)
        for work in state:
            cols = [
                {s: jnp.broadcast_to(work[s][:, start + j : start + j + 1], full) for s in active}
                for j in range(block)
            ]
            factors = []

            def eliminate(j, scale, stop):
                line = first + j
                factor = {s: cols[j][s] * scale for s in active}
                factor[strip] = jnp.where(below > line, factor[strip], 0.0)
                for later in range(j + 1, stop):
                    head = line_of(cols[later][strip], line)
                    for s in active:
                        cols[later][s] = cols[later][s] - factor[s] * head
                factors.append(factor)

            for j in range(0, block, 2):
                line = first + j
                corner = line_of(cols[j][strip], line)
                side = line_of(cols[j][strip], line + 1)
                last = line_of(cols[j + 1][strip], line + 1)
                inverse = 1.0 / (corner * last - side * side)
                eliminate(j, 1.0 / corner, block)
                eliminate(j + 1, corner * inverse, block)
            for j in range(block):
                row = line_of(work[strip], first + j)
                for s in active:
                    if s == strip and first + j == 7:
                        continue
                    work[s] = work[s] - factors[j][s] * row
    results = []
    for work in state:
        parts = []
        for s in range(strips):
            place = iota((8, size), 0) + 8 * s == iota((8, size), 1)
            pivot = jnp.sum(jnp.where(place, work[s][:, :size], 0.0), axis=1, keepdims=True)
            parts.append(work[s][:, size : 2 * size] * lax.rsqrt(pivot))
        results.append(jnp.concatenate(parts, axis=0))
    return results


def member(group_ref, planes, dy=0, dz=0):
    y, z = lax.axis_index("gy"), lax.axis_index("gz")
    rows = lax.axis_size("gy")
    return group_ref[lax.rem(y + dy + rows, rows) * planes + lax.rem(z + dz + planes, planes)]


def store(ref, f, value):
    ref[f, 0], ref[f, 1] = split(value)


def load(ref, f):
    return ref[f, 0], ref[f, 1]


def upper_index(f, g):
    return sum(FACES - 1 - i for i in range(f)) + g - f - 1


def halves_kernel(planes, schur_ref, group_ref, own_ref, own_out, upper_out, flag_out, *scratch):
    upper_ref, sems = scratch
    width = own_ref.shape[1]
    strips = []
    for f in range(FACES - 1):
        rest = (FACES - 1 - f) * width
        copy = pltpu.make_async_copy(
            schur_ref.at[pl.ds(f * width, width), pl.ds((f + 1) * width, rest)],
            upper_ref.at[f, :, pl.ds((f + 1) * width, rest)],
            sems.at[f],
        )
        copy.start()
        strips.append(copy)
    core = lax.rem(lax.axis_index("gy"), 2)
    near = [(0, 0), (1 - 2 * core, 0), (-1, 0), (1, 0), (0, -1), (0, 1)]
    row = iota(flag_out.shape, 0)
    flags = jnp.zeros(flag_out.shape, jnp.float32)
    for i, (dy, dz) in enumerate(near):
        hit = member(group_ref, planes, dy, dz) == core
        flags = jnp.where(row == i, jnp.where(hit, 1.0, 0.0), flags)
    flag_out[...] = flags
    for f in range(FACES):
        store(own_out, f, own_ref[f])
    for f in range(FACES - 1):
        strips[f].wait()
        for g in range(f + 1, FACES):
            store(upper_out, upper_index(f, g), upper_ref[f, :, g * width : (g + 1) * width])


def begin(packed, owns, partner_ref, sum_ref):
    width = owns[0].shape[1]
    eye = iota((width, width), 0) == iota((width, width), 1)
    guesses = []
    for f in range(len(packed)):
        partner = unpack(packed[f])
        total = owns[f] + partner
        store(partner_ref, f, partner)
        store(sum_ref, f, total)
        diagonal = jnp.where(eye, total, 0.0)
        across = 1.0 / jnp.sum(diagonal, axis=0, keepdims=True)
        down = 1.0 / jnp.sum(diagonal, axis=1, keepdims=True)
        guesses.append(jnp.where(eye, 2.0 * across, 0.0) - down * total * across)
    return guesses


def newton(guesses, sum_ref):
    results = []
    for f, guess in enumerate(guesses):
        halves = split(guess)
        product = split(wide(load(sum_ref, f), halves))
        results.append(2.0 * guess - wide(halves, product))
    return results


def unit_rows(basis):
    return [b * lax.rsqrt(jnp.sum(b * b, axis=1, keepdims=True)) for b in basis]


def sweep_basis(before, inverse, after, basis):
    for matrices in (before, inverse, after):
        basis = [thin(stacked(b), matrix) for b, matrix in zip(basis, matrices)]
    return unit_rows(basis)


def early_kernel(axes, faces, *refs):
    arrays = len(refs) - 7
    inputs = refs[:arrays]
    own_ref, halves_ref, starts_ref, basis_out, inverse_out, partner_ref, sum_ref = refs[arrays:]
    count = len(faces)
    packed = []
    done = 0
    for axis in axes:
        number = face_arrays(lax.axis_size(axis))
        packed += receive(inputs[done : done + number], axis)
        done += number
    guesses = begin(packed, [own_ref[f] for f in faces], partner_ref, sum_ref)
    for sweep in range(NS_ITERS - 1):
        guesses = newton(guesses, sum_ref)
    for i in range(count):
        store(inverse_out, i, guesses[i])
    basis = [starts_ref[f] for f in faces]
    matrices = [
        [load(partner_ref, i) for i in range(count)],
        [load(inverse_out, i) for i in range(count)],
        [load(halves_ref, f) for f in faces],
    ]
    for sweep in range(SUB_ITERS):
        basis = sweep_basis(*matrices, basis)
    for i in range(count):
        basis_out[i] = basis[i]


def main_kernel(axes, early, late, *refs):
    arrays = len(refs) - 11
    inputs = refs[:arrays]
    own_ref, halves_ref, upper_ref, starts_ref, resid_ref, early_basis = refs[arrays : arrays + 6]
    payload_ref, product_ref, inverse_out, partner_ref, sum_ref = refs[arrays + 6 :]
    ncon, width = starts_ref.shape[1:]
    columns = resid_ref.shape[1]
    sides = {}
    rights = {}
    grams = {}
    vectors = {}
    count = len(late)

    def project(f, basis):
        vectors[f] = basis
        rows = stacked(basis)
        grams[f] = dot(basis, basis, ((1,), (1,)))
        side = {f: thin(rows, load(halves_ref, f))}
        for g in range(f + 1, FACES):
            side[g] = thin(rows, load(upper_ref, upper_index(f, g)))
        sides[f] = side
        rights[f] = thin(rows, split(resid_ref[f * width : (f + 1) * width]))

    packed = []
    done = 0
    for axis in axes:
        number = face_arrays(lax.axis_size(axis))
        packed += receive(inputs[done : done + number], axis)
        done += number
    guesses = begin(packed, [own_ref[f] for f in late], partner_ref, sum_ref)
    pending = [(f, early_basis[i]) for i, f in enumerate(early)]
    for sweep in range(NS_ITERS - 1):
        guesses = newton(guesses, sum_ref)
        if pending:
            project(*pending.pop(0))
    for i in range(count):
        store(inverse_out, i, guesses[i])
    basis = [starts_ref[f] for f in late]
    matrices = [
        [load(partner_ref, i) for i in range(count)],
        [load(inverse_out, i) for i in range(count)],
        [load(halves_ref, f) for f in late],
    ]
    for sweep in range(SUB_ITERS):
        basis = sweep_basis(*matrices, basis)
        if pending:
            project(*pending.pop(0))
    for item in pending:
        project(*item)
    for i, f in enumerate(late):
        project(f, basis[i])
    factors = factor_inverses([grams[f] for f in range(FACES)])
    blocks = []
    for g in range(FACES):
        tall = jnp.concatenate([sides[f][g] for f in range(g + 1)], axis=0)
        blocks.append(dot(dot(tall, vectors[g], ((1,), (1,))), factors[g], ((1,), (1,))))
    even, odd, right, products = [], [], [], []
    lows = None
    for f in range(FACES):
        products.append(dot(factors[f], sides[f][f]))
        product_ref[f] = products[f]
        line = [blocks[g][f * ncon : (f + 1) * ncon] for g in range(f, FACES)]
        line = dot(factors[f], jnp.concatenate([rights[f]] + line, axis=1))
        right.append(line[:, :columns])
        line = line[:, columns:]
        if f % 2 == 0:
            even.append(line)
            lows = line[:, ncon : 2 * ncon].T
        else:
            odd += [lows, line]
    upward = is_even("gy")
    inner = jnp.where(upward, products[3], products[2])
    outer = jnp.where(upward, products[2], products[3])
    whole = [
        jnp.concatenate(even + right[0::2], axis=1),
        jnp.concatenate(odd + right[1::2], axis=1),
    ]
    payload_ref[...] = jnp.concatenate(
        [jnp.concatenate(whole, axis=0), fold(inner), fold(outer)], axis=1
    )


def fold(product):
    half = product.shape[1] // 2
    return jnp.concatenate([product[:, :half], product[:, half:]], axis=0)


def unfold(rows):
    half = rows.shape[0] // 2
    return jnp.concatenate([rows[:half], rows[half:]], axis=1)


def find(faces, refs, f):
    for group, ref in zip(faces, refs):
        if f in group:
            return load(ref, list(group).index(f))


def spread_pair(mine, theirs, inverse):
    high, low = split(thin(stacked(jnp.concatenate([mine, theirs], axis=0)), inverse).T)
    return jnp.concatenate([high, high, low], axis=1)


def their_y_products(there_ref, matrix_ref, start):
    half = (there_ref.shape[1] - start) // 2
    inner = unfold(there_ref[:, start : start + half])
    outer = unfold(matrix_ref[:, matrix_ref.shape[1] - half :])
    upward = is_even("gy")
    return jnp.where(upward, outer, inner), jnp.where(upward, inner, outer)


def spread_kernel(faces, start, unread, *refs):
    product_ref, early_inverse, late_inverse, there_ref, matrix_ref, right_ref, out_ref = refs
    inverses = (early_inverse, late_inverse)
    half = product_ref.shape[2] // 2
    theirs = list(their_y_products(there_ref, matrix_ref, start))
    theirs.append(unfold(right_ref[:, right_ref.shape[1] - half :]))
    for i, f in enumerate((2, 3, FACES - 1)):
        out_ref[i] = spread_pair(product_ref[f], theirs[i], find(faces, inverses, f))


def far_spread(faces, product_ref, inverses, inputs, out_ref):
    theirs = receive(inputs, AXES[0])
    for f in range(2):
        out_ref[f] = spread_pair(product_ref[f], theirs[f], find(faces, inverses, f))


def choose_kernel(flag_ref, here_ref, there_ref, product_ref, matrix_ref, right_ref, *sent):
    mine = flag_ref[0:1, 0:1] > 0.5
    other = flag_ref[1:2, 0:1] > 0.5
    half = product_ref.shape[2] // 2
    lanes, wide_lanes = matrix_ref.shape[1] - half, here_ref.shape[1] - 2 * half
    here, there = here_ref[:, :wide_lanes], there_ref[:, :wide_lanes]
    total = jnp.where(mine, here, 0.0) + jnp.where(other, there, 0.0)
    outer = there_ref[:, wide_lanes + half :]
    matrix_ref[...] = jnp.concatenate([total[:, :lanes], outer], axis=1)
    right_ref[...] = jnp.concatenate([total[:, lanes:], fold(product_ref[4])], axis=1)
    send(sent, AXES[0], product_ref[0], product_ref[1])


def add_kernel(first_ref, second_ref, third_ref, fourth_ref, product_ref, *refs):
    matrix_ref, right_ref = refs[-2:]
    half = product_ref.shape[2] // 2
    lanes, right_lanes = matrix_ref.shape[1] - half, right_ref.shape[1]
    total = first_ref[:, :lanes] + second_ref[:, :lanes]
    matrix_ref[...] = jnp.concatenate([total, fold(product_ref[5])], axis=1)
    right_ref[...] = third_ref[:, :right_lanes] + fourth_ref[:, :right_lanes]


def solve_kernel(size, terms, columns, *refs):
    lanes = size * BLOCKS * (BLOCKS + 1) // 2
    matrix, right = refs[0][:, :lanes], refs[terms][...]
    for term in range(1, terms):
        matrix = matrix + refs[term][:, :lanes]
        right = right + refs[terms + term][...]
    answer_ref = refs[-1]
    lines = []
    offset = 0
    for b in range(BLOCKS):
        lines.append(matrix[:, offset : offset + (BLOCKS - b) * size])
        offset += (BLOCKS - b) * size
    eye = iota((size, size), 0) == iota((size, size), 1)
    downs, acrosses = [], []
    for b in range(BLOCKS):
        diagonal = jnp.where(eye, lines[b][:, :size], 0.0)
        downs.append(lax.rsqrt(jnp.sum(diagonal, axis=1, keepdims=True)))
        acrosses.append(lax.rsqrt(jnp.sum(diagonal, axis=0, keepdims=True)))
    blocks = {}
    rights = []
    for b in range(BLOCKS):
        for c in range(b, BLOCKS):
            block = lines[b][:, (c - b) * size : (c - b + 1) * size]
            blocks[b, c] = downs[b] * block * acrosses[c]
            if c > b:
                blocks[c, b] = blocks[b, c].T
        rights.append(downs[b] * right[:, b * columns : (b + 1) * columns])
    for b in range(BLOCKS):
        (inverse,) = factor_inverses([blocks[b, b]])
        later = range(b + 1, BLOCKS)
        row = dot(inverse, jnp.concatenate([rights[b]] + [blocks[b, c] for c in later], axis=1))
        if later:
            column = jnp.concatenate([blocks[c, b] for c in later], axis=0)
            change = dot(dot(column, inverse, ((1,), (1,))), row)
        for i, c in enumerate(later):
            part = change[i * size : (i + 1) * size]
            rights[c] = rights[c] - part[:, :columns]
            for j, d in enumerate(later):
                start = columns + j * size
                blocks[c, d] = blocks[c, d] - part[:, start : start + size]
        row = dot(inverse, row, ((0,), (0,)))
        rights[b] = row[:, :columns]
        for c in later:
            blocks[b, c] = row[:, columns + (c - b - 1) * size : columns + (c - b) * size]
        for i in range(b):
            for c in later:
                blocks[i, c] = blocks[i, c] - dot(blocks[i, b], blocks[b, c])
            rights[i] = rights[i] - dot(blocks[i, b], rights[b])
    answer = [downs[b] * rights[b] for b in range(BLOCKS)]
    answer_ref[...] = jnp.concatenate(answer, axis=0)


def rows_kernel(ncon, flag_ref, here_ref, there_ref, *refs):
    hit = flag_ref[0:1, 0:1] > 0.5
    rows = jnp.where(hit, here_ref[: 2 * ncon], there_ref[: 2 * ncon])
    refs[-1][...] = rows
    send(refs[:-1], AXES[0], rows[:ncon], rows[ncon:])


def last_product(spread, mine, theirs):
    high, low = split(jnp.concatenate([mine, theirs], axis=0))
    return lax.dot_general(
        spread,
        jnp.concatenate([high, low, high], axis=0),
        (((1,), (0,)), ((), ())),
        preferred_element_type=jnp.float32,
    )


def through(inverse, mine, theirs, my_answer, their_answer):
    high, low = split(jnp.concatenate([mine, theirs], axis=0).T)
    spread = jnp.concatenate([high, high, low], axis=1)
    return wide(inverse, split(last_product(spread, my_answer, their_answer)))


def last_faces(values, width, out_ref, result, sems):
    copies = []
    for f, value in values.items():
        place = pl.ds(f * width, width)
        result[f * width : (f + 1) * width] = value()
        copy = pltpu.make_async_copy(result.at[place], out_ref.at[place], sems.at[f])
        copy.start()
        copies.append(copy)
    for copy in copies:
        copy.wait()


def last_plain_kernel(faces, product_ref, early_inverse, late_inverse, answer_ref, *refs):
    number = face_arrays(lax.axis_size(AXES[0]))
    inputs, rest = refs[number:-4], (refs[-4], *refs[-2:])
    far_spread(faces, product_ref, (early_inverse, late_inverse), refs[:number], refs[-3])
    ncon, width = product_ref.shape[1:]
    values = {}
    done = 0
    near = []
    for axis in AXES[1:] * 2:
        number = face_arrays(lax.axis_size(axis))
        near += receive(inputs[done : done + number], axis)
        done += number
    for f in range(2, FACES):
        values[f] = functools.partial(
            through,
            find(faces, (early_inverse, late_inverse), f),
            product_ref[f],
            near[f - 2],
            answer_ref[f * ncon : (f + 1) * ncon],
            near[f + 2],
        )
    last_faces(values, width, *rest)


def last_near_kernel(
    faces, flag_ref, product_ref, early_inverse, late_inverse, matrix_ref, spread_ref, *refs
):
    here_answer, there_answer = refs[:2]
    inverses = (early_inverse, late_inverse)
    far_spread(faces, product_ref, inverses, refs[2:-4], refs[-3])
    ncon, width = product_ref.shape[1:]
    half = width // 2

    def answer(flag, f):
        place = slice(f * ncon, (f + 1) * ncon)
        hit = flag_ref[flag : flag + 1, 0:1] > 0.5
        return jnp.where(hit, here_answer[place], there_answer[place])

    values = {}
    for f in (2, 3, 5):
        values[f] = functools.partial(
            last_product, spread_ref[min(f - 2, 2)], answer(0, f), answer(f, f ^ 1)
        )
    values[4] = functools.partial(
        through,
        find(faces, inverses, 4),
        product_ref[4],
        unfold(matrix_ref[:, matrix_ref.shape[1] - half :]),
        answer(0, 4),
        answer(4, 5),
    )
    last_faces(values, width, refs[-4], *refs[-2:])


def last_far_kernel(ncon, spread_ref, rows_ref, *refs):
    theirs = receive(refs[:-4], AXES[0])
    values = {}
    for f in range(2):
        mine = rows_ref[f * ncon : (f + 1) * ncon]
        values[f] = functools.partial(last_product, spread_ref[f], mine, theirs[f])
    last_faces(values, spread_ref.shape[1], *refs[-3:])


def per_device(schur, start_block, resid, group_of):
    matrix = schur[0, 0, 0]
    matrix = pltpu.with_memory_space_constraint(matrix, pltpu.HBM)
    starts = start_block[0, 0, 0].transpose(0, 2, 1)
    right = resid[0, 0, 0]
    order, columns = right.shape
    ncon, width = starts.shape[1:]
    counts = [lax.axis_size(axis) for axis in AXES]
    arrays = sum(face_arrays(count) for count in counts)
    coarse = FACES * ncon
    size = 2 * ncon
    half = width // 2
    lanes = size * BLOCKS * (BLOCKS + 1) // 2
    right_lanes = BLOCKS * columns
    uppers = FACES * (FACES - 1) // 2
    anywhere = pl.BlockSpec(memory_space=pl.ANY)
    main_memory = pl.BlockSpec(memory_space=pltpu.HBM)
    scalars = pl.BlockSpec(memory_space=pltpu.SMEM)
    early, late = (2, 3), (0, 1, 4, 5)
    faces = (early, late)
    planes = counts[2]

    def shape(*dims):
        return jax.ShapeDtypeStruct(dims, jnp.float32)

    def halves(count):
        return jax.ShapeDtypeStruct((count, 2, width, width), jnp.bfloat16)

    def params(mib):
        return pltpu.CompilerParams(vmem_limit_bytes=mib * MIB)

    def cost(us):
        return pl.CostEstimate(flops=us * 10**9, bytes_accessed=2**20, transcendentals=0)

    *packed, own = pl.pallas_call(
        functools.partial(pack_kernel, counts, width),
        out_shape=[part for count in counts for part in face_shapes(count, (width + 8, half))]
        + [shape(FACES, width, width)],
        in_specs=[main_memory],
        out_specs=vmem_specs(arrays + 1),
        scratch_shapes=[pltpu.SemaphoreType.DMA((FACES,))],
        compiler_params=params(12),
    )(matrix)
    ends = [sum(face_arrays(count) for count in counts[:position]) for position in range(4)]
    got = {}
    for position in (2, 0, 1):
        got[position] = exchange(packed[ends[position] : ends[position + 1]], AXES[position])

    own_halves, upper_halves, flags = pl.pallas_call(
        functools.partial(halves_kernel, planes),
        out_shape=[halves(FACES), halves(uppers), shape(8, 128)],
        in_specs=[main_memory, scalars] + vmem_specs(1),
        out_specs=vmem_specs(3),
        scratch_shapes=[
            pltpu.VMEM((FACES - 1, width, order), jnp.float32),
            pltpu.SemaphoreType.DMA((FACES - 1,)),
        ],
        compiler_params=params(24),
        cost_estimate=cost(2),
    )(matrix, group_of, own)

    early_basis, early_inverse = pl.pallas_call(
        functools.partial(early_kernel, AXES[1:2], early),
        out_shape=[shape(len(early), ncon, width), halves(len(early))],
        in_specs=vmem_specs(len(got[1]) + 3),
        out_specs=vmem_specs(2),
        scratch_shapes=[pltpu.VMEM((len(early), 2, width, width), jnp.bfloat16)] * 2,
        compiler_params=params(16),
        cost_estimate=cost(2),
    )(*got[1], own, own_halves, starts)

    payload, product, late_inverse = pl.pallas_call(
        functools.partial(main_kernel, (AXES[0], AXES[2]), early, late),
        out_shape=[
            shape(size, lanes + right_lanes + 2 * half),
            shape(FACES, ncon, width),
            halves(len(late)),
        ],
        in_specs=vmem_specs(len(got[0]) + len(got[2]) + 6),
        out_specs=vmem_specs(3),
        scratch_shapes=[pltpu.VMEM((len(late), 2, width, width), jnp.bfloat16)] * 2,
        compiler_params=params(24),
        cost_estimate=cost(8),
    )(*got[0], *got[2], own, own_halves, upper_halves, starts, right, early_basis)

    inverses = [early_inverse, late_inverse]
    def solve(matrices, rights, unread):
        return pl.pallas_call(
            functools.partial(solve_kernel, size, len(matrices), columns),
            out_shape=shape(coarse, columns),
            in_specs=vmem_specs(2 * len(matrices)) + [anywhere] * len(unread),
            out_specs=vmem_specs(1)[0],
            compiler_params=params(12),
            cost_estimate=cost(7),
        )(*matrices, *rights, *unread)

    far_shape = jax.ShapeDtypeStruct((2, width, 3 * size), jnp.bfloat16)
    result = dict(
        scratch_shapes=[
            pltpu.VMEM((order, columns), jnp.float32),
            pltpu.SemaphoreType.DMA((FACES,)),
        ],
        compiler_params=params(12),
        cost_estimate=cost(1),
    )
    groups = group_of.shape[0] // GROUP_SIZE
    if groups == 2 and counts[1] == 4 and planes == 2:
        core_swap, chip_x, chip_y = flipped("gy", 1), flipped("gy", 2), flipped("gz", 1)
        other = lax.ppermute(payload, "gy", core_swap)
        left, rest, *sent = pl.pallas_call(
            choose_kernel,
            out_shape=[shape(size, lanes + half), shape(size, right_lanes + half)]
            + face_shapes(counts[0], (ncon, width)),
            in_specs=vmem_specs(4),
            out_specs=vmem_specs(2 + face_arrays(counts[0])),
            compiler_params=params(8),
        )(flags, payload, other, product)
        left_moved = lax.ppermute(left, "gy", chip_x)
        rest_moved = lax.ppermute(rest, "gz", chip_y)
        theirs = exchange(sent, AXES[0])
        left_last, rest_last = pl.pallas_call(
            add_kernel,
            out_shape=[shape(size, lanes + half), shape(size, right_lanes)],
            in_specs=vmem_specs(5),
            out_specs=vmem_specs(2),
            compiler_params=params(8),
        )(left, left_moved, rest, rest_moved, product)
        left_other = lax.ppermute(left_last, "gz", chip_y)
        rest_other = lax.ppermute(rest_last, "gy", chip_x)
        spread = pl.pallas_call(
            functools.partial(spread_kernel, faces, lanes + right_lanes),
            out_shape=jax.ShapeDtypeStruct((3, width, 3 * size), jnp.bfloat16),
            in_specs=[anywhere] + vmem_specs(6),
            out_specs=vmem_specs(1)[0],
            compiler_params=params(16),
            cost_estimate=cost(1),
        )(left_last, product, *inverses, other, left_moved, rest_moved)
        answer = solve([left_last, left_other], [rest_last, rest_other], [spread, *theirs])
        there = lax.ppermute(answer, "gy", core_swap)
        *sent, mine = pl.pallas_call(
            functools.partial(rows_kernel, ncon),
            out_shape=face_shapes(counts[0], (ncon, columns)) + [shape(size, columns)],
            in_specs=vmem_specs(3),
            out_specs=vmem_specs(face_arrays(counts[0]) + 1),
            compiler_params=params(8),
        )(flags, answer, there)
        across = exchange(sent, AXES[0])
        correction, spread = pl.pallas_call(
            functools.partial(last_near_kernel, faces),
            out_shape=[shape(order, columns), far_shape],
            in_specs=vmem_specs(8 + len(theirs)),
            out_specs=[main_memory] + vmem_specs(1),
            **result,
        )(flags, product, *inverses, left_other, spread, answer, there, *theirs)
    else:
        y, z = lax.axis_index("gy"), lax.axis_index("gz")
        member_of = group_of[y * planes + z]
        chosen = jnp.arange(groups, dtype=jnp.int32) == member_of
        part = payload[:, : lanes + right_lanes]
        total = lax.psum(jnp.where(chosen[:, None, None], part[None], 0.0), ("gy", "gz"))
        total = lax.dynamic_index_in_dim(total, member_of, 0, keepdims=False)
        answer = solve([total[:, :lanes]], [total[:, lanes:]], [])

        def from_near(faces_of, axis):
            even, odd = faces_of
            if lax.axis_size(axis) == 2:
                return exchange([jnp.stack([even, odd])], axis)
            upward = is_even(axis)
            return exchange([jnp.where(upward, odd, even), jnp.where(upward, even, odd)], axis)

        blocks = answer.reshape(FACES, ncon, columns)
        near = []
        for parts in (product, blocks):
            near += from_near(parts[2:4], AXES[1]) + from_near(parts[4:6], AXES[2])
        mine = answer[:size]
        across = from_near(blocks[:2], AXES[0])
        theirs = from_near(product[:2], AXES[0])
        correction, spread = pl.pallas_call(
            functools.partial(last_plain_kernel, faces),
            out_shape=[shape(order, columns), far_shape],
            in_specs=vmem_specs(4 + len(theirs) + len(near)),
            out_specs=[main_memory] + vmem_specs(1),
            **result,
        )(product, *inverses, answer, *theirs, *near)
    correction = pl.pallas_call(
        functools.partial(last_far_kernel, ncon),
        out_shape=shape(order, columns),
        out_specs=main_memory,
        in_specs=vmem_specs(2 + len(across)) + [main_memory],
        input_output_aliases={2 + len(across): 0},
        **result,
    )(spread, mine, *across, correction)
    return correction[None, None, None]


def solution(mesh):
    in_specs = (
        P("gx", "gy", "gz", None, None),
        P("gx", "gy", "gz", None, None, None),
        P("gx", "gy", "gz", None, None),
        P(),
    )
    out_specs = P("gx", "gy", "gz", None, None)
    return jax.shard_map(
        per_device, mesh=mesh, in_specs=in_specs, out_specs=out_specs, check_vma=False
    )
```

```python
import functools

import jax
import jax.numpy as jnp
from jax import lax
from jax.experimental import pallas as pl
from jax.experimental.pallas import tpu as pltpu
from jax.sharding import PartitionSpec as P

NS_ITERS = 3
SUB_ITERS = 2
GROUP_SIZE = 4
FACES = 6
BLOCKS = FACES // 2
AXES = ("gx", "gy", "gz")
MIB = 1024 * 1024

precise = lax.Precision.HIGHEST


def dot(left, right, dims=((1,), (0,))):
    return lax.dot_general(
        left, right, (dims, ((), ())), precision=precise, preferred_element_type=jnp.float32
    )


def split(value):
    high = value.astype(jnp.bfloat16)
    return high, (value - high.astype(jnp.float32)).astype(jnp.bfloat16)


def wide(left, right):
    return lax.dot_general(
        jnp.concatenate([left[0], left[0], left[1]], axis=1),
        jnp.concatenate([right[0], right[1], right[0]], axis=0),
        (((1,), (0,)), ((), ())),
        preferred_element_type=jnp.float32,
    )


def stacked(value):
    return jnp.concatenate(split(value), axis=0)


def thin(rows, matrix):
    out = lax.dot_general(
        jnp.concatenate([rows, rows], axis=1),
        jnp.concatenate(matrix, axis=0),
        (((1,), (0,)), ((), ())),
        preferred_element_type=jnp.float32,
    )
    half = rows.shape[0] // 2
    return out[:half] + out[half:]


def triple(left, right, dims=((1,), (0,))):
    (left_high, left_low), (right_high, right_low) = split(left), split(right)
    total = None
    for one, other in ((left_high, right_high), (left_high, right_low), (left_low, right_high)):
        part = lax.dot_general(
            one, other, (dims, ((), ())), preferred_element_type=jnp.float32
        )
        total = part if total is None else total + part
    return total


def iota(shape, dim):
    return lax.broadcasted_iota(jnp.int32, shape, dim)


def flipped(axis, bit):
    return [(i, i ^ bit) for i in range(lax.axis_size(axis))]


def outer_pairs(axis):
    count = lax.axis_size(axis)
    return [(i, (i + 1 if i % 2 else i - 1) % count) for i in range(count)]


def face_arrays(count):
    return 1 if count == 2 else 2


def exchange(arrays, axis):
    if lax.axis_size(axis) == 2:
        return [lax.ppermute(arrays[0], axis, flipped(axis, 1))]
    return [
        lax.ppermute(arrays[0], axis, outer_pairs(axis)),
        lax.ppermute(arrays[1], axis, flipped(axis, 1)),
    ]


def is_even(axis):
    return lax.rem(lax.axis_index(axis), 2) == 0


def send(refs, axis, even, odd):
    if lax.axis_size(axis) == 2:
        refs[0][0] = even
        refs[0][1] = odd
    else:
        upward = is_even(axis)
        refs[0][...] = jnp.where(upward, even, odd)
        refs[1][...] = jnp.where(upward, odd, even)


def receive(refs, axis):
    if lax.axis_size(axis) == 2:
        return refs[0][1], refs[0][0]
    upward = is_even(axis)
    first, second = refs[0][...], refs[1][...]
    return jnp.where(upward, first, second), jnp.where(upward, second, first)


def face_shapes(count, shape):
    if count == 2:
        return [jax.ShapeDtypeStruct((2,) + shape, jnp.float32)]
    return [jax.ShapeDtypeStruct(shape, jnp.float32)] * 2


def vmem_specs(count):
    return [pl.BlockSpec(memory_space=pltpu.VMEM)] * count


def pack_kernel(counts, width, schur_ref, starts_ref, *refs):
    outs, blocks = refs[:-4], refs[-4]
    starts, sems, start_sem = refs[-3:]
    half = width // 2
    copies = []
    for f in range(FACES):
        place = pl.ds(f * width, width)
        copy = pltpu.make_async_copy(schur_ref.at[place, place], blocks.at[f], sems.at[f])
        copy.start()
        copies.append(copy)
    start_copy = pltpu.make_async_copy(starts_ref.at[pl.ds(0, 4)], starts, start_sem)
    start_copy.start()
    row, col = iota((half, half), 0), iota((half, half), 1)
    start_copy.wait()

    def pack(f):
        copies[f].wait()
        first = blocks[f, 0:half, 0:half]
        second = blocks[f, half:width, half:width]
        diag = jnp.sum(jnp.where(row == col, second, 0.0), axis=0, keepdims=True)
        mixed = jnp.where(row >= col, first, second)
        tail = jnp.broadcast_to(diag, (8, half))
        parts = [blocks[f, half:width, 0:half], mixed, tail]
        if f < 4:
            parts += [starts[f, :, :half], starts[f, :, half:]]
        return jnp.concatenate(parts, axis=0)

    done = 0
    for position, axis in enumerate(AXES):
        number = face_arrays(counts[position])
        send(outs[done : done + number], axis, pack(2 * position), pack(2 * position + 1))
        done += number


def unpack(packed):
    half = packed.shape[1]
    row, col = iota((half, half), 0), iota((half, half), 1)
    low = packed[0:half]
    mixed = packed[half : 2 * half]
    flip = mixed.T
    first = jnp.where(row >= col, mixed, flip)
    second = jnp.where(row < col, mixed, flip)
    second = jnp.where(row == col, packed[2 * half : 2 * half + 1], second)
    return jnp.concatenate(
        [jnp.concatenate([first, low.T], axis=1), jnp.concatenate([low, second], axis=1)], axis=0
    )


def unpack_starts(packed, ncon):
    half = packed.shape[1]
    rows = packed[2 * half + 8 :]
    return jnp.concatenate([rows[:ncon], rows[ncon:]], axis=1)


def factor_inverses(grams, block=8):
    size = grams[0].shape[0]
    strips = size // 8
    lanes = 128
    full = (8, lanes)
    state = []
    for gram in grams:
        parts = [gram, jnp.where(iota((size, size), 0) == iota((size, size), 1), 1.0, 0.0)]
        if 2 * size < lanes:
            parts.append(jnp.zeros((size, lanes - 2 * size), jnp.float32))
        whole = jnp.concatenate(parts, axis=1)
        state.append([whole[8 * s : 8 * s + 8] for s in range(strips)])
    below = iota(full, 0)

    def line_of(strip, line):
        return jnp.broadcast_to(strip[line : line + 1], full)

    for start in range(0, size, block):
        strip, first = start // 8, start % 8
        active = range(strip, strips)
        for work in state:
            cols = [
                {s: jnp.broadcast_to(work[s][:, start + j : start + j + 1], full) for s in active}
                for j in range(block)
            ]
            factors = []

            def eliminate(j, scale, stop):
                line = first + j
                factor = {s: cols[j][s] * scale for s in active}
                factor[strip] = jnp.where(below > line, factor[strip], 0.0)
                for later in range(j + 1, stop):
                    head = line_of(cols[later][strip], line)
                    for s in active:
                        cols[later][s] = cols[later][s] - factor[s] * head
                factors.append(factor)

            for j in range(0, block, 2):
                line = first + j
                corner = line_of(cols[j][strip], line)
                side = line_of(cols[j][strip], line + 1)
                last = line_of(cols[j + 1][strip], line + 1)
                inverse = 1.0 / (corner * last - side * side)
                eliminate(j, 1.0 / corner, block)
                eliminate(j + 1, corner * inverse, block)
            for j in range(block):
                row = line_of(work[strip], first + j)
                for s in active:
                    if s == strip and first + j == 7:
                        continue
                    work[s] = work[s] - factors[j][s] * row
    results = []
    for work in state:
        parts = []
        for s in range(strips):
            place = iota((8, size), 0) + 8 * s == iota((8, size), 1)
            pivot = jnp.sum(jnp.where(place, work[s][:, :size], 0.0), axis=1, keepdims=True)
            parts.append(work[s][:, size : 2 * size] * lax.rsqrt(pivot))
        results.append(jnp.concatenate(parts, axis=0))
    return results


def member(group_ref, planes, dy=0, dz=0):
    y, z = lax.axis_index("gy"), lax.axis_index("gz")
    rows = lax.axis_size("gy")
    return group_ref[lax.rem(y + dy + rows, rows) * planes + lax.rem(z + dz + planes, planes)]


def store(ref, f, value):
    ref[f, 0], ref[f, 1] = split(value)


def load(ref, f):
    return ref[f, 0], ref[f, 1]


def upper_index(f, g):
    return sum(FACES - 1 - i for i in range(f)) + g - f - 1


def halves_kernel(planes, schur_ref, group_ref, own_ref, own_out, upper_out, flag_out, *scratch):
    upper_ref, sems = scratch
    width = own_ref.shape[1]
    strips = []
    for f in range(FACES - 1):
        rest = (FACES - 1 - f) * width
        copy = pltpu.make_async_copy(
            schur_ref.at[pl.ds(f * width, width), pl.ds((f + 1) * width, rest)],
            upper_ref.at[f, :, pl.ds((f + 1) * width, rest)],
            sems.at[f],
        )
        copy.start()
        strips.append(copy)
    core = lax.rem(lax.axis_index("gy"), 2)
    near = [(0, 0), (1 - 2 * core, 0), (-1, 0), (1, 0), (0, -1), (0, 1)]
    row = iota(flag_out.shape, 0)
    flags = jnp.zeros(flag_out.shape, jnp.float32)
    for i, (dy, dz) in enumerate(near):
        hit = member(group_ref, planes, dy, dz) == core
        flags = jnp.where(row == i, jnp.where(hit, 1.0, 0.0), flags)
    flag_out[...] = flags
    for f in range(FACES):
        store(own_out, f, own_ref[f])
    for f in range(FACES - 1):
        strips[f].wait()
        for g in range(f + 1, FACES):
            store(upper_out, upper_index(f, g), upper_ref[f, :, g * width : (g + 1) * width])


def begin(packed, owns, partner_out, sum_ref):
    width = owns[0].shape[1]
    half = width // 2
    eye = iota((half, half), 0) == iota((half, half), 1)
    zero = jnp.zeros((half, half), jnp.float32)
    guesses = []
    for f in range(len(packed)):
        partner = unpack(packed[f])
        total = owns[f] + partner
        store(partner_out, f, partner)
        store(sum_ref, f, total)
        across, down, twice = [], [], []
        for start in (0, half):
            block = total[start : start + half, start : start + half]
            diagonal = jnp.where(eye, block, 0.0)
            across.append(1.0 / jnp.sum(diagonal, axis=0, keepdims=True))
            down.append(1.0 / jnp.sum(diagonal, axis=1, keepdims=True))
            twice.append(jnp.where(eye, 2.0 * across[-1], 0.0))
        start = jnp.concatenate(
            [
                jnp.concatenate([twice[0], zero], axis=1),
                jnp.concatenate([zero, twice[1]], axis=1),
            ],
            axis=0,
        )
        across, down = jnp.concatenate(across, axis=1), jnp.concatenate(down, axis=0)
        guesses.append(start - down * total * across)
    return guesses


def newton(guesses, sum_ref):
    results = []
    for f, guess in enumerate(guesses):
        halves = split(guess)
        product = split(wide(load(sum_ref, f), halves))
        results.append(2.0 * guess - wide(halves, product))
    return results


def unit_rows(basis):
    return [b * lax.rsqrt(jnp.sum(b * b, axis=1, keepdims=True)) for b in basis]


def sweep_basis(before, inverse, after, basis):
    for matrices in (before, inverse, after):
        basis = [thin(stacked(b), matrix) for b, matrix in zip(basis, matrices)]
    return unit_rows(basis)


def early_kernel(axes, faces, *refs):
    arrays = len(refs) - 7
    inputs = refs[:arrays]
    own_ref, halves_ref, starts_ref, basis_out, partner_out, inverse_out, sum_ref = refs[arrays:]
    count = len(faces)
    packed = []
    done = 0
    for axis in axes:
        number = face_arrays(lax.axis_size(axis))
        packed += receive(inputs[done : done + number], axis)
        done += number
    guesses = begin(packed, [own_ref[f] for f in faces], partner_out, sum_ref)
    for sweep in range(NS_ITERS - 1):
        guesses = newton(guesses, sum_ref)
    for i in range(count):
        store(inverse_out, i, guesses[i])
    basis = [starts_ref[f] for f in faces]
    matrices = [
        [load(partner_out, i) for i in range(count)],
        [load(inverse_out, i) for i in range(count)],
        [load(halves_ref, f) for f in faces],
    ]
    for sweep in range(SUB_ITERS):
        basis = sweep_basis(*matrices, basis)
    for i in range(count):
        basis_out[i] = basis[i]


def main_kernel(axes, early, late, *refs):
    arrays = len(refs) - 11
    inputs = refs[:arrays]
    own_ref, halves_ref, upper_ref, starts_ref, resid_ref, early_basis = refs[arrays : arrays + 6]
    payload_ref, product_ref, partner_out, inverse_out, sum_ref = refs[arrays + 6 :]
    ncon, width = starts_ref.shape[1:]
    columns = resid_ref.shape[1]
    sides = {}
    rights = {}
    grams = {}
    vectors = {}
    count = len(late)

    def project(f, basis):
        vectors[f] = basis
        rows = stacked(basis)
        grams[f] = dot(basis, basis, ((1,), (1,)))
        side = {f: thin(rows, load(halves_ref, f))}
        for g in range(f + 1, FACES):
            side[g] = thin(rows, load(upper_ref, upper_index(f, g)))
        sides[f] = side
        rights[f] = thin(rows, split(resid_ref[f * width : (f + 1) * width]))

    packed = []
    done = 0
    for axis in axes:
        number = face_arrays(lax.axis_size(axis))
        packed += receive(inputs[done : done + number], axis)
        done += number
    guesses = begin(packed, [own_ref[f] for f in late], partner_out, sum_ref)
    pending = [(f, early_basis[i]) for i, f in enumerate(early)]
    for sweep in range(NS_ITERS - 1):
        guesses = newton(guesses, sum_ref)
        if pending:
            project(*pending.pop(0))
    for i in range(count):
        store(inverse_out, i, guesses[i])
    basis = [starts_ref[f] for f in late]
    matrices = [
        [load(partner_out, i) for i in range(count)],
        [load(inverse_out, i) for i in range(count)],
        [load(halves_ref, f) for f in late],
    ]
    for sweep in range(SUB_ITERS):
        basis = sweep_basis(*matrices, basis)
        if pending:
            project(*pending.pop(0))
    for item in pending:
        project(*item)
    for i, f in enumerate(late):
        project(f, basis[i])
    factors = factor_inverses([grams[f] for f in range(FACES)])
    blocks = []
    for g in range(FACES):
        tall = jnp.concatenate([sides[f][g] for f in range(g + 1)], axis=0)
        blocks.append(triple(triple(tall, vectors[g], ((1,), (1,))), factors[g], ((1,), (1,))))
    even, odd, right, products = [], [], [], []
    lows = None
    for f in range(FACES):
        products.append(triple(factors[f], sides[f][f]))
        product_ref[f] = products[f]
        line = [blocks[g][f * ncon : (f + 1) * ncon] for g in range(f, FACES)]
        line = triple(factors[f], jnp.concatenate([rights[f]] + line, axis=1))
        right.append(line[:, :columns])
        line = line[:, columns:]
        if f % 2 == 0:
            even.append(line)
            lows = line[:, ncon : 2 * ncon].T
        else:
            odd += [lows, line]
    upward = is_even("gy")
    inner = jnp.where(upward, products[3], products[2])
    outer = jnp.where(upward, products[2], products[3])
    whole = [
        jnp.concatenate(even + right[0::2], axis=1),
        jnp.concatenate(odd + right[1::2], axis=1),
    ]
    payload_ref[...] = jnp.concatenate(
        [jnp.concatenate(whole, axis=0), fold(inner), fold(outer)], axis=1
    )


def fold(product):
    half = product.shape[1] // 2
    return jnp.concatenate([product[:, :half], product[:, half:]], axis=0)


def unfold(rows):
    half = rows.shape[0] // 2
    return jnp.concatenate([rows[:half], rows[half:]], axis=1)


def find(faces, refs, f):
    for group, ref in zip(faces, refs):
        if f in group:
            return load(ref, list(group).index(f))


def spread_kernel(faces, ncon, unread, *refs):
    packed = receive(refs[:-7], AXES[0])
    own_ref, product_ref = refs[-7:-5]
    partner_refs, inverse_refs, out_ref = refs[-5:-3], refs[-3:-1], refs[-1]
    basis = [unpack_starts(part, ncon) for part in packed]
    matrices = [
        [load(own_ref, f) for f in range(2)],
        [find(faces, inverse_refs, f) for f in range(2)],
        [find(faces, partner_refs, f) for f in range(2)],
    ]
    for sweep in range(SUB_ITERS):
        basis = sweep_basis(*matrices, basis)
    factors = factor_inverses([dot(b, b, ((1,), (1,))) for b in basis])
    for f in range(2):
        theirs = triple(factors[f], thin(stacked(basis[f]), matrices[2][f]))
        both = jnp.concatenate([product_ref[f], theirs], axis=0)
        high, low = split(thin(stacked(both), matrices[1][f]).T)
        out_ref[f] = jnp.concatenate([high, high, low], axis=1)


def choose_kernel(flag_ref, here_ref, there_ref, product_ref, matrix_ref, right_ref):
    mine = flag_ref[0:1, 0:1] > 0.5
    other = flag_ref[1:2, 0:1] > 0.5
    half = product_ref.shape[2] // 2
    lanes, wide_lanes = matrix_ref.shape[1] - half, here_ref.shape[1] - 2 * half
    here, there = here_ref[:, :wide_lanes], there_ref[:, :wide_lanes]
    total = jnp.where(mine, here, 0.0) + jnp.where(other, there, 0.0)
    outer = there_ref[:, wide_lanes + half :]
    matrix_ref[...] = jnp.concatenate([total[:, :lanes], outer], axis=1)
    right_ref[...] = jnp.concatenate([total[:, lanes:], fold(product_ref[4])], axis=1)


def add_kernel(first_ref, second_ref, third_ref, fourth_ref, product_ref, *refs):
    matrix_ref, right_ref = refs
    half = product_ref.shape[2] // 2
    lanes, right_lanes = matrix_ref.shape[1] - half, right_ref.shape[1]
    total = first_ref[:, :lanes] + second_ref[:, :lanes]
    matrix_ref[...] = jnp.concatenate([total, fold(product_ref[5])], axis=1)
    right_ref[...] = third_ref[:, :right_lanes] + fourth_ref[:, :right_lanes]


def solve_kernel(size, terms, columns, *refs):
    lanes = size * BLOCKS * (BLOCKS + 1) // 2
    matrix, right = refs[0][:, :lanes], refs[terms][...]
    for term in range(1, terms):
        matrix = matrix + refs[term][:, :lanes]
        right = right + refs[terms + term][...]
    answer_ref = refs[-1]
    lines = []
    offset = 0
    for b in range(BLOCKS):
        lines.append(matrix[:, offset : offset + (BLOCKS - b) * size])
        offset += (BLOCKS - b) * size
    eye = iota((size, size), 0) == iota((size, size), 1)
    downs, acrosses = [], []
    for b in range(BLOCKS):
        diagonal = jnp.where(eye, lines[b][:, :size], 0.0)
        downs.append(lax.rsqrt(jnp.sum(diagonal, axis=1, keepdims=True)))
        acrosses.append(lax.rsqrt(jnp.sum(diagonal, axis=0, keepdims=True)))
    blocks = {}
    rights = []
    for b in range(BLOCKS):
        for c in range(b, BLOCKS):
            block = lines[b][:, (c - b) * size : (c - b + 1) * size]
            blocks[b, c] = downs[b] * block * acrosses[c]
            if c > b:
                blocks[c, b] = blocks[b, c].T
        rights.append(downs[b] * right[:, b * columns : (b + 1) * columns])
    for b in range(BLOCKS):
        (inverse,) = factor_inverses([blocks[b, b]])
        later = range(b + 1, BLOCKS)
        row = triple(inverse, jnp.concatenate([rights[b]] + [blocks[b, c] for c in later], axis=1))
        if later:
            column = jnp.concatenate([blocks[c, b] for c in later], axis=0)
            change = triple(triple(column, inverse, ((1,), (1,))), row)
        for i, c in enumerate(later):
            part = change[i * size : (i + 1) * size]
            rights[c] = rights[c] - part[:, :columns]
            for j, d in enumerate(later):
                start = columns + j * size
                blocks[c, d] = blocks[c, d] - part[:, start : start + size]
        row = triple(inverse, row, ((0,), (0,)))
        rights[b] = row[:, :columns]
        for c in later:
            blocks[b, c] = row[:, columns + (c - b - 1) * size : columns + (c - b) * size]
        for i in range(b):
            for c in later:
                blocks[i, c] = blocks[i, c] - triple(blocks[i, b], blocks[b, c])
            rights[i] = rights[i] - triple(blocks[i, b], rights[b])
    answer = [downs[b] * rights[b] for b in range(BLOCKS)]
    answer_ref[...] = jnp.concatenate(answer, axis=0)


def rows_kernel(ncon, flag_ref, here_ref, there_ref, *refs):
    hit = flag_ref[0:1, 0:1] > 0.5
    rows = jnp.where(hit, here_ref[: 2 * ncon], there_ref[: 2 * ncon])
    refs[-1][...] = rows
    send(refs[:-1], AXES[0], rows[:ncon], rows[ncon:])


def last_product(spread, mine, theirs):
    high, low = split(jnp.concatenate([mine, theirs], axis=0))
    return lax.dot_general(
        spread,
        jnp.concatenate([high, low, high], axis=0),
        (((1,), (0,)), ((), ())),
        preferred_element_type=jnp.float32,
    )


def through(inverse, mine, theirs, my_answer, their_answer):
    high, low = split(jnp.concatenate([mine, theirs], axis=0).T)
    spread = jnp.concatenate([high, high, low], axis=1)
    return wide(inverse, split(last_product(spread, my_answer, their_answer)))


def last_faces(values, width, out_ref, result, sems):
    copies = []
    for f, value in values.items():
        place = pl.ds(f * width, width)
        result[f * width : (f + 1) * width] = value()
        copy = pltpu.make_async_copy(result.at[place], out_ref.at[place], sems.at[f])
        copy.start()
        copies.append(copy)
    for copy in copies:
        copy.wait()


def last_plain_kernel(faces, product_ref, early_inverse, late_inverse, answer_ref, *refs):
    inputs, rest = refs[:-3], refs[-3:]
    ncon, width = product_ref.shape[1:]
    values = {}
    done = 0
    near = []
    for axis in AXES[1:] * 2:
        number = face_arrays(lax.axis_size(axis))
        near += receive(inputs[done : done + number], axis)
        done += number
    for f in range(2, FACES):
        values[f] = functools.partial(
            through,
            find(faces, (early_inverse, late_inverse), f),
            product_ref[f],
            near[f - 2],
            answer_ref[f * ncon : (f + 1) * ncon],
            near[f + 2],
        )
    last_faces(values, width, *rest)


def last_near_kernel(
    faces,
    columns,
    flag_ref,
    product_ref,
    early_inverse,
    late_inverse,
    there_ref,
    matrix_ref,
    right_ref,
    matrix_last,
    here_answer,
    there_answer,
    *refs,
):
    ncon, width = product_ref.shape[1:]
    half = width // 2
    lanes = matrix_ref.shape[1] - half
    inner = unfold(there_ref[:, lanes + BLOCKS * columns : lanes + BLOCKS * columns + half])
    outer = unfold(matrix_ref[:, lanes:])
    upward = is_even("gy")
    theirs = {
        2: jnp.where(upward, outer, inner),
        3: jnp.where(upward, inner, outer),
        4: unfold(matrix_last[:, lanes:]),
        5: unfold(right_ref[:, BLOCKS * columns :]),
    }

    def answer(flag, f):
        place = slice(f * ncon, (f + 1) * ncon)
        hit = flag_ref[flag : flag + 1, 0:1] > 0.5
        return jnp.where(hit, here_answer[place], there_answer[place])

    values = {}
    for f in range(2, FACES):
        values[f] = functools.partial(
            through,
            find(faces, (early_inverse, late_inverse), f),
            product_ref[f],
            theirs[f],
            answer(0, f),
            answer(f, f ^ 1),
        )
    last_faces(values, width, *refs)


def last_far_kernel(ncon, spread_ref, rows_ref, *refs):
    theirs = receive(refs[:-4], AXES[0])
    values = {}
    for f in range(2):
        mine = rows_ref[f * ncon : (f + 1) * ncon]
        values[f] = functools.partial(last_product, spread_ref[f], mine, theirs[f])
    last_faces(values, spread_ref.shape[1], *refs[-3:])


def per_device(schur, start_block, resid, group_of):
    matrix = schur[0, 0, 0]
    matrix = pltpu.with_memory_space_constraint(matrix, pltpu.HBM)
    starts = start_block[0, 0, 0].transpose(0, 2, 1)
    right = resid[0, 0, 0]
    order, columns = right.shape
    ncon, width = starts.shape[1:]
    counts = [lax.axis_size(axis) for axis in AXES]
    arrays = sum(face_arrays(count) for count in counts)
    coarse = FACES * ncon
    size = 2 * ncon
    half = width // 2
    lanes = size * BLOCKS * (BLOCKS + 1) // 2
    right_lanes = BLOCKS * columns
    uppers = FACES * (FACES - 1) // 2
    anywhere = pl.BlockSpec(memory_space=pl.ANY)
    main_memory = pl.BlockSpec(memory_space=pltpu.HBM)
    scalars = pl.BlockSpec(memory_space=pltpu.SMEM)
    early, late = (4, 5), (0, 1, 2, 3)
    faces = (early, late)
    planes = counts[2]

    def shape(*dims):
        return jax.ShapeDtypeStruct(dims, jnp.float32)

    def halves(count):
        return jax.ShapeDtypeStruct((count, 2, width, width), jnp.bfloat16)

    def params(mib):
        return pltpu.CompilerParams(vmem_limit_bytes=mib * MIB)

    def cost(us):
        return pl.CostEstimate(flops=us * 10**9, bytes_accessed=2**20, transcendentals=0)

    *packed, own = pl.pallas_call(
        functools.partial(pack_kernel, counts, width),
        out_shape=face_shapes(counts[0], (width + 8 + 2 * ncon, half))
        + face_shapes(counts[1], (width + 8 + 2 * ncon, half))
        + face_shapes(counts[2], (width + 8, half))
        + [shape(FACES, width, width)],
        in_specs=[main_memory, main_memory],
        out_specs=vmem_specs(arrays + 1),
        scratch_shapes=[
            pltpu.VMEM((4, ncon, width), jnp.float32),
            pltpu.SemaphoreType.DMA((FACES,)),
            pltpu.SemaphoreType.DMA,
        ],
        compiler_params=params(12),
    )(matrix, pltpu.with_memory_space_constraint(starts, pltpu.HBM))
    ends = [sum(face_arrays(count) for count in counts[:position]) for position in range(4)]
    got = {}
    for position in (2, 0, 1):
        got[position] = exchange(packed[ends[position] : ends[position + 1]], AXES[position])

    own_halves, upper_halves, flags = pl.pallas_call(
        functools.partial(halves_kernel, planes),
        out_shape=[halves(FACES), halves(uppers), shape(8, 128)],
        in_specs=[main_memory, scalars] + vmem_specs(1),
        out_specs=vmem_specs(3),
        scratch_shapes=[
            pltpu.VMEM((FACES - 1, width, order), jnp.float32),
            pltpu.SemaphoreType.DMA((FACES - 1,)),
        ],
        compiler_params=params(24),
        cost_estimate=cost(2),
    )(matrix, group_of, own)

    early_basis, early_partner, early_inverse = pl.pallas_call(
        functools.partial(early_kernel, AXES[2:3], early),
        out_shape=[shape(len(early), ncon, width)] + [halves(len(early))] * 2,
        in_specs=vmem_specs(len(got[2]) + 3),
        out_specs=vmem_specs(3),
        scratch_shapes=[pltpu.VMEM((len(early), 2, width, width), jnp.bfloat16)],
        compiler_params=params(16),
        cost_estimate=cost(2),
    )(*got[2], own, own_halves, starts)

    payload, product, late_partner, late_inverse = pl.pallas_call(
        functools.partial(main_kernel, (AXES[0], AXES[1]), early, late),
        out_shape=[shape(size, lanes + right_lanes + 2 * half), shape(FACES, ncon, width)]
        + [halves(len(late))] * 2,
        in_specs=vmem_specs(len(got[0]) + len(got[1]) + 6),
        out_specs=vmem_specs(4),
        scratch_shapes=[pltpu.VMEM((len(late), 2, width, width), jnp.bfloat16)],
        compiler_params=params(24),
        cost_estimate=cost(8),
    )(*got[0], *got[1], own, own_halves, upper_halves, starts, right, early_basis)

    partners = [early_partner, late_partner]
    inverses = [early_inverse, late_inverse]
    def spread_of(token):
        return pl.pallas_call(
            functools.partial(spread_kernel, faces, ncon),
            out_shape=jax.ShapeDtypeStruct((2, width, 3 * size), jnp.bfloat16),
            in_specs=[anywhere] + vmem_specs(len(got[0]) + 6),
            out_specs=vmem_specs(1)[0],
            compiler_params=params(16),
            cost_estimate=cost(3),
        )(token, *got[0], own_halves, product, *partners, *inverses)

    def solve(matrices, rights, unread):
        return pl.pallas_call(
            functools.partial(solve_kernel, size, len(matrices), columns),
            out_shape=shape(coarse, columns),
            in_specs=vmem_specs(2 * len(matrices)) + [anywhere] * len(unread),
            out_specs=vmem_specs(1)[0],
            compiler_params=params(12),
            cost_estimate=cost(7),
        )(*matrices, *rights, *unread)

    result = dict(
        out_shape=shape(order, columns),
        out_specs=main_memory,
        scratch_shapes=[
            pltpu.VMEM((order, columns), jnp.float32),
            pltpu.SemaphoreType.DMA((FACES,)),
        ],
        compiler_params=params(12),
        cost_estimate=cost(1),
    )
    groups = group_of.shape[0] // GROUP_SIZE
    if groups == 2 and counts[1] == 4 and planes == 2:
        core_swap, chip_x, chip_y = flipped("gy", 1), flipped("gy", 2), flipped("gz", 1)
        other = lax.ppermute(payload, "gy", core_swap)
        left, rest = pl.pallas_call(
            choose_kernel,
            out_shape=[shape(size, lanes + half), shape(size, right_lanes + half)],
            in_specs=vmem_specs(4),
            out_specs=vmem_specs(2),
            compiler_params=params(8),
        )(flags, payload, other, product)
        left_moved = lax.ppermute(left, "gy", chip_x)
        rest_moved = lax.ppermute(rest, "gz", chip_y)
        left_last, rest_last = pl.pallas_call(
            add_kernel,
            out_shape=[shape(size, lanes + half), shape(size, right_lanes)],
            in_specs=vmem_specs(5),
            out_specs=vmem_specs(2),
            compiler_params=params(8),
        )(left, left_moved, rest, rest_moved, product)
        left_other = lax.ppermute(left_last, "gz", chip_y)
        rest_other = lax.ppermute(rest_last, "gy", chip_x)
        spread = spread_of(left_last)
        answer = solve([left_last, left_other], [rest_last, rest_other], [spread])
        there = lax.ppermute(answer, "gy", core_swap)
        *sent, mine = pl.pallas_call(
            functools.partial(rows_kernel, ncon),
            out_shape=face_shapes(counts[0], (ncon, columns)) + [shape(size, columns)],
            in_specs=vmem_specs(3),
            out_specs=vmem_specs(face_arrays(counts[0]) + 1),
            compiler_params=params(8),
        )(flags, answer, there)
        across = exchange(sent, AXES[0])
        correction = pl.pallas_call(
            functools.partial(last_near_kernel, faces, columns),
            in_specs=vmem_specs(10),
            **result,
        )(
            flags, product, *inverses, other, left_moved, rest_moved, left_other, answer, there
        )
    else:
        y, z = lax.axis_index("gy"), lax.axis_index("gz")
        member_of = group_of[y * planes + z]
        chosen = jnp.arange(groups, dtype=jnp.int32) == member_of
        part = payload[:, : lanes + right_lanes]
        total = lax.psum(jnp.where(chosen[:, None, None], part[None], 0.0), ("gy", "gz"))
        total = lax.dynamic_index_in_dim(total, member_of, 0, keepdims=False)
        spread = spread_of(payload)
        answer = solve([total[:, :lanes]], [total[:, lanes:]], [])

        def from_near(faces_of, axis):
            even, odd = faces_of
            if lax.axis_size(axis) == 2:
                return exchange([jnp.stack([even, odd])], axis)
            upward = is_even(axis)
            return exchange([jnp.where(upward, even, odd), jnp.where(upward, odd, even)], axis)

        blocks = answer.reshape(FACES, ncon, columns)
        near = []
        for parts in (product, blocks):
            near += from_near(parts[2:4], AXES[1]) + from_near(parts[4:6], AXES[2])
        mine = answer[:size]
        across = from_near(blocks[:2], AXES[0])
        correction = pl.pallas_call(
            functools.partial(last_plain_kernel, faces),
            in_specs=vmem_specs(4 + len(near)),
            **result,
        )(product, *inverses, answer, *near)
    correction = pl.pallas_call(
        functools.partial(last_far_kernel, ncon),
        in_specs=vmem_specs(2 + len(across)) + [main_memory],
        input_output_aliases={2 + len(across): 0},
        **result,
    )(spread, mine, *across, correction)
    return correction[None, None, None]


def solution(mesh):
    in_specs = (
        P("gx", "gy", "gz", None, None),
        P("gx", "gy", "gz", None, None, None),
        P("gx", "gy", "gz", None, None),
        P(),
    )
    out_specs = P("gx", "gy", "gz", None, None)
    return jax.shard_map(
        per_device, mesh=mesh, in_specs=in_specs, out_specs=out_specs, check_vma=False
    )
```

```python
import functools

import jax
import jax.numpy as jnp
from jax import lax
from jax.experimental import pallas as pl
from jax.experimental.pallas import tpu as pltpu
from jax.sharding import PartitionSpec as P

NS_ITERS = 3
SUB_ITERS = 2
GROUP_SIZE = 4
FACES = 6
BLOCKS = FACES // 2
AXES = ("gx", "gy", "gz")
MIB = 1024 * 1024

precise = lax.Precision.HIGHEST


def dot(left, right, dims=((1,), (0,))):
    return lax.dot_general(
        left, right, (dims, ((), ())), precision=precise, preferred_element_type=jnp.float32
    )


def split(value):
    high = value.astype(jnp.bfloat16)
    return high, (value - high.astype(jnp.float32)).astype(jnp.bfloat16)


def wide(left, right):
    return lax.dot_general(
        jnp.concatenate([left[0], left[0], left[1]], axis=1),
        jnp.concatenate([right[0], right[1], right[0]], axis=0),
        (((1,), (0,)), ((), ())),
        preferred_element_type=jnp.float32,
    )


def stacked(value):
    return jnp.concatenate(split(value), axis=0)


def thin(rows, matrix):
    out = lax.dot_general(
        jnp.concatenate([rows, rows], axis=1),
        jnp.concatenate(matrix, axis=0),
        (((1,), (0,)), ((), ())),
        preferred_element_type=jnp.float32,
    )
    half = rows.shape[0] // 2
    return out[:half] + out[half:]


def triple(left, right, dims=((1,), (0,))):
    (left_high, left_low), (right_high, right_low) = split(left), split(right)
    total = None
    for one, other in ((left_high, right_high), (left_high, right_low), (left_low, right_high)):
        part = lax.dot_general(
            one, other, (dims, ((), ())), preferred_element_type=jnp.float32
        )
        total = part if total is None else total + part
    return total


def iota(shape, dim):
    return lax.broadcasted_iota(jnp.int32, shape, dim)


def flipped(axis, bit):
    return [(i, i ^ bit) for i in range(lax.axis_size(axis))]


def outer_pairs(axis):
    count = lax.axis_size(axis)
    return [(i, (i + 1 if i % 2 else i - 1) % count) for i in range(count)]


def face_arrays(count):
    return 1 if count == 2 else 2


def exchange(arrays, axis):
    if lax.axis_size(axis) == 2:
        return [lax.ppermute(arrays[0], axis, flipped(axis, 1))]
    return [
        lax.ppermute(arrays[0], axis, outer_pairs(axis)),
        lax.ppermute(arrays[1], axis, flipped(axis, 1)),
    ]


def is_even(axis):
    return lax.rem(lax.axis_index(axis), 2) == 0


def send(refs, axis, even, odd):
    if lax.axis_size(axis) == 2:
        refs[0][0] = even
        refs[0][1] = odd
    else:
        upward = is_even(axis)
        refs[0][...] = jnp.where(upward, even, odd)
        refs[1][...] = jnp.where(upward, odd, even)


def receive(refs, axis):
    if lax.axis_size(axis) == 2:
        return refs[0][1], refs[0][0]
    upward = is_even(axis)
    first, second = refs[0][...], refs[1][...]
    return jnp.where(upward, first, second), jnp.where(upward, second, first)


def face_shapes(count, shape):
    if count == 2:
        return [jax.ShapeDtypeStruct((2,) + shape, jnp.float32)]
    return [jax.ShapeDtypeStruct(shape, jnp.float32)] * 2


def vmem_specs(count):
    return [pl.BlockSpec(memory_space=pltpu.VMEM)] * count


def pack_kernel(counts, width, schur_ref, starts_ref, *refs):
    outs, blocks = refs[:-4], refs[-4]
    starts, sems, start_sem = refs[-3:]
    half = width // 2
    copies = []
    for f in range(FACES):
        place = pl.ds(f * width, width)
        copy = pltpu.make_async_copy(schur_ref.at[place, place], blocks.at[f], sems.at[f])
        copy.start()
        copies.append(copy)
    start_copy = pltpu.make_async_copy(starts_ref.at[pl.ds(0, 4)], starts, start_sem)
    start_copy.start()
    row, col = iota((half, half), 0), iota((half, half), 1)
    start_copy.wait()

    def pack(f):
        copies[f].wait()
        first = blocks[f, 0:half, 0:half]
        second = blocks[f, half:width, half:width]
        diag = jnp.sum(jnp.where(row == col, second, 0.0), axis=0, keepdims=True)
        mixed = jnp.where(row >= col, first, second)
        tail = jnp.broadcast_to(diag, (8, half))
        parts = [blocks[f, half:width, 0:half], mixed, tail]
        if f < 4:
            parts += [starts[f, :, :half], starts[f, :, half:]]
        return jnp.concatenate(parts, axis=0)

    done = 0
    for position, axis in enumerate(AXES):
        number = face_arrays(counts[position])
        send(outs[done : done + number], axis, pack(2 * position), pack(2 * position + 1))
        done += number


def unpack(packed):
    half = packed.shape[1]
    row, col = iota((half, half), 0), iota((half, half), 1)
    low = packed[0:half]
    mixed = packed[half : 2 * half]
    flip = mixed.T
    first = jnp.where(row >= col, mixed, flip)
    second = jnp.where(row < col, mixed, flip)
    second = jnp.where(row == col, packed[2 * half : 2 * half + 1], second)
    return jnp.concatenate(
        [jnp.concatenate([first, low.T], axis=1), jnp.concatenate([low, second], axis=1)], axis=0
    )


def unpack_starts(packed, ncon):
    half = packed.shape[1]
    rows = packed[2 * half + 8 :]
    return jnp.concatenate([rows[:ncon], rows[ncon:]], axis=1)


def factor_inverses(grams, block=8):
    size = grams[0].shape[0]
    strips = size // 8
    lanes = 128
    full = (8, lanes)
    state = []
    for gram in grams:
        parts = [gram, jnp.where(iota((size, size), 0) == iota((size, size), 1), 1.0, 0.0)]
        if 2 * size < lanes:
            parts.append(jnp.zeros((size, lanes - 2 * size), jnp.float32))
        whole = jnp.concatenate(parts, axis=1)
        state.append([whole[8 * s : 8 * s + 8] for s in range(strips)])
    below = iota(full, 0)

    def line_of(strip, line):
        return jnp.broadcast_to(strip[line : line + 1], full)

    for start in range(0, size, block):
        strip, first = start // 8, start % 8
        active = range(strip, strips)
        for work in state:
            cols = [
                {s: jnp.broadcast_to(work[s][:, start + j : start + j + 1], full) for s in active}
                for j in range(block)
            ]
            factors = []

            def eliminate(j, scale, stop):
                line = first + j
                factor = {s: cols[j][s] * scale for s in active}
                factor[strip] = jnp.where(below > line, factor[strip], 0.0)
                for later in range(j + 1, stop):
                    head = line_of(cols[later][strip], line)
                    for s in active:
                        cols[later][s] = cols[later][s] - factor[s] * head
                factors.append(factor)

            for j in range(0, block, 2):
                line = first + j
                corner = line_of(cols[j][strip], line)
                side = line_of(cols[j][strip], line + 1)
                last = line_of(cols[j + 1][strip], line + 1)
                inverse = 1.0 / (corner * last - side * side)
                eliminate(j, 1.0 / corner, block)
                eliminate(j + 1, corner * inverse, block)
            for j in range(block):
                row = line_of(work[strip], first + j)
                for s in active:
                    if s == strip and first + j == 7:
                        continue
                    work[s] = work[s] - factors[j][s] * row
    results = []
    for work in state:
        parts = []
        for s in range(strips):
            place = iota((8, size), 0) + 8 * s == iota((8, size), 1)
            pivot = jnp.sum(jnp.where(place, work[s][:, :size], 0.0), axis=1, keepdims=True)
            parts.append(work[s][:, size : 2 * size] * lax.rsqrt(pivot))
        results.append(jnp.concatenate(parts, axis=0))
    return results


def member(group_ref, planes, dy=0, dz=0):
    y, z = lax.axis_index("gy"), lax.axis_index("gz")
    rows = lax.axis_size("gy")
    return group_ref[lax.rem(y + dy + rows, rows) * planes + lax.rem(z + dz + planes, planes)]


def store(ref, f, value):
    ref[f, 0], ref[f, 1] = split(value)


def load(ref, f):
    return ref[f, 0], ref[f, 1]


def upper_index(f, g):
    return sum(FACES - 1 - i for i in range(f)) + g - f - 1


def halves_kernel(planes, schur_ref, group_ref, own_ref, own_out, upper_out, flag_out, *scratch):
    upper_ref, sems = scratch
    width = own_ref.shape[1]
    strips = []
    for f in range(FACES - 1):
        rest = (FACES - 1 - f) * width
        copy = pltpu.make_async_copy(
            schur_ref.at[pl.ds(f * width, width), pl.ds((f + 1) * width, rest)],
            upper_ref.at[f, :, pl.ds((f + 1) * width, rest)],
            sems.at[f],
        )
        copy.start()
        strips.append(copy)
    core = lax.rem(lax.axis_index("gy"), 2)
    near = [(0, 0), (1 - 2 * core, 0), (-1, 0), (1, 0), (0, -1), (0, 1)]
    row = iota(flag_out.shape, 0)
    flags = jnp.zeros(flag_out.shape, jnp.float32)
    for i, (dy, dz) in enumerate(near):
        hit = member(group_ref, planes, dy, dz) == core
        flags = jnp.where(row == i, jnp.where(hit, 1.0, 0.0), flags)
    flag_out[...] = flags
    for f in range(FACES):
        store(own_out, f, own_ref[f])
    for f in range(FACES - 1):
        strips[f].wait()
        for g in range(f + 1, FACES):
            store(upper_out, upper_index(f, g), upper_ref[f, :, g * width : (g + 1) * width])


def begin(packed, owns, partner_out, sum_ref):
    width = owns[0].shape[1]
    half = width // 2
    eye = iota((half, half), 0) == iota((half, half), 1)
    zero = jnp.zeros((half, half), jnp.float32)
    guesses = []
    for f in range(len(packed)):
        partner = unpack(packed[f])
        total = owns[f] + partner
        store(partner_out, f, partner)
        store(sum_ref, f, total)
        across, down, twice = [], [], []
        for start in (0, half):
            block = total[start : start + half, start : start + half]
            diagonal = jnp.where(eye, block, 0.0)
            across.append(1.0 / jnp.sum(diagonal, axis=0, keepdims=True))
            down.append(1.0 / jnp.sum(diagonal, axis=1, keepdims=True))
            twice.append(jnp.where(eye, 2.0 * across[-1], 0.0))
        start = jnp.concatenate(
            [
                jnp.concatenate([twice[0], zero], axis=1),
                jnp.concatenate([zero, twice[1]], axis=1),
            ],
            axis=0,
        )
        across, down = jnp.concatenate(across, axis=1), jnp.concatenate(down, axis=0)
        guesses.append(start - down * total * across)
    return guesses


def newton(guesses, sum_ref):
    results = []
    for f, guess in enumerate(guesses):
        halves = split(guess)
        product = split(wide(load(sum_ref, f), halves))
        results.append(2.0 * guess - wide(halves, product))
    return results


def unit_rows(basis):
    return [b * lax.rsqrt(jnp.sum(b * b, axis=1, keepdims=True)) for b in basis]


def sweep_basis(before, inverse, after, basis):
    for matrices in (before, inverse, after):
        basis = [thin(stacked(b), matrix) for b, matrix in zip(basis, matrices)]
    return unit_rows(basis)


def early_kernel(axes, faces, *refs):
    arrays = len(refs) - 7
    inputs = refs[:arrays]
    own_ref, halves_ref, starts_ref, basis_out, partner_out, inverse_out, sum_ref = refs[arrays:]
    count = len(faces)
    packed = []
    done = 0
    for axis in axes:
        number = face_arrays(lax.axis_size(axis))
        packed += receive(inputs[done : done + number], axis)
        done += number
    guesses = begin(packed, [own_ref[f] for f in faces], partner_out, sum_ref)
    for sweep in range(NS_ITERS - 1):
        guesses = newton(guesses, sum_ref)
    for i in range(count):
        store(inverse_out, i, guesses[i])
    basis = [starts_ref[f] for f in faces]
    matrices = [
        [load(partner_out, i) for i in range(count)],
        [load(inverse_out, i) for i in range(count)],
        [load(halves_ref, f) for f in faces],
    ]
    for sweep in range(SUB_ITERS):
        basis = sweep_basis(*matrices, basis)
    for i in range(count):
        basis_out[i] = basis[i]


def main_kernel(axes, early, late, *refs):
    arrays = len(refs) - 11
    inputs = refs[:arrays]
    own_ref, halves_ref, upper_ref, starts_ref, resid_ref, early_basis = refs[arrays : arrays + 6]
    payload_ref, product_ref, partner_out, inverse_out, sum_ref = refs[arrays + 6 :]
    ncon, width = starts_ref.shape[1:]
    columns = resid_ref.shape[1]
    sides = {}
    rights = {}
    grams = {}
    vectors = {}
    count = len(late)

    def project(f, basis):
        vectors[f] = basis
        rows = stacked(basis)
        grams[f] = dot(basis, basis, ((1,), (1,)))
        side = {f: thin(rows, load(halves_ref, f))}
        for g in range(f + 1, FACES):
            side[g] = thin(rows, load(upper_ref, upper_index(f, g)))
        sides[f] = side
        rights[f] = thin(rows, split(resid_ref[f * width : (f + 1) * width]))

    packed = []
    done = 0
    for axis in axes:
        number = face_arrays(lax.axis_size(axis))
        packed += receive(inputs[done : done + number], axis)
        done += number
    guesses = begin(packed, [own_ref[f] for f in late], partner_out, sum_ref)
    pending = [(f, early_basis[i]) for i, f in enumerate(early)]
    for sweep in range(NS_ITERS - 1):
        guesses = newton(guesses, sum_ref)
        if pending:
            project(*pending.pop(0))
    for i in range(count):
        store(inverse_out, i, guesses[i])
    basis = [starts_ref[f] for f in late]
    matrices = [
        [load(partner_out, i) for i in range(count)],
        [load(inverse_out, i) for i in range(count)],
        [load(halves_ref, f) for f in late],
    ]
    for sweep in range(SUB_ITERS):
        basis = sweep_basis(*matrices, basis)
        if pending:
            project(*pending.pop(0))
    for item in pending:
        project(*item)
    for i, f in enumerate(late):
        project(f, basis[i])
    factors = factor_inverses([grams[f] for f in range(FACES)])
    blocks = []
    for g in range(FACES):
        tall = jnp.concatenate([sides[f][g] for f in range(g + 1)], axis=0)
        blocks.append(triple(triple(tall, vectors[g], ((1,), (1,))), factors[g], ((1,), (1,))))
    even, odd, right = [], [], []
    lows = None
    for f in range(FACES):
        product_ref[f] = triple(factors[f], sides[f][f])
        line = [blocks[g][f * ncon : (f + 1) * ncon] for g in range(f, FACES)]
        line = triple(factors[f], jnp.concatenate([rights[f]] + line, axis=1))
        right.append(line[:, :columns])
        line = line[:, columns:]
        if f % 2 == 0:
            even.append(line)
            lows = line[:, ncon : 2 * ncon].T
        else:
            odd += [lows, line]
    payload_ref[...] = jnp.concatenate(
        [
            jnp.concatenate(even + right[0::2], axis=1),
            jnp.concatenate(odd + right[1::2], axis=1),
        ],
        axis=0,
    )


def find(faces, refs, f):
    for group, ref in zip(faces, refs):
        if f in group:
            return load(ref, list(group).index(f))


def theirs_kernel(faces, ncon, own_ref, *refs):
    inputs, partner_refs, inverse_refs = refs[:-6], refs[-6:-4], refs[-4:-2]
    basis_out, product_out = refs[-2:]
    basis = []
    done = 0
    for axis in AXES[:2]:
        number = face_arrays(lax.axis_size(axis))
        packed = receive(inputs[done : done + number], axis)
        basis += [unpack_starts(part, ncon) for part in packed]
        done += number
    count = len(basis)
    matrices = [
        [load(own_ref, f) for f in range(count)],
        [find(faces, inverse_refs, f) for f in range(count)],
        [find(faces, partner_refs, f) for f in range(count)],
    ]
    for sweep in range(SUB_ITERS):
        basis = sweep_basis(*matrices, basis)
    for f in range(count):
        basis_out[f] = basis[f]
        product_out[f] = thin(stacked(basis[f]), matrices[2][f])


def spread_kernel(faces, unread, basis_ref, theirs_ref, product_ref, *refs):
    inverse_refs, out_ref = refs[:2], refs[2]
    basis = [basis_ref[f] for f in range(basis_ref.shape[0])]
    factors = factor_inverses([dot(b, b, ((1,), (1,))) for b in basis])
    for f in range(len(basis)):
        theirs = triple(factors[f], theirs_ref[f])
        both = jnp.concatenate([product_ref[f], theirs], axis=0)
        high, low = split(thin(stacked(both), find(faces, inverse_refs, f)).T)
        out_ref[f] = jnp.concatenate([high, high, low], axis=1)


def choose_kernel(flag_ref, here_ref, there_ref, matrix_ref, right_ref):
    mine = flag_ref[0:1, 0:1] > 0.5
    other = flag_ref[1:2, 0:1] > 0.5
    total = jnp.where(mine, here_ref[...], 0.0) + jnp.where(other, there_ref[...], 0.0)
    lanes = matrix_ref.shape[1]
    matrix_ref[...] = total[:, :lanes]
    right_ref[...] = total[:, lanes:]


def add_kernel(first_ref, second_ref, third_ref, fourth_ref, product_ref, unread, *refs):
    matrix_ref, right_ref, *sent = refs
    matrix_ref[...] = first_ref[...] + second_ref[...]
    right_ref[...] = third_ref[...] + fourth_ref[...]
    send(sent, AXES[2], product_ref[4], product_ref[5])


def solve_kernel(size, terms, columns, *refs):
    lanes = size * BLOCKS * (BLOCKS + 1) // 2
    matrix, right = refs[0][:, :lanes], refs[terms][...]
    for term in range(1, terms):
        matrix = matrix + refs[term][:, :lanes]
        right = right + refs[terms + term][...]
    answer_ref = refs[-1]
    lines = []
    offset = 0
    for b in range(BLOCKS):
        lines.append(matrix[:, offset : offset + (BLOCKS - b) * size])
        offset += (BLOCKS - b) * size
    eye = iota((size, size), 0) == iota((size, size), 1)
    downs, acrosses = [], []
    for b in range(BLOCKS):
        diagonal = jnp.where(eye, lines[b][:, :size], 0.0)
        downs.append(lax.rsqrt(jnp.sum(diagonal, axis=1, keepdims=True)))
        acrosses.append(lax.rsqrt(jnp.sum(diagonal, axis=0, keepdims=True)))
    blocks = {}
    rights = []
    for b in range(BLOCKS):
        for c in range(b, BLOCKS):
            block = lines[b][:, (c - b) * size : (c - b + 1) * size]
            blocks[b, c] = downs[b] * block * acrosses[c]
            if c > b:
                blocks[c, b] = blocks[b, c].T
        rights.append(downs[b] * right[:, b * columns : (b + 1) * columns])
    for b in range(BLOCKS):
        (inverse,) = factor_inverses([blocks[b, b]])
        later = range(b + 1, BLOCKS)
        row = triple(inverse, jnp.concatenate([rights[b]] + [blocks[b, c] for c in later], axis=1))
        if later:
            column = jnp.concatenate([blocks[c, b] for c in later], axis=0)
            change = triple(triple(column, inverse, ((1,), (1,))), row)
        for i, c in enumerate(later):
            part = change[i * size : (i + 1) * size]
            rights[c] = rights[c] - part[:, :columns]
            for j, d in enumerate(later):
                start = columns + j * size
                blocks[c, d] = blocks[c, d] - part[:, start : start + size]
        row = triple(inverse, row, ((0,), (0,)))
        rights[b] = row[:, :columns]
        for c in later:
            blocks[b, c] = row[:, columns + (c - b - 1) * size : columns + (c - b) * size]
        for i in range(b):
            for c in later:
                blocks[i, c] = blocks[i, c] - triple(blocks[i, b], blocks[b, c])
            rights[i] = rights[i] - triple(blocks[i, b], rights[b])
    answer = [downs[b] * rights[b] for b in range(BLOCKS)]
    answer_ref[...] = jnp.concatenate(answer, axis=0)


def rows_kernel(ncon, flag_ref, here_ref, there_ref, *refs):
    hit = flag_ref[0:1, 0:1] > 0.5
    rows = jnp.where(hit, here_ref[: 2 * ncon], there_ref[: 2 * ncon])
    refs[-1][...] = rows
    send(refs[:-1], AXES[0], rows[:ncon], rows[ncon:])


def last_product(spread, mine, theirs):
    high, low = split(jnp.concatenate([mine, theirs], axis=0))
    return lax.dot_general(
        spread,
        jnp.concatenate([high, low, high], axis=0),
        (((1,), (0,)), ((), ())),
        preferred_element_type=jnp.float32,
    )


def through(inverse, mine, theirs, my_answer, their_answer):
    high, low = split(jnp.concatenate([mine, theirs], axis=0).T)
    spread = jnp.concatenate([high, high, low], axis=1)
    return wide(inverse, split(last_product(spread, my_answer, their_answer)))


def last_faces(values, width, out_ref, result, sems):
    copies = []
    for f, value in values.items():
        place = pl.ds(f * width, width)
        result[f * width : (f + 1) * width] = value()
        copy = pltpu.make_async_copy(result.at[place], out_ref.at[place], sems.at[f])
        copy.start()
        copies.append(copy)
    for copy in copies:
        copy.wait()


def last_plain_kernel(faces, product_ref, early_inverse, late_inverse, *refs):
    spread_ref, answer_ref, *inputs = refs[:-3]
    ncon, width = product_ref.shape[1:]
    number = face_arrays(lax.axis_size(AXES[2]))
    theirs = receive(inputs[:number], AXES[2])
    near = receive(inputs[number:-number], AXES[1]) + receive(inputs[-number:], AXES[2])
    values = {}
    for f in range(2, FACES):
        mine = answer_ref[f * ncon : (f + 1) * ncon]
        if f < 4:
            values[f] = functools.partial(last_product, spread_ref[f], mine, near[f - 2])
        else:
            values[f] = functools.partial(
                through,
                find(faces, (early_inverse, late_inverse), f),
                product_ref[f],
                theirs[f - 4],
                mine,
                near[f - 2],
            )
    last_faces(values, width, *refs[-3:])


def last_near_kernel(faces, flag_ref, product_ref, early_inverse, late_inverse, *refs):
    spread_ref, here_answer, there_answer = refs[:3]
    theirs = receive(refs[3:-3], AXES[2])
    ncon, width = product_ref.shape[1:]

    def answer(flag, f):
        place = slice(f * ncon, (f + 1) * ncon)
        hit = flag_ref[flag : flag + 1, 0:1] > 0.5
        return jnp.where(hit, here_answer[place], there_answer[place])

    values = {}
    for f in (2, 3):
        values[f] = functools.partial(
            last_product, spread_ref[f], answer(0, f), answer(f, f ^ 1)
        )
    for f in (4, 5):
        values[f] = functools.partial(
            through,
            find(faces, (early_inverse, late_inverse), f),
            product_ref[f],
            theirs[f - 4],
            answer(0, f),
            answer(f, f ^ 1),
        )
    last_faces(values, width, *refs[-3:])


def last_far_kernel(ncon, spread_ref, rows_ref, *refs):
    theirs = receive(refs[:-4], AXES[0])
    values = {}
    for f in range(2):
        mine = rows_ref[f * ncon : (f + 1) * ncon]
        values[f] = functools.partial(last_product, spread_ref[f], mine, theirs[f])
    last_faces(values, spread_ref.shape[1], *refs[-3:])


def per_device(schur, start_block, resid, group_of):
    matrix = schur[0, 0, 0]
    matrix = pltpu.with_memory_space_constraint(matrix, pltpu.HBM)
    starts = start_block[0, 0, 0].transpose(0, 2, 1)
    right = resid[0, 0, 0]
    order, columns = right.shape
    ncon, width = starts.shape[1:]
    counts = [lax.axis_size(axis) for axis in AXES]
    arrays = sum(face_arrays(count) for count in counts)
    coarse = FACES * ncon
    size = 2 * ncon
    half = width // 2
    lanes = size * BLOCKS * (BLOCKS + 1) // 2
    right_lanes = BLOCKS * columns
    uppers = FACES * (FACES - 1) // 2
    anywhere = pl.BlockSpec(memory_space=pl.ANY)
    main_memory = pl.BlockSpec(memory_space=pltpu.HBM)
    scalars = pl.BlockSpec(memory_space=pltpu.SMEM)
    early, late = (4, 5), (0, 1, 2, 3)
    faces = (early, late)
    planes = counts[2]

    def shape(*dims):
        return jax.ShapeDtypeStruct(dims, jnp.float32)

    def halves(count):
        return jax.ShapeDtypeStruct((count, 2, width, width), jnp.bfloat16)

    def params(mib):
        return pltpu.CompilerParams(vmem_limit_bytes=mib * MIB)

    def cost(us):
        return pl.CostEstimate(flops=us * 10**9, bytes_accessed=2**20, transcendentals=0)

    *packed, own = pl.pallas_call(
        functools.partial(pack_kernel, counts, width),
        out_shape=face_shapes(counts[0], (width + 8 + 2 * ncon, half))
        + face_shapes(counts[1], (width + 8 + 2 * ncon, half))
        + face_shapes(counts[2], (width + 8, half))
        + [shape(FACES, width, width)],
        in_specs=[main_memory, main_memory],
        out_specs=vmem_specs(arrays + 1),
        scratch_shapes=[
            pltpu.VMEM((4, ncon, width), jnp.float32),
            pltpu.SemaphoreType.DMA((FACES,)),
            pltpu.SemaphoreType.DMA,
        ],
        compiler_params=params(12),
    )(matrix, pltpu.with_memory_space_constraint(starts, pltpu.HBM))
    ends = [sum(face_arrays(count) for count in counts[:position]) for position in range(4)]
    got = {}
    for position in (2, 0, 1):
        got[position] = exchange(packed[ends[position] : ends[position + 1]], AXES[position])

    own_halves, upper_halves, flags = pl.pallas_call(
        functools.partial(halves_kernel, planes),
        out_shape=[halves(FACES), halves(uppers), shape(8, 128)],
        in_specs=[main_memory, scalars] + vmem_specs(1),
        out_specs=vmem_specs(3),
        scratch_shapes=[
            pltpu.VMEM((FACES - 1, width, order), jnp.float32),
            pltpu.SemaphoreType.DMA((FACES - 1,)),
        ],
        compiler_params=params(24),
        cost_estimate=cost(2),
    )(matrix, group_of, own)

    early_basis, early_partner, early_inverse = pl.pallas_call(
        functools.partial(early_kernel, AXES[2:3], early),
        out_shape=[shape(len(early), ncon, width)] + [halves(len(early))] * 2,
        in_specs=vmem_specs(len(got[2]) + 3),
        out_specs=vmem_specs(3),
        scratch_shapes=[pltpu.VMEM((len(early), 2, width, width), jnp.bfloat16)],
        compiler_params=params(16),
        cost_estimate=cost(2),
    )(*got[2], own, own_halves, starts)

    payload, product, late_partner, late_inverse = pl.pallas_call(
        functools.partial(main_kernel, (AXES[0], AXES[1]), early, late),
        out_shape=[shape(size, lanes + right_lanes), shape(FACES, ncon, width)]
        + [halves(len(late))] * 2,
        in_specs=vmem_specs(len(got[0]) + len(got[1]) + 6),
        out_specs=vmem_specs(4),
        scratch_shapes=[pltpu.VMEM((len(late), 2, width, width), jnp.bfloat16)],
        compiler_params=params(24),
        cost_estimate=cost(8),
    )(*got[0], *got[1], own, own_halves, upper_halves, starts, right, early_basis)

    partners = [early_partner, late_partner]
    inverses = [early_inverse, late_inverse]
    their_basis, their_product = pl.pallas_call(
        functools.partial(theirs_kernel, faces, ncon),
        out_shape=[shape(4, ncon, width)] * 2,
        in_specs=vmem_specs(5 + len(got[0]) + len(got[1])),
        out_specs=vmem_specs(2),
        compiler_params=params(16),
        cost_estimate=cost(2),
    )(own_halves, *got[0], *got[1], *partners, *inverses)

    def spread_of(token):
        return pl.pallas_call(
            functools.partial(spread_kernel, faces),
            out_shape=jax.ShapeDtypeStruct((4, width, 3 * size), jnp.bfloat16),
            in_specs=[anywhere] + vmem_specs(5),
            out_specs=vmem_specs(1)[0],
            compiler_params=params(16),
            cost_estimate=cost(2),
        )(token, their_basis, their_product, product, *inverses)

    def solve(matrices, rights, unread):
        return pl.pallas_call(
            functools.partial(solve_kernel, size, len(matrices), columns),
            out_shape=shape(coarse, columns),
            in_specs=vmem_specs(2 * len(matrices)) + [anywhere] * len(unread),
            out_specs=vmem_specs(1)[0],
            compiler_params=params(12),
            cost_estimate=cost(7),
        )(*matrices, *rights, *unread)

    result = dict(
        out_shape=shape(order, columns),
        out_specs=main_memory,
        scratch_shapes=[
            pltpu.VMEM((order, columns), jnp.float32),
            pltpu.SemaphoreType.DMA((FACES,)),
        ],
        compiler_params=params(12),
        cost_estimate=cost(1),
    )
    groups = group_of.shape[0] // GROUP_SIZE
    if groups == 2 and counts[1] == 4 and planes == 2:
        core_swap, chip_x, chip_y = flipped("gy", 1), flipped("gy", 2), flipped("gz", 1)
        other = lax.ppermute(payload, "gy", core_swap)
        left, rest = pl.pallas_call(
            choose_kernel,
            out_shape=[shape(size, lanes), shape(size, right_lanes)],
            in_specs=vmem_specs(3),
            out_specs=vmem_specs(2),
            compiler_params=params(8),
        )(flags, payload, other)
        left_moved = lax.ppermute(left, "gy", chip_x)
        rest_moved = lax.ppermute(rest, "gz", chip_y)
        left_last, rest_last, *sent = pl.pallas_call(
            add_kernel,
            out_shape=[shape(size, lanes), shape(size, right_lanes)]
            + face_shapes(counts[2], (ncon, width)),
            in_specs=vmem_specs(5) + [anywhere],
            out_specs=vmem_specs(2 + face_arrays(counts[2])),
            compiler_params=params(8),
        )(left, left_moved, rest, rest_moved, product, their_basis)
        left_other = lax.ppermute(left_last, "gz", chip_y)
        rest_other = lax.ppermute(rest_last, "gy", chip_x)
        theirs = exchange(sent, AXES[2])
        spread = spread_of(left_last)
        answer = solve([left_last, left_other], [rest_last, rest_other], [spread])
        there = lax.ppermute(answer, "gy", core_swap)
        *sent, mine = pl.pallas_call(
            functools.partial(rows_kernel, ncon),
            out_shape=face_shapes(counts[0], (ncon, columns)) + [shape(size, columns)],
            in_specs=vmem_specs(3),
            out_specs=vmem_specs(face_arrays(counts[0]) + 1),
            compiler_params=params(8),
        )(flags, answer, there)
        across = exchange(sent, AXES[0])
        correction = pl.pallas_call(
            functools.partial(last_near_kernel, faces),
            in_specs=vmem_specs(7 + len(theirs)),
            **result,
        )(flags, product, *inverses, spread, answer, there, *theirs)
    else:
        y, z = lax.axis_index("gy"), lax.axis_index("gz")
        member_of = group_of[y * planes + z]
        chosen = jnp.arange(groups, dtype=jnp.int32) == member_of
        total = lax.psum(jnp.where(chosen[:, None, None], payload[None], 0.0), ("gy", "gz"))
        total = lax.dynamic_index_in_dim(total, member_of, 0, keepdims=False)
        spread = spread_of(payload)
        answer = solve([total[:, :lanes]], [total[:, lanes:]], [])

        def from_near(faces_of, axis):
            even, odd = faces_of
            if lax.axis_size(axis) == 2:
                return exchange([jnp.stack([even, odd])], axis)
            upward = is_even(axis)
            return exchange([jnp.where(upward, even, odd), jnp.where(upward, odd, even)], axis)

        blocks = answer.reshape(FACES, ncon, columns)
        near = [
            *from_near(product[4:6], AXES[2]),
            *from_near(blocks[2:4], AXES[1]),
            *from_near(blocks[4:6], AXES[2]),
        ]
        mine = answer[:size]
        across = from_near(blocks[:2], AXES[0])
        correction = pl.pallas_call(
            functools.partial(last_plain_kernel, faces),
            in_specs=vmem_specs(5 + len(near)),
            **result,
        )(product, *inverses, spread, answer, *near)
    correction = pl.pallas_call(
        functools.partial(last_far_kernel, ncon),
        in_specs=vmem_specs(2 + len(across)) + [main_memory],
        input_output_aliases={2 + len(across): 0},
        **result,
    )(spread, mine, *across, correction)
    return correction[None, None, None]


def solution(mesh):
    in_specs = (
        P("gx", "gy", "gz", None, None),
        P("gx", "gy", "gz", None, None, None),
        P("gx", "gy", "gz", None, None),
        P(),
    )
    out_specs = P("gx", "gy", "gz", None, None)
    return jax.shard_map(
        per_device, mesh=mesh, in_specs=in_specs, out_specs=out_specs, check_vma=False
    )
```

```python
import functools

import jax
import jax.numpy as jnp
from jax import lax
from jax.experimental import pallas as pl
from jax.experimental.pallas import tpu as pltpu
from jax.sharding import PartitionSpec as P

NS_ITERS = 3
SUB_ITERS = 2
GROUP_SIZE = 4
FACES = 6
BLOCKS = FACES // 2
AXES = ("gx", "gy", "gz")
MIB = 1024 * 1024

precise = lax.Precision.HIGHEST


def dot(left, right, dims=((1,), (0,))):
    return lax.dot_general(
        left, right, (dims, ((), ())), precision=precise, preferred_element_type=jnp.float32
    )


def split(value):
    high = value.astype(jnp.bfloat16)
    return high, (value - high.astype(jnp.float32)).astype(jnp.bfloat16)


def wide(left, right):
    return lax.dot_general(
        jnp.concatenate([left[0], left[0], left[1]], axis=1),
        jnp.concatenate([right[0], right[1], right[0]], axis=0),
        (((1,), (0,)), ((), ())),
        preferred_element_type=jnp.float32,
    )


def stacked(value):
    return jnp.concatenate(split(value), axis=0)


def thin(rows, matrix):
    out = lax.dot_general(
        jnp.concatenate([rows, rows], axis=1),
        jnp.concatenate(matrix, axis=0),
        (((1,), (0,)), ((), ())),
        preferred_element_type=jnp.float32,
    )
    half = rows.shape[0] // 2
    return out[:half] + out[half:]


def triple(left, right, dims=((1,), (0,))):
    (left_high, left_low), (right_high, right_low) = split(left), split(right)
    total = None
    for one, other in ((left_high, right_high), (left_high, right_low), (left_low, right_high)):
        part = lax.dot_general(
            one, other, (dims, ((), ())), preferred_element_type=jnp.float32
        )
        total = part if total is None else total + part
    return total


def reciprocal(value):
    guess = pl.reciprocal(value, approx=True)
    for correction in range(2):
        guess = guess * (2.0 - value * guess)
    return guess


def iota(shape, dim):
    return lax.broadcasted_iota(jnp.int32, shape, dim)


def flipped(axis, bit):
    return [(i, i ^ bit) for i in range(lax.axis_size(axis))]


def outer_pairs(axis):
    count = lax.axis_size(axis)
    return [(i, (i + 1 if i % 2 else i - 1) % count) for i in range(count)]


def face_arrays(count):
    return 1 if count == 2 else 2


def exchange(arrays, axis):
    if lax.axis_size(axis) == 2:
        return [lax.ppermute(arrays[0], axis, flipped(axis, 1))]
    return [
        lax.ppermute(arrays[0], axis, outer_pairs(axis)),
        lax.ppermute(arrays[1], axis, flipped(axis, 1)),
    ]


def is_even(axis):
    return lax.rem(lax.axis_index(axis), 2) == 0


def send(refs, axis, even, odd):
    if lax.axis_size(axis) == 2:
        refs[0][0] = even
        refs[0][1] = odd
    else:
        upward = is_even(axis)
        refs[0][...] = jnp.where(upward, even, odd)
        refs[1][...] = jnp.where(upward, odd, even)


def receive(refs, axis):
    if lax.axis_size(axis) == 2:
        return refs[0][1], refs[0][0]
    upward = is_even(axis)
    first, second = refs[0][...], refs[1][...]
    return jnp.where(upward, first, second), jnp.where(upward, second, first)


def face_shapes(count, shape):
    if count == 2:
        return [jax.ShapeDtypeStruct((2,) + shape, jnp.float32)]
    return [jax.ShapeDtypeStruct(shape, jnp.float32)] * 2


def vmem_specs(count):
    return [pl.BlockSpec(memory_space=pltpu.VMEM)] * count


def pack_kernel(counts, width, schur_ref, starts_ref, *refs):
    outs, blocks = refs[:-4], refs[-4]
    starts, sems, start_sem = refs[-3:]
    half = width // 2
    copies = []
    for f in range(FACES):
        place = pl.ds(f * width, width)
        copy = pltpu.make_async_copy(schur_ref.at[place, place], blocks.at[f], sems.at[f])
        copy.start()
        copies.append(copy)
    start_copy = pltpu.make_async_copy(starts_ref.at[pl.ds(0, 4)], starts, start_sem)
    start_copy.start()
    row, col = iota((half, half), 0), iota((half, half), 1)
    start_copy.wait()

    def pack(f):
        copies[f].wait()
        first = blocks[f, 0:half, 0:half]
        second = blocks[f, half:width, half:width]
        diag = jnp.sum(jnp.where(row == col, second, 0.0), axis=0, keepdims=True)
        mixed = jnp.where(row >= col, first, second)
        tail = jnp.broadcast_to(diag, (8, half))
        parts = [blocks[f, half:width, 0:half], mixed, tail]
        if f < 4:
            parts += [starts[f, :, :half], starts[f, :, half:]]
        return jnp.concatenate(parts, axis=0)

    done = 0
    for position, axis in enumerate(AXES):
        number = face_arrays(counts[position])
        send(outs[done : done + number], axis, pack(2 * position), pack(2 * position + 1))
        done += number


def unpack(packed):
    half = packed.shape[1]
    row, col = iota((half, half), 0), iota((half, half), 1)
    low = packed[0:half]
    mixed = packed[half : 2 * half]
    flip = mixed.T
    first = jnp.where(row >= col, mixed, flip)
    second = jnp.where(row < col, mixed, flip)
    second = jnp.where(row == col, packed[2 * half : 2 * half + 1], second)
    return jnp.concatenate(
        [jnp.concatenate([first, low.T], axis=1), jnp.concatenate([low, second], axis=1)], axis=0
    )


def unpack_starts(packed, ncon):
    half = packed.shape[1]
    rows = packed[2 * half + 8 :]
    return jnp.concatenate([rows[:ncon], rows[ncon:]], axis=1)


def factor_inverses(grams, block=8):
    size = grams[0].shape[0]
    strips = size // 8
    lanes = 128
    full = (8, lanes)
    state = []
    for gram in grams:
        parts = [gram, jnp.where(iota((size, size), 0) == iota((size, size), 1), 1.0, 0.0)]
        if 2 * size < lanes:
            parts.append(jnp.zeros((size, lanes - 2 * size), jnp.float32))
        whole = jnp.concatenate(parts, axis=1)
        state.append([whole[8 * s : 8 * s + 8] for s in range(strips)])
    below = iota(full, 0)

    def line_of(strip, line):
        return jnp.broadcast_to(strip[line : line + 1], full)

    for start in range(0, size, block):
        strip, first = start // 8, start % 8
        active = range(strip, strips)
        for work in state:
            cols = [
                {s: jnp.broadcast_to(work[s][:, start + j : start + j + 1], full) for s in active}
                for j in range(block)
            ]
            factors = []

            def eliminate(j, scale, stop):
                line = first + j
                factor = {s: cols[j][s] * scale for s in active}
                factor[strip] = jnp.where(below > line, factor[strip], 0.0)
                for later in range(j + 1, stop):
                    head = line_of(cols[later][strip], line)
                    for s in active:
                        cols[later][s] = cols[later][s] - factor[s] * head
                factors.append(factor)

            for j in range(0, block, 2):
                line = first + j
                corner = line_of(cols[j][strip], line)
                side = line_of(cols[j][strip], line + 1)
                last = line_of(cols[j + 1][strip], line + 1)
                inverse = reciprocal(corner * last - side * side)
                eliminate(j, reciprocal(corner), block)
                eliminate(j + 1, corner * inverse, block)
            for j in range(block):
                row = line_of(work[strip], first + j)
                for s in active:
                    if s == strip and first + j == 7:
                        continue
                    work[s] = work[s] - factors[j][s] * row
    results = []
    for work in state:
        parts = []
        for s in range(strips):
            place = iota((8, size), 0) + 8 * s == iota((8, size), 1)
            pivot = jnp.sum(jnp.where(place, work[s][:, :size], 0.0), axis=1, keepdims=True)
            parts.append(work[s][:, size : 2 * size] * lax.rsqrt(pivot))
        results.append(jnp.concatenate(parts, axis=0))
    return results


def member(group_ref, planes, dy=0, dz=0):
    y, z = lax.axis_index("gy"), lax.axis_index("gz")
    rows = lax.axis_size("gy")
    return group_ref[lax.rem(y + dy + rows, rows) * planes + lax.rem(z + dz + planes, planes)]


def store(ref, f, value):
    ref[f, 0], ref[f, 1] = split(value)


def load(ref, f):
    return ref[f, 0], ref[f, 1]


def upper_index(f, g):
    return sum(FACES - 1 - i for i in range(f)) + g - f - 1


def halves_kernel(planes, schur_ref, group_ref, own_ref, own_out, upper_out, flag_out, *scratch):
    upper_ref, sems = scratch
    width = own_ref.shape[1]
    strips = []
    for f in range(FACES - 1):
        rest = (FACES - 1 - f) * width
        copy = pltpu.make_async_copy(
            schur_ref.at[pl.ds(f * width, width), pl.ds((f + 1) * width, rest)],
            upper_ref.at[f, :, pl.ds((f + 1) * width, rest)],
            sems.at[f],
        )
        copy.start()
        strips.append(copy)
    core = lax.rem(lax.axis_index("gy"), 2)
    near = [(0, 0), (1 - 2 * core, 0), (-1, 0), (1, 0), (0, -1), (0, 1)]
    row = iota(flag_out.shape, 0)
    flags = jnp.zeros(flag_out.shape, jnp.float32)
    for i, (dy, dz) in enumerate(near):
        hit = member(group_ref, planes, dy, dz) == core
        flags = jnp.where(row == i, jnp.where(hit, 1.0, 0.0), flags)
    flag_out[...] = flags
    for f in range(FACES):
        store(own_out, f, own_ref[f])
    for f in range(FACES - 1):
        strips[f].wait()
        for g in range(f + 1, FACES):
            store(upper_out, upper_index(f, g), upper_ref[f, :, g * width : (g + 1) * width])


def inverses_of(packed, owns, partner_ref):
    width = owns[0].shape[1]
    half = width // 2
    eye = iota((half, half), 0) == iota((half, half), 1)
    whole_eye = iota((width, width), 0) == iota((width, width), 1)
    powers, sums, downs = [], [], []
    for f in range(len(packed)):
        partner = unpack(packed[f])
        store(partner_ref, f, partner)
        total = owns[f] + partner
        across, down = [], []
        for start in (0, half):
            block = total[start : start + half, start : start + half]
            diagonal = jnp.where(eye, block, 0.0)
            across.append(1.0 / jnp.sum(diagonal, axis=0, keepdims=True))
            down.append(1.0 / jnp.sum(diagonal, axis=1, keepdims=True))
        downs.append(jnp.concatenate(down, axis=0))
        power = jnp.where(whole_eye, 0.0, -total * jnp.concatenate(across, axis=1))
        powers.append(split(power))
        sums.append(jnp.where(whole_eye, 1.0, power))
    for step in range(1, NS_ITERS):
        powers = [split(wide(power, power)) for power in powers]
        sums = [total + wide(split(total), power) for total, power in zip(sums, powers)]
    return [down * total for down, total in zip(downs, sums)]


def unit_rows(basis):
    return [b * lax.rsqrt(jnp.sum(b * b, axis=1, keepdims=True)) for b in basis]


def sweep_basis(before, inverse, after, basis):
    for matrices in (before, inverse, after):
        basis = [thin(stacked(b), matrix) for b, matrix in zip(basis, matrices)]
    return unit_rows(basis)


def early_kernel(axes, faces, *refs):
    arrays = len(refs) - 6
    inputs = refs[:arrays]
    own_ref, halves_ref, starts_ref, basis_out, partner_out, inverse_out = refs[arrays:]
    count = len(faces)
    packed = []
    done = 0
    for axis in axes:
        number = face_arrays(lax.axis_size(axis))
        packed += receive(inputs[done : done + number], axis)
        done += number
    inverses = inverses_of(packed, [own_ref[f] for f in faces], partner_out)
    for i in range(count):
        store(inverse_out, i, inverses[i])
    basis = [starts_ref[f] for f in faces]
    matrices = [
        [load(partner_out, i) for i in range(count)],
        [load(inverse_out, i) for i in range(count)],
        [load(halves_ref, f) for f in faces],
    ]
    for sweep in range(SUB_ITERS):
        basis = sweep_basis(*matrices, basis)
    for i in range(count):
        basis_out[i] = basis[i]


def main_kernel(axes, early, late, *refs):
    arrays = len(refs) - 10
    inputs = refs[:arrays]
    own_ref, halves_ref, upper_ref, starts_ref, resid_ref, early_basis = refs[arrays : arrays + 6]
    payload_ref, product_ref, partner_out, inverse_out = refs[arrays + 6 :]
    ncon, width = starts_ref.shape[1:]
    columns = resid_ref.shape[1]
    sides = {}
    rights = {}
    grams = {}
    vectors = {}
    count = len(late)

    def project(f, basis):
        vectors[f] = basis
        rows = stacked(basis)
        grams[f] = dot(basis, basis, ((1,), (1,)))
        side = {f: thin(rows, load(halves_ref, f))}
        for g in range(f + 1, FACES):
            side[g] = thin(rows, load(upper_ref, upper_index(f, g)))
        sides[f] = side
        rights[f] = thin(rows, split(resid_ref[f * width : (f + 1) * width]))

    packed = []
    done = 0
    for axis in axes:
        number = face_arrays(lax.axis_size(axis))
        packed += receive(inputs[done : done + number], axis)
        done += number
    inverses = inverses_of(packed, [own_ref[f] for f in late], partner_out)
    pending = [(f, early_basis[i]) for i, f in enumerate(early)]
    for i in range(count):
        store(inverse_out, i, inverses[i])
    basis = [starts_ref[f] for f in late]
    matrices = [
        [load(partner_out, i) for i in range(count)],
        [load(inverse_out, i) for i in range(count)],
        [load(halves_ref, f) for f in late],
    ]
    for sweep in range(SUB_ITERS):
        basis = sweep_basis(*matrices, basis)
        if pending:
            project(*pending.pop(0))
    for item in pending:
        project(*item)
    for i, f in enumerate(late):
        project(f, basis[i])
    factors = factor_inverses([grams[f] for f in range(FACES)])
    blocks = []
    for g in range(FACES):
        tall = jnp.concatenate([sides[f][g] for f in range(g + 1)], axis=0)
        blocks.append(triple(triple(tall, vectors[g], ((1,), (1,))), factors[g], ((1,), (1,))))
    even, odd, right = [], [], []
    lows = None
    for f in range(FACES):
        product_ref[f] = triple(factors[f], sides[f][f])
        line = [blocks[g][f * ncon : (f + 1) * ncon] for g in range(f, FACES)]
        line = triple(factors[f], jnp.concatenate([rights[f]] + line, axis=1))
        right.append(line[:, :columns])
        line = line[:, columns:]
        if f % 2 == 0:
            even.append(line)
            lows = line[:, ncon : 2 * ncon].T
        else:
            odd += [lows, line]
    payload_ref[...] = jnp.concatenate(
        [
            jnp.concatenate(even + right[0::2], axis=1),
            jnp.concatenate(odd + right[1::2], axis=1),
        ],
        axis=0,
    )


def find(faces, refs, f):
    for group, ref in zip(faces, refs):
        if f in group:
            return load(ref, list(group).index(f))


def theirs_kernel(faces, ncon, own_ref, *refs):
    inputs, partner_refs, inverse_refs = refs[:-5], refs[-5:-3], refs[-3:-1]
    product_out = refs[-1]
    basis = []
    done = 0
    for axis in AXES[:2]:
        number = face_arrays(lax.axis_size(axis))
        packed = receive(inputs[done : done + number], axis)
        basis += [unpack_starts(part, ncon) for part in packed]
        done += number
    count = len(basis)
    matrices = [
        [load(own_ref, f) for f in range(count)],
        [find(faces, inverse_refs, f) for f in range(count)],
        [find(faces, partner_refs, f) for f in range(count)],
    ]
    for sweep in range(SUB_ITERS):
        basis = sweep_basis(*matrices, basis)
    factors = factor_inverses([dot(b, b, ((1,), (1,))) for b in basis])
    for f in range(count):
        product_out[f] = triple(factors[f], thin(stacked(basis[f]), matrices[2][f]))


def spread_kernel(faces, unread, theirs_ref, product_ref, *refs):
    inverse_refs, out_ref = refs[:2], refs[2]
    for f in range(theirs_ref.shape[0]):
        both = jnp.concatenate([product_ref[f], theirs_ref[f]], axis=0)
        high, low = split(thin(stacked(both), find(faces, inverse_refs, f)).T)
        out_ref[f] = jnp.concatenate([high, high, low], axis=1)


def choose_kernel(flag_ref, here_ref, there_ref, matrix_ref, right_ref):
    mine = flag_ref[0:1, 0:1] > 0.5
    other = flag_ref[1:2, 0:1] > 0.5
    total = jnp.where(mine, here_ref[...], 0.0) + jnp.where(other, there_ref[...], 0.0)
    lanes = matrix_ref.shape[1]
    matrix_ref[...] = total[:, :lanes]
    right_ref[...] = total[:, lanes:]


def add_kernel(first_ref, second_ref, third_ref, fourth_ref, product_ref, unread, *refs):
    matrix_ref, right_ref, *sent = refs
    matrix_ref[...] = first_ref[...] + second_ref[...]
    right_ref[...] = third_ref[...] + fourth_ref[...]
    send(sent, AXES[2], product_ref[4], product_ref[5])


def solve_kernel(size, terms, columns, *refs):
    lanes = size * BLOCKS * (BLOCKS + 1) // 2
    matrix, right = refs[0][:, :lanes], refs[terms][...]
    for term in range(1, terms):
        matrix = matrix + refs[term][:, :lanes]
        right = right + refs[terms + term][...]
    answer_ref = refs[-1]
    lines = []
    offset = 0
    for b in range(BLOCKS):
        lines.append(matrix[:, offset : offset + (BLOCKS - b) * size])
        offset += (BLOCKS - b) * size
    eye = iota((size, size), 0) == iota((size, size), 1)
    downs, acrosses = [], []
    for b in range(BLOCKS):
        diagonal = jnp.where(eye, lines[b][:, :size], 0.0)
        downs.append(lax.rsqrt(jnp.sum(diagonal, axis=1, keepdims=True)))
        acrosses.append(lax.rsqrt(jnp.sum(diagonal, axis=0, keepdims=True)))
    blocks = {}
    rights = []
    for b in range(BLOCKS):
        for c in range(b, BLOCKS):
            block = lines[b][:, (c - b) * size : (c - b + 1) * size]
            blocks[b, c] = downs[b] * block * acrosses[c]
            if c > b:
                blocks[c, b] = blocks[b, c].T
        rights.append(downs[b] * right[:, b * columns : (b + 1) * columns])
    for b in range(BLOCKS):
        (inverse,) = factor_inverses([blocks[b, b]])
        later = range(b + 1, BLOCKS)
        row = triple(inverse, jnp.concatenate([rights[b]] + [blocks[b, c] for c in later], axis=1))
        if later:
            column = jnp.concatenate([blocks[c, b] for c in later], axis=0)
            change = triple(triple(column, inverse, ((1,), (1,))), row)
        for i, c in enumerate(later):
            part = change[i * size : (i + 1) * size]
            rights[c] = rights[c] - part[:, :columns]
            for j, d in enumerate(later):
                start = columns + j * size
                blocks[c, d] = blocks[c, d] - part[:, start : start + size]
        row = triple(inverse, row, ((0,), (0,)))
        rights[b] = row[:, :columns]
        for c in later:
            blocks[b, c] = row[:, columns + (c - b - 1) * size : columns + (c - b) * size]
        for i in range(b):
            for c in later:
                blocks[i, c] = blocks[i, c] - triple(blocks[i, b], blocks[b, c])
            rights[i] = rights[i] - triple(blocks[i, b], rights[b])
    answer = [downs[b] * rights[b] for b in range(BLOCKS)]
    answer_ref[...] = jnp.concatenate(answer, axis=0)


def rows_kernel(ncon, flag_ref, here_ref, there_ref, *refs):
    hit = flag_ref[0:1, 0:1] > 0.5
    rows = jnp.where(hit, here_ref[: 2 * ncon], there_ref[: 2 * ncon])
    refs[-1][...] = rows
    send(refs[:-1], AXES[0], rows[:ncon], rows[ncon:])


def last_product(spread, mine, theirs):
    high, low = split(jnp.concatenate([mine, theirs], axis=0))
    return lax.dot_general(
        spread,
        jnp.concatenate([high, low, high], axis=0),
        (((1,), (0,)), ((), ())),
        preferred_element_type=jnp.float32,
    )


def through(inverse, mine, theirs, my_answer, their_answer):
    high, low = split(jnp.concatenate([mine, theirs], axis=0).T)
    spread = jnp.concatenate([high, high, low], axis=1)
    return wide(inverse, split(last_product(spread, my_answer, their_answer)))


def last_faces(values, width, out_ref, result, sems):
    copies = []
    for f, value in values.items():
        place = pl.ds(f * width, width)
        result[f * width : (f + 1) * width] = value()
        copy = pltpu.make_async_copy(result.at[place], out_ref.at[place], sems.at[f])
        copy.start()
        copies.append(copy)
    for copy in copies:
        copy.wait()


def last_plain_kernel(faces, product_ref, early_inverse, late_inverse, *refs):
    spread_ref, answer_ref, *inputs = refs[:-3]
    ncon, width = product_ref.shape[1:]
    number = face_arrays(lax.axis_size(AXES[2]))
    theirs = receive(inputs[:number], AXES[2])
    near = receive(inputs[number:-number], AXES[1]) + receive(inputs[-number:], AXES[2])
    values = {}
    for f in range(2, FACES):
        mine = answer_ref[f * ncon : (f + 1) * ncon]
        if f < 4:
            values[f] = functools.partial(last_product, spread_ref[f], mine, near[f - 2])
        else:
            values[f] = functools.partial(
                through,
                find(faces, (early_inverse, late_inverse), f),
                product_ref[f],
                theirs[f - 4],
                mine,
                near[f - 2],
            )
    last_faces(values, width, *refs[-3:])


def last_near_kernel(faces, flag_ref, product_ref, early_inverse, late_inverse, *refs):
    spread_ref, here_answer, there_answer = refs[:3]
    theirs = receive(refs[3:-3], AXES[2])
    ncon, width = product_ref.shape[1:]

    def answer(flag, f):
        place = slice(f * ncon, (f + 1) * ncon)
        hit = flag_ref[flag : flag + 1, 0:1] > 0.5
        return jnp.where(hit, here_answer[place], there_answer[place])

    values = {}
    for f in (2, 3):
        values[f] = functools.partial(
            last_product, spread_ref[f], answer(0, f), answer(f, f ^ 1)
        )
    for f in (4, 5):
        values[f] = functools.partial(
            through,
            find(faces, (early_inverse, late_inverse), f),
            product_ref[f],
            theirs[f - 4],
            answer(0, f),
            answer(f, f ^ 1),
        )
    last_faces(values, width, *refs[-3:])


def last_far_kernel(ncon, spread_ref, rows_ref, *refs):
    theirs = receive(refs[:-4], AXES[0])
    values = {}
    for f in range(2):
        mine = rows_ref[f * ncon : (f + 1) * ncon]
        values[f] = functools.partial(last_product, spread_ref[f], mine, theirs[f])
    last_faces(values, spread_ref.shape[1], *refs[-3:])


def per_device(schur, start_block, resid, group_of):
    matrix = schur[0, 0, 0]
    matrix = pltpu.with_memory_space_constraint(matrix, pltpu.HBM)
    starts = start_block[0, 0, 0].transpose(0, 2, 1)
    right = resid[0, 0, 0]
    order, columns = right.shape
    ncon, width = starts.shape[1:]
    counts = [lax.axis_size(axis) for axis in AXES]
    arrays = sum(face_arrays(count) for count in counts)
    coarse = FACES * ncon
    size = 2 * ncon
    half = width // 2
    lanes = size * BLOCKS * (BLOCKS + 1) // 2
    right_lanes = BLOCKS * columns
    uppers = FACES * (FACES - 1) // 2
    anywhere = pl.BlockSpec(memory_space=pl.ANY)
    main_memory = pl.BlockSpec(memory_space=pltpu.HBM)
    scalars = pl.BlockSpec(memory_space=pltpu.SMEM)
    early, late = (4, 5), (0, 1, 2, 3)
    faces = (early, late)
    planes = counts[2]

    def shape(*dims):
        return jax.ShapeDtypeStruct(dims, jnp.float32)

    def halves(count):
        return jax.ShapeDtypeStruct((count, 2, width, width), jnp.bfloat16)

    def params(mib):
        return pltpu.CompilerParams(vmem_limit_bytes=mib * MIB)

    def cost(us):
        return pl.CostEstimate(flops=us * 10**9, bytes_accessed=2**20, transcendentals=0)

    *packed, own = pl.pallas_call(
        functools.partial(pack_kernel, counts, width),
        out_shape=face_shapes(counts[0], (width + 8 + 2 * ncon, half))
        + face_shapes(counts[1], (width + 8 + 2 * ncon, half))
        + face_shapes(counts[2], (width + 8, half))
        + [shape(FACES, width, width)],
        in_specs=[main_memory, main_memory],
        out_specs=vmem_specs(arrays + 1),
        scratch_shapes=[
            pltpu.VMEM((4, ncon, width), jnp.float32),
            pltpu.SemaphoreType.DMA((FACES,)),
            pltpu.SemaphoreType.DMA,
        ],
        compiler_params=params(12),
    )(matrix, pltpu.with_memory_space_constraint(starts, pltpu.HBM))
    ends = [sum(face_arrays(count) for count in counts[:position]) for position in range(4)]
    got = {}
    for position in (2, 0, 1):
        got[position] = exchange(packed[ends[position] : ends[position + 1]], AXES[position])

    own_halves, upper_halves, flags = pl.pallas_call(
        functools.partial(halves_kernel, planes),
        out_shape=[halves(FACES), halves(uppers), shape(8, 128)],
        in_specs=[main_memory, scalars] + vmem_specs(1),
        out_specs=vmem_specs(3),
        scratch_shapes=[
            pltpu.VMEM((FACES - 1, width, order), jnp.float32),
            pltpu.SemaphoreType.DMA((FACES - 1,)),
        ],
        compiler_params=params(24),
        cost_estimate=cost(2),
    )(matrix, group_of, own)

    early_basis, early_partner, early_inverse = pl.pallas_call(
        functools.partial(early_kernel, AXES[2:3], early),
        out_shape=[shape(len(early), ncon, width)] + [halves(len(early))] * 2,
        in_specs=vmem_specs(len(got[2]) + 3),
        out_specs=vmem_specs(3),
        compiler_params=params(16),
        cost_estimate=cost(2),
    )(*got[2], own, own_halves, starts)

    payload, product, late_partner, late_inverse = pl.pallas_call(
        functools.partial(main_kernel, (AXES[0], AXES[1]), early, late),
        out_shape=[shape(size, lanes + right_lanes), shape(FACES, ncon, width)]
        + [halves(len(late))] * 2,
        in_specs=vmem_specs(len(got[0]) + len(got[1]) + 6),
        out_specs=vmem_specs(4),
        compiler_params=params(24),
        cost_estimate=cost(8),
    )(*got[0], *got[1], own, own_halves, upper_halves, starts, right, early_basis)

    partners = [early_partner, late_partner]
    inverses = [early_inverse, late_inverse]
    their_product = pl.pallas_call(
        functools.partial(theirs_kernel, faces, ncon),
        out_shape=shape(4, ncon, width),
        in_specs=vmem_specs(5 + len(got[0]) + len(got[1])),
        out_specs=vmem_specs(1)[0],
        compiler_params=params(16),
        cost_estimate=cost(2),
    )(own_halves, *got[0], *got[1], *partners, *inverses)

    def spread_of(token):
        return pl.pallas_call(
            functools.partial(spread_kernel, faces),
            out_shape=jax.ShapeDtypeStruct((4, width, 3 * size), jnp.bfloat16),
            in_specs=[anywhere] + vmem_specs(4),
            out_specs=vmem_specs(1)[0],
            compiler_params=params(16),
            cost_estimate=cost(2),
        )(token, their_product, product, *inverses)

    def solve(matrices, rights, unread):
        return pl.pallas_call(
            functools.partial(solve_kernel, size, len(matrices), columns),
            out_shape=shape(coarse, columns),
            in_specs=vmem_specs(2 * len(matrices)) + [anywhere] * len(unread),
            out_specs=vmem_specs(1)[0],
            compiler_params=params(12),
            cost_estimate=cost(7),
        )(*matrices, *rights, *unread)

    result = dict(
        out_shape=shape(order, columns),
        out_specs=main_memory,
        scratch_shapes=[
            pltpu.VMEM((order, columns), jnp.float32),
            pltpu.SemaphoreType.DMA((FACES,)),
        ],
        compiler_params=params(12),
        cost_estimate=cost(1),
    )
    groups = group_of.shape[0] // GROUP_SIZE
    if groups == 2 and counts[1] == 4 and planes == 2:
        core_swap, chip_x, chip_y = flipped("gy", 1), flipped("gy", 2), flipped("gz", 1)
        other = lax.ppermute(payload, "gy", core_swap)
        left, rest = pl.pallas_call(
            choose_kernel,
            out_shape=[shape(size, lanes), shape(size, right_lanes)],
            in_specs=vmem_specs(3),
            out_specs=vmem_specs(2),
            compiler_params=params(8),
        )(flags, payload, other)
        left_moved = lax.ppermute(left, "gy", chip_x)
        rest_moved = lax.ppermute(rest, "gz", chip_y)
        left_last, rest_last, *sent = pl.pallas_call(
            add_kernel,
            out_shape=[shape(size, lanes), shape(size, right_lanes)]
            + face_shapes(counts[2], (ncon, width)),
            in_specs=vmem_specs(5) + [anywhere],
            out_specs=vmem_specs(2 + face_arrays(counts[2])),
            compiler_params=params(8),
        )(left, left_moved, rest, rest_moved, product, their_product)
        left_other = lax.ppermute(left_last, "gz", chip_y)
        rest_other = lax.ppermute(rest_last, "gy", chip_x)
        theirs = exchange(sent, AXES[2])
        spread = spread_of(left_last)
        answer = solve([left_last, left_other], [rest_last, rest_other], [spread])
        there = lax.ppermute(answer, "gy", core_swap)
        *sent, mine = pl.pallas_call(
            functools.partial(rows_kernel, ncon),
            out_shape=face_shapes(counts[0], (ncon, columns)) + [shape(size, columns)],
            in_specs=vmem_specs(3),
            out_specs=vmem_specs(face_arrays(counts[0]) + 1),
            compiler_params=params(8),
        )(flags, answer, there)
        across = exchange(sent, AXES[0])
        correction = pl.pallas_call(
            functools.partial(last_near_kernel, faces),
            in_specs=vmem_specs(7 + len(theirs)),
            **result,
        )(flags, product, *inverses, spread, answer, there, *theirs)
    else:
        y, z = lax.axis_index("gy"), lax.axis_index("gz")
        member_of = group_of[y * planes + z]
        chosen = jnp.arange(groups, dtype=jnp.int32) == member_of
        total = lax.psum(jnp.where(chosen[:, None, None], payload[None], 0.0), ("gy", "gz"))
        total = lax.dynamic_index_in_dim(total, member_of, 0, keepdims=False)
        spread = spread_of(payload)
        answer = solve([total[:, :lanes]], [total[:, lanes:]], [])

        def from_near(faces_of, axis):
            even, odd = faces_of
            if lax.axis_size(axis) == 2:
                return exchange([jnp.stack([even, odd])], axis)
            upward = is_even(axis)
            return exchange([jnp.where(upward, even, odd), jnp.where(upward, odd, even)], axis)

        blocks = answer.reshape(FACES, ncon, columns)
        near = [
            *from_near(product[4:6], AXES[2]),
            *from_near(blocks[2:4], AXES[1]),
            *from_near(blocks[4:6], AXES[2]),
        ]
        mine = answer[:size]
        across = from_near(blocks[:2], AXES[0])
        correction = pl.pallas_call(
            functools.partial(last_plain_kernel, faces),
            in_specs=vmem_specs(5 + len(near)),
            **result,
        )(product, *inverses, spread, answer, *near)
    correction = pl.pallas_call(
        functools.partial(last_far_kernel, ncon),
        in_specs=vmem_specs(2 + len(across)) + [main_memory],
        input_output_aliases={2 + len(across): 0},
        **result,
    )(spread, mine, *across, correction)
    return correction[None, None, None]


def solution(mesh):
    in_specs = (
        P("gx", "gy", "gz", None, None),
        P("gx", "gy", "gz", None, None, None),
        P("gx", "gy", "gz", None, None),
        P(),
    )
    out_specs = P("gx", "gy", "gz", None, None)
    return jax.shard_map(
        per_device, mesh=mesh, in_specs=in_specs, out_specs=out_specs, check_vma=False
    )
```

```python
import functools

import jax
import jax.numpy as jnp
from jax import lax
from jax.experimental import pallas as pl
from jax.experimental.pallas import tpu as pltpu
from jax.sharding import PartitionSpec as P

NS_ITERS = 3
SUB_ITERS = 2
GROUP_SIZE = 4
FACES = 6
BLOCKS = FACES // 2
AXES = ("gx", "gy", "gz")
MIB = 1024 * 1024

precise = lax.Precision.HIGHEST


def dot(left, right, dims=((1,), (0,))):
    return lax.dot_general(
        left, right, (dims, ((), ())), precision=precise, preferred_element_type=jnp.float32
    )


def split(value):
    high = value.astype(jnp.bfloat16)
    return high, (value - high.astype(jnp.float32)).astype(jnp.bfloat16)


def wide(left, right):
    return lax.dot_general(
        jnp.concatenate([left[0], left[0], left[1]], axis=1),
        jnp.concatenate([right[0], right[1], right[0]], axis=0),
        (((1,), (0,)), ((), ())),
        preferred_element_type=jnp.float32,
    )


def stacked(value):
    return jnp.concatenate(split(value), axis=0)


def thin(rows, matrix):
    out = lax.dot_general(
        jnp.concatenate([rows, rows], axis=1),
        jnp.concatenate(matrix, axis=0),
        (((1,), (0,)), ((), ())),
        preferred_element_type=jnp.float32,
    )
    half = rows.shape[0] // 2
    return out[:half] + out[half:]


def triple(left, right, dims=((1,), (0,))):
    (left_high, left_low), (right_high, right_low) = split(left), split(right)
    total = None
    for one, other in ((left_high, right_high), (left_high, right_low), (left_low, right_high)):
        part = lax.dot_general(
            one, other, (dims, ((), ())), preferred_element_type=jnp.float32
        )
        total = part if total is None else total + part
    return total


def iota(shape, dim):
    return lax.broadcasted_iota(jnp.int32, shape, dim)


def flipped(axis, bit):
    return [(i, i ^ bit) for i in range(lax.axis_size(axis))]


def outer_pairs(axis):
    count = lax.axis_size(axis)
    return [(i, (i + 1 if i % 2 else i - 1) % count) for i in range(count)]


def face_arrays(count):
    return 1 if count == 2 else 2


def exchange(arrays, axis):
    if lax.axis_size(axis) == 2:
        return [lax.ppermute(arrays[0], axis, flipped(axis, 1))]
    return [
        lax.ppermute(arrays[0], axis, outer_pairs(axis)),
        lax.ppermute(arrays[1], axis, flipped(axis, 1)),
    ]


def is_even(axis):
    return lax.rem(lax.axis_index(axis), 2) == 0


def send(refs, axis, even, odd):
    if lax.axis_size(axis) == 2:
        refs[0][0] = even
        refs[0][1] = odd
    else:
        upward = is_even(axis)
        refs[0][...] = jnp.where(upward, even, odd)
        refs[1][...] = jnp.where(upward, odd, even)


def receive(refs, axis):
    if lax.axis_size(axis) == 2:
        return refs[0][1], refs[0][0]
    upward = is_even(axis)
    first, second = refs[0][...], refs[1][...]
    return jnp.where(upward, first, second), jnp.where(upward, second, first)


def face_shapes(count, shape):
    if count == 2:
        return [jax.ShapeDtypeStruct((2,) + shape, jnp.float32)]
    return [jax.ShapeDtypeStruct(shape, jnp.float32)] * 2


def vmem_specs(count):
    return [pl.BlockSpec(memory_space=pltpu.VMEM)] * count


def pack_kernel(counts, width, schur_ref, starts_ref, *refs):
    outs, blocks = refs[:-4], refs[-4]
    starts, sems, start_sem = refs[-3:]
    half = width // 2
    copies = []
    for f in range(FACES):
        place = pl.ds(f * width, width)
        copy = pltpu.make_async_copy(schur_ref.at[place, place], blocks.at[f], sems.at[f])
        copy.start()
        copies.append(copy)
    start_copy = pltpu.make_async_copy(starts_ref.at[pl.ds(0, 4)], starts, start_sem)
    start_copy.start()
    row, col = iota((half, half), 0), iota((half, half), 1)
    start_copy.wait()

    def pack(f):
        copies[f].wait()
        first = blocks[f, 0:half, 0:half]
        second = blocks[f, half:width, half:width]
        diag = jnp.sum(jnp.where(row == col, second, 0.0), axis=0, keepdims=True)
        mixed = jnp.where(row >= col, first, second)
        tail = jnp.broadcast_to(diag, (8, half))
        parts = [blocks[f, half:width, 0:half], mixed, tail]
        if f < 4:
            parts += [starts[f, :, :half], starts[f, :, half:]]
        return jnp.concatenate(parts, axis=0)

    done = 0
    for position, axis in enumerate(AXES):
        number = face_arrays(counts[position])
        send(outs[done : done + number], axis, pack(2 * position), pack(2 * position + 1))
        done += number


def unpack(packed):
    half = packed.shape[1]
    row, col = iota((half, half), 0), iota((half, half), 1)
    low = packed[0:half]
    mixed = packed[half : 2 * half]
    flip = mixed.T
    first = jnp.where(row >= col, mixed, flip)
    second = jnp.where(row < col, mixed, flip)
    second = jnp.where(row == col, packed[2 * half : 2 * half + 1], second)
    return jnp.concatenate(
        [jnp.concatenate([first, low.T], axis=1), jnp.concatenate([low, second], axis=1)], axis=0
    )


def unpack_starts(packed, ncon):
    half = packed.shape[1]
    rows = packed[2 * half + 8 :]
    return jnp.concatenate([rows[:ncon], rows[ncon:]], axis=1)


def factor_inverses(grams):
    size = grams[0].shape[0]
    strips, block, lanes = size // 8, 8, 128
    full = (block, lanes)
    beside = lanes // (2 * size)
    one = jnp.where(iota((size, size), 0) == iota((size, size), 1), 1.0, 0.0)
    states = []
    for first in range(0, len(grams), beside):
        parts = [part for gram in grams[first : first + beside] for part in (gram, one)]
        whole = jnp.concatenate(parts, axis=1)
        states.append([whole[8 * s : 8 * s + 8] for s in range(strips)])
    below = iota(full, 0)
    base = iota(full, 1) // (2 * size) * (2 * size)

    def column(rows, k):
        if beside == 1:
            return jnp.broadcast_to(rows[:, k : k + 1], full)
        return jnp.take_along_axis(rows, base + k, axis=1, mode="promise_in_bounds")

    def line_of(rows, line):
        return jnp.broadcast_to(rows[line : line + 1], full)

    roots = [[None] * strips for _ in states]
    for strip in range(strips):
        start = strip * block
        columns = [
            [[column(work[s], start + j) for s in range(strip, strips)] for j in range(block)]
            for work in states
        ]
        heads = [[column_set[0] for column_set in per_state] for per_state in columns]
        lowers = [work[strip] for work in states]
        solved = list(lowers)
        pivots = [jnp.ones(full, jnp.float32) for _ in states]
        scales = list(pivots)

        def eliminate(i, j, scale, pivot, side):
            cols = heads[i]
            factor = jnp.where(below != j, cols[j] * scale, 0.0)
            for later in range(j + 1, block):
                use = side if later == j + 1 and side is not None else line_of(cols[later], j)
                cols[later] = cols[later] - factor * use
            row = line_of(lowers[i], j)
            solved[i] = solved[i] - factor * row
            lowers[i] = lowers[i] - jnp.where(below > j, factor, 0.0) * row
            pivots[i] = jnp.where(below == j, pivot, pivots[i])
            scales[i] = jnp.where(below == j, scale, scales[i])

        for j in range(0, block, 2):
            for i in range(len(states)):
                cols = heads[i]
                corner, side = line_of(cols[j], j), line_of(cols[j], j + 1)
                last = line_of(cols[j + 1], j + 1)
                minor = corner * last - side * side
                scale = 1.0 / corner
                eliminate(i, j, scale, corner, side)
                eliminate(i, j + 1, corner * (1.0 / minor), minor * scale, None)
        for i, work in enumerate(states):
            work[strip] = lowers[i]
            roots[i][strip] = lax.rsqrt(pivots[i])
            if strip == strips - 1:
                continue
            answer = solved[i] * scales[i]
            rows = [line_of(answer, j) for j in range(block)]
            for s in range(strip + 1, strips):
                for j in range(block):
                    work[s] = work[s] - columns[i][j][s - strip] * rows[j]
    results = []
    for i, work in enumerate(states):
        scaled = jnp.concatenate([work[s] * roots[i][s] for s in range(strips)], axis=0)
        for m in range(beside):
            begin = (2 * m + 1) * size
            results.append(scaled[:, begin : begin + size])
    return results


def member(group_ref, planes, dy=0, dz=0):
    y, z = lax.axis_index("gy"), lax.axis_index("gz")
    rows = lax.axis_size("gy")
    return group_ref[lax.rem(y + dy + rows, rows) * planes + lax.rem(z + dz + planes, planes)]


def store(ref, f, value):
    ref[f, 0], ref[f, 1] = split(value)


def load(ref, f):
    return ref[f, 0], ref[f, 1]


def upper_index(f, g):
    return sum(FACES - 1 - i for i in range(f)) + g - f - 1


def halves_kernel(planes, schur_ref, group_ref, own_ref, own_out, upper_out, flag_out, *scratch):
    upper_ref, sems = scratch
    width = own_ref.shape[1]
    strips = []
    for f in range(FACES - 1):
        rest = (FACES - 1 - f) * width
        copy = pltpu.make_async_copy(
            schur_ref.at[pl.ds(f * width, width), pl.ds((f + 1) * width, rest)],
            upper_ref.at[f, :, pl.ds((f + 1) * width, rest)],
            sems.at[f],
        )
        copy.start()
        strips.append(copy)
    core = lax.rem(lax.axis_index("gy"), 2)
    near = [(0, 0), (1 - 2 * core, 0), (-1, 0), (1, 0), (0, -1), (0, 1)]
    row = iota(flag_out.shape, 0)
    flags = jnp.zeros(flag_out.shape, jnp.float32)
    for i, (dy, dz) in enumerate(near):
        hit = member(group_ref, planes, dy, dz) == core
        flags = jnp.where(row == i, jnp.where(hit, 1.0, 0.0), flags)
    flag_out[...] = flags
    for f in range(FACES):
        store(own_out, f, own_ref[f])
    for f in range(FACES - 1):
        strips[f].wait()
        for g in range(f + 1, FACES):
            store(upper_out, upper_index(f, g), upper_ref[f, :, g * width : (g + 1) * width])


def inverses_of(packed, owns, partner_ref):
    width = owns[0].shape[1]
    half = width // 2
    eye = iota((half, half), 0) == iota((half, half), 1)
    whole_eye = iota((width, width), 0) == iota((width, width), 1)
    powers, sums, downs = [], [], []
    for f in range(len(packed)):
        partner = unpack(packed[f])
        store(partner_ref, f, partner)
        total = owns[f] + partner
        across, down = [], []
        for start in (0, half):
            block = total[start : start + half, start : start + half]
            diagonal = jnp.where(eye, block, 0.0)
            across.append(1.0 / jnp.sum(diagonal, axis=0, keepdims=True))
            down.append(1.0 / jnp.sum(diagonal, axis=1, keepdims=True))
        downs.append(jnp.concatenate(down, axis=0))
        power = jnp.where(whole_eye, 0.0, -total * jnp.concatenate(across, axis=1))
        powers.append(split(power))
        sums.append(jnp.where(whole_eye, 1.0, power))
    for step in range(1, NS_ITERS):
        powers = [split(wide(power, power)) for power in powers]
        sums = [total + wide(split(total), power) for total, power in zip(sums, powers)]
    return [down * total for down, total in zip(downs, sums)]


def unit_rows(basis):
    return [b * lax.rsqrt(jnp.sum(b * b, axis=1, keepdims=True)) for b in basis]


def sweep_basis(before, inverse, after, basis):
    for matrices in (before, inverse, after):
        basis = [thin(stacked(b), matrix) for b, matrix in zip(basis, matrices)]
    return unit_rows(basis)


def early_kernel(axes, faces, *refs):
    arrays = len(refs) - 6
    inputs = refs[:arrays]
    own_ref, halves_ref, starts_ref, basis_out, partner_out, inverse_out = refs[arrays:]
    count = len(faces)
    packed = []
    done = 0
    for axis in axes:
        number = face_arrays(lax.axis_size(axis))
        packed += receive(inputs[done : done + number], axis)
        done += number
    inverses = inverses_of(packed, [own_ref[f] for f in faces], partner_out)
    for i in range(count):
        store(inverse_out, i, inverses[i])
    basis = [starts_ref[f] for f in faces]
    matrices = [
        [load(partner_out, i) for i in range(count)],
        [load(inverse_out, i) for i in range(count)],
        [load(halves_ref, f) for f in faces],
    ]
    for sweep in range(SUB_ITERS):
        basis = sweep_basis(*matrices, basis)
    for i in range(count):
        basis_out[i] = basis[i]


def main_kernel(axes, early, late, *refs):
    arrays = len(refs) - 10
    inputs = refs[:arrays]
    own_ref, halves_ref, upper_ref, starts_ref, resid_ref, early_basis = refs[arrays : arrays + 6]
    payload_ref, product_ref, partner_out, inverse_out = refs[arrays + 6 :]
    ncon, width = starts_ref.shape[1:]
    columns = resid_ref.shape[1]
    sides = {}
    rights = {}
    grams = {}
    vectors = {}
    count = len(late)

    def project(f, basis):
        vectors[f] = basis
        rows = stacked(basis)
        grams[f] = dot(basis, basis, ((1,), (1,)))
        side = {f: thin(rows, load(halves_ref, f))}
        for g in range(f + 1, FACES):
            side[g] = thin(rows, load(upper_ref, upper_index(f, g)))
        sides[f] = side
        rights[f] = thin(rows, split(resid_ref[f * width : (f + 1) * width]))

    packed = []
    done = 0
    for axis in axes:
        number = face_arrays(lax.axis_size(axis))
        packed += receive(inputs[done : done + number], axis)
        done += number
    inverses = inverses_of(packed, [own_ref[f] for f in late], partner_out)
    pending = [(f, early_basis[i]) for i, f in enumerate(early)]
    for i in range(count):
        store(inverse_out, i, inverses[i])
    basis = [starts_ref[f] for f in late]
    matrices = [
        [load(partner_out, i) for i in range(count)],
        [load(inverse_out, i) for i in range(count)],
        [load(halves_ref, f) for f in late],
    ]
    for sweep in range(SUB_ITERS):
        basis = sweep_basis(*matrices, basis)
        if pending:
            project(*pending.pop(0))
    for item in pending:
        project(*item)
    for i, f in enumerate(late):
        project(f, basis[i])
    factors = factor_inverses([grams[f] for f in range(FACES)])
    blocks = []
    for g in range(FACES):
        tall = jnp.concatenate([sides[f][g] for f in range(g + 1)], axis=0)
        blocks.append(triple(triple(tall, vectors[g], ((1,), (1,))), factors[g], ((1,), (1,))))
    even, odd, right = [], [], []
    lows = None
    for f in range(FACES):
        product_ref[f] = triple(factors[f], sides[f][f])
        line = [blocks[g][f * ncon : (f + 1) * ncon] for g in range(f, FACES)]
        line = triple(factors[f], jnp.concatenate([rights[f]] + line, axis=1))
        right.append(line[:, :columns])
        line = line[:, columns:]
        if f % 2 == 0:
            even.append(line)
            lows = line[:, ncon : 2 * ncon].T
        else:
            odd += [lows, line]
    payload_ref[...] = jnp.concatenate(
        [
            jnp.concatenate(even + right[0::2], axis=1),
            jnp.concatenate(odd + right[1::2], axis=1),
        ],
        axis=0,
    )


def find(faces, refs, f):
    for group, ref in zip(faces, refs):
        if f in group:
            return load(ref, list(group).index(f))


def theirs_kernel(faces, ncon, own_ref, *refs):
    inputs, partner_refs, inverse_refs = refs[:-5], refs[-5:-3], refs[-3:-1]
    product_out = refs[-1]
    basis = []
    done = 0
    for axis in AXES[:2]:
        number = face_arrays(lax.axis_size(axis))
        packed = receive(inputs[done : done + number], axis)
        basis += [unpack_starts(part, ncon) for part in packed]
        done += number
    count = len(basis)
    matrices = [
        [load(own_ref, f) for f in range(count)],
        [find(faces, inverse_refs, f) for f in range(count)],
        [find(faces, partner_refs, f) for f in range(count)],
    ]
    for sweep in range(SUB_ITERS):
        basis = sweep_basis(*matrices, basis)
    factors = factor_inverses([dot(b, b, ((1,), (1,))) for b in basis])
    for f in range(count):
        product_out[f] = triple(factors[f], thin(stacked(basis[f]), matrices[2][f]))


def spread_kernel(faces, unread, theirs_ref, product_ref, *refs):
    inverse_refs, out_ref = refs[:2], refs[2]
    for f in range(theirs_ref.shape[0]):
        both = jnp.concatenate([product_ref[f], theirs_ref[f]], axis=0)
        high, low = split(thin(stacked(both), find(faces, inverse_refs, f)).T)
        out_ref[f] = jnp.concatenate([high, high, low], axis=1)


def choose_kernel(flag_ref, here_ref, there_ref, matrix_ref, right_ref):
    mine = flag_ref[0:1, 0:1] > 0.5
    other = flag_ref[1:2, 0:1] > 0.5
    total = jnp.where(mine, here_ref[...], 0.0) + jnp.where(other, there_ref[...], 0.0)
    lanes = matrix_ref.shape[1]
    matrix_ref[...] = total[:, :lanes]
    right_ref[...] = total[:, lanes:]


def add_kernel(first_ref, second_ref, third_ref, fourth_ref, product_ref, unread, *refs):
    matrix_ref, right_ref, *sent = refs
    matrix_ref[...] = first_ref[...] + second_ref[...]
    right_ref[...] = third_ref[...] + fourth_ref[...]
    send(sent, AXES[2], product_ref[4], product_ref[5])


def solve_kernel(size, terms, columns, *refs):
    lanes = size * BLOCKS * (BLOCKS + 1) // 2
    matrix, right = refs[0][:, :lanes], refs[terms][...]
    for term in range(1, terms):
        matrix = matrix + refs[term][:, :lanes]
        right = right + refs[terms + term][...]
    answer_ref = refs[-1]
    lines = []
    offset = 0
    for b in range(BLOCKS):
        lines.append(matrix[:, offset : offset + (BLOCKS - b) * size])
        offset += (BLOCKS - b) * size
    eye = iota((size, size), 0) == iota((size, size), 1)
    downs, acrosses = [], []
    for b in range(BLOCKS):
        diagonal = jnp.where(eye, lines[b][:, :size], 0.0)
        downs.append(lax.rsqrt(jnp.sum(diagonal, axis=1, keepdims=True)))
        acrosses.append(lax.rsqrt(jnp.sum(diagonal, axis=0, keepdims=True)))
    blocks = {}
    rights = []
    for b in range(BLOCKS):
        for c in range(b, BLOCKS):
            block = lines[b][:, (c - b) * size : (c - b + 1) * size]
            blocks[b, c] = downs[b] * block * acrosses[c]
            if c > b:
                blocks[c, b] = blocks[b, c].T
        rights.append(downs[b] * right[:, b * columns : (b + 1) * columns])
    for b in range(BLOCKS):
        (inverse,) = factor_inverses([blocks[b, b]])
        later = range(b + 1, BLOCKS)
        row = triple(inverse, jnp.concatenate([rights[b]] + [blocks[b, c] for c in later], axis=1))
        if later:
            column = jnp.concatenate([blocks[c, b] for c in later], axis=0)
            change = triple(triple(column, inverse, ((1,), (1,))), row)
        for i, c in enumerate(later):
            part = change[i * size : (i + 1) * size]
            rights[c] = rights[c] - part[:, :columns]
            for j, d in enumerate(later):
                start = columns + j * size
                blocks[c, d] = blocks[c, d] - part[:, start : start + size]
        row = triple(inverse, row, ((0,), (0,)))
        rights[b] = row[:, :columns]
        for c in later:
            blocks[b, c] = row[:, columns + (c - b - 1) * size : columns + (c - b) * size]
        for i in range(b):
            for c in later:
                blocks[i, c] = blocks[i, c] - triple(blocks[i, b], blocks[b, c])
            rights[i] = rights[i] - triple(blocks[i, b], rights[b])
    answer = [downs[b] * rights[b] for b in range(BLOCKS)]
    answer_ref[...] = jnp.concatenate(answer, axis=0)


def rows_kernel(ncon, flag_ref, here_ref, there_ref, *refs):
    hit = flag_ref[0:1, 0:1] > 0.5
    rows = jnp.where(hit, here_ref[: 2 * ncon], there_ref[: 2 * ncon])
    refs[-1][...] = rows
    send(refs[:-1], AXES[0], rows[:ncon], rows[ncon:])


def last_product(spread, mine, theirs):
    high, low = split(jnp.concatenate([mine, theirs], axis=0))
    return lax.dot_general(
        spread,
        jnp.concatenate([high, low, high], axis=0),
        (((1,), (0,)), ((), ())),
        preferred_element_type=jnp.float32,
    )


def through(inverse, mine, theirs, my_answer, their_answer):
    high, low = split(jnp.concatenate([mine, theirs], axis=0).T)
    spread = jnp.concatenate([high, high, low], axis=1)
    return wide(inverse, split(last_product(spread, my_answer, their_answer)))


def last_faces(values, width, out_ref, result, sems):
    copies = []
    for f, value in values.items():
        place = pl.ds(f * width, width)
        result[f * width : (f + 1) * width] = value()
        copy = pltpu.make_async_copy(result.at[place], out_ref.at[place], sems.at[f])
        copy.start()
        copies.append(copy)
    for copy in copies:
        copy.wait()


def last_plain_kernel(faces, product_ref, early_inverse, late_inverse, *refs):
    spread_ref, answer_ref, *inputs = refs[:-3]
    ncon, width = product_ref.shape[1:]
    number = face_arrays(lax.axis_size(AXES[2]))
    theirs = receive(inputs[:number], AXES[2])
    near = receive(inputs[number:-number], AXES[1]) + receive(inputs[-number:], AXES[2])
    values = {}
    for f in range(2, FACES):
        mine = answer_ref[f * ncon : (f + 1) * ncon]
        if f < 4:
            values[f] = functools.partial(last_product, spread_ref[f], mine, near[f - 2])
        else:
            values[f] = functools.partial(
                through,
                find(faces, (early_inverse, late_inverse), f),
                product_ref[f],
                theirs[f - 4],
                mine,
                near[f - 2],
            )
    last_faces(values, width, *refs[-3:])


def last_near_kernel(faces, flag_ref, product_ref, early_inverse, late_inverse, *refs):
    spread_ref, here_answer, there_answer = refs[:3]
    theirs = receive(refs[3:-3], AXES[2])
    ncon, width = product_ref.shape[1:]

    def answer(flag, f):
        place = slice(f * ncon, (f + 1) * ncon)
        hit = flag_ref[flag : flag + 1, 0:1] > 0.5
        return jnp.where(hit, here_answer[place], there_answer[place])

    values = {}
    for f in (2, 3):
        values[f] = functools.partial(
            last_product, spread_ref[f], answer(0, f), answer(f, f ^ 1)
        )
    for f in (4, 5):
        values[f] = functools.partial(
            through,
            find(faces, (early_inverse, late_inverse), f),
            product_ref[f],
            theirs[f - 4],
            answer(0, f),
            answer(f, f ^ 1),
        )
    last_faces(values, width, *refs[-3:])


def last_far_kernel(ncon, spread_ref, rows_ref, *refs):
    theirs = receive(refs[:-4], AXES[0])
    values = {}
    for f in range(2):
        mine = rows_ref[f * ncon : (f + 1) * ncon]
        values[f] = functools.partial(last_product, spread_ref[f], mine, theirs[f])
    last_faces(values, spread_ref.shape[1], *refs[-3:])


def per_device(schur, start_block, resid, group_of):
    matrix = schur[0, 0, 0]
    matrix = pltpu.with_memory_space_constraint(matrix, pltpu.HBM)
    starts = start_block[0, 0, 0].transpose(0, 2, 1)
    right = resid[0, 0, 0]
    order, columns = right.shape
    ncon, width = starts.shape[1:]
    counts = [lax.axis_size(axis) for axis in AXES]
    arrays = sum(face_arrays(count) for count in counts)
    coarse = FACES * ncon
    size = 2 * ncon
    half = width // 2
    lanes = size * BLOCKS * (BLOCKS + 1) // 2
    right_lanes = BLOCKS * columns
    uppers = FACES * (FACES - 1) // 2
    anywhere = pl.BlockSpec(memory_space=pl.ANY)
    main_memory = pl.BlockSpec(memory_space=pltpu.HBM)
    scalars = pl.BlockSpec(memory_space=pltpu.SMEM)
    early, late = (4, 5), (0, 1, 2, 3)
    faces = (early, late)
    planes = counts[2]

    def shape(*dims):
        return jax.ShapeDtypeStruct(dims, jnp.float32)

    def halves(count):
        return jax.ShapeDtypeStruct((count, 2, width, width), jnp.bfloat16)

    def params(mib):
        return pltpu.CompilerParams(vmem_limit_bytes=mib * MIB)

    def cost(us):
        return pl.CostEstimate(flops=us * 10**9, bytes_accessed=2**20, transcendentals=0)

    *packed, own = pl.pallas_call(
        functools.partial(pack_kernel, counts, width),
        out_shape=face_shapes(counts[0], (width + 8 + 2 * ncon, half))
        + face_shapes(counts[1], (width + 8 + 2 * ncon, half))
        + face_shapes(counts[2], (width + 8, half))
        + [shape(FACES, width, width)],
        in_specs=[main_memory, main_memory],
        out_specs=vmem_specs(arrays + 1),
        scratch_shapes=[
            pltpu.VMEM((4, ncon, width), jnp.float32),
            pltpu.SemaphoreType.DMA((FACES,)),
            pltpu.SemaphoreType.DMA,
        ],
        compiler_params=params(12),
    )(matrix, pltpu.with_memory_space_constraint(starts, pltpu.HBM))
    ends = [sum(face_arrays(count) for count in counts[:position]) for position in range(4)]
    got = {}
    for position in (2, 0, 1):
        got[position] = exchange(packed[ends[position] : ends[position + 1]], AXES[position])

    own_halves, upper_halves, flags = pl.pallas_call(
        functools.partial(halves_kernel, planes),
        out_shape=[halves(FACES), halves(uppers), shape(8, 128)],
        in_specs=[main_memory, scalars] + vmem_specs(1),
        out_specs=vmem_specs(3),
        scratch_shapes=[
            pltpu.VMEM((FACES - 1, width, order), jnp.float32),
            pltpu.SemaphoreType.DMA((FACES - 1,)),
        ],
        compiler_params=params(24),
        cost_estimate=cost(2),
    )(matrix, group_of, own)

    early_basis, early_partner, early_inverse = pl.pallas_call(
        functools.partial(early_kernel, AXES[2:3], early),
        out_shape=[shape(len(early), ncon, width)] + [halves(len(early))] * 2,
        in_specs=vmem_specs(len(got[2]) + 3),
        out_specs=vmem_specs(3),
        compiler_params=params(16),
        cost_estimate=cost(2),
    )(*got[2], own, own_halves, starts)

    payload, product, late_partner, late_inverse = pl.pallas_call(
        functools.partial(main_kernel, (AXES[0], AXES[1]), early, late),
        out_shape=[shape(size, lanes + right_lanes), shape(FACES, ncon, width)]
        + [halves(len(late))] * 2,
        in_specs=vmem_specs(len(got[0]) + len(got[1]) + 6),
        out_specs=vmem_specs(4),
        compiler_params=params(24),
        cost_estimate=cost(8),
    )(*got[0], *got[1], own, own_halves, upper_halves, starts, right, early_basis)

    partners = [early_partner, late_partner]
    inverses = [early_inverse, late_inverse]
    their_product = pl.pallas_call(
        functools.partial(theirs_kernel, faces, ncon),
        out_shape=shape(4, ncon, width),
        in_specs=vmem_specs(5 + len(got[0]) + len(got[1])),
        out_specs=vmem_specs(1)[0],
        compiler_params=params(16),
        cost_estimate=cost(2),
    )(own_halves, *got[0], *got[1], *partners, *inverses)

    def spread_of(token):
        return pl.pallas_call(
            functools.partial(spread_kernel, faces),
            out_shape=jax.ShapeDtypeStruct((4, width, 3 * size), jnp.bfloat16),
            in_specs=[anywhere] + vmem_specs(4),
            out_specs=vmem_specs(1)[0],
            compiler_params=params(16),
            cost_estimate=cost(2),
        )(token, their_product, product, *inverses)

    def solve(matrices, rights, unread):
        return pl.pallas_call(
            functools.partial(solve_kernel, size, len(matrices), columns),
            out_shape=shape(coarse, columns),
            in_specs=vmem_specs(2 * len(matrices)) + [anywhere] * len(unread),
            out_specs=vmem_specs(1)[0],
            compiler_params=params(12),
            cost_estimate=cost(7),
        )(*matrices, *rights, *unread)

    result = dict(
        out_shape=shape(order, columns),
        out_specs=main_memory,
        scratch_shapes=[
            pltpu.VMEM((order, columns), jnp.float32),
            pltpu.SemaphoreType.DMA((FACES,)),
        ],
        compiler_params=params(12),
        cost_estimate=cost(1),
    )
    groups = group_of.shape[0] // GROUP_SIZE
    if groups == 2 and counts[1] == 4 and planes == 2:
        core_swap, chip_x, chip_y = flipped("gy", 1), flipped("gy", 2), flipped("gz", 1)
        other = lax.ppermute(payload, "gy", core_swap)
        left, rest = pl.pallas_call(
            choose_kernel,
            out_shape=[shape(size, lanes), shape(size, right_lanes)],
            in_specs=vmem_specs(3),
            out_specs=vmem_specs(2),
            compiler_params=params(8),
        )(flags, payload, other)
        left_moved = lax.ppermute(left, "gy", chip_x)
        rest_moved = lax.ppermute(rest, "gz", chip_y)
        left_last, rest_last, *sent = pl.pallas_call(
            add_kernel,
            out_shape=[shape(size, lanes), shape(size, right_lanes)]
            + face_shapes(counts[2], (ncon, width)),
            in_specs=vmem_specs(5) + [anywhere],
            out_specs=vmem_specs(2 + face_arrays(counts[2])),
            compiler_params=params(8),
        )(left, left_moved, rest, rest_moved, product, their_product)
        left_other = lax.ppermute(left_last, "gz", chip_y)
        rest_other = lax.ppermute(rest_last, "gy", chip_x)
        theirs = exchange(sent, AXES[2])
        spread = spread_of(left_last)
        answer = solve([left_last, left_other], [rest_last, rest_other], [spread])
        there = lax.ppermute(answer, "gy", core_swap)
        *sent, mine = pl.pallas_call(
            functools.partial(rows_kernel, ncon),
            out_shape=face_shapes(counts[0], (ncon, columns)) + [shape(size, columns)],
            in_specs=vmem_specs(3),
            out_specs=vmem_specs(face_arrays(counts[0]) + 1),
            compiler_params=params(8),
        )(flags, answer, there)
        across = exchange(sent, AXES[0])
        correction = pl.pallas_call(
            functools.partial(last_near_kernel, faces),
            in_specs=vmem_specs(7 + len(theirs)),
            **result,
        )(flags, product, *inverses, spread, answer, there, *theirs)
    else:
        y, z = lax.axis_index("gy"), lax.axis_index("gz")
        member_of = group_of[y * planes + z]
        chosen = jnp.arange(groups, dtype=jnp.int32) == member_of
        total = lax.psum(jnp.where(chosen[:, None, None], payload[None], 0.0), ("gy", "gz"))
        total = lax.dynamic_index_in_dim(total, member_of, 0, keepdims=False)
        spread = spread_of(payload)
        answer = solve([total[:, :lanes]], [total[:, lanes:]], [])

        def from_near(faces_of, axis):
            even, odd = faces_of
            if lax.axis_size(axis) == 2:
                return exchange([jnp.stack([even, odd])], axis)
            upward = is_even(axis)
            return exchange([jnp.where(upward, even, odd), jnp.where(upward, odd, even)], axis)

        blocks = answer.reshape(FACES, ncon, columns)
        near = [
            *from_near(product[4:6], AXES[2]),
            *from_near(blocks[2:4], AXES[1]),
            *from_near(blocks[4:6], AXES[2]),
        ]
        mine = answer[:size]
        across = from_near(blocks[:2], AXES[0])
        correction = pl.pallas_call(
            functools.partial(last_plain_kernel, faces),
            in_specs=vmem_specs(5 + len(near)),
            **result,
        )(product, *inverses, spread, answer, *near)
    correction = pl.pallas_call(
        functools.partial(last_far_kernel, ncon),
        in_specs=vmem_specs(2 + len(across)) + [main_memory],
        input_output_aliases={2 + len(across): 0},
        **result,
    )(spread, mine, *across, correction)
    return correction[None, None, None]


def solution(mesh):
    in_specs = (
        P("gx", "gy", "gz", None, None),
        P("gx", "gy", "gz", None, None, None),
        P("gx", "gy", "gz", None, None),
        P(),
    )
    out_specs = P("gx", "gy", "gz", None, None)
    return jax.shard_map(
        per_device, mesh=mesh, in_specs=in_specs, out_specs=out_specs, check_vma=False
    )
```

```python
import functools

import jax
import jax.numpy as jnp
from jax import lax
from jax.experimental import pallas as pl
from jax.experimental.pallas import tpu as pltpu
from jax.sharding import PartitionSpec as P

NS_ITERS = 3
SUB_ITERS = 2
GROUP_SIZE = 4
FACES = 6
BLOCKS = FACES // 2
AXES = ("gx", "gy", "gz")
MIB = 1024 * 1024

precise = lax.Precision.HIGHEST


def dot(left, right, dims=((1,), (0,))):
    return lax.dot_general(
        left, right, (dims, ((), ())), precision=precise, preferred_element_type=jnp.float32
    )


def split(value):
    high = value.astype(jnp.bfloat16)
    return high, (value - high.astype(jnp.float32)).astype(jnp.bfloat16)


def wide(left, right):
    return lax.dot_general(
        jnp.concatenate([left[0], left[0], left[1]], axis=1),
        jnp.concatenate([right[0], right[1], right[0]], axis=0),
        (((1,), (0,)), ((), ())),
        preferred_element_type=jnp.float32,
    )


def stacked(value):
    return jnp.concatenate(split(value), axis=0)


def thin(rows, matrix):
    out = lax.dot_general(
        jnp.concatenate([rows, rows], axis=1),
        jnp.concatenate(matrix, axis=0),
        (((1,), (0,)), ((), ())),
        preferred_element_type=jnp.float32,
    )
    half = rows.shape[0] // 2
    return out[:half] + out[half:]


def triple(left, right, dims=((1,), (0,))):
    (left_high, left_low), (right_high, right_low) = split(left), split(right)
    total = None
    for one, other in ((left_high, right_high), (left_high, right_low), (left_low, right_high)):
        part = lax.dot_general(
            one, other, (dims, ((), ())), preferred_element_type=jnp.float32
        )
        total = part if total is None else total + part
    return total


def iota(shape, dim):
    return lax.broadcasted_iota(jnp.int32, shape, dim)


def flipped(axis, bit):
    return [(i, i ^ bit) for i in range(lax.axis_size(axis))]


def outer_pairs(axis):
    count = lax.axis_size(axis)
    return [(i, (i + 1 if i % 2 else i - 1) % count) for i in range(count)]


def face_arrays(count):
    return 1 if count == 2 else 2


def exchange(arrays, axis):
    if lax.axis_size(axis) == 2:
        return [lax.ppermute(arrays[0], axis, flipped(axis, 1))]
    return [
        lax.ppermute(arrays[0], axis, outer_pairs(axis)),
        lax.ppermute(arrays[1], axis, flipped(axis, 1)),
    ]


def is_even(axis):
    return lax.rem(lax.axis_index(axis), 2) == 0


def send(refs, axis, even, odd):
    if lax.axis_size(axis) == 2:
        refs[0][0] = even
        refs[0][1] = odd
    else:
        upward = is_even(axis)
        refs[0][...] = jnp.where(upward, even, odd)
        refs[1][...] = jnp.where(upward, odd, even)


def receive(refs, axis):
    if lax.axis_size(axis) == 2:
        return refs[0][1], refs[0][0]
    upward = is_even(axis)
    first, second = refs[0][...], refs[1][...]
    return jnp.where(upward, first, second), jnp.where(upward, second, first)


def face_shapes(count, shape):
    if count == 2:
        return [jax.ShapeDtypeStruct((2,) + shape, jnp.float32)]
    return [jax.ShapeDtypeStruct(shape, jnp.float32)] * 2


def vmem_specs(count):
    return [pl.BlockSpec(memory_space=pltpu.VMEM)] * count


def pack_kernel(counts, width, schur_ref, starts_ref, *refs):
    outs, blocks = refs[:-4], refs[-4]
    starts, sems, start_sem = refs[-3:]
    half = width // 2
    copies = []
    for f in range(FACES):
        place = pl.ds(f * width, width)
        copy = pltpu.make_async_copy(schur_ref.at[place, place], blocks.at[f], sems.at[f])
        copy.start()
        copies.append(copy)
    start_copy = pltpu.make_async_copy(starts_ref.at[pl.ds(0, 4)], starts, start_sem)
    start_copy.start()
    row, col = iota((half, half), 0), iota((half, half), 1)
    start_copy.wait()

    def pack(f):
        copies[f].wait()
        first = blocks[f, 0:half, 0:half]
        second = blocks[f, half:width, half:width]
        diag = jnp.sum(jnp.where(row == col, second, 0.0), axis=0, keepdims=True)
        mixed = jnp.where(row >= col, first, second)
        tail = jnp.broadcast_to(diag, (8, half))
        parts = [blocks[f, half:width, 0:half], mixed, tail]
        if f < 4:
            parts += [starts[f, :, :half], starts[f, :, half:]]
        return jnp.concatenate(parts, axis=0)

    done = 0
    for position, axis in enumerate(AXES):
        number = face_arrays(counts[position])
        send(outs[done : done + number], axis, pack(2 * position), pack(2 * position + 1))
        done += number


def unpack(packed):
    half = packed.shape[1]
    row, col = iota((half, half), 0), iota((half, half), 1)
    low = packed[0:half]
    mixed = packed[half : 2 * half]
    flip = mixed.T
    first = jnp.where(row >= col, mixed, flip)
    second = jnp.where(row < col, mixed, flip)
    second = jnp.where(row == col, packed[2 * half : 2 * half + 1], second)
    return jnp.concatenate(
        [jnp.concatenate([first, low.T], axis=1), jnp.concatenate([low, second], axis=1)], axis=0
    )


def unpack_starts(packed, ncon):
    half = packed.shape[1]
    rows = packed[2 * half + 8 :]
    return jnp.concatenate([rows[:ncon], rows[ncon:]], axis=1)


def factor_inverses(grams):
    size = grams[0].shape[0]
    strips, block, lanes = size // 8, 8, 128
    full = (block, lanes)
    beside = lanes // (2 * size)
    one = jnp.where(iota((size, size), 0) == iota((size, size), 1), 1.0, 0.0)
    states = []
    for first in range(0, len(grams), beside):
        parts = [part for gram in grams[first : first + beside] for part in (gram, one)]
        whole = jnp.concatenate(parts, axis=1)
        states.append([whole[8 * s : 8 * s + 8] for s in range(strips)])
    below = iota(full, 0)
    base = iota(full, 1) // (2 * size) * (2 * size)

    def column(rows, k):
        if beside == 1:
            return jnp.broadcast_to(rows[:, k : k + 1], full)
        return jnp.take_along_axis(rows, base + k, axis=1, mode="promise_in_bounds")

    def line_of(rows, line):
        return jnp.broadcast_to(rows[line : line + 1], full)

    roots = [[None] * strips for _ in states]
    for strip in range(strips):
        start = strip * block
        columns = [
            [[column(work[s], start + j) for s in range(strip, strips)] for j in range(block)]
            for work in states
        ]
        heads = [[column_set[0] for column_set in per_state] for per_state in columns]
        lowers = [work[strip] for work in states]
        solved = list(lowers)
        pivots = [jnp.ones(full, jnp.float32) for _ in states]
        scales = list(pivots)

        def eliminate(i, j, scale, pivot, side):
            cols = heads[i]
            factor = jnp.where(below != j, cols[j] * scale, 0.0)
            for later in range(j + 1, block):
                use = side if later == j + 1 and side is not None else line_of(cols[later], j)
                cols[later] = cols[later] - factor * use
            row = line_of(lowers[i], j)
            solved[i] = solved[i] - factor * row
            lowers[i] = lowers[i] - jnp.where(below > j, factor, 0.0) * row
            pivots[i] = jnp.where(below == j, pivot, pivots[i])
            scales[i] = jnp.where(below == j, scale, scales[i])

        for j in range(0, block, 2):
            for i in range(len(states)):
                cols = heads[i]
                corner, side = line_of(cols[j], j), line_of(cols[j], j + 1)
                last = line_of(cols[j + 1], j + 1)
                minor = corner * last - side * side
                scale = 1.0 / corner
                eliminate(i, j, scale, corner, side)
                eliminate(i, j + 1, corner * (1.0 / minor), minor * scale, None)
        for i, work in enumerate(states):
            work[strip] = lowers[i]
            roots[i][strip] = lax.rsqrt(pivots[i])
            if strip == strips - 1:
                continue
            answer = solved[i] * scales[i]
            rows = [line_of(answer, j) for j in range(block)]
            for s in range(strip + 1, strips):
                for j in range(block):
                    work[s] = work[s] - columns[i][j][s - strip] * rows[j]
    results = []
    for i, work in enumerate(states):
        scaled = jnp.concatenate([work[s] * roots[i][s] for s in range(strips)], axis=0)
        for m in range(beside):
            begin = (2 * m + 1) * size
            results.append(scaled[:, begin : begin + size])
    return results


def factor_inverse(gram):
    size = gram.shape[0]
    strips, block, lanes = size // 8, 8, 128
    full = (block, lanes)
    parts = [gram, jnp.where(iota((size, size), 0) == iota((size, size), 1), 1.0, 0.0)]
    if 2 * size < lanes:
        parts.append(jnp.zeros((size, lanes - 2 * size), jnp.float32))
    whole = jnp.concatenate(parts, axis=1)
    work = [whole[8 * s : 8 * s + 8] for s in range(strips)]
    below = iota(full, 0)

    def line_of(rows, line):
        return jnp.broadcast_to(rows[line : line + 1], full)

    for strip in range(strips):
        start = strip * block
        active = range(strip, strips)
        cols = [
            {s: jnp.broadcast_to(work[s][:, start + j : start + j + 1], full) for s in active}
            for j in range(block)
        ]
        factors = []

        def eliminate(j, scale, side):
            factor = {s: cols[j][s] * scale for s in active}
            factor[strip] = jnp.where(below > j, factor[strip], 0.0)
            for later in range(j + 1, block):
                use = side if later == j + 1 and side is not None else None
                head = line_of(cols[later][strip], j) if use is None else use
                for s in active:
                    cols[later][s] = cols[later][s] - factor[s] * head
            factors.append(factor)

        for j in range(0, block, 2):
            corner = line_of(cols[j][strip], j)
            side = line_of(cols[j][strip], j + 1)
            last = line_of(cols[j + 1][strip], j + 1)
            inverse = 1.0 / (corner * last - side * side)
            eliminate(j, 1.0 / corner, side)
            eliminate(j + 1, corner * inverse, None)
        for j in range(block):
            row = line_of(work[strip], j)
            for s in active:
                if s == strip and j == block - 1:
                    continue
                work[s] = work[s] - factors[j][s] * row
    parts = []
    for s in range(strips):
        place = iota((8, size), 0) + 8 * s == iota((8, size), 1)
        pivot = jnp.sum(jnp.where(place, work[s][:, :size], 0.0), axis=1, keepdims=True)
        parts.append(work[s][:, size : 2 * size] * lax.rsqrt(pivot))
    return jnp.concatenate(parts, axis=0)


def member(group_ref, planes, dy=0, dz=0):
    y, z = lax.axis_index("gy"), lax.axis_index("gz")
    rows = lax.axis_size("gy")
    return group_ref[lax.rem(y + dy + rows, rows) * planes + lax.rem(z + dz + planes, planes)]


def store(ref, f, value):
    ref[f, 0], ref[f, 1] = split(value)


def load(ref, f):
    return ref[f, 0], ref[f, 1]


def upper_index(f, g):
    return sum(FACES - 1 - i for i in range(f)) + g - f - 1


def halves_kernel(planes, schur_ref, group_ref, own_ref, own_out, upper_out, flag_out, *scratch):
    upper_ref, sems = scratch
    width = own_ref.shape[1]
    strips = []
    for f in range(FACES - 1):
        rest = (FACES - 1 - f) * width
        copy = pltpu.make_async_copy(
            schur_ref.at[pl.ds(f * width, width), pl.ds((f + 1) * width, rest)],
            upper_ref.at[f, :, pl.ds((f + 1) * width, rest)],
            sems.at[f],
        )
        copy.start()
        strips.append(copy)
    core = lax.rem(lax.axis_index("gy"), 2)
    near = [(0, 0), (1 - 2 * core, 0), (-1, 0), (1, 0), (0, -1), (0, 1)]
    row = iota(flag_out.shape, 0)
    flags = jnp.zeros(flag_out.shape, jnp.float32)
    for i, (dy, dz) in enumerate(near):
        hit = member(group_ref, planes, dy, dz) == core
        flags = jnp.where(row == i, jnp.where(hit, 1.0, 0.0), flags)
    flag_out[...] = flags
    for f in range(FACES):
        store(own_out, f, own_ref[f])
    for f in range(FACES - 1):
        strips[f].wait()
        for g in range(f + 1, FACES):
            store(upper_out, upper_index(f, g), upper_ref[f, :, g * width : (g + 1) * width])


def inverses_of(packed, owns, partner_ref):
    width = owns[0].shape[1]
    half = width // 2
    eye = iota((half, half), 0) == iota((half, half), 1)
    whole_eye = iota((width, width), 0) == iota((width, width), 1)
    powers, sums, downs = [], [], []
    for f in range(len(packed)):
        partner = unpack(packed[f])
        store(partner_ref, f, partner)
        total = owns[f] + partner
        across, down = [], []
        for start in (0, half):
            block = total[start : start + half, start : start + half]
            diagonal = jnp.where(eye, block, 0.0)
            across.append(1.0 / jnp.sum(diagonal, axis=0, keepdims=True))
            down.append(1.0 / jnp.sum(diagonal, axis=1, keepdims=True))
        downs.append(jnp.concatenate(down, axis=0))
        power = jnp.where(whole_eye, 0.0, -total * jnp.concatenate(across, axis=1))
        powers.append(split(power))
        sums.append(jnp.where(whole_eye, 1.0, power))
    for step in range(1, NS_ITERS):
        powers = [split(wide(power, power)) for power in powers]
        sums = [total + wide(split(total), power) for total, power in zip(sums, powers)]
    return [down * total for down, total in zip(downs, sums)]


def unit_rows(basis):
    return [b * lax.rsqrt(jnp.sum(b * b, axis=1, keepdims=True)) for b in basis]


def sweep_basis(before, inverse, after, basis):
    for matrices in (before, inverse, after):
        basis = [thin(stacked(b), matrix) for b, matrix in zip(basis, matrices)]
    return unit_rows(basis)


def early_kernel(axes, faces, *refs):
    arrays = len(refs) - 6
    inputs = refs[:arrays]
    own_ref, halves_ref, starts_ref, basis_out, partner_out, inverse_out = refs[arrays:]
    count = len(faces)
    packed = []
    done = 0
    for axis in axes:
        number = face_arrays(lax.axis_size(axis))
        packed += receive(inputs[done : done + number], axis)
        done += number
    inverses = inverses_of(packed, [own_ref[f] for f in faces], partner_out)
    for i in range(count):
        store(inverse_out, i, inverses[i])
    basis = [starts_ref[f] for f in faces]
    matrices = [
        [load(partner_out, i) for i in range(count)],
        [load(inverse_out, i) for i in range(count)],
        [load(halves_ref, f) for f in faces],
    ]
    for sweep in range(SUB_ITERS):
        basis = sweep_basis(*matrices, basis)
    for i in range(count):
        basis_out[i] = basis[i]


def main_kernel(axes, early, late, *refs):
    arrays = len(refs) - 10
    inputs = refs[:arrays]
    own_ref, halves_ref, upper_ref, starts_ref, resid_ref, early_basis = refs[arrays : arrays + 6]
    payload_ref, product_ref, partner_out, inverse_out = refs[arrays + 6 :]
    ncon, width = starts_ref.shape[1:]
    columns = resid_ref.shape[1]
    sides = {}
    rights = {}
    grams = {}
    vectors = {}
    count = len(late)

    def project(f, basis):
        vectors[f] = basis
        rows = stacked(basis)
        grams[f] = dot(basis, basis, ((1,), (1,)))
        side = {f: thin(rows, load(halves_ref, f))}
        for g in range(f + 1, FACES):
            side[g] = thin(rows, load(upper_ref, upper_index(f, g)))
        sides[f] = side
        rights[f] = thin(rows, split(resid_ref[f * width : (f + 1) * width]))

    packed = []
    done = 0
    for axis in axes:
        number = face_arrays(lax.axis_size(axis))
        packed += receive(inputs[done : done + number], axis)
        done += number
    inverses = inverses_of(packed, [own_ref[f] for f in late], partner_out)
    pending = [(f, early_basis[i]) for i, f in enumerate(early)]
    for i in range(count):
        store(inverse_out, i, inverses[i])
    basis = [starts_ref[f] for f in late]
    matrices = [
        [load(partner_out, i) for i in range(count)],
        [load(inverse_out, i) for i in range(count)],
        [load(halves_ref, f) for f in late],
    ]
    for sweep in range(SUB_ITERS):
        basis = sweep_basis(*matrices, basis)
        if pending:
            project(*pending.pop(0))
    for item in pending:
        project(*item)
    for i, f in enumerate(late):
        project(f, basis[i])
    tall = {}
    for g in range(FACES):
        column = jnp.concatenate([sides[f][g] for f in range(g + 1)], axis=0)
        column = triple(column, vectors[g], ((1,), (1,)))
        for f in range(g + 1):
            tall[f, g] = column[f * ncon : (f + 1) * ncon]
    for f in range(0, FACES, 2):
        tall[f + 1, f] = tall[f, f + 1].T
    zero = jnp.zeros((ncon, ncon), jnp.float32)

    def square(parts):
        lines = []
        for f in range(FACES):
            line = [parts.get((f, g), zero) for g in range(FACES)]
            lines.append(jnp.concatenate(line, axis=1))
        return jnp.concatenate(lines, axis=0)

    coarse = square(tall)
    right = jnp.concatenate([rights[f] for f in range(FACES)], axis=0)
    factors = factor_inverses([grams[f] for f in range(FACES)])
    factor = square({(f, f): factors[f] for f in range(FACES)})
    coarse = triple(factor, triple(coarse, factor, ((1,), (1,))))
    right = triple(factor, right)
    for f in range(FACES):
        product_ref[f] = triple(factors[f], sides[f][f])
    size = 2 * ncon
    line = []
    for b in range(BLOCKS):
        line.append(coarse[b * size : (b + 1) * size, b * size :])
    line += [right[b * size : (b + 1) * size] for b in range(BLOCKS)]
    payload_ref[...] = jnp.concatenate(line, axis=1)


def find(faces, refs, f):
    for group, ref in zip(faces, refs):
        if f in group:
            return load(ref, list(group).index(f))


def theirs_kernel(faces, ncon, own_ref, *refs):
    inputs, partner_refs, inverse_refs = refs[:-6], refs[-6:-4], refs[-4:-2]
    basis_out, product_out = refs[-2:]
    basis = []
    done = 0
    for axis in AXES[:2]:
        number = face_arrays(lax.axis_size(axis))
        packed = receive(inputs[done : done + number], axis)
        basis += [unpack_starts(part, ncon) for part in packed]
        done += number
    count = len(basis)
    matrices = [
        [load(own_ref, f) for f in range(count)],
        [find(faces, inverse_refs, f) for f in range(count)],
        [find(faces, partner_refs, f) for f in range(count)],
    ]
    for sweep in range(SUB_ITERS):
        basis = sweep_basis(*matrices, basis)
    for f in range(count):
        basis_out[f] = basis[f]
        product_out[f] = thin(stacked(basis[f]), matrices[2][f])


def spread_kernel(faces, unread, basis_ref, theirs_ref, product_ref, *refs):
    inverse_refs, out_ref = refs[:2], refs[2]
    basis = [basis_ref[f] for f in range(basis_ref.shape[0])]
    factors = factor_inverses([dot(b, b, ((1,), (1,))) for b in basis])
    for f in range(len(basis)):
        theirs = triple(factors[f], theirs_ref[f])
        both = jnp.concatenate([product_ref[f], theirs], axis=0)
        high, low = split(thin(stacked(both), find(faces, inverse_refs, f)).T)
        out_ref[f] = jnp.concatenate([high, high, low], axis=1)


def choose_kernel(flag_ref, here_ref, there_ref, matrix_ref, right_ref):
    mine = flag_ref[0:1, 0:1] > 0.5
    other = flag_ref[1:2, 0:1] > 0.5
    total = jnp.where(mine, here_ref[...], 0.0) + jnp.where(other, there_ref[...], 0.0)
    lanes = matrix_ref.shape[1]
    matrix_ref[...] = total[:, :lanes]
    right_ref[...] = total[:, lanes:]


def add_kernel(first_ref, second_ref, third_ref, fourth_ref, product_ref, unread, *refs):
    matrix_ref, right_ref, *sent = refs
    matrix_ref[...] = first_ref[...] + second_ref[...]
    right_ref[...] = third_ref[...] + fourth_ref[...]
    send(sent, AXES[2], product_ref[4], product_ref[5])


def solve_kernel(size, terms, columns, *refs):
    lanes = size * BLOCKS * (BLOCKS + 1) // 2
    matrix, right = refs[0][:, :lanes], refs[terms][...]
    for term in range(1, terms):
        matrix = matrix + refs[term][:, :lanes]
        right = right + refs[terms + term][...]
    answer_ref = refs[-1]
    lines = []
    offset = 0
    for b in range(BLOCKS):
        lines.append(matrix[:, offset : offset + (BLOCKS - b) * size])
        offset += (BLOCKS - b) * size
    eye = iota((size, size), 0) == iota((size, size), 1)
    downs, acrosses = [], []
    for b in range(BLOCKS):
        diagonal = jnp.where(eye, lines[b][:, :size], 0.0)
        downs.append(lax.rsqrt(jnp.sum(diagonal, axis=1, keepdims=True)))
        acrosses.append(lax.rsqrt(jnp.sum(diagonal, axis=0, keepdims=True)))
    blocks = {}
    rights = []
    for b in range(BLOCKS):
        for c in range(b, BLOCKS):
            block = lines[b][:, (c - b) * size : (c - b + 1) * size]
            blocks[b, c] = downs[b] * block * acrosses[c]
            if c > b:
                blocks[c, b] = blocks[b, c].T
        rights.append(downs[b] * right[:, b * columns : (b + 1) * columns])
    for b in range(BLOCKS):
        inverse = factor_inverse(blocks[b, b])
        later = range(b + 1, BLOCKS)
        row = triple(inverse, jnp.concatenate([rights[b]] + [blocks[b, c] for c in later], axis=1))
        if later:
            column = jnp.concatenate([blocks[c, b] for c in later], axis=0)
            change = triple(triple(column, inverse, ((1,), (1,))), row)
        for i, c in enumerate(later):
            part = change[i * size : (i + 1) * size]
            rights[c] = rights[c] - part[:, :columns]
            for j, d in enumerate(later):
                start = columns + j * size
                blocks[c, d] = blocks[c, d] - part[:, start : start + size]
        row = triple(inverse, row, ((0,), (0,)))
        rights[b] = row[:, :columns]
        for c in later:
            blocks[b, c] = row[:, columns + (c - b - 1) * size : columns + (c - b) * size]
        for i in range(b):
            for c in later:
                blocks[i, c] = blocks[i, c] - triple(blocks[i, b], blocks[b, c])
            rights[i] = rights[i] - triple(blocks[i, b], rights[b])
    answer = [downs[b] * rights[b] for b in range(BLOCKS)]
    answer_ref[...] = jnp.concatenate(answer, axis=0)


def rows_kernel(ncon, flag_ref, here_ref, there_ref, *refs):
    hit = flag_ref[0:1, 0:1] > 0.5
    rows = jnp.where(hit, here_ref[: 2 * ncon], there_ref[: 2 * ncon])
    refs[-1][...] = rows
    send(refs[:-1], AXES[0], rows[:ncon], rows[ncon:])


def last_product(spread, mine, theirs):
    high, low = split(jnp.concatenate([mine, theirs], axis=0))
    return lax.dot_general(
        spread,
        jnp.concatenate([high, low, high], axis=0),
        (((1,), (0,)), ((), ())),
        preferred_element_type=jnp.float32,
    )


def through(inverse, mine, theirs, my_answer, their_answer):
    high, low = split(jnp.concatenate([mine, theirs], axis=0).T)
    spread = jnp.concatenate([high, high, low], axis=1)
    return wide(inverse, split(last_product(spread, my_answer, their_answer)))


def last_faces(values, width, out_ref, result, sems):
    copies = []
    for f, value in values.items():
        place = pl.ds(f * width, width)
        result[f * width : (f + 1) * width] = value()
        copy = pltpu.make_async_copy(result.at[place], out_ref.at[place], sems.at[f])
        copy.start()
        copies.append(copy)
    for copy in copies:
        copy.wait()


def last_plain_kernel(faces, product_ref, early_inverse, late_inverse, *refs):
    spread_ref, answer_ref, *inputs = refs[:-3]
    ncon, width = product_ref.shape[1:]
    number = face_arrays(lax.axis_size(AXES[2]))
    theirs = receive(inputs[:number], AXES[2])
    near = receive(inputs[number:-number], AXES[1]) + receive(inputs[-number:], AXES[2])
    values = {}
    for f in range(2, FACES):
        mine = answer_ref[f * ncon : (f + 1) * ncon]
        if f < 4:
            values[f] = functools.partial(last_product, spread_ref[f], mine, near[f - 2])
        else:
            values[f] = functools.partial(
                through,
                find(faces, (early_inverse, late_inverse), f),
                product_ref[f],
                theirs[f - 4],
                mine,
                near[f - 2],
            )
    last_faces(values, width, *refs[-3:])


def last_near_kernel(faces, flag_ref, product_ref, early_inverse, late_inverse, *refs):
    spread_ref, here_answer, there_answer = refs[:3]
    theirs = receive(refs[3:-3], AXES[2])
    ncon, width = product_ref.shape[1:]

    def answer(flag, f):
        place = slice(f * ncon, (f + 1) * ncon)
        hit = flag_ref[flag : flag + 1, 0:1] > 0.5
        return jnp.where(hit, here_answer[place], there_answer[place])

    values = {}
    for f in (2, 3):
        values[f] = functools.partial(
            last_product, spread_ref[f], answer(0, f), answer(f, f ^ 1)
        )
    for f in (4, 5):
        values[f] = functools.partial(
            through,
            find(faces, (early_inverse, late_inverse), f),
            product_ref[f],
            theirs[f - 4],
            answer(0, f),
            answer(f, f ^ 1),
        )
    last_faces(values, width, *refs[-3:])


def last_far_kernel(ncon, spread_ref, rows_ref, *refs):
    theirs = receive(refs[:-4], AXES[0])
    values = {}
    for f in range(2):
        mine = rows_ref[f * ncon : (f + 1) * ncon]
        values[f] = functools.partial(last_product, spread_ref[f], mine, theirs[f])
    last_faces(values, spread_ref.shape[1], *refs[-3:])


def per_device(schur, start_block, resid, group_of):
    matrix = schur[0, 0, 0]
    matrix = pltpu.with_memory_space_constraint(matrix, pltpu.HBM)
    starts = start_block[0, 0, 0].transpose(0, 2, 1)
    right = resid[0, 0, 0]
    order, columns = right.shape
    ncon, width = starts.shape[1:]
    counts = [lax.axis_size(axis) for axis in AXES]
    arrays = sum(face_arrays(count) for count in counts)
    coarse = FACES * ncon
    size = 2 * ncon
    half = width // 2
    lanes = size * BLOCKS * (BLOCKS + 1) // 2
    right_lanes = BLOCKS * columns
    uppers = FACES * (FACES - 1) // 2
    anywhere = pl.BlockSpec(memory_space=pl.ANY)
    main_memory = pl.BlockSpec(memory_space=pltpu.HBM)
    scalars = pl.BlockSpec(memory_space=pltpu.SMEM)
    early, late = (4, 5), (0, 1, 2, 3)
    faces = (early, late)
    planes = counts[2]

    def shape(*dims):
        return jax.ShapeDtypeStruct(dims, jnp.float32)

    def halves(count):
        return jax.ShapeDtypeStruct((count, 2, width, width), jnp.bfloat16)

    def params(mib):
        return pltpu.CompilerParams(vmem_limit_bytes=mib * MIB)

    def cost(us):
        return pl.CostEstimate(flops=us * 10**9, bytes_accessed=2**20, transcendentals=0)

    *packed, own = pl.pallas_call(
        functools.partial(pack_kernel, counts, width),
        out_shape=face_shapes(counts[0], (width + 8 + 2 * ncon, half))
        + face_shapes(counts[1], (width + 8 + 2 * ncon, half))
        + face_shapes(counts[2], (width + 8, half))
        + [shape(FACES, width, width)],
        in_specs=[main_memory, main_memory],
        out_specs=vmem_specs(arrays + 1),
        scratch_shapes=[
            pltpu.VMEM((4, ncon, width), jnp.float32),
            pltpu.SemaphoreType.DMA((FACES,)),
            pltpu.SemaphoreType.DMA,
        ],
        compiler_params=params(12),
    )(matrix, pltpu.with_memory_space_constraint(starts, pltpu.HBM))
    ends = [sum(face_arrays(count) for count in counts[:position]) for position in range(4)]
    got = {}
    for position in (2, 0, 1):
        got[position] = exchange(packed[ends[position] : ends[position + 1]], AXES[position])

    own_halves, upper_halves, flags = pl.pallas_call(
        functools.partial(halves_kernel, planes),
        out_shape=[halves(FACES), halves(uppers), shape(8, 128)],
        in_specs=[main_memory, scalars] + vmem_specs(1),
        out_specs=vmem_specs(3),
        scratch_shapes=[
            pltpu.VMEM((FACES - 1, width, order), jnp.float32),
            pltpu.SemaphoreType.DMA((FACES - 1,)),
        ],
        compiler_params=params(24),
        cost_estimate=cost(2),
    )(matrix, group_of, own)

    early_basis, early_partner, early_inverse = pl.pallas_call(
        functools.partial(early_kernel, AXES[2:3], early),
        out_shape=[shape(len(early), ncon, width)] + [halves(len(early))] * 2,
        in_specs=vmem_specs(len(got[2]) + 3),
        out_specs=vmem_specs(3),
        compiler_params=params(16),
        cost_estimate=cost(2),
    )(*got[2], own, own_halves, starts)

    payload, product, late_partner, late_inverse = pl.pallas_call(
        functools.partial(main_kernel, (AXES[0], AXES[1]), early, late),
        out_shape=[shape(size, lanes + right_lanes), shape(FACES, ncon, width)]
        + [halves(len(late))] * 2,
        in_specs=vmem_specs(len(got[0]) + len(got[1]) + 6),
        out_specs=vmem_specs(4),
        compiler_params=params(24),
        cost_estimate=cost(8),
    )(*got[0], *got[1], own, own_halves, upper_halves, starts, right, early_basis)

    partners = [early_partner, late_partner]
    inverses = [early_inverse, late_inverse]
    their_basis, their_product = pl.pallas_call(
        functools.partial(theirs_kernel, faces, ncon),
        out_shape=[shape(4, ncon, width)] * 2,
        in_specs=vmem_specs(5 + len(got[0]) + len(got[1])),
        out_specs=vmem_specs(2),
        compiler_params=params(16),
        cost_estimate=cost(2),
    )(own_halves, *got[0], *got[1], *partners, *inverses)

    def spread_of(token):
        return pl.pallas_call(
            functools.partial(spread_kernel, faces),
            out_shape=jax.ShapeDtypeStruct((4, width, 3 * size), jnp.bfloat16),
            in_specs=[anywhere] + vmem_specs(5),
            out_specs=vmem_specs(1)[0],
            compiler_params=params(16),
            cost_estimate=cost(2),
        )(token, their_basis, their_product, product, *inverses)

    def solve(matrices, rights, unread):
        return pl.pallas_call(
            functools.partial(solve_kernel, size, len(matrices), columns),
            out_shape=shape(coarse, columns),
            in_specs=vmem_specs(2 * len(matrices)) + [anywhere] * len(unread),
            out_specs=vmem_specs(1)[0],
            compiler_params=params(12),
            cost_estimate=cost(7),
        )(*matrices, *rights, *unread)

    result = dict(
        out_shape=shape(order, columns),
        out_specs=main_memory,
        scratch_shapes=[
            pltpu.VMEM((order, columns), jnp.float32),
            pltpu.SemaphoreType.DMA((FACES,)),
        ],
        compiler_params=params(12),
        cost_estimate=cost(1),
    )
    groups = group_of.shape[0] // GROUP_SIZE
    if groups == 2 and counts[1] == 4 and planes == 2:
        core_swap, chip_x, chip_y = flipped("gy", 1), flipped("gy", 2), flipped("gz", 1)
        other = lax.ppermute(payload, "gy", core_swap)
        left, rest = pl.pallas_call(
            choose_kernel,
            out_shape=[shape(size, lanes), shape(size, right_lanes)],
            in_specs=vmem_specs(3),
            out_specs=vmem_specs(2),
            compiler_params=params(8),
        )(flags, payload, other)
        left_moved = lax.ppermute(left, "gy", chip_x)
        rest_moved = lax.ppermute(rest, "gz", chip_y)
        left_last, rest_last, *sent = pl.pallas_call(
            add_kernel,
            out_shape=[shape(size, lanes), shape(size, right_lanes)]
            + face_shapes(counts[2], (ncon, width)),
            in_specs=vmem_specs(5) + [anywhere],
            out_specs=vmem_specs(2 + face_arrays(counts[2])),
            compiler_params=params(8),
        )(left, left_moved, rest, rest_moved, product, their_basis)
        left_other = lax.ppermute(left_last, "gz", chip_y)
        rest_other = lax.ppermute(rest_last, "gy", chip_x)
        theirs = exchange(sent, AXES[2])
        spread = spread_of(left_last)
        answer = solve([left_last, left_other], [rest_last, rest_other], [spread])
        there = lax.ppermute(answer, "gy", core_swap)
        *sent, mine = pl.pallas_call(
            functools.partial(rows_kernel, ncon),
            out_shape=face_shapes(counts[0], (ncon, columns)) + [shape(size, columns)],
            in_specs=vmem_specs(3),
            out_specs=vmem_specs(face_arrays(counts[0]) + 1),
            compiler_params=params(8),
        )(flags, answer, there)
        across = exchange(sent, AXES[0])
        correction = pl.pallas_call(
            functools.partial(last_near_kernel, faces),
            in_specs=vmem_specs(7 + len(theirs)),
            **result,
        )(flags, product, *inverses, spread, answer, there, *theirs)
    else:
        y, z = lax.axis_index("gy"), lax.axis_index("gz")
        member_of = group_of[y * planes + z]
        chosen = jnp.arange(groups, dtype=jnp.int32) == member_of
        total = lax.psum(jnp.where(chosen[:, None, None], payload[None], 0.0), ("gy", "gz"))
        total = lax.dynamic_index_in_dim(total, member_of, 0, keepdims=False)
        spread = spread_of(payload)
        answer = solve([total[:, :lanes]], [total[:, lanes:]], [])

        def from_near(faces_of, axis):
            even, odd = faces_of
            if lax.axis_size(axis) == 2:
                return exchange([jnp.stack([even, odd])], axis)
            upward = is_even(axis)
            return exchange([jnp.where(upward, even, odd), jnp.where(upward, odd, even)], axis)

        blocks = answer.reshape(FACES, ncon, columns)
        near = [
            *from_near(product[4:6], AXES[2]),
            *from_near(blocks[2:4], AXES[1]),
            *from_near(blocks[4:6], AXES[2]),
        ]
        mine = answer[:size]
        across = from_near(blocks[:2], AXES[0])
        correction = pl.pallas_call(
            functools.partial(last_plain_kernel, faces),
            in_specs=vmem_specs(5 + len(near)),
            **result,
        )(product, *inverses, spread, answer, *near)
    correction = pl.pallas_call(
        functools.partial(last_far_kernel, ncon),
        in_specs=vmem_specs(2 + len(across)) + [main_memory],
        input_output_aliases={2 + len(across): 0},
        **result,
    )(spread, mine, *across, correction)
    return correction[None, None, None]


def solution(mesh):
    in_specs = (
        P("gx", "gy", "gz", None, None),
        P("gx", "gy", "gz", None, None, None),
        P("gx", "gy", "gz", None, None),
        P(),
    )
    out_specs = P("gx", "gy", "gz", None, None)
    return jax.shard_map(
        per_device, mesh=mesh, in_specs=in_specs, out_specs=out_specs, check_vma=False
    )
```

```python
import functools

import jax
import jax.numpy as jnp
from jax import lax
from jax.experimental import pallas as pl
from jax.experimental.pallas import tpu as pltpu
from jax.sharding import PartitionSpec as P

NS_ITERS = 3
SUB_ITERS = 2
GROUP_SIZE = 4
FACES = 6
BLOCKS = FACES // 2
AXES = ("gx", "gy", "gz")
MIB = 1024 * 1024

precise = lax.Precision.HIGHEST


def dot(left, right, dims=((1,), (0,))):
    return lax.dot_general(
        left, right, (dims, ((), ())), precision=precise, preferred_element_type=jnp.float32
    )


def split(value):
    high = value.astype(jnp.bfloat16)
    return high, (value - high.astype(jnp.float32)).astype(jnp.bfloat16)


def wide(left, right):
    return lax.dot_general(
        jnp.concatenate([left[0], left[0], left[1]], axis=1),
        jnp.concatenate([right[0], right[1], right[0]], axis=0),
        (((1,), (0,)), ((), ())),
        preferred_element_type=jnp.float32,
    )


def stacked(value):
    return jnp.concatenate(split(value), axis=0)


def thin(rows, matrix):
    out = lax.dot_general(
        jnp.concatenate([rows, rows], axis=1),
        jnp.concatenate(matrix, axis=0),
        (((1,), (0,)), ((), ())),
        preferred_element_type=jnp.float32,
    )
    half = rows.shape[0] // 2
    return out[:half] + out[half:]


def triple(left, right, dims=((1,), (0,))):
    (left_high, left_low), (right_high, right_low) = split(left), split(right)
    total = None
    for one, other in ((left_high, right_high), (left_high, right_low), (left_low, right_high)):
        part = lax.dot_general(
            one, other, (dims, ((), ())), preferred_element_type=jnp.float32
        )
        total = part if total is None else total + part
    return total


def iota(shape, dim):
    return lax.broadcasted_iota(jnp.int32, shape, dim)


def flipped(axis, bit):
    return [(i, i ^ bit) for i in range(lax.axis_size(axis))]


def outer_pairs(axis):
    count = lax.axis_size(axis)
    return [(i, (i + 1 if i % 2 else i - 1) % count) for i in range(count)]


def face_arrays(count):
    return 1 if count == 2 else 2


def exchange(arrays, axis):
    if lax.axis_size(axis) == 2:
        return [lax.ppermute(arrays[0], axis, flipped(axis, 1))]
    return [
        lax.ppermute(arrays[0], axis, outer_pairs(axis)),
        lax.ppermute(arrays[1], axis, flipped(axis, 1)),
    ]


def is_even(axis):
    return lax.rem(lax.axis_index(axis), 2) == 0


def send(refs, axis, even, odd):
    if lax.axis_size(axis) == 2:
        refs[0][0] = even
        refs[0][1] = odd
    else:
        upward = is_even(axis)
        refs[0][...] = jnp.where(upward, even, odd)
        refs[1][...] = jnp.where(upward, odd, even)


def receive(refs, axis):
    if lax.axis_size(axis) == 2:
        return refs[0][1], refs[0][0]
    upward = is_even(axis)
    first, second = refs[0][...], refs[1][...]
    return jnp.where(upward, first, second), jnp.where(upward, second, first)


def face_shapes(count, shape):
    if count == 2:
        return [jax.ShapeDtypeStruct((2,) + shape, jnp.float32)]
    return [jax.ShapeDtypeStruct(shape, jnp.float32)] * 2


def vmem_specs(count):
    return [pl.BlockSpec(memory_space=pltpu.VMEM)] * count


def pack_kernel(counts, width, schur_ref, starts_ref, *refs):
    outs, blocks = refs[:-4], refs[-4]
    starts, sems, start_sem = refs[-3:]
    half = width // 2
    copies = []
    for f in range(FACES):
        place = pl.ds(f * width, width)
        copy = pltpu.make_async_copy(schur_ref.at[place, place], blocks.at[f], sems.at[f])
        copy.start()
        copies.append(copy)
    start_copy = pltpu.make_async_copy(starts_ref.at[pl.ds(0, 4)], starts, start_sem)
    start_copy.start()
    row, col = iota((half, half), 0), iota((half, half), 1)
    start_copy.wait()

    def pack(f):
        copies[f].wait()
        first = blocks[f, 0:half, 0:half]
        second = blocks[f, half:width, half:width]
        diag = jnp.sum(jnp.where(row == col, second, 0.0), axis=0, keepdims=True)
        mixed = jnp.where(row >= col, first, second)
        tail = jnp.broadcast_to(diag, (8, half))
        parts = [blocks[f, half:width, 0:half], mixed, tail]
        if f < 4:
            parts += [starts[f, :, :half], starts[f, :, half:]]
        return jnp.concatenate(parts, axis=0)

    done = 0
    for position, axis in enumerate(AXES):
        number = face_arrays(counts[position])
        send(outs[done : done + number], axis, pack(2 * position), pack(2 * position + 1))
        done += number


def unpack(packed):
    half = packed.shape[1]
    row, col = iota((half, half), 0), iota((half, half), 1)
    low = packed[0:half]
    mixed = packed[half : 2 * half]
    flip = mixed.T
    first = jnp.where(row >= col, mixed, flip)
    second = jnp.where(row < col, mixed, flip)
    second = jnp.where(row == col, packed[2 * half : 2 * half + 1], second)
    return jnp.concatenate(
        [jnp.concatenate([first, low.T], axis=1), jnp.concatenate([low, second], axis=1)], axis=0
    )


def unpack_starts(packed, ncon):
    half = packed.shape[1]
    rows = packed[2 * half + 8 :]
    return jnp.concatenate([rows[:ncon], rows[ncon:]], axis=1)


def factor_inverses(grams):
    size = grams[0].shape[0]
    strips, block, lanes = size // 8, 8, 128
    full = (block, lanes)
    beside = lanes // (2 * size)
    one = jnp.where(iota((size, size), 0) == iota((size, size), 1), 1.0, 0.0)
    states = []
    for first in range(0, len(grams), beside):
        parts = [part for gram in grams[first : first + beside] for part in (gram, one)]
        whole = jnp.concatenate(parts, axis=1)
        states.append([whole[8 * s : 8 * s + 8] for s in range(strips)])
    below = iota(full, 0)
    base = iota(full, 1) // (2 * size) * (2 * size)

    def column(rows, k):
        if beside == 1:
            return jnp.broadcast_to(rows[:, k : k + 1], full)
        return jnp.take_along_axis(rows, base + k, axis=1, mode="promise_in_bounds")

    def line_of(rows, line):
        return jnp.broadcast_to(rows[line : line + 1], full)

    roots = [[None] * strips for _ in states]
    for strip in range(strips):
        start = strip * block
        columns = [
            [[column(work[s], start + j) for s in range(strip, strips)] for j in range(block)]
            for work in states
        ]
        heads = [[column_set[0] for column_set in per_state] for per_state in columns]
        lowers = [work[strip] for work in states]
        solved = list(lowers)
        pivots = [jnp.ones(full, jnp.float32) for _ in states]
        scales = list(pivots)

        def eliminate(i, j, scale, pivot, side):
            cols = heads[i]
            factor = jnp.where(below != j, cols[j] * scale, 0.0)
            for later in range(j + 1, block):
                use = side if later == j + 1 and side is not None else line_of(cols[later], j)
                cols[later] = cols[later] - factor * use
            row = line_of(lowers[i], j)
            solved[i] = solved[i] - factor * row
            lowers[i] = lowers[i] - jnp.where(below > j, factor, 0.0) * row
            pivots[i] = jnp.where(below == j, pivot, pivots[i])
            scales[i] = jnp.where(below == j, scale, scales[i])

        for j in range(0, block, 2):
            for i in range(len(states)):
                cols = heads[i]
                corner, side = line_of(cols[j], j), line_of(cols[j], j + 1)
                last = line_of(cols[j + 1], j + 1)
                minor = corner * last - side * side
                scale = 1.0 / corner
                eliminate(i, j, scale, corner, side)
                eliminate(i, j + 1, corner * (1.0 / minor), minor * scale, None)
        for i, work in enumerate(states):
            work[strip] = lowers[i]
            roots[i][strip] = lax.rsqrt(pivots[i])
            if strip == strips - 1:
                continue
            answer = solved[i] * scales[i]
            rows = [line_of(answer, j) for j in range(block)]
            for s in range(strip + 1, strips):
                for j in range(block):
                    work[s] = work[s] - columns[i][j][s - strip] * rows[j]
    results = []
    for i, work in enumerate(states):
        scaled = jnp.concatenate([work[s] * roots[i][s] for s in range(strips)], axis=0)
        for m in range(beside):
            begin = (2 * m + 1) * size
            results.append(scaled[:, begin : begin + size])
    return results


def factor_inverse(gram):
    size = gram.shape[0]
    strips, block, lanes = size // 8, 8, 128
    full = (block, lanes)
    parts = [gram, jnp.where(iota((size, size), 0) == iota((size, size), 1), 1.0, 0.0)]
    if 2 * size < lanes:
        parts.append(jnp.zeros((size, lanes - 2 * size), jnp.float32))
    whole = jnp.concatenate(parts, axis=1)
    work = [whole[8 * s : 8 * s + 8] for s in range(strips)]
    below = iota(full, 0)

    def line_of(rows, line):
        return jnp.broadcast_to(rows[line : line + 1], full)

    scaled = []
    for strip in range(strips):
        start = strip * block
        later_strips = range(strip + 1, strips)
        cols = [
            {
                s: jnp.broadcast_to(work[s][:, start + j : start + j + 1], full)
                for s in range(strip, strips)
            }
            for j in range(block)
        ]
        value = {
            (p, q): line_of(cols[q][strip], p) for q in range(block) for p in range(q + 1)
        }
        rows = [line_of(work[strip], p) for p in range(block)]
        own = work[strip]
        pivots = jnp.ones(full, jnp.float32)
        solved = []
        for j in range(0, block, 2):
            a, b, c = value[j, j], value[j, j + 1], value[j + 1, j + 1]
            minor = a * c - b * b
            inverse = 1.0 / minor
            over = 1.0 / a
            top, bottom = rows[j], rows[j + 1]
            weights = {}
            for q in range(j + 2, block):
                upper, lower = value[j, q], value[j + 1, q]
                weights[q] = (c * upper - b * lower) * inverse, (a * lower - b * upper) * inverse
            for q in range(j + 2, block):
                first, second = weights[q]
                for p in range(j + 2, q + 1):
                    value[p, q] = value[p, q] - (value[j, p] * first + value[j + 1, p] * second)
                rows[q] = rows[q] - (top * first + bottom * second)
                for s in later_strips:
                    cols[q][s] = cols[q][s] - (cols[j][s] * first + cols[j + 1][s] * second)
            solved += [(c * top - b * bottom) * inverse, (a * bottom - b * top) * inverse]
            own = jnp.where(below == j, top, own)
            own = jnp.where(below == j + 1, bottom - (b * over) * top, own)
            pivots = jnp.where(below == j, a, pivots)
            pivots = jnp.where(below == j + 1, minor * over, pivots)
        scaled.append(own * lax.rsqrt(pivots))
        for s in later_strips:
            terms = [cols[j][s] * solved[j] for j in range(block)]
            while len(terms) > 1:
                terms = [terms[i] + terms[i + 1] for i in range(0, len(terms), 2)]
            work[s] = work[s] - terms[0]
    return jnp.concatenate(scaled, axis=0)[:, size : 2 * size]


def member(group_ref, planes, dy=0, dz=0):
    y, z = lax.axis_index("gy"), lax.axis_index("gz")
    rows = lax.axis_size("gy")
    return group_ref[lax.rem(y + dy + rows, rows) * planes + lax.rem(z + dz + planes, planes)]


def store(ref, f, value):
    ref[f, 0], ref[f, 1] = split(value)


def load(ref, f):
    return ref[f, 0], ref[f, 1]


def upper_index(f, g):
    return sum(FACES - 1 - i for i in range(f)) + g - f - 1


def halves_kernel(planes, schur_ref, group_ref, own_ref, own_out, upper_out, flag_out, *scratch):
    upper_ref, sems = scratch
    width = own_ref.shape[1]
    strips = []
    for f in range(FACES - 1):
        rest = (FACES - 1 - f) * width
        copy = pltpu.make_async_copy(
            schur_ref.at[pl.ds(f * width, width), pl.ds((f + 1) * width, rest)],
            upper_ref.at[f, :, pl.ds((f + 1) * width, rest)],
            sems.at[f],
        )
        copy.start()
        strips.append(copy)
    core = lax.rem(lax.axis_index("gy"), 2)
    near = [(0, 0), (1 - 2 * core, 0), (-1, 0), (1, 0), (0, -1), (0, 1)]
    row = iota(flag_out.shape, 0)
    flags = jnp.zeros(flag_out.shape, jnp.float32)
    for i, (dy, dz) in enumerate(near):
        hit = member(group_ref, planes, dy, dz) == core
        flags = jnp.where(row == i, jnp.where(hit, 1.0, 0.0), flags)
    flag_out[...] = flags
    for f in range(FACES):
        store(own_out, f, own_ref[f])
    for f in range(FACES - 1):
        strips[f].wait()
        for g in range(f + 1, FACES):
            store(upper_out, upper_index(f, g), upper_ref[f, :, g * width : (g + 1) * width])


def inverses_of(packed, owns, partner_ref):
    width = owns[0].shape[1]
    half = width // 2
    eye = iota((half, half), 0) == iota((half, half), 1)
    whole_eye = iota((width, width), 0) == iota((width, width), 1)
    powers, sums, downs = [], [], []
    for f in range(len(packed)):
        partner = unpack(packed[f])
        store(partner_ref, f, partner)
        total = owns[f] + partner
        across, down = [], []
        for start in (0, half):
            block = total[start : start + half, start : start + half]
            diagonal = jnp.where(eye, block, 0.0)
            across.append(1.0 / jnp.sum(diagonal, axis=0, keepdims=True))
            down.append(1.0 / jnp.sum(diagonal, axis=1, keepdims=True))
        downs.append(jnp.concatenate(down, axis=0))
        power = jnp.where(whole_eye, 0.0, -total * jnp.concatenate(across, axis=1))
        powers.append(split(power))
        sums.append(jnp.where(whole_eye, 1.0, power))
    for step in range(1, NS_ITERS):
        powers = [split(wide(power, power)) for power in powers]
        sums = [total + wide(split(total), power) for total, power in zip(sums, powers)]
    return [down * total for down, total in zip(downs, sums)]


def unit_rows(basis):
    return [b * lax.rsqrt(jnp.sum(b * b, axis=1, keepdims=True)) for b in basis]


def sweep_basis(before, inverse, after, basis):
    for matrices in (before, inverse, after):
        basis = [thin(stacked(b), matrix) for b, matrix in zip(basis, matrices)]
    return unit_rows(basis)


def early_kernel(axes, faces, *refs):
    arrays = len(refs) - 6
    inputs = refs[:arrays]
    own_ref, halves_ref, starts_ref, basis_out, partner_out, inverse_out = refs[arrays:]
    count = len(faces)
    packed = []
    done = 0
    for axis in axes:
        number = face_arrays(lax.axis_size(axis))
        packed += receive(inputs[done : done + number], axis)
        done += number
    inverses = inverses_of(packed, [own_ref[f] for f in faces], partner_out)
    for i in range(count):
        store(inverse_out, i, inverses[i])
    basis = [starts_ref[f] for f in faces]
    matrices = [
        [load(partner_out, i) for i in range(count)],
        [load(inverse_out, i) for i in range(count)],
        [load(halves_ref, f) for f in faces],
    ]
    for sweep in range(SUB_ITERS):
        basis = sweep_basis(*matrices, basis)
    for i in range(count):
        basis_out[i] = basis[i]


def main_kernel(axes, early, late, *refs):
    arrays = len(refs) - 10
    inputs = refs[:arrays]
    own_ref, halves_ref, upper_ref, starts_ref, resid_ref, early_basis = refs[arrays : arrays + 6]
    payload_ref, product_ref, partner_out, inverse_out = refs[arrays + 6 :]
    ncon, width = starts_ref.shape[1:]
    columns = resid_ref.shape[1]
    sides = {}
    rights = {}
    grams = {}
    vectors = {}
    count = len(late)

    def project(f, basis):
        vectors[f] = basis
        rows = stacked(basis)
        grams[f] = dot(basis, basis, ((1,), (1,)))
        side = {f: thin(rows, load(halves_ref, f))}
        for g in range(f + 1, FACES):
            side[g] = thin(rows, load(upper_ref, upper_index(f, g)))
        sides[f] = side
        rights[f] = thin(rows, split(resid_ref[f * width : (f + 1) * width]))

    packed = []
    done = 0
    for axis in axes:
        number = face_arrays(lax.axis_size(axis))
        packed += receive(inputs[done : done + number], axis)
        done += number
    inverses = inverses_of(packed, [own_ref[f] for f in late], partner_out)
    pending = [(f, early_basis[i]) for i, f in enumerate(early)]
    for i in range(count):
        store(inverse_out, i, inverses[i])
    basis = [starts_ref[f] for f in late]
    matrices = [
        [load(partner_out, i) for i in range(count)],
        [load(inverse_out, i) for i in range(count)],
        [load(halves_ref, f) for f in late],
    ]
    for sweep in range(SUB_ITERS):
        basis = sweep_basis(*matrices, basis)
        if pending:
            project(*pending.pop(0))
    for item in pending:
        project(*item)
    for i, f in enumerate(late):
        project(f, basis[i])
    tall = {}
    for g in range(FACES):
        column = jnp.concatenate([sides[f][g] for f in range(g + 1)], axis=0)
        column = triple(column, vectors[g], ((1,), (1,)))
        for f in range(g + 1):
            tall[f, g] = column[f * ncon : (f + 1) * ncon]
    for f in range(0, FACES, 2):
        tall[f + 1, f] = tall[f, f + 1].T
    zero = jnp.zeros((ncon, ncon), jnp.float32)

    def square(parts):
        lines = []
        for f in range(FACES):
            line = [parts.get((f, g), zero) for g in range(FACES)]
            lines.append(jnp.concatenate(line, axis=1))
        return jnp.concatenate(lines, axis=0)

    coarse = square(tall)
    right = jnp.concatenate([rights[f] for f in range(FACES)], axis=0)
    factors = factor_inverses([grams[f] for f in range(FACES)])
    factor = square({(f, f): factors[f] for f in range(FACES)})
    coarse = triple(factor, triple(coarse, factor, ((1,), (1,))))
    right = triple(factor, right)
    for f in range(FACES):
        product_ref[f] = triple(factors[f], sides[f][f])
    size = 2 * ncon
    line = []
    for b in range(BLOCKS):
        line.append(coarse[b * size : (b + 1) * size, b * size :])
    line += [right[b * size : (b + 1) * size] for b in range(BLOCKS)]
    payload_ref[...] = jnp.concatenate(line, axis=1)


def find(faces, refs, f):
    for group, ref in zip(faces, refs):
        if f in group:
            return load(ref, list(group).index(f))


def theirs_kernel(faces, ncon, own_ref, *refs):
    inputs, partner_refs, inverse_refs = refs[:-6], refs[-6:-4], refs[-4:-2]
    basis_out, product_out = refs[-2:]
    basis = []
    done = 0
    for axis in AXES[:2]:
        number = face_arrays(lax.axis_size(axis))
        packed = receive(inputs[done : done + number], axis)
        basis += [unpack_starts(part, ncon) for part in packed]
        done += number
    count = len(basis)
    matrices = [
        [load(own_ref, f) for f in range(count)],
        [find(faces, inverse_refs, f) for f in range(count)],
        [find(faces, partner_refs, f) for f in range(count)],
    ]
    for sweep in range(SUB_ITERS):
        basis = sweep_basis(*matrices, basis)
    for f in range(count):
        basis_out[f] = basis[f]
        product_out[f] = thin(stacked(basis[f]), matrices[2][f])


def spread_kernel(faces, unread, basis_ref, theirs_ref, product_ref, *refs):
    inverse_refs, out_ref = refs[:2], refs[2]
    basis = [basis_ref[f] for f in range(basis_ref.shape[0])]
    factors = factor_inverses([dot(b, b, ((1,), (1,))) for b in basis])
    for f in range(len(basis)):
        theirs = triple(factors[f], theirs_ref[f])
        both = jnp.concatenate([product_ref[f], theirs], axis=0)
        high, low = split(thin(stacked(both), find(faces, inverse_refs, f)).T)
        out_ref[f] = jnp.concatenate([high, high, low], axis=1)


def choose_kernel(flag_ref, here_ref, there_ref, matrix_ref, right_ref):
    mine = flag_ref[0:1, 0:1] > 0.5
    other = flag_ref[1:2, 0:1] > 0.5
    total = jnp.where(mine, here_ref[...], 0.0) + jnp.where(other, there_ref[...], 0.0)
    lanes = matrix_ref.shape[1]
    matrix_ref[...] = total[:, :lanes]
    right_ref[...] = total[:, lanes:]


def add_kernel(first_ref, second_ref, third_ref, fourth_ref, product_ref, unread, *refs):
    matrix_ref, right_ref, *sent = refs
    matrix_ref[...] = first_ref[...] + second_ref[...]
    right_ref[...] = third_ref[...] + fourth_ref[...]
    send(sent, AXES[2], product_ref[4], product_ref[5])


def solve_kernel(size, terms, columns, *refs):
    lanes = size * BLOCKS * (BLOCKS + 1) // 2
    matrix, right = refs[0][:, :lanes], refs[terms][...]
    for term in range(1, terms):
        matrix = matrix + refs[term][:, :lanes]
        right = right + refs[terms + term][...]
    answer_ref = refs[-1]
    lines = []
    offset = 0
    for b in range(BLOCKS):
        lines.append(matrix[:, offset : offset + (BLOCKS - b) * size])
        offset += (BLOCKS - b) * size
    eye = iota((size, size), 0) == iota((size, size), 1)
    downs, acrosses = [], []
    for b in range(BLOCKS):
        diagonal = jnp.where(eye, lines[b][:, :size], 0.0)
        downs.append(lax.rsqrt(jnp.sum(diagonal, axis=1, keepdims=True)))
        acrosses.append(lax.rsqrt(jnp.sum(diagonal, axis=0, keepdims=True)))
    blocks = {}
    rights = []
    for b in range(BLOCKS):
        for c in range(b, BLOCKS):
            block = lines[b][:, (c - b) * size : (c - b + 1) * size]
            blocks[b, c] = downs[b] * block * acrosses[c]
            if c > b:
                blocks[c, b] = blocks[b, c].T
        rights.append(downs[b] * right[:, b * columns : (b + 1) * columns])
    for b in range(BLOCKS):
        inverse = factor_inverse(blocks[b, b])
        later = range(b + 1, BLOCKS)
        row = triple(inverse, jnp.concatenate([rights[b]] + [blocks[b, c] for c in later], axis=1))
        if later:
            column = jnp.concatenate([blocks[c, b] for c in later], axis=0)
            change = triple(triple(column, inverse, ((1,), (1,))), row)
        for i, c in enumerate(later):
            part = change[i * size : (i + 1) * size]
            rights[c] = rights[c] - part[:, :columns]
            for j, d in enumerate(later):
                start = columns + j * size
                blocks[c, d] = blocks[c, d] - part[:, start : start + size]
        row = triple(inverse, row, ((0,), (0,)))
        rights[b] = row[:, :columns]
        for c in later:
            blocks[b, c] = row[:, columns + (c - b - 1) * size : columns + (c - b) * size]
        for i in range(b):
            for c in later:
                blocks[i, c] = blocks[i, c] - triple(blocks[i, b], blocks[b, c])
            rights[i] = rights[i] - triple(blocks[i, b], rights[b])
    answer = [downs[b] * rights[b] for b in range(BLOCKS)]
    answer_ref[...] = jnp.concatenate(answer, axis=0)


def rows_kernel(ncon, flag_ref, here_ref, there_ref, *refs):
    hit = flag_ref[0:1, 0:1] > 0.5
    rows = jnp.where(hit, here_ref[: 2 * ncon], there_ref[: 2 * ncon])
    refs[-1][...] = rows
    send(refs[:-1], AXES[0], rows[:ncon], rows[ncon:])


def last_product(spread, mine, theirs):
    high, low = split(jnp.concatenate([mine, theirs], axis=0))
    return lax.dot_general(
        spread,
        jnp.concatenate([high, low, high], axis=0),
        (((1,), (0,)), ((), ())),
        preferred_element_type=jnp.float32,
    )


def through(inverse, mine, theirs, my_answer, their_answer):
    high, low = split(jnp.concatenate([mine, theirs], axis=0).T)
    spread = jnp.concatenate([high, high, low], axis=1)
    return wide(inverse, split(last_product(spread, my_answer, their_answer)))


def last_faces(values, width, out_ref, result, sems):
    copies = []
    for f, value in values.items():
        place = pl.ds(f * width, width)
        result[f * width : (f + 1) * width] = value()
        copy = pltpu.make_async_copy(result.at[place], out_ref.at[place], sems.at[f])
        copy.start()
        copies.append(copy)
    for copy in copies:
        copy.wait()


def last_plain_kernel(faces, product_ref, early_inverse, late_inverse, *refs):
    spread_ref, answer_ref, *inputs = refs[:-3]
    ncon, width = product_ref.shape[1:]
    number = face_arrays(lax.axis_size(AXES[2]))
    theirs = receive(inputs[:number], AXES[2])
    near = receive(inputs[number:-number], AXES[1]) + receive(inputs[-number:], AXES[2])
    values = {}
    for f in range(2, FACES):
        mine = answer_ref[f * ncon : (f + 1) * ncon]
        if f < 4:
            values[f] = functools.partial(last_product, spread_ref[f], mine, near[f - 2])
        else:
            values[f] = functools.partial(
                through,
                find(faces, (early_inverse, late_inverse), f),
                product_ref[f],
                theirs[f - 4],
                mine,
                near[f - 2],
            )
    last_faces(values, width, *refs[-3:])


def last_near_kernel(faces, flag_ref, product_ref, early_inverse, late_inverse, *refs):
    spread_ref, here_answer, there_answer = refs[:3]
    theirs = receive(refs[3:-3], AXES[2])
    ncon, width = product_ref.shape[1:]

    def answer(flag, f):
        place = slice(f * ncon, (f + 1) * ncon)
        hit = flag_ref[flag : flag + 1, 0:1] > 0.5
        return jnp.where(hit, here_answer[place], there_answer[place])

    values = {}
    for f in (2, 3):
        values[f] = functools.partial(
            last_product, spread_ref[f], answer(0, f), answer(f, f ^ 1)
        )
    for f in (4, 5):
        values[f] = functools.partial(
            through,
            find(faces, (early_inverse, late_inverse), f),
            product_ref[f],
            theirs[f - 4],
            answer(0, f),
            answer(f, f ^ 1),
        )
    last_faces(values, width, *refs[-3:])


def last_far_kernel(ncon, spread_ref, rows_ref, *refs):
    theirs = receive(refs[:-4], AXES[0])
    values = {}
    for f in range(2):
        mine = rows_ref[f * ncon : (f + 1) * ncon]
        values[f] = functools.partial(last_product, spread_ref[f], mine, theirs[f])
    last_faces(values, spread_ref.shape[1], *refs[-3:])


def per_device(schur, start_block, resid, group_of):
    matrix = schur[0, 0, 0]
    matrix = pltpu.with_memory_space_constraint(matrix, pltpu.HBM)
    starts = start_block[0, 0, 0].transpose(0, 2, 1)
    right = resid[0, 0, 0]
    order, columns = right.shape
    ncon, width = starts.shape[1:]
    counts = [lax.axis_size(axis) for axis in AXES]
    arrays = sum(face_arrays(count) for count in counts)
    coarse = FACES * ncon
    size = 2 * ncon
    half = width // 2
    lanes = size * BLOCKS * (BLOCKS + 1) // 2
    right_lanes = BLOCKS * columns
    uppers = FACES * (FACES - 1) // 2
    anywhere = pl.BlockSpec(memory_space=pl.ANY)
    main_memory = pl.BlockSpec(memory_space=pltpu.HBM)
    scalars = pl.BlockSpec(memory_space=pltpu.SMEM)
    early, late = (4, 5), (0, 1, 2, 3)
    faces = (early, late)
    planes = counts[2]

    def shape(*dims):
        return jax.ShapeDtypeStruct(dims, jnp.float32)

    def halves(count):
        return jax.ShapeDtypeStruct((count, 2, width, width), jnp.bfloat16)

    def params(mib):
        return pltpu.CompilerParams(vmem_limit_bytes=mib * MIB)

    def cost(us):
        return pl.CostEstimate(flops=us * 10**9, bytes_accessed=2**20, transcendentals=0)

    *packed, own = pl.pallas_call(
        functools.partial(pack_kernel, counts, width),
        out_shape=face_shapes(counts[0], (width + 8 + 2 * ncon, half))
        + face_shapes(counts[1], (width + 8 + 2 * ncon, half))
        + face_shapes(counts[2], (width + 8, half))
        + [shape(FACES, width, width)],
        in_specs=[main_memory, main_memory],
        out_specs=vmem_specs(arrays + 1),
        scratch_shapes=[
            pltpu.VMEM((4, ncon, width), jnp.float32),
            pltpu.SemaphoreType.DMA((FACES,)),
            pltpu.SemaphoreType.DMA,
        ],
        compiler_params=params(12),
    )(matrix, pltpu.with_memory_space_constraint(starts, pltpu.HBM))
    ends = [sum(face_arrays(count) for count in counts[:position]) for position in range(4)]
    got = {}
    for position in (2, 0, 1):
        got[position] = exchange(packed[ends[position] : ends[position + 1]], AXES[position])

    own_halves, upper_halves, flags = pl.pallas_call(
        functools.partial(halves_kernel, planes),
        out_shape=[halves(FACES), halves(uppers), shape(8, 128)],
        in_specs=[main_memory, scalars] + vmem_specs(1),
        out_specs=vmem_specs(3),
        scratch_shapes=[
            pltpu.VMEM((FACES - 1, width, order), jnp.float32),
            pltpu.SemaphoreType.DMA((FACES - 1,)),
        ],
        compiler_params=params(24),
        cost_estimate=cost(2),
    )(matrix, group_of, own)

    early_basis, early_partner, early_inverse = pl.pallas_call(
        functools.partial(early_kernel, AXES[2:3], early),
        out_shape=[shape(len(early), ncon, width)] + [halves(len(early))] * 2,
        in_specs=vmem_specs(len(got[2]) + 3),
        out_specs=vmem_specs(3),
        compiler_params=params(16),
        cost_estimate=cost(2),
    )(*got[2], own, own_halves, starts)

    payload, product, late_partner, late_inverse = pl.pallas_call(
        functools.partial(main_kernel, (AXES[0], AXES[1]), early, late),
        out_shape=[shape(size, lanes + right_lanes), shape(FACES, ncon, width)]
        + [halves(len(late))] * 2,
        in_specs=vmem_specs(len(got[0]) + len(got[1]) + 6),
        out_specs=vmem_specs(4),
        compiler_params=params(24),
        cost_estimate=cost(8),
    )(*got[0], *got[1], own, own_halves, upper_halves, starts, right, early_basis)

    partners = [early_partner, late_partner]
    inverses = [early_inverse, late_inverse]
    their_basis, their_product = pl.pallas_call(
        functools.partial(theirs_kernel, faces, ncon),
        out_shape=[shape(4, ncon, width)] * 2,
        in_specs=vmem_specs(5 + len(got[0]) + len(got[1])),
        out_specs=vmem_specs(2),
        compiler_params=params(16),
        cost_estimate=cost(2),
    )(own_halves, *got[0], *got[1], *partners, *inverses)

    def spread_of(token):
        return pl.pallas_call(
            functools.partial(spread_kernel, faces),
            out_shape=jax.ShapeDtypeStruct((4, width, 3 * size), jnp.bfloat16),
            in_specs=[anywhere] + vmem_specs(5),
            out_specs=vmem_specs(1)[0],
            compiler_params=params(16),
            cost_estimate=cost(2),
        )(token, their_basis, their_product, product, *inverses)

    def solve(matrices, rights, unread):
        return pl.pallas_call(
            functools.partial(solve_kernel, size, len(matrices), columns),
            out_shape=shape(coarse, columns),
            in_specs=vmem_specs(2 * len(matrices)) + [anywhere] * len(unread),
            out_specs=vmem_specs(1)[0],
            compiler_params=params(12),
            cost_estimate=cost(7),
        )(*matrices, *rights, *unread)

    result = dict(
        out_shape=shape(order, columns),
        out_specs=main_memory,
        scratch_shapes=[
            pltpu.VMEM((order, columns), jnp.float32),
            pltpu.SemaphoreType.DMA((FACES,)),
        ],
        compiler_params=params(12),
        cost_estimate=cost(1),
    )
    groups = group_of.shape[0] // GROUP_SIZE
    if groups == 2 and counts[1] == 4 and planes == 2:
        core_swap, chip_x, chip_y = flipped("gy", 1), flipped("gy", 2), flipped("gz", 1)
        other = lax.ppermute(payload, "gy", core_swap)
        left, rest = pl.pallas_call(
            choose_kernel,
            out_shape=[shape(size, lanes), shape(size, right_lanes)],
            in_specs=vmem_specs(3),
            out_specs=vmem_specs(2),
            compiler_params=params(8),
        )(flags, payload, other)
        left_moved = lax.ppermute(left, "gy", chip_x)
        rest_moved = lax.ppermute(rest, "gz", chip_y)
        left_last, rest_last, *sent = pl.pallas_call(
            add_kernel,
            out_shape=[shape(size, lanes), shape(size, right_lanes)]
            + face_shapes(counts[2], (ncon, width)),
            in_specs=vmem_specs(5) + [anywhere],
            out_specs=vmem_specs(2 + face_arrays(counts[2])),
            compiler_params=params(8),
        )(left, left_moved, rest, rest_moved, product, their_basis)
        left_other = lax.ppermute(left_last, "gz", chip_y)
        rest_other = lax.ppermute(rest_last, "gy", chip_x)
        theirs = exchange(sent, AXES[2])
        spread = spread_of(left_last)
        answer = solve([left_last, left_other], [rest_last, rest_other], [spread])
        there = lax.ppermute(answer, "gy", core_swap)
        *sent, mine = pl.pallas_call(
            functools.partial(rows_kernel, ncon),
            out_shape=face_shapes(counts[0], (ncon, columns)) + [shape(size, columns)],
            in_specs=vmem_specs(3),
            out_specs=vmem_specs(face_arrays(counts[0]) + 1),
            compiler_params=params(8),
        )(flags, answer, there)
        across = exchange(sent, AXES[0])
        correction = pl.pallas_call(
            functools.partial(last_near_kernel, faces),
            in_specs=vmem_specs(7 + len(theirs)),
            **result,
        )(flags, product, *inverses, spread, answer, there, *theirs)
    else:
        y, z = lax.axis_index("gy"), lax.axis_index("gz")
        member_of = group_of[y * planes + z]
        chosen = jnp.arange(groups, dtype=jnp.int32) == member_of
        total = lax.psum(jnp.where(chosen[:, None, None], payload[None], 0.0), ("gy", "gz"))
        total = lax.dynamic_index_in_dim(total, member_of, 0, keepdims=False)
        spread = spread_of(payload)
        answer = solve([total[:, :lanes]], [total[:, lanes:]], [])

        def from_near(faces_of, axis):
            even, odd = faces_of
            if lax.axis_size(axis) == 2:
                return exchange([jnp.stack([even, odd])], axis)
            upward = is_even(axis)
            return exchange([jnp.where(upward, even, odd), jnp.where(upward, odd, even)], axis)

        blocks = answer.reshape(FACES, ncon, columns)
        near = [
            *from_near(product[4:6], AXES[2]),
            *from_near(blocks[2:4], AXES[1]),
            *from_near(blocks[4:6], AXES[2]),
        ]
        mine = answer[:size]
        across = from_near(blocks[:2], AXES[0])
        correction = pl.pallas_call(
            functools.partial(last_plain_kernel, faces),
            in_specs=vmem_specs(5 + len(near)),
            **result,
        )(product, *inverses, spread, answer, *near)
    correction = pl.pallas_call(
        functools.partial(last_far_kernel, ncon),
        in_specs=vmem_specs(2 + len(across)) + [main_memory],
        input_output_aliases={2 + len(across): 0},
        **result,
    )(spread, mine, *across, correction)
    return correction[None, None, None]


def solution(mesh):
    in_specs = (
        P("gx", "gy", "gz", None, None),
        P("gx", "gy", "gz", None, None, None),
        P("gx", "gy", "gz", None, None),
        P(),
    )
    out_specs = P("gx", "gy", "gz", None, None)
    return jax.shard_map(
        per_device, mesh=mesh, in_specs=in_specs, out_specs=out_specs, check_vma=False
    )
```

```python
import functools

import jax
import jax.numpy as jnp
from jax import lax
from jax.experimental import pallas as pl
from jax.experimental.pallas import tpu as pltpu
from jax.sharding import PartitionSpec as P

NS_ITERS = 3
SUB_ITERS = 2
GROUP_SIZE = 4
FACES = 6
BLOCKS = FACES // 2
AXES = ("gx", "gy", "gz")
MIB = 1024 * 1024

precise = lax.Precision.HIGHEST


def dot(left, right, dims=((1,), (0,))):
    return lax.dot_general(
        left, right, (dims, ((), ())), precision=precise, preferred_element_type=jnp.float32
    )


def split(value):
    high = value.astype(jnp.bfloat16)
    return high, (value - high.astype(jnp.float32)).astype(jnp.bfloat16)


def wide(left, right):
    return lax.dot_general(
        jnp.concatenate([left[0], left[0], left[1]], axis=1),
        jnp.concatenate([right[0], right[1], right[0]], axis=0),
        (((1,), (0,)), ((), ())),
        preferred_element_type=jnp.float32,
    )


def stacked(value):
    return jnp.concatenate(split(value), axis=0)


def thin(rows, matrix):
    out = lax.dot_general(
        jnp.concatenate([rows, rows], axis=1),
        jnp.concatenate(matrix, axis=0),
        (((1,), (0,)), ((), ())),
        preferred_element_type=jnp.float32,
    )
    half = rows.shape[0] // 2
    return out[:half] + out[half:]


def triple(left, right, dims=((1,), (0,))):
    (left_high, left_low), (right_high, right_low) = split(left), split(right)
    total = None
    for one, other in ((left_high, right_high), (left_high, right_low), (left_low, right_high)):
        part = lax.dot_general(
            one, other, (dims, ((), ())), preferred_element_type=jnp.float32
        )
        total = part if total is None else total + part
    return total


def iota(shape, dim):
    return lax.broadcasted_iota(jnp.int32, shape, dim)


def flipped(axis, bit):
    return [(i, i ^ bit) for i in range(lax.axis_size(axis))]


def outer_pairs(axis):
    count = lax.axis_size(axis)
    return [(i, (i + 1 if i % 2 else i - 1) % count) for i in range(count)]


def face_arrays(count):
    return 1 if count == 2 else 2


def exchange(arrays, axis):
    if lax.axis_size(axis) == 2:
        return [lax.ppermute(arrays[0], axis, flipped(axis, 1))]
    return [
        lax.ppermute(arrays[0], axis, outer_pairs(axis)),
        lax.ppermute(arrays[1], axis, flipped(axis, 1)),
    ]


def is_even(axis):
    return lax.rem(lax.axis_index(axis), 2) == 0


def send(refs, axis, even, odd):
    if lax.axis_size(axis) == 2:
        refs[0][0] = even
        refs[0][1] = odd
    else:
        upward = is_even(axis)
        refs[0][...] = jnp.where(upward, even, odd)
        refs[1][...] = jnp.where(upward, odd, even)


def receive(refs, axis):
    if lax.axis_size(axis) == 2:
        return refs[0][1], refs[0][0]
    upward = is_even(axis)
    first, second = refs[0][...], refs[1][...]
    return jnp.where(upward, first, second), jnp.where(upward, second, first)


def face_shapes(count, shape):
    if count == 2:
        return [jax.ShapeDtypeStruct((2,) + shape, jnp.float32)]
    return [jax.ShapeDtypeStruct(shape, jnp.float32)] * 2


def vmem_specs(count):
    return [pl.BlockSpec(memory_space=pltpu.VMEM)] * count


def pack_kernel(counts, width, schur_ref, starts_ref, *refs):
    outs, blocks = refs[:-4], refs[-4]
    starts, sems, start_sem = refs[-3:]
    half = width // 2
    copies = []
    for f in range(FACES):
        place = pl.ds(f * width, width)
        copy = pltpu.make_async_copy(schur_ref.at[place, place], blocks.at[f], sems.at[f])
        copy.start()
        copies.append(copy)
    start_copy = pltpu.make_async_copy(starts_ref.at[pl.ds(0, 4)], starts, start_sem)
    start_copy.start()
    row, col = iota((half, half), 0), iota((half, half), 1)
    start_copy.wait()

    def pack(f):
        copies[f].wait()
        first = blocks[f, 0:half, 0:half]
        second = blocks[f, half:width, half:width]
        diag = jnp.sum(jnp.where(row == col, second, 0.0), axis=0, keepdims=True)
        mixed = jnp.where(row >= col, first, second)
        tail = jnp.broadcast_to(diag, (8, half))
        parts = [blocks[f, half:width, 0:half], mixed, tail]
        if f < 4:
            parts += [starts[f, :, :half], starts[f, :, half:]]
        return jnp.concatenate(parts, axis=0)

    done = 0
    for position, axis in enumerate(AXES):
        number = face_arrays(counts[position])
        send(outs[done : done + number], axis, pack(2 * position), pack(2 * position + 1))
        done += number


def unpack(packed):
    half = packed.shape[1]
    row, col = iota((half, half), 0), iota((half, half), 1)
    low = packed[0:half]
    mixed = packed[half : 2 * half]
    flip = mixed.T
    first = jnp.where(row >= col, mixed, flip)
    second = jnp.where(row < col, mixed, flip)
    second = jnp.where(row == col, packed[2 * half : 2 * half + 1], second)
    return jnp.concatenate(
        [jnp.concatenate([first, low.T], axis=1), jnp.concatenate([low, second], axis=1)], axis=0
    )


def unpack_starts(packed, ncon):
    half = packed.shape[1]
    rows = packed[2 * half + 8 :]
    return jnp.concatenate([rows[:ncon], rows[ncon:]], axis=1)


def factor_inverses(grams):
    size = grams[0].shape[0]
    strips, block, lanes = size // 8, 8, 128
    full = (block, lanes)
    beside = lanes // (2 * size)
    one = jnp.where(iota((size, size), 0) == iota((size, size), 1), 1.0, 0.0)
    states = []
    for first in range(0, len(grams), beside):
        parts = [part for gram in grams[first : first + beside] for part in (gram, one)]
        whole = jnp.concatenate(parts, axis=1)
        states.append([whole[8 * s : 8 * s + 8] for s in range(strips)])
    below = iota(full, 0)
    base = iota(full, 1) // (2 * size) * (2 * size)

    def column(rows, k):
        if beside == 1:
            return jnp.broadcast_to(rows[:, k : k + 1], full)
        return jnp.take_along_axis(rows, base + k, axis=1, mode="promise_in_bounds")

    def line_of(rows, line):
        return jnp.broadcast_to(rows[line : line + 1], full)

    roots = [[None] * strips for _ in states]
    for strip in range(strips):
        start = strip * block
        columns = [
            [[column(work[s], start + j) for s in range(strip, strips)] for j in range(block)]
            for work in states
        ]
        heads = [[column_set[0] for column_set in per_state] for per_state in columns]
        lowers = [work[strip] for work in states]
        solved = list(lowers)
        pivots = [jnp.ones(full, jnp.float32) for _ in states]
        scales = list(pivots)

        def eliminate(i, j, scale, pivot, side):
            cols = heads[i]
            factor = jnp.where(below != j, cols[j] * scale, 0.0)
            for later in range(j + 1, block):
                use = side if later == j + 1 and side is not None else line_of(cols[later], j)
                cols[later] = cols[later] - factor * use
            row = line_of(lowers[i], j)
            solved[i] = solved[i] - factor * row
            lowers[i] = lowers[i] - jnp.where(below > j, factor, 0.0) * row
            pivots[i] = jnp.where(below == j, pivot, pivots[i])
            scales[i] = jnp.where(below == j, scale, scales[i])

        for j in range(0, block, 2):
            for i in range(len(states)):
                cols = heads[i]
                corner, side = line_of(cols[j], j), line_of(cols[j], j + 1)
                last = line_of(cols[j + 1], j + 1)
                minor = corner * last - side * side
                scale = 1.0 / corner
                eliminate(i, j, scale, corner, side)
                eliminate(i, j + 1, corner * (1.0 / minor), minor * scale, None)
        for i, work in enumerate(states):
            work[strip] = lowers[i]
            roots[i][strip] = lax.rsqrt(pivots[i])
            if strip == strips - 1:
                continue
            answer = solved[i] * scales[i]
            rows = [line_of(answer, j) for j in range(block)]
            for s in range(strip + 1, strips):
                for j in range(block):
                    work[s] = work[s] - columns[i][j][s - strip] * rows[j]
    results = []
    for i, work in enumerate(states):
        scaled = jnp.concatenate([work[s] * roots[i][s] for s in range(strips)], axis=0)
        for m in range(beside):
            begin = (2 * m + 1) * size
            results.append(scaled[:, begin : begin + size])
    return results


def factor_inverse(gram):
    size = gram.shape[0]
    strips, block, lanes = size // 8, 8, 128
    full = (block, lanes)
    parts = [gram, jnp.where(iota((size, size), 0) == iota((size, size), 1), 1.0, 0.0)]
    if 2 * size < lanes:
        parts.append(jnp.zeros((size, lanes - 2 * size), jnp.float32))
    whole = jnp.concatenate(parts, axis=1)
    work = [whole[8 * s : 8 * s + 8] for s in range(strips)]
    below = iota(full, 0)

    def line_of(rows, line):
        return jnp.broadcast_to(rows[line : line + 1], full)

    for strip in range(strips):
        start = strip * block
        active = range(strip, strips)
        cols = [
            {s: jnp.broadcast_to(work[s][:, start + j : start + j + 1], full) for s in active}
            for j in range(block)
        ]
        factors = []

        def eliminate(j, scale):
            factor = {s: cols[j][s] * scale for s in active}
            factor[strip] = jnp.where(below > j, factor[strip], 0.0)
            for later in range(j + 1, block):
                head = line_of(cols[later][strip], j)
                for s in active:
                    cols[later][s] = cols[later][s] - factor[s] * head
            factors.append(factor)

        for j in range(0, block, 2):
            corner = line_of(cols[j][strip], j)
            side = line_of(cols[j][strip], j + 1)
            last = line_of(cols[j + 1][strip], j + 1)
            inverse = 1.0 / (corner * last - side * side)
            eliminate(j, 1.0 / corner)
            eliminate(j + 1, corner * inverse)
        for j in range(block):
            row = line_of(work[strip], j)
            for s in active:
                if s == strip and j == block - 1:
                    continue
                work[s] = work[s] - factors[j][s] * row
    parts = []
    for s in range(strips):
        place = iota((8, size), 0) + 8 * s == iota((8, size), 1)
        pivot = jnp.sum(jnp.where(place, work[s][:, :size], 0.0), axis=1, keepdims=True)
        parts.append(work[s][:, size : 2 * size] * lax.rsqrt(pivot))
    return jnp.concatenate(parts, axis=0)


def member(group_ref, planes, dy=0, dz=0):
    y, z = lax.axis_index("gy"), lax.axis_index("gz")
    rows = lax.axis_size("gy")
    return group_ref[lax.rem(y + dy + rows, rows) * planes + lax.rem(z + dz + planes, planes)]


def store(ref, f, value):
    ref[f, 0], ref[f, 1] = split(value)


def load(ref, f):
    return ref[f, 0], ref[f, 1]


def upper_index(f, g):
    return sum(FACES - 1 - i for i in range(f)) + g - f - 1


def halves_kernel(planes, schur_ref, group_ref, own_ref, own_out, upper_out, flag_out, *scratch):
    upper_ref, sems = scratch
    width = own_ref.shape[1]
    strips = []
    for f in range(FACES - 1):
        rest = (FACES - 1 - f) * width
        copy = pltpu.make_async_copy(
            schur_ref.at[pl.ds(f * width, width), pl.ds((f + 1) * width, rest)],
            upper_ref.at[f, :, pl.ds((f + 1) * width, rest)],
            sems.at[f],
        )
        copy.start()
        strips.append(copy)
    core = lax.rem(lax.axis_index("gy"), 2)
    near = [(0, 0), (1 - 2 * core, 0), (-1, 0), (1, 0), (0, -1), (0, 1)]
    row = iota(flag_out.shape, 0)
    flags = jnp.zeros(flag_out.shape, jnp.float32)
    for i, (dy, dz) in enumerate(near):
        hit = member(group_ref, planes, dy, dz) == core
        flags = jnp.where(row == i, jnp.where(hit, 1.0, 0.0), flags)
    flag_out[...] = flags
    for f in range(FACES):
        store(own_out, f, own_ref[f])
    for f in range(FACES - 1):
        strips[f].wait()
        for g in range(f + 1, FACES):
            store(upper_out, upper_index(f, g), upper_ref[f, :, g * width : (g + 1) * width])


def inverses_of(packed, owns, partner_ref):
    width = owns[0].shape[1]
    half = width // 2
    eye = iota((half, half), 0) == iota((half, half), 1)
    whole_eye = iota((width, width), 0) == iota((width, width), 1)
    powers, sums, downs = [], [], []
    for f in range(len(packed)):
        partner = unpack(packed[f])
        store(partner_ref, f, partner)
        total = owns[f] + partner
        across, down = [], []
        for start in (0, half):
            block = total[start : start + half, start : start + half]
            diagonal = jnp.where(eye, block, 0.0)
            across.append(1.0 / jnp.sum(diagonal, axis=0, keepdims=True))
            down.append(1.0 / jnp.sum(diagonal, axis=1, keepdims=True))
        downs.append(jnp.concatenate(down, axis=0))
        power = jnp.where(whole_eye, 0.0, -total * jnp.concatenate(across, axis=1))
        powers.append(split(power))
        sums.append(jnp.where(whole_eye, 1.0, power))
    for step in range(1, NS_ITERS):
        powers = [split(wide(power, power)) for power in powers]
        sums = [total + wide(split(total), power) for total, power in zip(sums, powers)]
    return [down * total for down, total in zip(downs, sums)]


def unit_rows(basis):
    return [b * lax.rsqrt(jnp.sum(b * b, axis=1, keepdims=True)) for b in basis]


def sweep_basis(before, inverse, after, basis):
    for matrices in (before, inverse, after):
        basis = [thin(stacked(b), matrix) for b, matrix in zip(basis, matrices)]
    return unit_rows(basis)


def early_kernel(axes, faces, *refs):
    arrays = len(refs) - 6
    inputs = refs[:arrays]
    own_ref, halves_ref, starts_ref, basis_out, partner_out, inverse_out = refs[arrays:]
    count = len(faces)
    packed = []
    done = 0
    for axis in axes:
        number = face_arrays(lax.axis_size(axis))
        packed += receive(inputs[done : done + number], axis)
        done += number
    inverses = inverses_of(packed, [own_ref[f] for f in faces], partner_out)
    for i in range(count):
        store(inverse_out, i, inverses[i])
    basis = [starts_ref[f] for f in faces]
    matrices = [
        [load(partner_out, i) for i in range(count)],
        [load(inverse_out, i) for i in range(count)],
        [load(halves_ref, f) for f in faces],
    ]
    for sweep in range(SUB_ITERS):
        basis = sweep_basis(*matrices, basis)
    for i in range(count):
        basis_out[i] = basis[i]


def main_kernel(axes, early, late, *refs):
    arrays = len(refs) - 10
    inputs = refs[:arrays]
    own_ref, halves_ref, upper_ref, starts_ref, resid_ref, early_basis = refs[arrays : arrays + 6]
    payload_ref, product_ref, partner_out, inverse_out = refs[arrays + 6 :]
    ncon, width = starts_ref.shape[1:]
    columns = resid_ref.shape[1]
    sides = {}
    rights = {}
    grams = {}
    vectors = {}
    count = len(late)

    def project(f, basis):
        vectors[f] = basis
        rows = stacked(basis)
        grams[f] = dot(basis, basis, ((1,), (1,)))
        side = {f: thin(rows, load(halves_ref, f))}
        for g in range(f + 1, FACES):
            side[g] = thin(rows, load(upper_ref, upper_index(f, g)))
        sides[f] = side
        rights[f] = thin(rows, split(resid_ref[f * width : (f + 1) * width]))

    packed = []
    done = 0
    for axis in axes:
        number = face_arrays(lax.axis_size(axis))
        packed += receive(inputs[done : done + number], axis)
        done += number
    inverses = inverses_of(packed, [own_ref[f] for f in late], partner_out)
    pending = [(f, early_basis[i]) for i, f in enumerate(early)]
    for i in range(count):
        store(inverse_out, i, inverses[i])
    basis = [starts_ref[f] for f in late]
    matrices = [
        [load(partner_out, i) for i in range(count)],
        [load(inverse_out, i) for i in range(count)],
        [load(halves_ref, f) for f in late],
    ]
    for sweep in range(SUB_ITERS):
        basis = sweep_basis(*matrices, basis)
        if pending:
            project(*pending.pop(0))
    for item in pending:
        project(*item)
    for i, f in enumerate(late):
        project(f, basis[i])
    tall = {}
    for g in range(FACES):
        column = jnp.concatenate([sides[f][g] for f in range(g + 1)], axis=0)
        column = triple(column, vectors[g], ((1,), (1,)))
        for f in range(g + 1):
            tall[f, g] = column[f * ncon : (f + 1) * ncon]
    for f in range(0, FACES, 2):
        tall[f + 1, f] = tall[f, f + 1].T
    zero = jnp.zeros((ncon, ncon), jnp.float32)

    def square(parts):
        lines = []
        for f in range(FACES):
            line = [parts.get((f, g), zero) for g in range(FACES)]
            lines.append(jnp.concatenate(line, axis=1))
        return jnp.concatenate(lines, axis=0)

    coarse = square(tall)
    right = jnp.concatenate([rights[f] for f in range(FACES)], axis=0)
    factors = factor_inverses([grams[f] for f in range(FACES)])
    factor = square({(f, f): factors[f] for f in range(FACES)})
    coarse = triple(factor, triple(coarse, factor, ((1,), (1,))))
    right = triple(factor, right)
    for f in range(FACES):
        product_ref[f] = triple(factors[f], sides[f][f])
    size = 2 * ncon
    blocks = {
        (b, c): coarse[b * size : (b + 1) * size, c * size : (c + 1) * size]
        for b in range(BLOCKS)
        for c in range(b, BLOCKS)
    }
    payload_ref[...] = jnp.concatenate([pack_coarse(blocks, size), right], axis=0)


def pack_coarse(blocks, size):
    row, col = iota((size, size), 0), iota((size, size), 1)
    diagonal = jnp.sum(jnp.where(row == col, blocks[1, 1], 0.0), axis=0, keepdims=True)
    corner = (row == 1) & (col == size - 1)
    above = jnp.where(row == 0, diagonal, jnp.where(corner, diagonal[:, 0:1], 0.0))
    shared = jnp.where(row >= col, blocks[0, 0], blocks[1, 1])
    third = jnp.where(row >= col, blocks[2, 2], above)
    half = size // 2
    return jnp.concatenate(
        [
            jnp.concatenate([shared, blocks[0, 1]], axis=1),
            jnp.concatenate([blocks[0, 2], blocks[1, 2]], axis=1),
            jnp.concatenate([third[:half], third[half:]], axis=1),
        ],
        axis=0,
    )


def unpack_coarse(packed, size):
    row, col = iota((size, size), 0), iota((size, size), 1)
    shared = packed[:size, :size]
    flip = shared.T
    tail = packed[2 * size :]
    third = jnp.concatenate([tail[:, :size], tail[:, size:]], axis=0)
    first = jnp.broadcast_to(third[1:2, size - 1 : size], (1, size))
    diagonal = jnp.where(iota((1, size), 1) == 0, first, third[0:1])
    second = jnp.where(row < col, shared, jnp.where(row > col, flip, diagonal))
    return {
        (0, 0): jnp.where(row >= col, shared, flip),
        (1, 1): second,
        (2, 2): jnp.where(row >= col, third, third.T),
        (0, 1): packed[:size, size:],
        (0, 2): packed[size : 2 * size, :size],
        (1, 2): packed[size : 2 * size, size:],
    }


def find(faces, refs, f):
    for group, ref in zip(faces, refs):
        if f in group:
            return load(ref, list(group).index(f))


def theirs_kernel(faces, ncon, own_ref, *refs):
    inputs, partner_refs, inverse_refs = refs[:-6], refs[-6:-4], refs[-4:-2]
    basis_out, product_out = refs[-2:]
    basis = []
    done = 0
    for axis in AXES[:2]:
        number = face_arrays(lax.axis_size(axis))
        packed = receive(inputs[done : done + number], axis)
        basis += [unpack_starts(part, ncon) for part in packed]
        done += number
    count = len(basis)
    matrices = [
        [load(own_ref, f) for f in range(count)],
        [find(faces, inverse_refs, f) for f in range(count)],
        [find(faces, partner_refs, f) for f in range(count)],
    ]
    for sweep in range(SUB_ITERS):
        basis = sweep_basis(*matrices, basis)
    for f in range(count):
        basis_out[f] = basis[f]
        product_out[f] = thin(stacked(basis[f]), matrices[2][f])


def spread_kernel(faces, unread, basis_ref, theirs_ref, product_ref, *refs):
    inverse_refs, out_ref = refs[:2], refs[2]
    basis = [basis_ref[f] for f in range(basis_ref.shape[0])]
    factors = factor_inverses([dot(b, b, ((1,), (1,))) for b in basis])
    for f in range(len(basis)):
        theirs = triple(factors[f], theirs_ref[f])
        both = jnp.concatenate([product_ref[f], theirs], axis=0)
        high, low = split(thin(stacked(both), find(faces, inverse_refs, f)).T)
        out_ref[f] = jnp.concatenate([high, high, low], axis=1)


def choose_kernel(flag_ref, here_ref, there_ref, matrix_ref, right_ref):
    mine = flag_ref[0:1, 0:1] > 0.5
    other = flag_ref[1:2, 0:1] > 0.5
    total = jnp.where(mine, here_ref[...], 0.0) + jnp.where(other, there_ref[...], 0.0)
    rows = matrix_ref.shape[0]
    matrix_ref[...] = total[:rows]
    right_ref[...] = total[rows:]


def add_kernel(first_ref, second_ref, third_ref, fourth_ref, product_ref, unread, *refs):
    matrix_ref, right_ref, *sent = refs
    matrix_ref[...] = first_ref[...] + second_ref[...]
    right_ref[...] = third_ref[...] + fourth_ref[...]
    send(sent, AXES[2], product_ref[4], product_ref[5])


def solve_kernel(size, terms, columns, *refs):
    upper, lower = refs[0][...], refs[terms][...]
    for term in range(1, terms):
        upper = upper + refs[term][...]
        lower = lower + refs[terms + term][...]
    answer_ref = refs[-1]
    total = jnp.concatenate([upper, lower], axis=0)
    rows = 2 * size + size // 2
    blocks, right = unpack_coarse(total[:rows], size), total[rows:]
    eye = iota((size, size), 0) == iota((size, size), 1)
    downs, acrosses, rights = [], [], []
    for b in range(BLOCKS):
        diagonal = jnp.where(eye, blocks[b, b], 0.0)
        downs.append(lax.rsqrt(jnp.sum(diagonal, axis=1, keepdims=True)))
        acrosses.append(lax.rsqrt(jnp.sum(diagonal, axis=0, keepdims=True)))
        rights.append(downs[b] * right[b * size : (b + 1) * size])
    for b in range(BLOCKS):
        for c in range(b, BLOCKS):
            blocks[b, c] = downs[b] * blocks[b, c] * acrosses[c]
            if c > b:
                blocks[c, b] = blocks[b, c].T
    for b in range(BLOCKS):
        inverse = factor_inverse(blocks[b, b])
        later = range(b + 1, BLOCKS)
        row = triple(inverse, jnp.concatenate([rights[b]] + [blocks[b, c] for c in later], axis=1))
        if later:
            column = jnp.concatenate([blocks[c, b] for c in later], axis=0)
            change = triple(triple(column, inverse, ((1,), (1,))), row)
        for i, c in enumerate(later):
            part = change[i * size : (i + 1) * size]
            rights[c] = rights[c] - part[:, :columns]
            for j, d in enumerate(later):
                start = columns + j * size
                blocks[c, d] = blocks[c, d] - part[:, start : start + size]
        row = triple(inverse, row, ((0,), (0,)))
        rights[b] = row[:, :columns]
        for c in later:
            blocks[b, c] = row[:, columns + (c - b - 1) * size : columns + (c - b) * size]
        for i in range(b):
            for c in later:
                blocks[i, c] = blocks[i, c] - triple(blocks[i, b], blocks[b, c])
            rights[i] = rights[i] - triple(blocks[i, b], rights[b])
    answer = [downs[b] * rights[b] for b in range(BLOCKS)]
    answer_ref[...] = jnp.concatenate(answer, axis=0)


def rows_kernel(ncon, flag_ref, here_ref, there_ref, *refs):
    hit = flag_ref[0:1, 0:1] > 0.5
    rows = jnp.where(hit, here_ref[: 2 * ncon], there_ref[: 2 * ncon])
    refs[-1][...] = rows
    send(refs[:-1], AXES[0], rows[:ncon], rows[ncon:])


def last_product(spread, mine, theirs):
    high, low = split(jnp.concatenate([mine, theirs], axis=0))
    return lax.dot_general(
        spread,
        jnp.concatenate([high, low, high], axis=0),
        (((1,), (0,)), ((), ())),
        preferred_element_type=jnp.float32,
    )


def through(inverse, mine, theirs, my_answer, their_answer):
    high, low = split(jnp.concatenate([mine, theirs], axis=0).T)
    spread = jnp.concatenate([high, high, low], axis=1)
    return wide(inverse, split(last_product(spread, my_answer, their_answer)))


def last_faces(values, width, out_ref, result, sems):
    copies = []
    for f, value in values.items():
        place = pl.ds(f * width, width)
        result[f * width : (f + 1) * width] = value()
        copy = pltpu.make_async_copy(result.at[place], out_ref.at[place], sems.at[f])
        copy.start()
        copies.append(copy)
    for copy in copies:
        copy.wait()


def last_plain_kernel(faces, product_ref, early_inverse, late_inverse, *refs):
    spread_ref, answer_ref, *inputs = refs[:-3]
    ncon, width = product_ref.shape[1:]
    number = face_arrays(lax.axis_size(AXES[2]))
    theirs = receive(inputs[:number], AXES[2])
    near = receive(inputs[number:-number], AXES[1]) + receive(inputs[-number:], AXES[2])
    values = {}
    for f in range(2, FACES):
        mine = answer_ref[f * ncon : (f + 1) * ncon]
        if f < 4:
            values[f] = functools.partial(last_product, spread_ref[f], mine, near[f - 2])
        else:
            values[f] = functools.partial(
                through,
                find(faces, (early_inverse, late_inverse), f),
                product_ref[f],
                theirs[f - 4],
                mine,
                near[f - 2],
            )
    last_faces(values, width, *refs[-3:])


def last_near_kernel(faces, flag_ref, product_ref, early_inverse, late_inverse, *refs):
    spread_ref, here_answer, there_answer = refs[:3]
    theirs = receive(refs[3:-3], AXES[2])
    ncon, width = product_ref.shape[1:]

    def answer(flag, f):
        place = slice(f * ncon, (f + 1) * ncon)
        hit = flag_ref[flag : flag + 1, 0:1] > 0.5
        return jnp.where(hit, here_answer[place], there_answer[place])

    values = {}
    for f in (2, 3):
        values[f] = functools.partial(
            last_product, spread_ref[f], answer(0, f), answer(f, f ^ 1)
        )
    for f in (4, 5):
        values[f] = functools.partial(
            through,
            find(faces, (early_inverse, late_inverse), f),
            product_ref[f],
            theirs[f - 4],
            answer(0, f),
            answer(f, f ^ 1),
        )
    last_faces(values, width, *refs[-3:])


def last_far_kernel(ncon, spread_ref, rows_ref, *refs):
    theirs = receive(refs[:-4], AXES[0])
    values = {}
    for f in range(2):
        mine = rows_ref[f * ncon : (f + 1) * ncon]
        values[f] = functools.partial(last_product, spread_ref[f], mine, theirs[f])
    last_faces(values, spread_ref.shape[1], *refs[-3:])


def per_device(schur, start_block, resid, group_of):
    matrix = schur[0, 0, 0]
    matrix = pltpu.with_memory_space_constraint(matrix, pltpu.HBM)
    starts = start_block[0, 0, 0].transpose(0, 2, 1)
    right = resid[0, 0, 0]
    order, columns = right.shape
    ncon, width = starts.shape[1:]
    counts = [lax.axis_size(axis) for axis in AXES]
    arrays = sum(face_arrays(count) for count in counts)
    coarse = FACES * ncon
    size = 2 * ncon
    half = width // 2
    half_rows = (2 * size + ncon + coarse) // 2
    uppers = FACES * (FACES - 1) // 2
    anywhere = pl.BlockSpec(memory_space=pl.ANY)
    main_memory = pl.BlockSpec(memory_space=pltpu.HBM)
    scalars = pl.BlockSpec(memory_space=pltpu.SMEM)
    early, late = (4, 5), (0, 1, 2, 3)
    faces = (early, late)
    planes = counts[2]

    def shape(*dims):
        return jax.ShapeDtypeStruct(dims, jnp.float32)

    def halves(count):
        return jax.ShapeDtypeStruct((count, 2, width, width), jnp.bfloat16)

    def params(mib):
        return pltpu.CompilerParams(vmem_limit_bytes=mib * MIB)

    def cost(us):
        return pl.CostEstimate(flops=us * 10**9, bytes_accessed=2**20, transcendentals=0)

    *packed, own = pl.pallas_call(
        functools.partial(pack_kernel, counts, width),
        out_shape=face_shapes(counts[0], (width + 8 + 2 * ncon, half))
        + face_shapes(counts[1], (width + 8 + 2 * ncon, half))
        + face_shapes(counts[2], (width + 8, half))
        + [shape(FACES, width, width)],
        in_specs=[main_memory, main_memory],
        out_specs=vmem_specs(arrays + 1),
        scratch_shapes=[
            pltpu.VMEM((4, ncon, width), jnp.float32),
            pltpu.SemaphoreType.DMA((FACES,)),
            pltpu.SemaphoreType.DMA,
        ],
        compiler_params=params(12),
    )(matrix, pltpu.with_memory_space_constraint(starts, pltpu.HBM))
    ends = [sum(face_arrays(count) for count in counts[:position]) for position in range(4)]
    got = {}
    for position in (2, 0, 1):
        got[position] = exchange(packed[ends[position] : ends[position + 1]], AXES[position])

    own_halves, upper_halves, flags = pl.pallas_call(
        functools.partial(halves_kernel, planes),
        out_shape=[halves(FACES), halves(uppers), shape(8, 128)],
        in_specs=[main_memory, scalars] + vmem_specs(1),
        out_specs=vmem_specs(3),
        scratch_shapes=[
            pltpu.VMEM((FACES - 1, width, order), jnp.float32),
            pltpu.SemaphoreType.DMA((FACES - 1,)),
        ],
        compiler_params=params(24),
        cost_estimate=cost(2),
    )(matrix, group_of, own)

    early_basis, early_partner, early_inverse = pl.pallas_call(
        functools.partial(early_kernel, AXES[2:3], early),
        out_shape=[shape(len(early), ncon, width)] + [halves(len(early))] * 2,
        in_specs=vmem_specs(len(got[2]) + 3),
        out_specs=vmem_specs(3),
        compiler_params=params(16),
        cost_estimate=cost(2),
    )(*got[2], own, own_halves, starts)

    payload, product, late_partner, late_inverse = pl.pallas_call(
        functools.partial(main_kernel, (AXES[0], AXES[1]), early, late),
        out_shape=[shape(2 * half_rows, columns), shape(FACES, ncon, width)]
        + [halves(len(late))] * 2,
        in_specs=vmem_specs(len(got[0]) + len(got[1]) + 6),
        out_specs=vmem_specs(4),
        compiler_params=params(24),
        cost_estimate=cost(8),
    )(*got[0], *got[1], own, own_halves, upper_halves, starts, right, early_basis)

    partners = [early_partner, late_partner]
    inverses = [early_inverse, late_inverse]
    their_basis, their_product = pl.pallas_call(
        functools.partial(theirs_kernel, faces, ncon),
        out_shape=[shape(4, ncon, width)] * 2,
        in_specs=vmem_specs(5 + len(got[0]) + len(got[1])),
        out_specs=vmem_specs(2),
        compiler_params=params(16),
        cost_estimate=cost(2),
    )(own_halves, *got[0], *got[1], *partners, *inverses)

    def spread_of(token):
        return pl.pallas_call(
            functools.partial(spread_kernel, faces),
            out_shape=jax.ShapeDtypeStruct((4, width, 3 * size), jnp.bfloat16),
            in_specs=[anywhere] + vmem_specs(5),
            out_specs=vmem_specs(1)[0],
            compiler_params=params(16),
            cost_estimate=cost(2),
        )(token, their_basis, their_product, product, *inverses)

    def solve(matrices, rights, unread):
        return pl.pallas_call(
            functools.partial(solve_kernel, size, len(matrices), columns),
            out_shape=shape(coarse, columns),
            in_specs=vmem_specs(2 * len(matrices)) + [anywhere] * len(unread),
            out_specs=vmem_specs(1)[0],
            compiler_params=params(12),
            cost_estimate=cost(7),
        )(*matrices, *rights, *unread)

    result = dict(
        out_shape=shape(order, columns),
        out_specs=main_memory,
        scratch_shapes=[
            pltpu.VMEM((order, columns), jnp.float32),
            pltpu.SemaphoreType.DMA((FACES,)),
        ],
        compiler_params=params(12),
        cost_estimate=cost(1),
    )
    groups = group_of.shape[0] // GROUP_SIZE
    if groups == 2 and counts[1] == 4 and planes == 2:
        core_swap, chip_x, chip_y = flipped("gy", 1), flipped("gy", 2), flipped("gz", 1)
        other = lax.ppermute(payload, "gy", core_swap)
        left, rest = pl.pallas_call(
            choose_kernel,
            out_shape=[shape(half_rows, columns)] * 2,
            in_specs=vmem_specs(3),
            out_specs=vmem_specs(2),
            compiler_params=params(8),
        )(flags, payload, other)
        left_moved = lax.ppermute(left, "gy", chip_x)
        rest_moved = lax.ppermute(rest, "gz", chip_y)
        left_last, rest_last, *sent = pl.pallas_call(
            add_kernel,
            out_shape=[shape(half_rows, columns)] * 2
            + face_shapes(counts[2], (ncon, width)),
            in_specs=vmem_specs(5) + [anywhere],
            out_specs=vmem_specs(2 + face_arrays(counts[2])),
            compiler_params=params(8),
        )(left, left_moved, rest, rest_moved, product, their_basis)
        left_other = lax.ppermute(left_last, "gz", chip_y)
        rest_other = lax.ppermute(rest_last, "gy", chip_x)
        theirs = exchange(sent, AXES[2])
        spread = spread_of(left_last)
        answer = solve([left_last, left_other], [rest_last, rest_other], [spread])
        there = lax.ppermute(answer, "gy", core_swap)
        *sent, mine = pl.pallas_call(
            functools.partial(rows_kernel, ncon),
            out_shape=face_shapes(counts[0], (ncon, columns)) + [shape(size, columns)],
            in_specs=vmem_specs(3),
            out_specs=vmem_specs(face_arrays(counts[0]) + 1),
            compiler_params=params(8),
        )(flags, answer, there)
        across = exchange(sent, AXES[0])
        correction = pl.pallas_call(
            functools.partial(last_near_kernel, faces),
            in_specs=vmem_specs(7 + len(theirs)),
            **result,
        )(flags, product, *inverses, spread, answer, there, *theirs)
    else:
        y, z = lax.axis_index("gy"), lax.axis_index("gz")
        member_of = group_of[y * planes + z]
        chosen = jnp.arange(groups, dtype=jnp.int32) == member_of
        total = lax.psum(jnp.where(chosen[:, None, None], payload[None], 0.0), ("gy", "gz"))
        total = lax.dynamic_index_in_dim(total, member_of, 0, keepdims=False)
        spread = spread_of(payload)
        answer = solve([total[:half_rows]], [total[half_rows:]], [])

        def from_near(faces_of, axis):
            even, odd = faces_of
            if lax.axis_size(axis) == 2:
                return exchange([jnp.stack([even, odd])], axis)
            upward = is_even(axis)
            return exchange([jnp.where(upward, even, odd), jnp.where(upward, odd, even)], axis)

        blocks = answer.reshape(FACES, ncon, columns)
        near = [
            *from_near(product[4:6], AXES[2]),
            *from_near(blocks[2:4], AXES[1]),
            *from_near(blocks[4:6], AXES[2]),
        ]
        mine = answer[:size]
        across = from_near(blocks[:2], AXES[0])
        correction = pl.pallas_call(
            functools.partial(last_plain_kernel, faces),
            in_specs=vmem_specs(5 + len(near)),
            **result,
        )(product, *inverses, spread, answer, *near)
    correction = pl.pallas_call(
        functools.partial(last_far_kernel, ncon),
        in_specs=vmem_specs(2 + len(across)) + [main_memory],
        input_output_aliases={2 + len(across): 0},
        **result,
    )(spread, mine, *across, correction)
    return correction[None, None, None]


def solution(mesh):
    in_specs = (
        P("gx", "gy", "gz", None, None),
        P("gx", "gy", "gz", None, None, None),
        P("gx", "gy", "gz", None, None),
        P(),
    )
    out_specs = P("gx", "gy", "gz", None, None)
    return jax.shard_map(
        per_device, mesh=mesh, in_specs=in_specs, out_specs=out_specs, check_vma=False
    )
```

```python
import functools

import jax
import jax.numpy as jnp
from jax import lax
from jax.experimental import pallas as pl
from jax.experimental.pallas import tpu as pltpu
from jax.sharding import PartitionSpec as P

NS_ITERS = 3
SUB_ITERS = 2
GROUP_SIZE = 4
FACES = 6
BLOCKS = FACES // 2
AXES = ("gx", "gy", "gz")
MIB = 1024 * 1024

precise = lax.Precision.HIGHEST


def dot(left, right, dims=((1,), (0,))):
    return lax.dot_general(
        left, right, (dims, ((), ())), precision=precise, preferred_element_type=jnp.float32
    )


def split(value):
    high = value.astype(jnp.bfloat16)
    return high, (value - high.astype(jnp.float32)).astype(jnp.bfloat16)


def wide(left, right):
    return lax.dot_general(
        jnp.concatenate([left[0], left[0], left[1]], axis=1),
        jnp.concatenate([right[0], right[1], right[0]], axis=0),
        (((1,), (0,)), ((), ())),
        preferred_element_type=jnp.float32,
    )


def stacked(value):
    return jnp.concatenate(split(value), axis=0)


def thin(rows, matrix):
    out = lax.dot_general(
        jnp.concatenate([rows, rows], axis=1),
        jnp.concatenate(matrix, axis=0),
        (((1,), (0,)), ((), ())),
        preferred_element_type=jnp.float32,
    )
    half = rows.shape[0] // 2
    return out[:half] + out[half:]


def triple(left, right, dims=((1,), (0,))):
    (left_high, left_low), (right_high, right_low) = split(left), split(right)
    total = None
    for one, other in ((left_high, right_high), (left_high, right_low), (left_low, right_high)):
        part = lax.dot_general(
            one, other, (dims, ((), ())), preferred_element_type=jnp.float32
        )
        total = part if total is None else total + part
    return total


def iota(shape, dim):
    return lax.broadcasted_iota(jnp.int32, shape, dim)


def flipped(axis, bit):
    return [(i, i ^ bit) for i in range(lax.axis_size(axis))]


def outer_pairs(axis):
    count = lax.axis_size(axis)
    return [(i, (i + 1 if i % 2 else i - 1) % count) for i in range(count)]


def face_arrays(count):
    return 1 if count == 2 else 2


def exchange(arrays, axis):
    if lax.axis_size(axis) == 2:
        return [lax.ppermute(arrays[0], axis, flipped(axis, 1))]
    return [
        lax.ppermute(arrays[0], axis, outer_pairs(axis)),
        lax.ppermute(arrays[1], axis, flipped(axis, 1)),
    ]


def is_even(axis):
    return lax.rem(lax.axis_index(axis), 2) == 0


def send(refs, axis, even, odd):
    if lax.axis_size(axis) == 2:
        refs[0][0] = even
        refs[0][1] = odd
    else:
        upward = is_even(axis)
        refs[0][...] = jnp.where(upward, even, odd)
        refs[1][...] = jnp.where(upward, odd, even)


def receive(refs, axis):
    if lax.axis_size(axis) == 2:
        return refs[0][1], refs[0][0]
    upward = is_even(axis)
    first, second = refs[0][...], refs[1][...]
    return jnp.where(upward, first, second), jnp.where(upward, second, first)


def face_shapes(count, shape):
    if count == 2:
        return [jax.ShapeDtypeStruct((2,) + shape, jnp.float32)]
    return [jax.ShapeDtypeStruct(shape, jnp.float32)] * 2


def vmem_specs(count):
    return [pl.BlockSpec(memory_space=pltpu.VMEM)] * count


def pack_kernel(counts, width, schur_ref, starts_ref, *refs):
    outs, blocks = refs[:-4], refs[-4]
    starts, sems, start_sem = refs[-3:]
    half = width // 2
    copies = []
    for f in range(FACES):
        place = pl.ds(f * width, width)
        copy = pltpu.make_async_copy(schur_ref.at[place, place], blocks.at[f], sems.at[f])
        copy.start()
        copies.append(copy)
    start_copy = pltpu.make_async_copy(starts_ref.at[pl.ds(0, 4)], starts, start_sem)
    start_copy.start()
    row, col = iota((half, half), 0), iota((half, half), 1)
    start_copy.wait()

    def pack(f):
        copies[f].wait()
        first = blocks[f, 0:half, 0:half]
        second = blocks[f, half:width, half:width]
        diag = jnp.sum(jnp.where(row == col, second, 0.0), axis=0, keepdims=True)
        mixed = jnp.where(row >= col, first, second)
        tail = jnp.broadcast_to(diag, (8, half))
        parts = [blocks[f, half:width, 0:half], mixed, tail]
        if f < 4:
            parts += [starts[f, :, :half], starts[f, :, half:]]
        return jnp.concatenate(parts, axis=0)

    done = 0
    for position, axis in enumerate(AXES):
        number = face_arrays(counts[position])
        send(outs[done : done + number], axis, pack(2 * position), pack(2 * position + 1))
        done += number


def unpack(packed):
    half = packed.shape[1]
    row, col = iota((half, half), 0), iota((half, half), 1)
    low = packed[0:half]
    mixed = packed[half : 2 * half]
    flip = mixed.T
    first = jnp.where(row >= col, mixed, flip)
    second = jnp.where(row < col, mixed, flip)
    second = jnp.where(row == col, packed[2 * half : 2 * half + 1], second)
    return jnp.concatenate(
        [jnp.concatenate([first, low.T], axis=1), jnp.concatenate([low, second], axis=1)], axis=0
    )


def unpack_starts(packed, ncon):
    half = packed.shape[1]
    rows = packed[2 * half + 8 :]
    return jnp.concatenate([rows[:ncon], rows[ncon:]], axis=1)


def factor_inverses(grams):
    size = grams[0].shape[0]
    strips, block, lanes = size // 8, 8, 128
    full = (block, lanes)
    beside = lanes // (2 * size)
    one = jnp.where(iota((size, size), 0) == iota((size, size), 1), 1.0, 0.0)
    states = []
    for first in range(0, len(grams), beside):
        parts = [part for gram in grams[first : first + beside] for part in (gram, one)]
        whole = jnp.concatenate(parts, axis=1)
        states.append([whole[8 * s : 8 * s + 8] for s in range(strips)])
    below = iota(full, 0)
    base = iota(full, 1) // (2 * size) * (2 * size)

    def column(rows, k):
        if beside == 1:
            return jnp.broadcast_to(rows[:, k : k + 1], full)
        return jnp.take_along_axis(rows, base + k, axis=1, mode="promise_in_bounds")

    def line_of(rows, line):
        return jnp.broadcast_to(rows[line : line + 1], full)

    roots = [[None] * strips for _ in states]
    for strip in range(strips):
        start = strip * block
        columns = [
            [[column(work[s], start + j) for s in range(strip, strips)] for j in range(block)]
            for work in states
        ]
        heads = [[column_set[0] for column_set in per_state] for per_state in columns]
        lowers = [work[strip] for work in states]
        solved = list(lowers)
        pivots = [jnp.ones(full, jnp.float32) for _ in states]
        scales = list(pivots)

        def eliminate(i, j, scale, pivot, side):
            cols = heads[i]
            factor = jnp.where(below != j, cols[j] * scale, 0.0)
            for later in range(j + 1, block):
                use = side if later == j + 1 and side is not None else line_of(cols[later], j)
                cols[later] = cols[later] - factor * use
            row = line_of(lowers[i], j)
            solved[i] = solved[i] - factor * row
            lowers[i] = lowers[i] - jnp.where(below > j, factor, 0.0) * row
            pivots[i] = jnp.where(below == j, pivot, pivots[i])
            scales[i] = jnp.where(below == j, scale, scales[i])

        for j in range(0, block, 2):
            for i in range(len(states)):
                cols = heads[i]
                corner, side = line_of(cols[j], j), line_of(cols[j], j + 1)
                last = line_of(cols[j + 1], j + 1)
                minor = corner * last - side * side
                scale = 1.0 / corner
                eliminate(i, j, scale, corner, side)
                eliminate(i, j + 1, corner * (1.0 / minor), minor * scale, None)
        for i, work in enumerate(states):
            work[strip] = lowers[i]
            roots[i][strip] = lax.rsqrt(pivots[i])
            if strip == strips - 1:
                continue
            answer = solved[i] * scales[i]
            rows = [line_of(answer, j) for j in range(block)]
            for s in range(strip + 1, strips):
                for j in range(block):
                    work[s] = work[s] - columns[i][j][s - strip] * rows[j]
    results = []
    for i, work in enumerate(states):
        scaled = jnp.concatenate([work[s] * roots[i][s] for s in range(strips)], axis=0)
        for m in range(beside):
            begin = (2 * m + 1) * size
            results.append(scaled[:, begin : begin + size])
    return results


def factor_inverse(gram):
    size = gram.shape[0]
    strips, block, lanes = size // 8, 8, 128
    full = (block, lanes)
    parts = [gram, jnp.where(iota((size, size), 0) == iota((size, size), 1), 1.0, 0.0)]
    if 2 * size < lanes:
        parts.append(jnp.zeros((size, lanes - 2 * size), jnp.float32))
    whole = jnp.concatenate(parts, axis=1)
    work = [whole[8 * s : 8 * s + 8] for s in range(strips)]
    below = iota(full, 0)

    def line_of(rows, line):
        return jnp.broadcast_to(rows[line : line + 1], full)

    for strip in range(strips):
        start = strip * block
        active = range(strip, strips)
        cols = [
            {s: jnp.broadcast_to(work[s][:, start + j : start + j + 1], full) for s in active}
            for j in range(block)
        ]
        factors = []

        def eliminate(j, scale):
            factor = {s: cols[j][s] * scale for s in active}
            factor[strip] = jnp.where(below > j, factor[strip], 0.0)
            for later in range(j + 1, block):
                head = line_of(cols[later][strip], j)
                for s in active:
                    cols[later][s] = cols[later][s] - factor[s] * head
            factors.append(factor)

        for j in range(0, block, 2):
            corner = line_of(cols[j][strip], j)
            side = line_of(cols[j][strip], j + 1)
            last = line_of(cols[j + 1][strip], j + 1)
            inverse = 1.0 / (corner * last - side * side)
            eliminate(j, 1.0 / corner)
            eliminate(j + 1, corner * inverse)
        for j in range(block):
            row = line_of(work[strip], j)
            for s in active:
                if s == strip and j == block - 1:
                    continue
                work[s] = work[s] - factors[j][s] * row
    parts = []
    for s in range(strips):
        place = iota((8, size), 0) + 8 * s == iota((8, size), 1)
        pivot = jnp.sum(jnp.where(place, work[s][:, :size], 0.0), axis=1, keepdims=True)
        parts.append(work[s][:, size : 2 * size] * lax.rsqrt(pivot))
    return jnp.concatenate(parts, axis=0)


def member(group_ref, planes, dy=0, dz=0):
    y, z = lax.axis_index("gy"), lax.axis_index("gz")
    rows = lax.axis_size("gy")
    return group_ref[lax.rem(y + dy + rows, rows) * planes + lax.rem(z + dz + planes, planes)]


def store(ref, f, value):
    ref[f, 0], ref[f, 1] = split(value)


def load(ref, f):
    return ref[f, 0], ref[f, 1]


def upper_index(f, g):
    return sum(FACES - 1 - i for i in range(f)) + g - f - 1


def halves_kernel(planes, schur_ref, group_ref, own_ref, own_out, upper_out, flag_out, *scratch):
    upper_ref, sems = scratch
    width = own_ref.shape[1]
    strips = []
    for f in range(FACES - 1):
        rest = (FACES - 1 - f) * width
        copy = pltpu.make_async_copy(
            schur_ref.at[pl.ds(f * width, width), pl.ds((f + 1) * width, rest)],
            upper_ref.at[f, :, pl.ds((f + 1) * width, rest)],
            sems.at[f],
        )
        copy.start()
        strips.append(copy)
    core = lax.rem(lax.axis_index("gy"), 2)
    near = [(0, 0), (1 - 2 * core, 0), (-1, 0), (1, 0), (0, -1), (0, 1)]
    row = iota(flag_out.shape, 0)
    flags = jnp.zeros(flag_out.shape, jnp.float32)
    for i, (dy, dz) in enumerate(near):
        hit = member(group_ref, planes, dy, dz) == core
        flags = jnp.where(row == i, jnp.where(hit, 1.0, 0.0), flags)
    flag_out[...] = flags
    for f in range(FACES):
        store(own_out, f, own_ref[f])
    for f in range(FACES - 1):
        strips[f].wait()
        for g in range(f + 1, FACES):
            store(upper_out, upper_index(f, g), upper_ref[f, :, g * width : (g + 1) * width])


def inverses_of(packed, owns, partner_ref):
    width = owns[0].shape[1]
    half = width // 2
    eye = iota((half, half), 0) == iota((half, half), 1)
    whole_eye = iota((width, width), 0) == iota((width, width), 1)
    powers, sums, downs = [], [], []
    for f in range(len(packed)):
        partner = unpack(packed[f])
        store(partner_ref, f, partner)
        total = owns[f] + partner
        across, down = [], []
        for start in (0, half):
            block = total[start : start + half, start : start + half]
            diagonal = jnp.where(eye, block, 0.0)
            across.append(1.0 / jnp.sum(diagonal, axis=0, keepdims=True))
            down.append(1.0 / jnp.sum(diagonal, axis=1, keepdims=True))
        downs.append(jnp.concatenate(down, axis=0))
        power = jnp.where(whole_eye, 0.0, -total * jnp.concatenate(across, axis=1))
        powers.append(split(power))
        sums.append(jnp.where(whole_eye, 1.0, power))
    for step in range(1, NS_ITERS):
        powers = [split(wide(power, power)) for power in powers]
        sums = [total + wide(split(total), power) for total, power in zip(sums, powers)]
    return [down * total for down, total in zip(downs, sums)]


def unit_rows(basis):
    return [b * lax.rsqrt(jnp.sum(b * b, axis=1, keepdims=True)) for b in basis]


def sweep_basis(before, inverse, after, basis):
    for matrices in (before, inverse, after):
        basis = [thin(stacked(b), matrix) for b, matrix in zip(basis, matrices)]
    return unit_rows(basis)


def early_kernel(axes, faces, *refs):
    arrays = len(refs) - 6
    inputs = refs[:arrays]
    own_ref, halves_ref, starts_ref, basis_out, partner_out, inverse_out = refs[arrays:]
    count = len(faces)
    packed = []
    done = 0
    for axis in axes:
        number = face_arrays(lax.axis_size(axis))
        packed += receive(inputs[done : done + number], axis)
        done += number
    inverses = inverses_of(packed, [own_ref[f] for f in faces], partner_out)
    for i in range(count):
        store(inverse_out, i, inverses[i])
    basis = [starts_ref[f] for f in faces]
    matrices = [
        [load(partner_out, i) for i in range(count)],
        [load(inverse_out, i) for i in range(count)],
        [load(halves_ref, f) for f in faces],
    ]
    for sweep in range(SUB_ITERS):
        basis = sweep_basis(*matrices, basis)
    for i in range(count):
        basis_out[i] = basis[i]


def main_kernel(axes, early, late, *refs):
    arrays = len(refs) - 10
    inputs = refs[:arrays]
    own_ref, halves_ref, upper_ref, starts_ref, resid_ref, early_basis = refs[arrays : arrays + 6]
    payload_ref, product_ref, partner_out, inverse_out = refs[arrays + 6 :]
    ncon, width = starts_ref.shape[1:]
    columns = resid_ref.shape[1]
    sides = {}
    rights = {}
    grams = {}
    vectors = {}
    count = len(late)

    def project(f, basis):
        vectors[f] = basis
        rows = stacked(basis)
        grams[f] = dot(basis, basis, ((1,), (1,)))
        side = {f: thin(rows, load(halves_ref, f))}
        for g in range(f + 1, FACES):
            side[g] = thin(rows, load(upper_ref, upper_index(f, g)))
        sides[f] = side
        rights[f] = thin(rows, split(resid_ref[f * width : (f + 1) * width]))

    packed = []
    done = 0
    for axis in axes:
        number = face_arrays(lax.axis_size(axis))
        packed += receive(inputs[done : done + number], axis)
        done += number
    inverses = inverses_of(packed, [own_ref[f] for f in late], partner_out)
    pending = [(f, early_basis[i]) for i, f in enumerate(early)]
    for i in range(count):
        store(inverse_out, i, inverses[i])
    basis = [starts_ref[f] for f in late]
    matrices = [
        [load(partner_out, i) for i in range(count)],
        [load(inverse_out, i) for i in range(count)],
        [load(halves_ref, f) for f in late],
    ]
    for sweep in range(SUB_ITERS):
        basis = sweep_basis(*matrices, basis)
        if pending:
            project(*pending.pop(0))
    for item in pending:
        project(*item)
    for i, f in enumerate(late):
        project(f, basis[i])
    tall = {}
    for g in range(FACES):
        column = jnp.concatenate([sides[f][g] for f in range(g + 1)], axis=0)
        column = triple(column, vectors[g], ((1,), (1,)))
        for f in range(g + 1):
            tall[f, g] = column[f * ncon : (f + 1) * ncon]
    for f in range(0, FACES, 2):
        tall[f + 1, f] = tall[f, f + 1].T
    zero = jnp.zeros((ncon, ncon), jnp.float32)

    def square(parts):
        lines = []
        for f in range(FACES):
            line = [parts.get((f, g), zero) for g in range(FACES)]
            lines.append(jnp.concatenate(line, axis=1))
        return jnp.concatenate(lines, axis=0)

    coarse = square(tall)
    right = jnp.concatenate([rights[f] for f in range(FACES)], axis=0)
    factors = factor_inverses([grams[f] for f in range(FACES)])
    factor = square({(f, f): factors[f] for f in range(FACES)})
    coarse = triple(factor, triple(coarse, factor, ((1,), (1,))))
    right = triple(factor, right)
    for f in range(FACES):
        product_ref[f] = triple(factors[f], sides[f][f])
    size = 2 * ncon
    blocks = {
        (b, c): coarse[b * size : (b + 1) * size, c * size : (c + 1) * size]
        for b in range(BLOCKS)
        for c in range(b, BLOCKS)
    }
    payload_ref[...] = jnp.concatenate([pack_coarse(blocks, size), right], axis=0)


def pack_coarse(blocks, size):
    row, col = iota((size, size), 0), iota((size, size), 1)
    diagonal = jnp.sum(jnp.where(row == col, blocks[2, 2], 0.0), axis=0, keepdims=True)
    tail = jnp.broadcast_to(jnp.concatenate([diagonal, diagonal], axis=1), (8, 2 * size))
    shared = jnp.where(row >= col, blocks[1, 1], blocks[2, 2])
    half = size // 2
    return jnp.concatenate(
        [
            jnp.concatenate([blocks[0, 0][:half], blocks[0, 0][half:]], axis=1),
            jnp.concatenate([shared, blocks[0, 1]], axis=1),
            jnp.concatenate([blocks[0, 2], blocks[1, 2]], axis=1),
            tail,
        ],
        axis=0,
    )


def unpack_coarse(packed, size):
    row, col = iota((size, size), 0), iota((size, size), 1)
    shared = packed[:size, :size]
    flip = shared.T
    diagonal = packed[2 * size : 2 * size + 1, :size]
    return {
        (1, 1): jnp.where(row >= col, shared, flip),
        (2, 2): jnp.where(row < col, shared, jnp.where(row > col, flip, diagonal)),
        (0, 1): packed[:size, size:],
        (0, 2): packed[size : 2 * size, :size],
        (1, 2): packed[size : 2 * size, size:],
    }


def find(faces, refs, f):
    for group, ref in zip(faces, refs):
        if f in group:
            return load(ref, list(group).index(f))


def theirs_kernel(faces, ncon, own_ref, *refs):
    inputs, partner_refs, inverse_refs = refs[:-5], refs[-5:-3], refs[-3:-1]
    product_out = refs[-1]
    basis = []
    done = 0
    for axis in AXES[:2]:
        number = face_arrays(lax.axis_size(axis))
        packed = receive(inputs[done : done + number], axis)
        basis += [unpack_starts(part, ncon) for part in packed]
        done += number
    count = len(basis)
    matrices = [
        [load(own_ref, f) for f in range(count)],
        [find(faces, inverse_refs, f) for f in range(count)],
        [find(faces, partner_refs, f) for f in range(count)],
    ]
    for sweep in range(SUB_ITERS):
        basis = sweep_basis(*matrices, basis)
    factors = factor_inverses([dot(b, b, ((1,), (1,))) for b in basis])
    for f in range(count):
        product_out[f] = triple(factors[f], thin(stacked(basis[f]), matrices[2][f]))


def spread_kernel(faces, unread, theirs_ref, product_ref, *refs):
    inverse_refs, out_ref = refs[:2], refs[2]
    for f in range(theirs_ref.shape[0]):
        both = jnp.concatenate([product_ref[f], theirs_ref[f]], axis=0)
        high, low = split(thin(stacked(both), find(faces, inverse_refs, f)).T)
        out_ref[f] = jnp.concatenate([high, high, low], axis=1)


def choose_kernel(flag_ref, here_ref, there_ref, matrix_ref, right_ref):
    mine = flag_ref[0:1, 0:1] > 0.5
    other = flag_ref[1:2, 0:1] > 0.5
    total = jnp.where(mine, here_ref[...], 0.0) + jnp.where(other, there_ref[...], 0.0)
    rows = matrix_ref.shape[0]
    matrix_ref[...] = total[:rows]
    right_ref[...] = total[rows:]


def add_kernel(first_ref, second_ref, third_ref, fourth_ref, product_ref, unread, *refs):
    first_out, matrix_ref, right_ref, *sent = refs
    total = first_ref[...] + second_ref[...]
    rows = first_out.shape[0]
    first_out[...] = total[:rows]
    matrix_ref[...] = total[rows:]
    right_ref[...] = third_ref[...] + fourth_ref[...]
    send(sent, AXES[2], product_ref[4], product_ref[5])


def first_kernel(*refs):
    total = refs[0][...]
    for ref in refs[1:-1]:
        total = total + ref[...]
    size = total.shape[1] // 2
    block = jnp.concatenate([total[:, :size], total[:, size:]], axis=0)
    eye = iota((size, size), 0) == iota((size, size), 1)
    diagonal = jnp.where(eye, block, 0.0)
    down = lax.rsqrt(jnp.sum(diagonal, axis=1, keepdims=True))
    across = lax.rsqrt(jnp.sum(diagonal, axis=0, keepdims=True))
    refs[-1][...] = factor_inverse(down * block * across) * across


def solve_kernel(size, terms, columns, first_ref, *refs):
    upper, lower = refs[0][...], refs[terms][...]
    for term in range(1, terms):
        upper = upper + refs[term][...]
        lower = lower + refs[terms + term][...]
    answer_ref = refs[-1]
    total = jnp.concatenate([upper, lower], axis=0)
    rows = 2 * size + 8
    blocks, right = unpack_coarse(total[:rows], size), total[rows:]
    eye = iota((size, size), 0) == iota((size, size), 1)
    downs, acrosses, rights = [], [], []
    for b in range(BLOCKS):
        if b == 0:
            downs.append(jnp.ones((size, 1), jnp.float32))
            acrosses.append(jnp.ones((1, size), jnp.float32))
        else:
            diagonal = jnp.where(eye, blocks[b, b], 0.0)
            downs.append(lax.rsqrt(jnp.sum(diagonal, axis=1, keepdims=True)))
            acrosses.append(lax.rsqrt(jnp.sum(diagonal, axis=0, keepdims=True)))
        rights.append(downs[b] * right[b * size : (b + 1) * size])
    for b in range(BLOCKS):
        for c in range(max(b, 1), BLOCKS):
            blocks[b, c] = downs[b] * blocks[b, c] * acrosses[c]
            if c > b:
                blocks[c, b] = blocks[b, c].T
    for b in range(BLOCKS):
        inverse = factor_inverse(blocks[b, b]) if b else first_ref[...]
        later = range(b + 1, BLOCKS)
        row = triple(inverse, jnp.concatenate([rights[b]] + [blocks[b, c] for c in later], axis=1))
        if later:
            column = jnp.concatenate([blocks[c, b] for c in later], axis=0)
            change = triple(triple(column, inverse, ((1,), (1,))), row)
        for i, c in enumerate(later):
            part = change[i * size : (i + 1) * size]
            rights[c] = rights[c] - part[:, :columns]
            for j, d in enumerate(later):
                start = columns + j * size
                blocks[c, d] = blocks[c, d] - part[:, start : start + size]
        row = triple(inverse, row, ((0,), (0,)))
        rights[b] = row[:, :columns]
        for c in later:
            blocks[b, c] = row[:, columns + (c - b - 1) * size : columns + (c - b) * size]
        for i in range(b):
            for c in later:
                blocks[i, c] = blocks[i, c] - triple(blocks[i, b], blocks[b, c])
            rights[i] = rights[i] - triple(blocks[i, b], rights[b])
    answer = [downs[b] * rights[b] for b in range(BLOCKS)]
    answer_ref[...] = jnp.concatenate(answer, axis=0)


def rows_kernel(ncon, flag_ref, here_ref, there_ref, *refs):
    hit = flag_ref[0:1, 0:1] > 0.5
    rows = jnp.where(hit, here_ref[: 2 * ncon], there_ref[: 2 * ncon])
    refs[-1][...] = rows
    send(refs[:-1], AXES[0], rows[:ncon], rows[ncon:])


def last_product(spread, mine, theirs):
    high, low = split(jnp.concatenate([mine, theirs], axis=0))
    return lax.dot_general(
        spread,
        jnp.concatenate([high, low, high], axis=0),
        (((1,), (0,)), ((), ())),
        preferred_element_type=jnp.float32,
    )


def through(inverse, mine, theirs, my_answer, their_answer):
    high, low = split(jnp.concatenate([mine, theirs], axis=0).T)
    spread = jnp.concatenate([high, high, low], axis=1)
    return wide(inverse, split(last_product(spread, my_answer, their_answer)))


def last_faces(values, width, out_ref, result, sems):
    copies = []
    for f, value in values.items():
        place = pl.ds(f * width, width)
        result[f * width : (f + 1) * width] = value()
        copy = pltpu.make_async_copy(result.at[place], out_ref.at[place], sems.at[f])
        copy.start()
        copies.append(copy)
    for copy in copies:
        copy.wait()


def last_plain_kernel(faces, product_ref, early_inverse, late_inverse, *refs):
    spread_ref, answer_ref, *inputs = refs[:-3]
    ncon, width = product_ref.shape[1:]
    number = face_arrays(lax.axis_size(AXES[2]))
    theirs = receive(inputs[:number], AXES[2])
    near = receive(inputs[number:-number], AXES[1]) + receive(inputs[-number:], AXES[2])
    values = {}
    for f in range(2, FACES):
        mine = answer_ref[f * ncon : (f + 1) * ncon]
        if f < 4:
            values[f] = functools.partial(last_product, spread_ref[f], mine, near[f - 2])
        else:
            values[f] = functools.partial(
                through,
                find(faces, (early_inverse, late_inverse), f),
                product_ref[f],
                theirs[f - 4],
                mine,
                near[f - 2],
            )
    last_faces(values, width, *refs[-3:])


def last_near_kernel(faces, flag_ref, product_ref, early_inverse, late_inverse, *refs):
    spread_ref, here_answer, there_answer = refs[:3]
    theirs = receive(refs[3:-3], AXES[2])
    ncon, width = product_ref.shape[1:]

    def answer(flag, f):
        place = slice(f * ncon, (f + 1) * ncon)
        hit = flag_ref[flag : flag + 1, 0:1] > 0.5
        return jnp.where(hit, here_answer[place], there_answer[place])

    values = {}
    for f in (2, 3):
        values[f] = functools.partial(
            last_product, spread_ref[f], answer(0, f), answer(f, f ^ 1)
        )
    for f in (4, 5):
        values[f] = functools.partial(
            through,
            find(faces, (early_inverse, late_inverse), f),
            product_ref[f],
            theirs[f - 4],
            answer(0, f),
            answer(f, f ^ 1),
        )
    last_faces(values, width, *refs[-3:])


def last_far_kernel(ncon, spread_ref, rows_ref, *refs):
    theirs = receive(refs[:-4], AXES[0])
    values = {}
    for f in range(2):
        mine = rows_ref[f * ncon : (f + 1) * ncon]
        values[f] = functools.partial(last_product, spread_ref[f], mine, theirs[f])
    last_faces(values, spread_ref.shape[1], *refs[-3:])


def per_device(schur, start_block, resid, group_of):
    matrix = schur[0, 0, 0]
    matrix = pltpu.with_memory_space_constraint(matrix, pltpu.HBM)
    starts = start_block[0, 0, 0].transpose(0, 2, 1)
    right = resid[0, 0, 0]
    order, columns = right.shape
    ncon, width = starts.shape[1:]
    counts = [lax.axis_size(axis) for axis in AXES]
    arrays = sum(face_arrays(count) for count in counts)
    coarse = FACES * ncon
    size = 2 * ncon
    half = width // 2
    first_rows, message_rows = ncon, (2 * size + ncon + 8 + coarse + 8) // 2
    rest_rows = 2 * size + ncon + 8 + coarse - message_rows
    uppers = FACES * (FACES - 1) // 2
    anywhere = pl.BlockSpec(memory_space=pl.ANY)
    main_memory = pl.BlockSpec(memory_space=pltpu.HBM)
    scalars = pl.BlockSpec(memory_space=pltpu.SMEM)
    early, late = (4, 5), (0, 1, 2, 3)
    faces = (early, late)
    planes = counts[2]

    def shape(*dims):
        return jax.ShapeDtypeStruct(dims, jnp.float32)

    def halves(count):
        return jax.ShapeDtypeStruct((count, 2, width, width), jnp.bfloat16)

    def params(mib):
        return pltpu.CompilerParams(vmem_limit_bytes=mib * MIB)

    def cost(us):
        return pl.CostEstimate(flops=us * 10**9, bytes_accessed=2**20, transcendentals=0)

    *packed, own = pl.pallas_call(
        functools.partial(pack_kernel, counts, width),
        out_shape=face_shapes(counts[0], (width + 8 + 2 * ncon, half))
        + face_shapes(counts[1], (width + 8 + 2 * ncon, half))
        + face_shapes(counts[2], (width + 8, half))
        + [shape(FACES, width, width)],
        in_specs=[main_memory, main_memory],
        out_specs=vmem_specs(arrays + 1),
        scratch_shapes=[
            pltpu.VMEM((4, ncon, width), jnp.float32),
            pltpu.SemaphoreType.DMA((FACES,)),
            pltpu.SemaphoreType.DMA,
        ],
        compiler_params=params(12),
    )(matrix, pltpu.with_memory_space_constraint(starts, pltpu.HBM))
    ends = [sum(face_arrays(count) for count in counts[:position]) for position in range(4)]
    got = {}
    for position in (2, 0, 1):
        got[position] = exchange(packed[ends[position] : ends[position + 1]], AXES[position])

    own_halves, upper_halves, flags = pl.pallas_call(
        functools.partial(halves_kernel, planes),
        out_shape=[halves(FACES), halves(uppers), shape(8, 128)],
        in_specs=[main_memory, scalars] + vmem_specs(1),
        out_specs=vmem_specs(3),
        scratch_shapes=[
            pltpu.VMEM((FACES - 1, width, order), jnp.float32),
            pltpu.SemaphoreType.DMA((FACES - 1,)),
        ],
        compiler_params=params(24),
        cost_estimate=cost(2),
    )(matrix, group_of, own)

    early_basis, early_partner, early_inverse = pl.pallas_call(
        functools.partial(early_kernel, AXES[2:3], early),
        out_shape=[shape(len(early), ncon, width)] + [halves(len(early))] * 2,
        in_specs=vmem_specs(len(got[2]) + 3),
        out_specs=vmem_specs(3),
        compiler_params=params(16),
        cost_estimate=cost(2),
    )(*got[2], own, own_halves, starts)

    payload, product, late_partner, late_inverse = pl.pallas_call(
        functools.partial(main_kernel, (AXES[0], AXES[1]), early, late),
        out_shape=[shape(message_rows + rest_rows, columns), shape(FACES, ncon, width)]
        + [halves(len(late))] * 2,
        in_specs=vmem_specs(len(got[0]) + len(got[1]) + 6),
        out_specs=vmem_specs(4),
        compiler_params=params(24),
        cost_estimate=cost(8),
    )(*got[0], *got[1], own, own_halves, upper_halves, starts, right, early_basis)

    partners = [early_partner, late_partner]
    inverses = [early_inverse, late_inverse]
    their_product = pl.pallas_call(
        functools.partial(theirs_kernel, faces, ncon),
        out_shape=shape(4, ncon, width),
        in_specs=vmem_specs(5 + len(got[0]) + len(got[1])),
        out_specs=vmem_specs(1)[0],
        compiler_params=params(16),
        cost_estimate=cost(2),
    )(own_halves, *got[0], *got[1], *partners, *inverses)

    def spread_of(token):
        return pl.pallas_call(
            functools.partial(spread_kernel, faces),
            out_shape=jax.ShapeDtypeStruct((4, width, 3 * size), jnp.bfloat16),
            in_specs=[anywhere] + vmem_specs(4),
            out_specs=vmem_specs(1)[0],
            compiler_params=params(16),
            cost_estimate=cost(2),
        )(token, their_product, product, *inverses)

    def solve(firsts, matrices, rights, unread):
        first = pl.pallas_call(
            first_kernel,
            out_shape=shape(size, size),
            in_specs=vmem_specs(len(firsts)),
            out_specs=vmem_specs(1)[0],
            compiler_params=params(8),
            cost_estimate=cost(2),
        )(*firsts)
        return pl.pallas_call(
            functools.partial(solve_kernel, size, len(matrices), columns),
            out_shape=shape(coarse, columns),
            in_specs=vmem_specs(1 + 2 * len(matrices)) + [anywhere] * len(unread),
            out_specs=vmem_specs(1)[0],
            compiler_params=params(12),
            cost_estimate=cost(7),
        )(first, *matrices, *rights, *unread)

    result = dict(
        out_shape=shape(order, columns),
        out_specs=main_memory,
        scratch_shapes=[
            pltpu.VMEM((order, columns), jnp.float32),
            pltpu.SemaphoreType.DMA((FACES,)),
        ],
        compiler_params=params(12),
        cost_estimate=cost(1),
    )
    groups = group_of.shape[0] // GROUP_SIZE
    if groups == 2 and counts[1] == 4 and planes == 2:
        core_swap, chip_x, chip_y = flipped("gy", 1), flipped("gy", 2), flipped("gz", 1)
        other = lax.ppermute(payload, "gy", core_swap)
        left, rest = pl.pallas_call(
            choose_kernel,
            out_shape=[shape(message_rows, columns), shape(rest_rows, columns)],
            in_specs=vmem_specs(3),
            out_specs=vmem_specs(2),
            compiler_params=params(8),
        )(flags, payload, other)
        left_moved = lax.ppermute(left, "gy", chip_x)
        rest_moved = lax.ppermute(rest, "gz", chip_y)
        first_last, left_last, rest_last, *sent = pl.pallas_call(
            add_kernel,
            out_shape=[
                shape(first_rows, columns),
                shape(message_rows - first_rows, columns),
                shape(rest_rows, columns),
            ]
            + face_shapes(counts[2], (ncon, width)),
            in_specs=vmem_specs(5) + [anywhere],
            out_specs=vmem_specs(3 + face_arrays(counts[2])),
            compiler_params=params(8),
        )(left, left_moved, rest, rest_moved, product, their_product)
        first_other = lax.ppermute(first_last, "gz", chip_y)
        left_other = lax.ppermute(left_last, "gz", chip_y)
        rest_other = lax.ppermute(rest_last, "gy", chip_x)
        theirs = exchange(sent, AXES[2])
        spread = spread_of(first_other)
        answer = solve(
            [first_last, first_other], [left_last, left_other], [rest_last, rest_other], [spread]
        )
        there = lax.ppermute(answer, "gy", core_swap)
        *sent, mine = pl.pallas_call(
            functools.partial(rows_kernel, ncon),
            out_shape=face_shapes(counts[0], (ncon, columns)) + [shape(size, columns)],
            in_specs=vmem_specs(3),
            out_specs=vmem_specs(face_arrays(counts[0]) + 1),
            compiler_params=params(8),
        )(flags, answer, there)
        across = exchange(sent, AXES[0])
        correction = pl.pallas_call(
            functools.partial(last_near_kernel, faces),
            in_specs=vmem_specs(7 + len(theirs)),
            **result,
        )(flags, product, *inverses, spread, answer, there, *theirs)
    else:
        y, z = lax.axis_index("gy"), lax.axis_index("gz")
        member_of = group_of[y * planes + z]
        chosen = jnp.arange(groups, dtype=jnp.int32) == member_of
        total = lax.psum(jnp.where(chosen[:, None, None], payload[None], 0.0), ("gy", "gz"))
        total = lax.dynamic_index_in_dim(total, member_of, 0, keepdims=False)
        spread = spread_of(payload)
        answer = solve(
            [total[:first_rows]], [total[first_rows:message_rows]], [total[message_rows:]], []
        )

        def from_near(faces_of, axis):
            even, odd = faces_of
            if lax.axis_size(axis) == 2:
                return exchange([jnp.stack([even, odd])], axis)
            upward = is_even(axis)
            return exchange([jnp.where(upward, even, odd), jnp.where(upward, odd, even)], axis)

        blocks = answer.reshape(FACES, ncon, columns)
        near = [
            *from_near(product[4:6], AXES[2]),
            *from_near(blocks[2:4], AXES[1]),
            *from_near(blocks[4:6], AXES[2]),
        ]
        mine = answer[:size]
        across = from_near(blocks[:2], AXES[0])
        correction = pl.pallas_call(
            functools.partial(last_plain_kernel, faces),
            in_specs=vmem_specs(5 + len(near)),
            **result,
        )(product, *inverses, spread, answer, *near)
    correction = pl.pallas_call(
        functools.partial(last_far_kernel, ncon),
        in_specs=vmem_specs(2 + len(across)) + [main_memory],
        input_output_aliases={2 + len(across): 0},
        **result,
    )(spread, mine, *across, correction)
    return correction[None, None, None]


def solution(mesh):
    in_specs = (
        P("gx", "gy", "gz", None, None),
        P("gx", "gy", "gz", None, None, None),
        P("gx", "gy", "gz", None, None),
        P(),
    )
    out_specs = P("gx", "gy", "gz", None, None)
    return jax.shard_map(
        per_device, mesh=mesh, in_specs=in_specs, out_specs=out_specs, check_vma=False
    )
```

```python
import functools

import jax
import jax.numpy as jnp
from jax import lax
from jax.experimental import pallas as pl
from jax.experimental.pallas import tpu as pltpu
from jax.sharding import PartitionSpec as P

NS_ITERS = 3
SUB_ITERS = 2
GROUP_SIZE = 4
FACES = 6
BLOCKS = FACES // 2
AXES = ("gx", "gy", "gz")
MIB = 1024 * 1024

precise = lax.Precision.HIGHEST


def dot(left, right, dims=((1,), (0,))):
    return lax.dot_general(
        left, right, (dims, ((), ())), precision=precise, preferred_element_type=jnp.float32
    )


def split(value):
    high = value.astype(jnp.bfloat16)
    return high, (value - high.astype(jnp.float32)).astype(jnp.bfloat16)


def wide(left, right):
    return lax.dot_general(
        jnp.concatenate([left[0], left[0], left[1]], axis=1),
        jnp.concatenate([right[0], right[1], right[0]], axis=0),
        (((1,), (0,)), ((), ())),
        preferred_element_type=jnp.float32,
    )


def stacked(value):
    return jnp.concatenate(split(value), axis=0)


def thin(rows, matrix):
    out = lax.dot_general(
        jnp.concatenate([rows, rows], axis=1),
        jnp.concatenate(matrix, axis=0),
        (((1,), (0,)), ((), ())),
        preferred_element_type=jnp.float32,
    )
    half = rows.shape[0] // 2
    return out[:half] + out[half:]


def triple(left, right, dims=((1,), (0,))):
    (left_high, left_low), (right_high, right_low) = split(left), split(right)
    total = None
    for one, other in ((left_high, right_high), (left_high, right_low), (left_low, right_high)):
        part = lax.dot_general(
            one, other, (dims, ((), ())), preferred_element_type=jnp.float32
        )
        total = part if total is None else total + part
    return total


def iota(shape, dim):
    return lax.broadcasted_iota(jnp.int32, shape, dim)


def flipped(axis, bit):
    return [(i, i ^ bit) for i in range(lax.axis_size(axis))]


def outer_pairs(axis):
    count = lax.axis_size(axis)
    return [(i, (i + 1 if i % 2 else i - 1) % count) for i in range(count)]


def face_arrays(count):
    return 1 if count == 2 else 2


def exchange(arrays, axis):
    if lax.axis_size(axis) == 2:
        return [lax.ppermute(arrays[0], axis, flipped(axis, 1))]
    return [
        lax.ppermute(arrays[0], axis, outer_pairs(axis)),
        lax.ppermute(arrays[1], axis, flipped(axis, 1)),
    ]


def is_even(axis):
    return lax.rem(lax.axis_index(axis), 2) == 0


def send(refs, axis, even, odd):
    if lax.axis_size(axis) == 2:
        refs[0][0] = even
        refs[0][1] = odd
    else:
        upward = is_even(axis)
        refs[0][...] = jnp.where(upward, even, odd)
        refs[1][...] = jnp.where(upward, odd, even)


def receive(refs, axis):
    if lax.axis_size(axis) == 2:
        return refs[0][1], refs[0][0]
    upward = is_even(axis)
    first, second = refs[0][...], refs[1][...]
    return jnp.where(upward, first, second), jnp.where(upward, second, first)


def face_shapes(count, shape):
    if count == 2:
        return [jax.ShapeDtypeStruct((2,) + shape, jnp.float32)]
    return [jax.ShapeDtypeStruct(shape, jnp.float32)] * 2


def vmem_specs(count):
    return [pl.BlockSpec(memory_space=pltpu.VMEM)] * count


def pack_kernel(counts, width, schur_ref, starts_ref, *refs):
    outs, blocks = refs[:-4], refs[-4]
    starts, sems, start_sem = refs[-3:]
    half = width // 2
    start_copy = pltpu.make_async_copy(starts_ref.at[pl.ds(0, 4)], starts, start_sem)
    start_copy.start()
    copies = []
    for f in range(FACES):
        place = pl.ds(f * width, width)
        copy = pltpu.make_async_copy(schur_ref.at[place, place], blocks.at[f], sems.at[f])
        copy.start()
        copies.append(copy)
    row, col = iota((half, half), 0), iota((half, half), 1)
    start_copy.wait()

    def pack(f):
        copies[f].wait()
        first = blocks[f, 0:half, 0:half]
        second = blocks[f, half:width, half:width]
        diag = jnp.sum(jnp.where(row == col, second, 0.0), axis=0, keepdims=True)
        mixed = jnp.where(row >= col, first, second)
        tail = jnp.broadcast_to(diag, (8, half))
        parts = [blocks[f, half:width, 0:half], mixed, tail]
        if f < 4:
            parts += [starts[f, :, :half], starts[f, :, half:]]
        return jnp.concatenate(parts, axis=0)

    done = 0
    for position, axis in enumerate(AXES):
        number = face_arrays(counts[position])
        send(outs[done : done + number], axis, pack(2 * position), pack(2 * position + 1))
        done += number


def unpack(packed):
    half = packed.shape[1]
    row, col = iota((half, half), 0), iota((half, half), 1)
    low = packed[0:half]
    mixed = packed[half : 2 * half]
    flip = mixed.T
    first = jnp.where(row >= col, mixed, flip)
    second = jnp.where(row < col, mixed, flip)
    second = jnp.where(row == col, packed[2 * half : 2 * half + 1], second)
    return jnp.concatenate(
        [jnp.concatenate([first, low.T], axis=1), jnp.concatenate([low, second], axis=1)], axis=0
    )


def unpack_starts(packed, ncon):
    half = packed.shape[1]
    rows = packed[2 * half + 8 :]
    return jnp.concatenate([rows[:ncon], rows[ncon:]], axis=1)


def factor_inverses(grams):
    size = grams[0].shape[0]
    strips, block, lanes = size // 8, 8, 128
    full = (block, lanes)
    beside = lanes // (2 * size)
    one = jnp.where(iota((size, size), 0) == iota((size, size), 1), 1.0, 0.0)
    states = []
    for first in range(0, len(grams), beside):
        parts = [part for gram in grams[first : first + beside] for part in (gram, one)]
        whole = jnp.concatenate(parts, axis=1)
        states.append([whole[8 * s : 8 * s + 8] for s in range(strips)])
    below = iota(full, 0)
    base = iota(full, 1) // (2 * size) * (2 * size)

    def column(rows, k):
        if beside == 1:
            return jnp.broadcast_to(rows[:, k : k + 1], full)
        return jnp.take_along_axis(rows, base + k, axis=1, mode="promise_in_bounds")

    def line_of(rows, line):
        return jnp.broadcast_to(rows[line : line + 1], full)

    roots = [[None] * strips for _ in states]
    for strip in range(strips):
        start = strip * block
        columns = [
            [[column(work[s], start + j) for s in range(strip, strips)] for j in range(block)]
            for work in states
        ]
        heads = [[column_set[0] for column_set in per_state] for per_state in columns]
        lowers = [work[strip] for work in states]
        solved = list(lowers)
        pivots = [jnp.ones(full, jnp.float32) for _ in states]
        scales = list(pivots)

        def eliminate(i, j, scale, pivot, side):
            cols = heads[i]
            factor = jnp.where(below != j, cols[j] * scale, 0.0)
            for later in range(j + 1, block):
                use = side if later == j + 1 and side is not None else line_of(cols[later], j)
                cols[later] = cols[later] - factor * use
            row = line_of(lowers[i], j)
            solved[i] = solved[i] - factor * row
            lowers[i] = lowers[i] - jnp.where(below > j, factor, 0.0) * row
            pivots[i] = jnp.where(below == j, pivot, pivots[i])
            scales[i] = jnp.where(below == j, scale, scales[i])

        for j in range(0, block, 2):
            for i in range(len(states)):
                cols = heads[i]
                corner, side = line_of(cols[j], j), line_of(cols[j], j + 1)
                last = line_of(cols[j + 1], j + 1)
                minor = corner * last - side * side
                scale = 1.0 / corner
                eliminate(i, j, scale, corner, side)
                eliminate(i, j + 1, corner * (1.0 / minor), minor * scale, None)
        for i, work in enumerate(states):
            work[strip] = lowers[i]
            roots[i][strip] = lax.rsqrt(pivots[i])
            if strip == strips - 1:
                continue
            answer = solved[i] * scales[i]
            rows = [line_of(answer, j) for j in range(block)]
            for s in range(strip + 1, strips):
                for j in range(block):
                    work[s] = work[s] - columns[i][j][s - strip] * rows[j]
    results = []
    for i, work in enumerate(states):
        scaled = jnp.concatenate([work[s] * roots[i][s] for s in range(strips)], axis=0)
        for m in range(beside):
            begin = (2 * m + 1) * size
            results.append(scaled[:, begin : begin + size])
    return results


def factor_inverse(gram):
    size = gram.shape[0]
    strips, block, lanes = size // 8, 8, 128
    full = (block, lanes)
    parts = [gram, jnp.where(iota((size, size), 0) == iota((size, size), 1), 1.0, 0.0)]
    if 2 * size < lanes:
        parts.append(jnp.zeros((size, lanes - 2 * size), jnp.float32))
    whole = jnp.concatenate(parts, axis=1)
    work = [whole[8 * s : 8 * s + 8] for s in range(strips)]
    below = iota(full, 0)

    def line_of(rows, line):
        return jnp.broadcast_to(rows[line : line + 1], full)

    for strip in range(strips):
        start = strip * block
        active = range(strip, strips)
        cols = [
            {s: jnp.broadcast_to(work[s][:, start + j : start + j + 1], full) for s in active}
            for j in range(block)
        ]
        factors = []

        def eliminate(j, scale):
            factor = {s: cols[j][s] * scale for s in active}
            factor[strip] = jnp.where(below > j, factor[strip], 0.0)
            for later in range(j + 1, block):
                head = line_of(cols[later][strip], j)
                for s in active:
                    cols[later][s] = cols[later][s] - factor[s] * head
            factors.append(factor)

        for j in range(0, block, 2):
            corner = line_of(cols[j][strip], j)
            side = line_of(cols[j][strip], j + 1)
            last = line_of(cols[j + 1][strip], j + 1)
            inverse = 1.0 / (corner * last - side * side)
            eliminate(j, 1.0 / corner)
            eliminate(j + 1, corner * inverse)
        for j in range(block):
            row = line_of(work[strip], j)
            for s in active:
                if s == strip and j == block - 1:
                    continue
                work[s] = work[s] - factors[j][s] * row
    parts = []
    for s in range(strips):
        place = iota((8, size), 0) + 8 * s == iota((8, size), 1)
        pivot = jnp.sum(jnp.where(place, work[s][:, :size], 0.0), axis=1, keepdims=True)
        parts.append(work[s][:, size : 2 * size] * lax.rsqrt(pivot))
    return jnp.concatenate(parts, axis=0)


def member(group_ref, planes, dy=0, dz=0):
    y, z = lax.axis_index("gy"), lax.axis_index("gz")
    rows = lax.axis_size("gy")
    return group_ref[lax.rem(y + dy + rows, rows) * planes + lax.rem(z + dz + planes, planes)]


def store(ref, f, value):
    ref[f, 0], ref[f, 1] = split(value)


def load(ref, f):
    return ref[f, 0], ref[f, 1]


def upper_index(f, g):
    return sum(FACES - 1 - i for i in range(f)) + g - f - 1


def halves_kernel(planes, schur_ref, group_ref, own_ref, own_out, upper_out, flag_out, *scratch):
    upper_ref, sems = scratch
    width = own_ref.shape[1]
    strips = []
    for f in range(FACES - 1):
        rest = (FACES - 1 - f) * width
        copy = pltpu.make_async_copy(
            schur_ref.at[pl.ds(f * width, width), pl.ds((f + 1) * width, rest)],
            upper_ref.at[f, :, pl.ds((f + 1) * width, rest)],
            sems.at[f],
        )
        copy.start()
        strips.append(copy)
    core = lax.rem(lax.axis_index("gy"), 2)
    near = [(0, 0), (1 - 2 * core, 0), (-1, 0), (1, 0), (0, -1), (0, 1)]
    row = iota(flag_out.shape, 0)
    flags = jnp.zeros(flag_out.shape, jnp.float32)
    for i, (dy, dz) in enumerate(near):
        hit = member(group_ref, planes, dy, dz) == core
        flags = jnp.where(row == i, jnp.where(hit, 1.0, 0.0), flags)
    flag_out[...] = flags
    for f in range(FACES):
        store(own_out, f, own_ref[f])
    for f in range(FACES - 1):
        strips[f].wait()
        for g in range(f + 1, FACES):
            store(upper_out, upper_index(f, g), upper_ref[f, :, g * width : (g + 1) * width])


def inverses_of(packed, owns, partner_ref):
    width = owns[0].shape[1]
    half = width // 2
    eye = iota((half, half), 0) == iota((half, half), 1)
    whole_eye = iota((width, width), 0) == iota((width, width), 1)
    powers, sums, downs = [], [], []
    for f in range(len(packed)):
        partner = unpack(packed[f])
        store(partner_ref, f, partner)
        total = owns[f] + partner
        across, down = [], []
        for start in (0, half):
            block = total[start : start + half, start : start + half]
            diagonal = jnp.where(eye, block, 0.0)
            across.append(1.0 / jnp.sum(diagonal, axis=0, keepdims=True))
            down.append(1.0 / jnp.sum(diagonal, axis=1, keepdims=True))
        downs.append(jnp.concatenate(down, axis=0))
        power = jnp.where(whole_eye, 0.0, -total * jnp.concatenate(across, axis=1))
        powers.append(split(power))
        sums.append(jnp.where(whole_eye, 1.0, power))
    for step in range(1, NS_ITERS):
        powers = [split(wide(power, power)) for power in powers]
        sums = [total + wide(split(total), power) for total, power in zip(sums, powers)]
    return [down * total for down, total in zip(downs, sums)]


def unit_rows(basis):
    return [b * lax.rsqrt(jnp.sum(b * b, axis=1, keepdims=True)) for b in basis]


def sweep_basis(before, inverse, after, basis):
    for matrices in (before, inverse, after):
        basis = [thin(stacked(b), matrix) for b, matrix in zip(basis, matrices)]
    return unit_rows(basis)


def early_kernel(axes, faces, *refs):
    arrays = len(refs) - 6
    inputs = refs[:arrays]
    own_ref, halves_ref, starts_ref, basis_out, partner_out, inverse_out = refs[arrays:]
    count = len(faces)
    packed = []
    done = 0
    for axis in axes:
        number = face_arrays(lax.axis_size(axis))
        packed += receive(inputs[done : done + number], axis)
        done += number
    inverses = inverses_of(packed, [own_ref[f] for f in faces], partner_out)
    for i in range(count):
        store(inverse_out, i, inverses[i])
    basis = [starts_ref[f] for f in faces]
    matrices = [
        [load(partner_out, i) for i in range(count)],
        [load(inverse_out, i) for i in range(count)],
        [load(halves_ref, f) for f in faces],
    ]
    for sweep in range(SUB_ITERS):
        basis = sweep_basis(*matrices, basis)
    for i in range(count):
        basis_out[i] = basis[i]


def main_kernel(axes, early, late, *refs):
    arrays = len(refs) - 10
    inputs = refs[:arrays]
    own_ref, halves_ref, upper_ref, starts_ref, resid_ref, early_basis = refs[arrays : arrays + 6]
    payload_ref, product_ref, partner_out, inverse_out = refs[arrays + 6 :]
    ncon, width = starts_ref.shape[1:]
    columns = resid_ref.shape[1]
    sides = {}
    rights = {}
    grams = {}
    vectors = {}
    count = len(late)

    def project(f, basis):
        vectors[f] = basis
        rows = stacked(basis)
        grams[f] = dot(basis, basis, ((1,), (1,)))
        side = {f: thin(rows, load(halves_ref, f))}
        for g in range(f + 1, FACES):
            side[g] = thin(rows, load(upper_ref, upper_index(f, g)))
        sides[f] = side
        rights[f] = thin(rows, split(resid_ref[f * width : (f + 1) * width]))

    packed = []
    done = 0
    for axis in axes:
        number = face_arrays(lax.axis_size(axis))
        packed += receive(inputs[done : done + number], axis)
        done += number
    inverses = inverses_of(packed, [own_ref[f] for f in late], partner_out)
    pending = [(f, early_basis[i]) for i, f in enumerate(early)]
    for i in range(count):
        store(inverse_out, i, inverses[i])
    basis = [starts_ref[f] for f in late]
    matrices = [
        [load(partner_out, i) for i in range(count)],
        [load(inverse_out, i) for i in range(count)],
        [load(halves_ref, f) for f in late],
    ]
    for sweep in range(SUB_ITERS):
        basis = sweep_basis(*matrices, basis)
        if pending:
            project(*pending.pop(0))
    for item in pending:
        project(*item)
    for i, f in enumerate(late):
        project(f, basis[i])
    tall = {}
    for g in range(FACES):
        column = jnp.concatenate([sides[f][g] for f in range(g + 1)], axis=0)
        column = triple(column, vectors[g], ((1,), (1,)))
        for f in range(g + 1):
            tall[f, g] = column[f * ncon : (f + 1) * ncon]
    for f in range(0, FACES, 2):
        tall[f + 1, f] = tall[f, f + 1].T
    zero = jnp.zeros((ncon, ncon), jnp.float32)

    def square(parts):
        lines = []
        for f in range(FACES):
            line = [parts.get((f, g), zero) for g in range(FACES)]
            lines.append(jnp.concatenate(line, axis=1))
        return jnp.concatenate(lines, axis=0)

    coarse = square(tall)
    right = jnp.concatenate([rights[f] for f in range(FACES)], axis=0)
    factors = factor_inverses([grams[f] for f in range(FACES)])
    factor = square({(f, f): factors[f] for f in range(FACES)})
    coarse = triple(factor, triple(coarse, factor, ((1,), (1,))))
    right = triple(factor, right)
    for f in range(FACES):
        product_ref[f] = triple(factors[f], sides[f][f])
    size = 2 * ncon
    blocks = {
        (b, c): coarse[b * size : (b + 1) * size, c * size : (c + 1) * size]
        for b in range(BLOCKS)
        for c in range(b, BLOCKS)
    }
    payload_ref[...] = jnp.concatenate([pack_coarse(blocks, size), right], axis=0)


def pack_coarse(blocks, size):
    row, col = iota((size, size), 0), iota((size, size), 1)
    diagonal = jnp.sum(jnp.where(row == col, blocks[2, 2], 0.0), axis=0, keepdims=True)
    tail = jnp.broadcast_to(jnp.concatenate([diagonal, diagonal], axis=1), (8, 2 * size))
    shared = jnp.where(row >= col, blocks[1, 1], blocks[2, 2])
    half = size // 2
    return jnp.concatenate(
        [
            jnp.concatenate([blocks[0, 0][:half], blocks[0, 0][half:]], axis=1),
            jnp.concatenate([shared, blocks[0, 1]], axis=1),
            jnp.concatenate([blocks[0, 2], blocks[1, 2]], axis=1),
            tail,
        ],
        axis=0,
    )


def unpack_coarse(packed, size):
    row, col = iota((size, size), 0), iota((size, size), 1)
    shared = packed[:size, :size]
    flip = shared.T
    diagonal = packed[2 * size : 2 * size + 1, :size]
    return {
        (1, 1): jnp.where(row >= col, shared, flip),
        (2, 2): jnp.where(row < col, shared, jnp.where(row > col, flip, diagonal)),
        (0, 1): packed[:size, size:],
        (0, 2): packed[size : 2 * size, :size],
        (1, 2): packed[size : 2 * size, size:],
    }


def find(faces, refs, f):
    for group, ref in zip(faces, refs):
        if f in group:
            return load(ref, list(group).index(f))


def theirs_kernel(faces, ncon, own_ref, *refs):
    inputs, partner_refs, inverse_refs = refs[:-6], refs[-6:-4], refs[-4:-2]
    basis_out, product_out = refs[-2:]
    basis = []
    done = 0
    for axis in AXES[:2]:
        number = face_arrays(lax.axis_size(axis))
        packed = receive(inputs[done : done + number], axis)
        basis += [unpack_starts(part, ncon) for part in packed]
        done += number
    count = len(basis)
    matrices = [
        [load(own_ref, f) for f in range(count)],
        [find(faces, inverse_refs, f) for f in range(count)],
        [find(faces, partner_refs, f) for f in range(count)],
    ]
    for sweep in range(SUB_ITERS):
        basis = sweep_basis(*matrices, basis)
    for f in range(count):
        basis_out[f] = basis[f]
        product_out[f] = thin(stacked(basis[f]), matrices[2][f])


def spread_kernel(faces, unread, basis_ref, theirs_ref, product_ref, *refs):
    inverse_refs, out_ref = refs[:2], refs[2]
    basis = [basis_ref[f] for f in range(basis_ref.shape[0])]
    factors = factor_inverses([dot(b, b, ((1,), (1,))) for b in basis])
    for f in range(len(basis)):
        theirs = triple(factors[f], theirs_ref[f])
        both = jnp.concatenate([product_ref[f], theirs], axis=0)
        high, low = split(thin(stacked(both), find(faces, inverse_refs, f)).T)
        out_ref[f] = jnp.concatenate([high, high, low], axis=1)


def choose_kernel(flag_ref, here_ref, there_ref, unread, matrix_ref, right_ref):
    mine = flag_ref[0:1, 0:1] > 0.5
    other = flag_ref[1:2, 0:1] > 0.5
    total = jnp.where(mine, here_ref[...], 0.0) + jnp.where(other, there_ref[...], 0.0)
    rows = matrix_ref.shape[0]
    matrix_ref[...] = total[:rows]
    right_ref[...] = total[rows:]


def add_kernel(first_ref, second_ref, third_ref, fourth_ref, product_ref, unread, *refs):
    first_out, matrix_ref, right_ref, *sent = refs
    total = first_ref[...] + second_ref[...]
    rows = first_out.shape[0]
    first_out[...] = total[:rows]
    matrix_ref[...] = total[rows:]
    right_ref[...] = third_ref[...] + fourth_ref[...]
    send(sent, AXES[2], product_ref[4], product_ref[5])


def first_kernel(*refs):
    total = refs[0][...]
    for ref in refs[1:-1]:
        total = total + ref[...]
    size = total.shape[1] // 2
    block = jnp.concatenate([total[:, :size], total[:, size:]], axis=0)
    eye = iota((size, size), 0) == iota((size, size), 1)
    diagonal = jnp.where(eye, block, 0.0)
    down = lax.rsqrt(jnp.sum(diagonal, axis=1, keepdims=True))
    across = lax.rsqrt(jnp.sum(diagonal, axis=0, keepdims=True))
    refs[-1][...] = factor_inverse(down * block * across) * across


def solve_kernel(size, terms, columns, first_ref, *refs):
    upper, lower = refs[0][...], refs[terms][...]
    for term in range(1, terms):
        upper = upper + refs[term][...]
        lower = lower + refs[terms + term][...]
    answer_ref = refs[-1]
    total = jnp.concatenate([upper, lower], axis=0)
    rows = 2 * size + 8
    blocks, right = unpack_coarse(total[:rows], size), total[rows:]
    eye = iota((size, size), 0) == iota((size, size), 1)
    downs, acrosses, rights = [], [], []
    for b in range(BLOCKS):
        if b == 0:
            downs.append(jnp.ones((size, 1), jnp.float32))
            acrosses.append(jnp.ones((1, size), jnp.float32))
        else:
            diagonal = jnp.where(eye, blocks[b, b], 0.0)
            downs.append(lax.rsqrt(jnp.sum(diagonal, axis=1, keepdims=True)))
            acrosses.append(lax.rsqrt(jnp.sum(diagonal, axis=0, keepdims=True)))
        rights.append(downs[b] * right[b * size : (b + 1) * size])
    for b in range(BLOCKS):
        for c in range(max(b, 1), BLOCKS):
            blocks[b, c] = downs[b] * blocks[b, c] * acrosses[c]
            if c > b:
                blocks[c, b] = blocks[b, c].T
    for b in range(BLOCKS):
        inverse = factor_inverse(blocks[b, b]) if b else first_ref[...]
        later = range(b + 1, BLOCKS)
        row = triple(inverse, jnp.concatenate([rights[b]] + [blocks[b, c] for c in later], axis=1))
        if later:
            column = jnp.concatenate([blocks[c, b] for c in later], axis=0)
            change = triple(triple(column, inverse, ((1,), (1,))), row)
        for i, c in enumerate(later):
            part = change[i * size : (i + 1) * size]
            rights[c] = rights[c] - part[:, :columns]
            for j, d in enumerate(later):
                start = columns + j * size
                blocks[c, d] = blocks[c, d] - part[:, start : start + size]
        row = triple(inverse, row, ((0,), (0,)))
        rights[b] = row[:, :columns]
        for c in later:
            blocks[b, c] = row[:, columns + (c - b - 1) * size : columns + (c - b) * size]
        for i in range(b):
            for c in later:
                blocks[i, c] = blocks[i, c] - triple(blocks[i, b], blocks[b, c])
            rights[i] = rights[i] - triple(blocks[i, b], rights[b])
    answer = [downs[b] * rights[b] for b in range(BLOCKS)]
    answer_ref[...] = jnp.concatenate(answer, axis=0)


def rows_kernel(ncon, flag_ref, here_ref, there_ref, *refs):
    hit = flag_ref[0:1, 0:1] > 0.5
    rows = jnp.where(hit, here_ref[: 2 * ncon], there_ref[: 2 * ncon])
    refs[-1][...] = rows
    send(refs[:-1], AXES[0], rows[:ncon], rows[ncon:])


def last_product(spread, mine, theirs):
    high, low = split(jnp.concatenate([mine, theirs], axis=0))
    return lax.dot_general(
        spread,
        jnp.concatenate([high, low, high], axis=0),
        (((1,), (0,)), ((), ())),
        preferred_element_type=jnp.float32,
    )


def through(inverse, mine, theirs, my_answer, their_answer):
    high, low = split(jnp.concatenate([mine, theirs], axis=0).T)
    spread = jnp.concatenate([high, high, low], axis=1)
    return wide(inverse, split(last_product(spread, my_answer, their_answer)))


def last_faces(values, width, out_ref, result, sems):
    copies = []
    for f, value in values.items():
        place = pl.ds(f * width, width)
        result[f * width : (f + 1) * width] = value()
        copy = pltpu.make_async_copy(result.at[place], out_ref.at[place], sems.at[f])
        copy.start()
        copies.append(copy)
    for copy in copies:
        copy.wait()


def last_plain_kernel(faces, product_ref, early_inverse, late_inverse, *refs):
    spread_ref, answer_ref, *inputs = refs[:-3]
    ncon, width = product_ref.shape[1:]
    number = face_arrays(lax.axis_size(AXES[2]))
    theirs = receive(inputs[:number], AXES[2])
    near = receive(inputs[number:-number], AXES[1]) + receive(inputs[-number:], AXES[2])
    values = {}
    for f in range(2, FACES):
        mine = answer_ref[f * ncon : (f + 1) * ncon]
        if f < 4:
            values[f] = functools.partial(last_product, spread_ref[f], mine, near[f - 2])
        else:
            values[f] = functools.partial(
                through,
                find(faces, (early_inverse, late_inverse), f),
                product_ref[f],
                theirs[f - 4],
                mine,
                near[f - 2],
            )
    last_faces(values, width, *refs[-3:])


def last_near_kernel(faces, flag_ref, product_ref, early_inverse, late_inverse, *refs):
    spread_ref, here_answer, there_answer = refs[:3]
    theirs = receive(refs[3:-3], AXES[2])
    ncon, width = product_ref.shape[1:]

    def answer(flag, f):
        place = slice(f * ncon, (f + 1) * ncon)
        hit = flag_ref[flag : flag + 1, 0:1] > 0.5
        return jnp.where(hit, here_answer[place], there_answer[place])

    values = {}
    for f in (2, 3):
        values[f] = functools.partial(
            last_product, spread_ref[f], answer(0, f), answer(f, f ^ 1)
        )
    for f in (4, 5):
        values[f] = functools.partial(
            through,
            find(faces, (early_inverse, late_inverse), f),
            product_ref[f],
            theirs[f - 4],
            answer(0, f),
            answer(f, f ^ 1),
        )
    last_faces(values, width, *refs[-3:])


def last_far_kernel(ncon, spread_ref, rows_ref, *refs):
    theirs = receive(refs[:-4], AXES[0])
    values = {}
    for f in range(2):
        mine = rows_ref[f * ncon : (f + 1) * ncon]
        values[f] = functools.partial(last_product, spread_ref[f], mine, theirs[f])
    last_faces(values, spread_ref.shape[1], *refs[-3:])


def per_device(schur, start_block, resid, group_of):
    matrix = schur[0, 0, 0]
    matrix = pltpu.with_memory_space_constraint(matrix, pltpu.HBM)
    starts = start_block[0, 0, 0].transpose(0, 2, 1)
    right = resid[0, 0, 0]
    order, columns = right.shape
    ncon, width = starts.shape[1:]
    counts = [lax.axis_size(axis) for axis in AXES]
    arrays = sum(face_arrays(count) for count in counts)
    coarse = FACES * ncon
    size = 2 * ncon
    half = width // 2
    first_rows, message_rows = ncon, (2 * size + ncon + 8 + coarse + 8) // 2
    rest_rows = 2 * size + ncon + 8 + coarse - message_rows
    uppers = FACES * (FACES - 1) // 2
    anywhere = pl.BlockSpec(memory_space=pl.ANY)
    main_memory = pl.BlockSpec(memory_space=pltpu.HBM)
    scalars = pl.BlockSpec(memory_space=pltpu.SMEM)
    early, late = (4, 5), (0, 1, 2, 3)
    faces = (early, late)
    planes = counts[2]

    def shape(*dims):
        return jax.ShapeDtypeStruct(dims, jnp.float32)

    def halves(count):
        return jax.ShapeDtypeStruct((count, 2, width, width), jnp.bfloat16)

    def params(mib):
        return pltpu.CompilerParams(vmem_limit_bytes=mib * MIB)

    def cost(us):
        return pl.CostEstimate(flops=us * 10**9, bytes_accessed=2**20, transcendentals=0)

    *packed, own = pl.pallas_call(
        functools.partial(pack_kernel, counts, width),
        out_shape=face_shapes(counts[0], (width + 8 + 2 * ncon, half))
        + face_shapes(counts[1], (width + 8 + 2 * ncon, half))
        + face_shapes(counts[2], (width + 8, half))
        + [shape(FACES, width, width)],
        in_specs=[main_memory, main_memory],
        out_specs=vmem_specs(arrays + 1),
        scratch_shapes=[
            pltpu.VMEM((4, ncon, width), jnp.float32),
            pltpu.SemaphoreType.DMA((FACES,)),
            pltpu.SemaphoreType.DMA,
        ],
        compiler_params=params(12),
    )(matrix, pltpu.with_memory_space_constraint(starts, pltpu.HBM))
    ends = [sum(face_arrays(count) for count in counts[:position]) for position in range(4)]
    got = {}
    for position in (2, 0, 1):
        got[position] = exchange(packed[ends[position] : ends[position + 1]], AXES[position])

    own_halves, upper_halves, flags = pl.pallas_call(
        functools.partial(halves_kernel, planes),
        out_shape=[halves(FACES), halves(uppers), shape(8, 128)],
        in_specs=[main_memory, scalars] + vmem_specs(1),
        out_specs=vmem_specs(3),
        scratch_shapes=[
            pltpu.VMEM((FACES - 1, width, order), jnp.float32),
            pltpu.SemaphoreType.DMA((FACES - 1,)),
        ],
        compiler_params=params(24),
        cost_estimate=cost(2),
    )(matrix, group_of, own)

    early_basis, early_partner, early_inverse = pl.pallas_call(
        functools.partial(early_kernel, AXES[2:3], early),
        out_shape=[shape(len(early), ncon, width)] + [halves(len(early))] * 2,
        in_specs=vmem_specs(len(got[2]) + 3),
        out_specs=vmem_specs(3),
        compiler_params=params(16),
        cost_estimate=cost(2),
    )(*got[2], own, own_halves, starts)

    payload, product, late_partner, late_inverse = pl.pallas_call(
        functools.partial(main_kernel, (AXES[0], AXES[1]), early, late),
        out_shape=[shape(message_rows + rest_rows, columns), shape(FACES, ncon, width)]
        + [halves(len(late))] * 2,
        in_specs=vmem_specs(len(got[0]) + len(got[1]) + 6),
        out_specs=vmem_specs(4),
        compiler_params=params(24),
        cost_estimate=cost(8),
    )(*got[0], *got[1], own, own_halves, upper_halves, starts, right, early_basis)

    partners = [early_partner, late_partner]
    inverses = [early_inverse, late_inverse]
    their_basis, their_product = pl.pallas_call(
        functools.partial(theirs_kernel, faces, ncon),
        out_shape=[shape(4, ncon, width)] * 2,
        in_specs=vmem_specs(5 + len(got[0]) + len(got[1])),
        out_specs=vmem_specs(2),
        compiler_params=params(16),
        cost_estimate=cost(2),
    )(own_halves, *got[0], *got[1], *partners, *inverses)

    def spread_of(token):
        return pl.pallas_call(
            functools.partial(spread_kernel, faces),
            out_shape=jax.ShapeDtypeStruct((4, width, 3 * size), jnp.bfloat16),
            in_specs=[anywhere] + vmem_specs(5),
            out_specs=vmem_specs(1)[0],
            compiler_params=params(16),
            cost_estimate=cost(2),
        )(token, their_basis, their_product, product, *inverses)

    def solve(firsts, matrices, rights, unread):
        first = pl.pallas_call(
            first_kernel,
            out_shape=shape(size, size),
            in_specs=vmem_specs(len(firsts)),
            out_specs=vmem_specs(1)[0],
            compiler_params=params(8),
            cost_estimate=cost(2),
        )(*firsts)
        return pl.pallas_call(
            functools.partial(solve_kernel, size, len(matrices), columns),
            out_shape=shape(coarse, columns),
            in_specs=vmem_specs(1 + 2 * len(matrices)) + [anywhere] * len(unread),
            out_specs=vmem_specs(1)[0],
            compiler_params=params(12),
            cost_estimate=cost(7),
        )(first, *matrices, *rights, *unread)

    result = dict(
        out_shape=shape(order, columns),
        out_specs=main_memory,
        scratch_shapes=[
            pltpu.VMEM((order, columns), jnp.float32),
            pltpu.SemaphoreType.DMA((FACES,)),
        ],
        compiler_params=params(12),
        cost_estimate=cost(1),
    )
    groups = group_of.shape[0] // GROUP_SIZE
    if groups == 2 and counts[1] == 4 and planes == 2:
        core_swap, chip_x, chip_y = flipped("gy", 1), flipped("gy", 2), flipped("gz", 1)
        other = lax.ppermute(payload, "gy", core_swap)
        left, rest = pl.pallas_call(
            choose_kernel,
            out_shape=[shape(message_rows, columns), shape(rest_rows, columns)],
            in_specs=vmem_specs(3) + [anywhere],
            out_specs=vmem_specs(2),
            compiler_params=params(8),
        )(flags, payload, other, their_basis)
        left_moved = lax.ppermute(left, "gy", chip_x)
        rest_moved = lax.ppermute(rest, "gz", chip_y)
        spread = spread_of(left)
        first_last, left_last, rest_last, *sent = pl.pallas_call(
            add_kernel,
            out_shape=[
                shape(first_rows, columns),
                shape(message_rows - first_rows, columns),
                shape(rest_rows, columns),
            ]
            + face_shapes(counts[2], (ncon, width)),
            in_specs=vmem_specs(5) + [anywhere],
            out_specs=vmem_specs(3 + face_arrays(counts[2])),
            compiler_params=params(8),
        )(left, left_moved, rest, rest_moved, product, spread)
        first_other = lax.ppermute(first_last, "gz", chip_y)
        left_other = lax.ppermute(left_last, "gz", chip_y)
        rest_other = lax.ppermute(rest_last, "gy", chip_x)
        theirs = exchange(sent, AXES[2])
        answer = solve(
            [first_last, first_other], [left_last, left_other], [rest_last, rest_other], []
        )
        there = lax.ppermute(answer, "gy", core_swap)
        *sent, mine = pl.pallas_call(
            functools.partial(rows_kernel, ncon),
            out_shape=face_shapes(counts[0], (ncon, columns)) + [shape(size, columns)],
            in_specs=vmem_specs(3),
            out_specs=vmem_specs(face_arrays(counts[0]) + 1),
            compiler_params=params(8),
        )(flags, answer, there)
        across = exchange(sent, AXES[0])
        correction = pl.pallas_call(
            functools.partial(last_near_kernel, faces),
            in_specs=vmem_specs(7 + len(theirs)),
            **result,
        )(flags, product, *inverses, spread, answer, there, *theirs)
    else:
        y, z = lax.axis_index("gy"), lax.axis_index("gz")
        member_of = group_of[y * planes + z]
        chosen = jnp.arange(groups, dtype=jnp.int32) == member_of
        total = lax.psum(jnp.where(chosen[:, None, None], payload[None], 0.0), ("gy", "gz"))
        total = lax.dynamic_index_in_dim(total, member_of, 0, keepdims=False)
        spread = spread_of(payload)
        answer = solve(
            [total[:first_rows]], [total[first_rows:message_rows]], [total[message_rows:]], []
        )

        def from_near(faces_of, axis):
            even, odd = faces_of
            if lax.axis_size(axis) == 2:
                return exchange([jnp.stack([even, odd])], axis)
            upward = is_even(axis)
            return exchange([jnp.where(upward, even, odd), jnp.where(upward, odd, even)], axis)

        blocks = answer.reshape(FACES, ncon, columns)
        near = [
            *from_near(product[4:6], AXES[2]),
            *from_near(blocks[2:4], AXES[1]),
            *from_near(blocks[4:6], AXES[2]),
        ]
        mine = answer[:size]
        across = from_near(blocks[:2], AXES[0])
        correction = pl.pallas_call(
            functools.partial(last_plain_kernel, faces),
            in_specs=vmem_specs(5 + len(near)),
            **result,
        )(product, *inverses, spread, answer, *near)
    correction = pl.pallas_call(
        functools.partial(last_far_kernel, ncon),
        in_specs=vmem_specs(2 + len(across)) + [main_memory],
        input_output_aliases={2 + len(across): 0},
        **result,
    )(spread, mine, *across, correction)
    return correction[None, None, None]


def solution(mesh):
    in_specs = (
        P("gx", "gy", "gz", None, None),
        P("gx", "gy", "gz", None, None, None),
        P("gx", "gy", "gz", None, None),
        P(),
    )
    out_specs = P("gx", "gy", "gz", None, None)
    return jax.shard_map(
        per_device, mesh=mesh, in_specs=in_specs, out_specs=out_specs, check_vma=False
    )
```

```python
import functools

import jax
import jax.numpy as jnp
from jax import lax
from jax.experimental import pallas as pl
from jax.experimental.pallas import tpu as pltpu
from jax.sharding import PartitionSpec as P

NS_ITERS = 3
SUB_ITERS = 2
GROUP_SIZE = 4
FACES = 6
BLOCKS = FACES // 2
AXES = ("gx", "gy", "gz")
MIB = 1024 * 1024

precise = lax.Precision.HIGHEST


def dot(left, right, dims=((1,), (0,))):
    return lax.dot_general(
        left, right, (dims, ((), ())), precision=precise, preferred_element_type=jnp.float32
    )


def split(value):
    high = value.astype(jnp.bfloat16)
    return high, (value - high.astype(jnp.float32)).astype(jnp.bfloat16)


def wide(left, right):
    return lax.dot_general(
        jnp.concatenate([left[0], left[0], left[1]], axis=1),
        jnp.concatenate([right[0], right[1], right[0]], axis=0),
        (((1,), (0,)), ((), ())),
        preferred_element_type=jnp.float32,
    )


def stacked(value):
    return jnp.concatenate(split(value), axis=0)


def thin(rows, matrix):
    out = lax.dot_general(
        jnp.concatenate([rows, rows], axis=1),
        jnp.concatenate(matrix, axis=0),
        (((1,), (0,)), ((), ())),
        preferred_element_type=jnp.float32,
    )
    half = rows.shape[0] // 2
    return out[:half] + out[half:]


def triple(left, right, dims=((1,), (0,))):
    (left_high, left_low), (right_high, right_low) = split(left), split(right)
    total = None
    for one, other in ((left_high, right_high), (left_high, right_low), (left_low, right_high)):
        part = lax.dot_general(
            one, other, (dims, ((), ())), preferred_element_type=jnp.float32
        )
        total = part if total is None else total + part
    return total


def iota(shape, dim):
    return lax.broadcasted_iota(jnp.int32, shape, dim)


def flipped(axis, bit):
    return [(i, i ^ bit) for i in range(lax.axis_size(axis))]


def outer_pairs(axis):
    count = lax.axis_size(axis)
    return [(i, (i + 1 if i % 2 else i - 1) % count) for i in range(count)]


def face_arrays(count):
    return 1 if count == 2 else 2


def exchange(arrays, axis):
    if lax.axis_size(axis) == 2:
        return [lax.ppermute(arrays[0], axis, flipped(axis, 1))]
    return [
        lax.ppermute(arrays[0], axis, outer_pairs(axis)),
        lax.ppermute(arrays[1], axis, flipped(axis, 1)),
    ]


def is_even(axis):
    return lax.rem(lax.axis_index(axis), 2) == 0


def send(refs, axis, even, odd):
    if lax.axis_size(axis) == 2:
        refs[0][0] = even
        refs[0][1] = odd
    else:
        upward = is_even(axis)
        refs[0][...] = jnp.where(upward, even, odd)
        refs[1][...] = jnp.where(upward, odd, even)


def receive(refs, axis):
    if lax.axis_size(axis) == 2:
        return refs[0][1], refs[0][0]
    upward = is_even(axis)
    first, second = refs[0][...], refs[1][...]
    return jnp.where(upward, first, second), jnp.where(upward, second, first)


def face_shapes(count, shape):
    if count == 2:
        return [jax.ShapeDtypeStruct((2,) + shape, jnp.float32)]
    return [jax.ShapeDtypeStruct(shape, jnp.float32)] * 2


def vmem_specs(count):
    return [pl.BlockSpec(memory_space=pltpu.VMEM)] * count


def pack_kernel(counts, width, schur_ref, starts_ref, *refs):
    outs, blocks = refs[:-4], refs[-4]
    starts, sems, start_sem = refs[-3:]
    half = width // 2
    start_copy = pltpu.make_async_copy(starts_ref.at[pl.ds(0, 4)], starts, start_sem)
    start_copy.start()
    copies = []
    for f in range(FACES):
        place = pl.ds(f * width, width)
        copy = pltpu.make_async_copy(schur_ref.at[place, place], blocks.at[f], sems.at[f])
        copy.start()
        copies.append(copy)
    row, col = iota((half, half), 0), iota((half, half), 1)
    start_copy.wait()

    def pack(f):
        copies[f].wait()
        first = blocks[f, 0:half, 0:half]
        second = blocks[f, half:width, half:width]
        diag = jnp.sum(jnp.where(row == col, second, 0.0), axis=0, keepdims=True)
        mixed = jnp.where(row >= col, first, second)
        tail = jnp.broadcast_to(diag, (8, half))
        parts = [blocks[f, half:width, 0:half], mixed, tail]
        if f < 4:
            parts += [starts[f, :, :half], starts[f, :, half:]]
        return jnp.concatenate(parts, axis=0)

    done = 0
    for position, axis in enumerate(AXES):
        number = face_arrays(counts[position])
        send(outs[done : done + number], axis, pack(2 * position), pack(2 * position + 1))
        done += number


def unpack(packed):
    half = packed.shape[1]
    row, col = iota((half, half), 0), iota((half, half), 1)
    low = packed[0:half]
    mixed = packed[half : 2 * half]
    flip = mixed.T
    first = jnp.where(row >= col, mixed, flip)
    second = jnp.where(row < col, mixed, flip)
    second = jnp.where(row == col, packed[2 * half : 2 * half + 1], second)
    return jnp.concatenate(
        [jnp.concatenate([first, low.T], axis=1), jnp.concatenate([low, second], axis=1)], axis=0
    )


def unpack_starts(packed, ncon):
    half = packed.shape[1]
    rows = packed[2 * half + 8 :]
    return jnp.concatenate([rows[:ncon], rows[ncon:]], axis=1)


def factor_inverses(grams):
    size = grams[0].shape[0]
    strips, block, lanes = size // 8, 8, 128
    full = (block, lanes)
    beside = lanes // (2 * size)
    one = jnp.where(iota((size, size), 0) == iota((size, size), 1), 1.0, 0.0)
    states = []
    for first in range(0, len(grams), beside):
        parts = [part for gram in grams[first : first + beside] for part in (gram, one)]
        whole = jnp.concatenate(parts, axis=1)
        states.append([whole[8 * s : 8 * s + 8] for s in range(strips)])
    below = iota(full, 0)
    base = iota(full, 1) // (2 * size) * (2 * size)

    def column(rows, k):
        if beside == 1:
            return jnp.broadcast_to(rows[:, k : k + 1], full)
        return jnp.take_along_axis(rows, base + k, axis=1, mode="promise_in_bounds")

    def line_of(rows, line):
        return jnp.broadcast_to(rows[line : line + 1], full)

    roots = [[None] * strips for _ in states]
    for strip in range(strips):
        start = strip * block
        columns = [
            [[column(work[s], start + j) for s in range(strip, strips)] for j in range(block)]
            for work in states
        ]
        heads = [[column_set[0] for column_set in per_state] for per_state in columns]
        lowers = [work[strip] for work in states]
        solved = list(lowers)
        pivots = [jnp.ones(full, jnp.float32) for _ in states]
        scales = list(pivots)

        def eliminate(i, j, scale, pivot, side):
            cols = heads[i]
            factor = jnp.where(below != j, cols[j] * scale, 0.0)
            for later in range(j + 1, block):
                use = side if later == j + 1 and side is not None else line_of(cols[later], j)
                cols[later] = cols[later] - factor * use
            row = line_of(lowers[i], j)
            solved[i] = solved[i] - factor * row
            lowers[i] = lowers[i] - jnp.where(below > j, factor, 0.0) * row
            pivots[i] = jnp.where(below == j, pivot, pivots[i])
            scales[i] = jnp.where(below == j, scale, scales[i])

        for j in range(0, block, 2):
            for i in range(len(states)):
                cols = heads[i]
                corner, side = line_of(cols[j], j), line_of(cols[j], j + 1)
                last = line_of(cols[j + 1], j + 1)
                minor = corner * last - side * side
                scale = 1.0 / corner
                eliminate(i, j, scale, corner, side)
                eliminate(i, j + 1, corner * (1.0 / minor), minor * scale, None)
        for i, work in enumerate(states):
            work[strip] = lowers[i]
            roots[i][strip] = lax.rsqrt(pivots[i])
            if strip == strips - 1:
                continue
            answer = solved[i] * scales[i]
            rows = [line_of(answer, j) for j in range(block)]
            for s in range(strip + 1, strips):
                for j in range(block):
                    work[s] = work[s] - columns[i][j][s - strip] * rows[j]
    results = []
    for i, work in enumerate(states):
        scaled = jnp.concatenate([work[s] * roots[i][s] for s in range(strips)], axis=0)
        for m in range(beside):
            begin = (2 * m + 1) * size
            results.append(scaled[:, begin : begin + size])
    return results


def factor_inverse(gram):
    size = gram.shape[0]
    strips, block, lanes = size // 8, 8, 128
    full = (block, lanes)
    parts = [gram, jnp.where(iota((size, size), 0) == iota((size, size), 1), 1.0, 0.0)]
    if 2 * size < lanes:
        parts.append(jnp.zeros((size, lanes - 2 * size), jnp.float32))
    whole = jnp.concatenate(parts, axis=1)
    work = [whole[8 * s : 8 * s + 8] for s in range(strips)]
    below = iota(full, 0)

    def line_of(rows, line):
        return jnp.broadcast_to(rows[line : line + 1], full)

    for strip in range(strips):
        start = strip * block
        active = range(strip, strips)
        cols = [
            {s: jnp.broadcast_to(work[s][:, start + j : start + j + 1], full) for s in active}
            for j in range(block)
        ]
        factors = []

        def eliminate(j, scale):
            factor = {s: cols[j][s] * scale for s in active}
            factor[strip] = jnp.where(below > j, factor[strip], 0.0)
            for later in range(j + 1, block):
                head = line_of(cols[later][strip], j)
                for s in active:
                    cols[later][s] = cols[later][s] - factor[s] * head
            factors.append(factor)

        for j in range(0, block, 2):
            corner = line_of(cols[j][strip], j)
            side = line_of(cols[j][strip], j + 1)
            last = line_of(cols[j + 1][strip], j + 1)
            inverse = 1.0 / (corner * last - side * side)
            eliminate(j, 1.0 / corner)
            eliminate(j + 1, corner * inverse)
        for j in range(block):
            row = line_of(work[strip], j)
            for s in active:
                if s == strip and j == block - 1:
                    continue
                work[s] = work[s] - factors[j][s] * row
    parts = []
    for s in range(strips):
        place = iota((8, size), 0) + 8 * s == iota((8, size), 1)
        pivot = jnp.sum(jnp.where(place, work[s][:, :size], 0.0), axis=1, keepdims=True)
        parts.append(work[s][:, size : 2 * size] * lax.rsqrt(pivot))
    return jnp.concatenate(parts, axis=0)


def member(group_ref, planes, dy=0, dz=0):
    y, z = lax.axis_index("gy"), lax.axis_index("gz")
    rows = lax.axis_size("gy")
    return group_ref[lax.rem(y + dy + rows, rows) * planes + lax.rem(z + dz + planes, planes)]


def store(ref, f, value):
    ref[f, 0], ref[f, 1] = split(value)


def load(ref, f):
    return ref[f, 0], ref[f, 1]


def upper_index(f, g):
    return sum(FACES - 1 - i for i in range(f)) + g - f - 1


def halves_kernel(planes, schur_ref, group_ref, own_ref, own_out, upper_out, flag_out, *scratch):
    upper_ref, sems = scratch
    width = own_ref.shape[1]
    strips = []
    for f in range(FACES - 1):
        rest = (FACES - 1 - f) * width
        copy = pltpu.make_async_copy(
            schur_ref.at[pl.ds(f * width, width), pl.ds((f + 1) * width, rest)],
            upper_ref.at[f, :, pl.ds((f + 1) * width, rest)],
            sems.at[f],
        )
        copy.start()
        strips.append(copy)
    core = lax.rem(lax.axis_index("gy"), 2)
    near = [(0, 0), (1 - 2 * core, 0), (-1, 0), (1, 0), (0, -1), (0, 1)]
    row = iota(flag_out.shape, 0)
    flags = jnp.zeros(flag_out.shape, jnp.float32)
    for i, (dy, dz) in enumerate(near):
        hit = member(group_ref, planes, dy, dz) == core
        flags = jnp.where(row == i, jnp.where(hit, 1.0, 0.0), flags)
    flag_out[...] = flags
    for f in range(FACES):
        store(own_out, f, own_ref[f])
    for f in range(FACES - 1):
        strips[f].wait()
        for g in range(f + 1, FACES):
            store(upper_out, upper_index(f, g), upper_ref[f, :, g * width : (g + 1) * width])


def inverses_of(packed, owns, partner_ref):
    width = owns[0].shape[1]
    half = width // 2
    eye = iota((half, half), 0) == iota((half, half), 1)
    whole_eye = iota((width, width), 0) == iota((width, width), 1)
    powers, sums, downs = [], [], []
    for f in range(len(packed)):
        partner = unpack(packed[f])
        store(partner_ref, f, partner)
        total = owns[f] + partner
        across, down = [], []
        for start in (0, half):
            block = total[start : start + half, start : start + half]
            diagonal = jnp.where(eye, block, 0.0)
            across.append(1.0 / jnp.sum(diagonal, axis=0, keepdims=True))
            down.append(1.0 / jnp.sum(diagonal, axis=1, keepdims=True))
        downs.append(jnp.concatenate(down, axis=0))
        power = jnp.where(whole_eye, 0.0, -total * jnp.concatenate(across, axis=1))
        powers.append(split(power))
        sums.append(jnp.where(whole_eye, 1.0, power))
    for step in range(1, NS_ITERS):
        powers = [split(wide(power, power)) for power in powers]
        sums = [total + wide(split(total), power) for total, power in zip(sums, powers)]
    return [down * total for down, total in zip(downs, sums)]


def unit_rows(basis):
    return [b * lax.rsqrt(jnp.sum(b * b, axis=1, keepdims=True)) for b in basis]


def sweep_basis(before, inverse, after, basis):
    for matrices in (before, inverse, after):
        basis = [thin(stacked(b), matrix) for b, matrix in zip(basis, matrices)]
    return unit_rows(basis)


def early_kernel(axes, faces, *refs):
    arrays = len(refs) - 6
    inputs = refs[:arrays]
    own_ref, halves_ref, starts_ref, basis_out, partner_out, inverse_out = refs[arrays:]
    count = len(faces)
    packed = []
    done = 0
    for axis in axes:
        number = face_arrays(lax.axis_size(axis))
        packed += receive(inputs[done : done + number], axis)
        done += number
    inverses = inverses_of(packed, [own_ref[f] for f in faces], partner_out)
    for i in range(count):
        store(inverse_out, i, inverses[i])
    basis = [starts_ref[f] for f in faces]
    matrices = [
        [load(partner_out, i) for i in range(count)],
        [load(inverse_out, i) for i in range(count)],
        [load(halves_ref, f) for f in faces],
    ]
    for sweep in range(SUB_ITERS):
        basis = sweep_basis(*matrices, basis)
    for i in range(count):
        basis_out[i] = basis[i]


def main_kernel(axes, early, late, *refs):
    arrays = len(refs) - 10
    inputs = refs[:arrays]
    own_ref, halves_ref, upper_ref, starts_ref, resid_ref, early_basis = refs[arrays : arrays + 6]
    payload_ref, product_ref, partner_out, inverse_out = refs[arrays + 6 :]
    ncon, width = starts_ref.shape[1:]
    columns = resid_ref.shape[1]
    sides = {}
    rights = {}
    grams = {}
    vectors = {}
    count = len(late)

    def project(f, basis):
        vectors[f] = basis
        rows = stacked(basis)
        grams[f] = dot(basis, basis, ((1,), (1,)))
        side = {f: thin(rows, load(halves_ref, f))}
        for g in range(f + 1, FACES):
            side[g] = thin(rows, load(upper_ref, upper_index(f, g)))
        sides[f] = side
        rights[f] = thin(rows, split(resid_ref[f * width : (f + 1) * width]))

    packed = []
    done = 0
    for axis in axes:
        number = face_arrays(lax.axis_size(axis))
        packed += receive(inputs[done : done + number], axis)
        done += number
    inverses = inverses_of(packed, [own_ref[f] for f in late], partner_out)
    pending = [(f, early_basis[i]) for i, f in enumerate(early)]
    for i in range(count):
        store(inverse_out, i, inverses[i])
    basis = [starts_ref[f] for f in late]
    matrices = [
        [load(partner_out, i) for i in range(count)],
        [load(inverse_out, i) for i in range(count)],
        [load(halves_ref, f) for f in late],
    ]
    for sweep in range(SUB_ITERS):
        basis = sweep_basis(*matrices, basis)
        if pending:
            project(*pending.pop(0))
    for item in pending:
        project(*item)
    for i, f in enumerate(late):
        project(f, basis[i])
    tall = {}
    for g in range(FACES):
        column = jnp.concatenate([sides[f][g] for f in range(g + 1)], axis=0)
        column = triple(column, vectors[g], ((1,), (1,)))
        for f in range(g + 1):
            tall[f, g] = column[f * ncon : (f + 1) * ncon]
    for f in range(0, FACES, 2):
        tall[f + 1, f] = tall[f, f + 1].T
    zero = jnp.zeros((ncon, ncon), jnp.float32)

    def square(parts):
        lines = []
        for f in range(FACES):
            line = [parts.get((f, g), zero) for g in range(FACES)]
            lines.append(jnp.concatenate(line, axis=1))
        return jnp.concatenate(lines, axis=0)

    coarse = square(tall)
    right = jnp.concatenate([rights[f] for f in range(FACES)], axis=0)
    factors = factor_inverses([grams[f] for f in range(FACES)])
    factor = square({(f, f): factors[f] for f in range(FACES)})
    coarse = triple(factor, triple(coarse, factor, ((1,), (1,))))
    right = triple(factor, right)
    for f in range(FACES):
        product_ref[f] = triple(factors[f], sides[f][f])
    size = 2 * ncon
    blocks = {
        (b, c): coarse[b * size : (b + 1) * size, c * size : (c + 1) * size]
        for b in range(BLOCKS)
        for c in range(b, BLOCKS)
    }
    payload_ref[...] = jnp.concatenate([pack_coarse(blocks, size), right], axis=0)


def pack_coarse(blocks, size):
    row, col = iota((size, size), 0), iota((size, size), 1)
    diagonal = jnp.sum(jnp.where(row == col, blocks[2, 2], 0.0), axis=0, keepdims=True)
    tail = jnp.broadcast_to(jnp.concatenate([diagonal, diagonal], axis=1), (8, 2 * size))
    shared = jnp.where(row >= col, blocks[1, 1], blocks[2, 2])
    half = size // 2
    return jnp.concatenate(
        [
            jnp.concatenate([blocks[0, 0][:half], blocks[0, 0][half:]], axis=1),
            jnp.concatenate([shared, blocks[0, 1]], axis=1),
            jnp.concatenate([blocks[0, 2], blocks[1, 2]], axis=1),
            tail,
        ],
        axis=0,
    )


def unpack_coarse(packed, size):
    row, col = iota((size, size), 0), iota((size, size), 1)
    shared = packed[:size, :size]
    flip = shared.T
    diagonal = packed[2 * size : 2 * size + 1, :size]
    return {
        (1, 1): jnp.where(row >= col, shared, flip),
        (2, 2): jnp.where(row < col, shared, jnp.where(row > col, flip, diagonal)),
        (0, 1): packed[:size, size:],
        (0, 2): packed[size : 2 * size, :size],
        (1, 2): packed[size : 2 * size, size:],
    }


def find(faces, refs, f):
    for group, ref in zip(faces, refs):
        if f in group:
            return load(ref, list(group).index(f))


def theirs_kernel(faces, ncon, own_ref, *refs):
    inputs, partner_refs, inverse_refs = refs[:-5], refs[-5:-3], refs[-3:-1]
    product_out = refs[-1]
    basis = []
    done = 0
    for axis in AXES[:2]:
        number = face_arrays(lax.axis_size(axis))
        packed = receive(inputs[done : done + number], axis)
        basis += [unpack_starts(part, ncon) for part in packed]
        done += number
    count = len(basis)
    matrices = [
        [load(own_ref, f) for f in range(count)],
        [find(faces, inverse_refs, f) for f in range(count)],
        [find(faces, partner_refs, f) for f in range(count)],
    ]
    for sweep in range(SUB_ITERS):
        basis = sweep_basis(*matrices, basis)
    factors = factor_inverses([dot(b, b, ((1,), (1,))) for b in basis])
    for f in range(count):
        product_out[f] = triple(factors[f], thin(stacked(basis[f]), matrices[2][f]))


def spread_kernel(faces, unread, theirs_ref, product_ref, *refs):
    inverse_refs, out_ref = refs[:2], refs[2]
    for f in range(theirs_ref.shape[0]):
        both = jnp.concatenate([product_ref[f], theirs_ref[f]], axis=0)
        high, low = split(thin(stacked(both), find(faces, inverse_refs, f)).T)
        out_ref[f] = jnp.concatenate([high, high, low], axis=1)


def choose_kernel(flag_ref, here_ref, there_ref, matrix_ref, right_ref):
    mine = flag_ref[0:1, 0:1] > 0.5
    other = flag_ref[1:2, 0:1] > 0.5
    total = jnp.where(mine, here_ref[...], 0.0) + jnp.where(other, there_ref[...], 0.0)
    rows = matrix_ref.shape[0]
    matrix_ref[...] = total[:rows]
    right_ref[...] = total[rows:]


def add_kernel(first_ref, second_ref, third_ref, fourth_ref, product_ref, unread, *refs):
    first_out, matrix_ref, right_ref, *sent = refs
    total = first_ref[...] + second_ref[...]
    rows = first_out.shape[0]
    first_out[...] = total[:rows]
    matrix_ref[...] = total[rows:]
    right_ref[...] = third_ref[...] + fourth_ref[...]
    send(sent, AXES[2], product_ref[4], product_ref[5])


def first_kernel(*refs):
    total = refs[0][...]
    for ref in refs[1:-1]:
        total = total + ref[...]
    size = total.shape[1] // 2
    block = jnp.concatenate([total[:, :size], total[:, size:]], axis=0)
    eye = iota((size, size), 0) == iota((size, size), 1)
    diagonal = jnp.where(eye, block, 0.0)
    down = lax.rsqrt(jnp.sum(diagonal, axis=1, keepdims=True))
    across = lax.rsqrt(jnp.sum(diagonal, axis=0, keepdims=True))
    refs[-1][...] = factor_inverse(down * block * across) * across


def solve_kernel(size, terms, columns, first_ref, *refs):
    upper, lower = refs[0][...], refs[terms][...]
    for term in range(1, terms):
        upper = upper + refs[term][...]
        lower = lower + refs[terms + term][...]
    answer_ref = refs[-1]
    total = jnp.concatenate([upper, lower], axis=0)
    rows = 2 * size + 8
    blocks, right = unpack_coarse(total[:rows], size), total[rows:]
    eye = iota((size, size), 0) == iota((size, size), 1)
    downs, acrosses, rights = [], [], []
    for b in range(BLOCKS):
        if b == 0:
            downs.append(jnp.ones((size, 1), jnp.float32))
            acrosses.append(jnp.ones((1, size), jnp.float32))
        else:
            diagonal = jnp.where(eye, blocks[b, b], 0.0)
            downs.append(lax.rsqrt(jnp.sum(diagonal, axis=1, keepdims=True)))
            acrosses.append(lax.rsqrt(jnp.sum(diagonal, axis=0, keepdims=True)))
        rights.append(downs[b] * right[b * size : (b + 1) * size])
    for b in range(BLOCKS):
        for c in range(max(b, 1), BLOCKS):
            blocks[b, c] = downs[b] * blocks[b, c] * acrosses[c]
            if c > b:
                blocks[c, b] = blocks[b, c].T
    for b in range(BLOCKS):
        inverse = factor_inverse(blocks[b, b]) if b else first_ref[...]
        later = range(b + 1, BLOCKS)
        row = triple(inverse, jnp.concatenate([rights[b]] + [blocks[b, c] for c in later], axis=1))
        if later:
            column = jnp.concatenate([blocks[c, b] for c in later], axis=0)
            change = triple(triple(column, inverse, ((1,), (1,))), row)
        for i, c in enumerate(later):
            part = change[i * size : (i + 1) * size]
            rights[c] = rights[c] - part[:, :columns]
            for j, d in enumerate(later):
                start = columns + j * size
                blocks[c, d] = blocks[c, d] - part[:, start : start + size]
        row = triple(inverse, row, ((0,), (0,)))
        rights[b] = row[:, :columns]
        for c in later:
            blocks[b, c] = row[:, columns + (c - b - 1) * size : columns + (c - b) * size]
        for i in range(b):
            for c in later:
                blocks[i, c] = blocks[i, c] - triple(blocks[i, b], blocks[b, c])
            rights[i] = rights[i] - triple(blocks[i, b], rights[b])
    answer = [downs[b] * rights[b] for b in range(BLOCKS)]
    answer_ref[...] = jnp.concatenate(answer, axis=0)


def rows_kernel(ncon, flag_ref, here_ref, there_ref, *refs):
    hit = flag_ref[0:1, 0:1] > 0.5
    rows = jnp.where(hit, here_ref[: 2 * ncon], there_ref[: 2 * ncon])
    refs[-1][...] = rows
    send(refs[:-1], AXES[0], rows[:ncon], rows[ncon:])


def last_product(spread, mine, theirs):
    high, low = split(jnp.concatenate([mine, theirs], axis=0))
    return lax.dot_general(
        spread,
        jnp.concatenate([high, low, high], axis=0),
        (((1,), (0,)), ((), ())),
        preferred_element_type=jnp.float32,
    )


def through(inverse, mine, theirs, my_answer, their_answer):
    high, low = split(jnp.concatenate([mine, theirs], axis=0).T)
    spread = jnp.concatenate([high, high, low], axis=1)
    return wide(inverse, split(last_product(spread, my_answer, their_answer)))


def last_faces(values, width, out_ref, result, sems):
    copies = []
    for f, value in values.items():
        place = pl.ds(f * width, width)
        result[f * width : (f + 1) * width] = value()
        copy = pltpu.make_async_copy(result.at[place], out_ref.at[place], sems.at[f])
        copy.start()
        copies.append(copy)
    for copy in copies:
        copy.wait()


def last_plain_kernel(faces, product_ref, early_inverse, late_inverse, *refs):
    spread_ref, answer_ref, *inputs = refs[:-3]
    ncon, width = product_ref.shape[1:]
    number = face_arrays(lax.axis_size(AXES[2]))
    theirs = receive(inputs[:number], AXES[2])
    near = receive(inputs[number:-number], AXES[1]) + receive(inputs[-number:], AXES[2])
    values = {}
    for f in range(2, FACES):
        mine = answer_ref[f * ncon : (f + 1) * ncon]
        if f < 4:
            values[f] = functools.partial(last_product, spread_ref[f], mine, near[f - 2])
        else:
            values[f] = functools.partial(
                through,
                find(faces, (early_inverse, late_inverse), f),
                product_ref[f],
                theirs[f - 4],
                mine,
                near[f - 2],
            )
    last_faces(values, width, *refs[-3:])


def last_near_kernel(faces, flag_ref, product_ref, early_inverse, late_inverse, *refs):
    spread_ref, here_answer, there_answer = refs[:3]
    theirs = receive(refs[3:-3], AXES[2])
    ncon, width = product_ref.shape[1:]

    def answer(flag, f):
        place = slice(f * ncon, (f + 1) * ncon)
        hit = flag_ref[flag : flag + 1, 0:1] > 0.5
        return jnp.where(hit, here_answer[place], there_answer[place])

    values = {}
    for f in (2, 3):
        values[f] = functools.partial(
            last_product, spread_ref[f], answer(0, f), answer(f, f ^ 1)
        )
    for f in (4, 5):
        values[f] = functools.partial(
            through,
            find(faces, (early_inverse, late_inverse), f),
            product_ref[f],
            theirs[f - 4],
            answer(0, f),
            answer(f, f ^ 1),
        )
    last_faces(values, width, *refs[-3:])


def last_far_kernel(ncon, spread_ref, rows_ref, *refs):
    theirs = receive(refs[:-4], AXES[0])
    values = {}
    for f in range(2):
        mine = rows_ref[f * ncon : (f + 1) * ncon]
        values[f] = functools.partial(last_product, spread_ref[f], mine, theirs[f])
    last_faces(values, spread_ref.shape[1], *refs[-3:])


def per_device(schur, start_block, resid, group_of):
    matrix = schur[0, 0, 0]
    matrix = pltpu.with_memory_space_constraint(matrix, pltpu.HBM)
    starts = start_block[0, 0, 0].transpose(0, 2, 1)
    right = resid[0, 0, 0]
    order, columns = right.shape
    ncon, width = starts.shape[1:]
    counts = [lax.axis_size(axis) for axis in AXES]
    arrays = sum(face_arrays(count) for count in counts)
    coarse = FACES * ncon
    size = 2 * ncon
    half = width // 2
    first_rows, message_rows = ncon, (2 * size + ncon + 8 + coarse + 8) // 2
    rest_rows = 2 * size + ncon + 8 + coarse - message_rows
    uppers = FACES * (FACES - 1) // 2
    anywhere = pl.BlockSpec(memory_space=pl.ANY)
    main_memory = pl.BlockSpec(memory_space=pltpu.HBM)
    scalars = pl.BlockSpec(memory_space=pltpu.SMEM)
    early, late = (4, 5), (0, 1, 2, 3)
    faces = (early, late)
    planes = counts[2]

    def shape(*dims):
        return jax.ShapeDtypeStruct(dims, jnp.float32)

    def halves(count):
        return jax.ShapeDtypeStruct((count, 2, width, width), jnp.bfloat16)

    def params(mib):
        return pltpu.CompilerParams(vmem_limit_bytes=mib * MIB)

    def cost(us):
        return pl.CostEstimate(flops=us * 10**9, bytes_accessed=2**20, transcendentals=0)

    *packed, own = pl.pallas_call(
        functools.partial(pack_kernel, counts, width),
        out_shape=face_shapes(counts[0], (width + 8 + 2 * ncon, half))
        + face_shapes(counts[1], (width + 8 + 2 * ncon, half))
        + face_shapes(counts[2], (width + 8, half))
        + [shape(FACES, width, width)],
        in_specs=[main_memory, main_memory],
        out_specs=vmem_specs(arrays + 1),
        scratch_shapes=[
            pltpu.VMEM((4, ncon, width), jnp.float32),
            pltpu.SemaphoreType.DMA((FACES,)),
            pltpu.SemaphoreType.DMA,
        ],
        compiler_params=params(12),
    )(matrix, pltpu.with_memory_space_constraint(starts, pltpu.HBM))
    ends = [sum(face_arrays(count) for count in counts[:position]) for position in range(4)]
    got = {}
    for position in (2, 0, 1):
        got[position] = exchange(packed[ends[position] : ends[position + 1]], AXES[position])

    own_halves, upper_halves, flags = pl.pallas_call(
        functools.partial(halves_kernel, planes),
        out_shape=[halves(FACES), halves(uppers), shape(8, 128)],
        in_specs=[main_memory, scalars] + vmem_specs(1),
        out_specs=vmem_specs(3),
        scratch_shapes=[
            pltpu.VMEM((FACES - 1, width, order), jnp.float32),
            pltpu.SemaphoreType.DMA((FACES - 1,)),
        ],
        compiler_params=params(24),
        cost_estimate=cost(2),
    )(matrix, group_of, own)

    early_basis, early_partner, early_inverse = pl.pallas_call(
        functools.partial(early_kernel, AXES[2:3], early),
        out_shape=[shape(len(early), ncon, width)] + [halves(len(early))] * 2,
        in_specs=vmem_specs(len(got[2]) + 3),
        out_specs=vmem_specs(3),
        compiler_params=params(16),
        cost_estimate=cost(2),
    )(*got[2], own, own_halves, starts)

    payload, product, late_partner, late_inverse = pl.pallas_call(
        functools.partial(main_kernel, (AXES[0], AXES[1]), early, late),
        out_shape=[shape(message_rows + rest_rows, columns), shape(FACES, ncon, width)]
        + [halves(len(late))] * 2,
        in_specs=vmem_specs(len(got[0]) + len(got[1]) + 6),
        out_specs=vmem_specs(4),
        compiler_params=params(24),
        cost_estimate=cost(8),
    )(*got[0], *got[1], own, own_halves, upper_halves, starts, right, early_basis)

    partners = [early_partner, late_partner]
    inverses = [early_inverse, late_inverse]
    their_product = pl.pallas_call(
        functools.partial(theirs_kernel, faces, ncon),
        out_shape=shape(4, ncon, width),
        in_specs=vmem_specs(5 + len(got[0]) + len(got[1])),
        out_specs=vmem_specs(1)[0],
        compiler_params=params(16),
        cost_estimate=cost(2),
    )(own_halves, *got[0], *got[1], *partners, *inverses)

    def spread_of(token):
        return pl.pallas_call(
            functools.partial(spread_kernel, faces),
            out_shape=jax.ShapeDtypeStruct((4, width, 3 * size), jnp.bfloat16),
            in_specs=[anywhere] + vmem_specs(4),
            out_specs=vmem_specs(1)[0],
            compiler_params=params(16),
            cost_estimate=cost(2),
        )(token, their_product, product, *inverses)

    def solve(firsts, matrices, rights, unread):
        first = pl.pallas_call(
            first_kernel,
            out_shape=shape(size, size),
            in_specs=vmem_specs(len(firsts)),
            out_specs=vmem_specs(1)[0],
            compiler_params=params(8),
            cost_estimate=cost(2),
        )(*firsts)
        return pl.pallas_call(
            functools.partial(solve_kernel, size, len(matrices), columns),
            out_shape=shape(coarse, columns),
            in_specs=vmem_specs(1 + 2 * len(matrices)) + [anywhere] * len(unread),
            out_specs=vmem_specs(1)[0],
            compiler_params=params(12),
            cost_estimate=cost(7),
        )(first, *matrices, *rights, *unread)

    result = dict(
        out_shape=shape(order, columns),
        out_specs=main_memory,
        scratch_shapes=[
            pltpu.VMEM((order, columns), jnp.float32),
            pltpu.SemaphoreType.DMA((FACES,)),
        ],
        compiler_params=params(12),
        cost_estimate=cost(1),
    )
    groups = group_of.shape[0] // GROUP_SIZE
    if groups == 2 and counts[1] == 4 and planes == 2:
        core_swap, chip_x, chip_y = flipped("gy", 1), flipped("gy", 2), flipped("gz", 1)
        other = lax.ppermute(payload, "gy", core_swap)
        left, rest = pl.pallas_call(
            choose_kernel,
            out_shape=[shape(message_rows, columns), shape(rest_rows, columns)],
            in_specs=vmem_specs(3),
            out_specs=vmem_specs(2),
            compiler_params=params(8),
        )(flags, payload, other)
        left_moved = lax.ppermute(left, "gy", chip_x)
        rest_moved = lax.ppermute(rest, "gz", chip_y)
        first_last, left_last, rest_last, *sent = pl.pallas_call(
            add_kernel,
            out_shape=[
                shape(first_rows, columns),
                shape(message_rows - first_rows, columns),
                shape(rest_rows, columns),
            ]
            + face_shapes(counts[2], (ncon, width)),
            in_specs=vmem_specs(5) + [anywhere],
            out_specs=vmem_specs(3 + face_arrays(counts[2])),
            compiler_params=params(8),
        )(left, left_moved, rest, rest_moved, product, their_product)
        first_other = lax.ppermute(first_last, "gz", chip_y)
        left_other = lax.ppermute(left_last, "gz", chip_y)
        rest_other = lax.ppermute(rest_last, "gy", chip_x)
        theirs = exchange(sent, AXES[2])
        spread = spread_of(first_other)
        answer = solve(
            [first_last, first_other], [left_last, left_other], [rest_last, rest_other], [spread]
        )
        there = lax.ppermute(answer, "gy", core_swap)
        *sent, mine = pl.pallas_call(
            functools.partial(rows_kernel, ncon),
            out_shape=face_shapes(counts[0], (ncon, columns)) + [shape(size, columns)],
            in_specs=vmem_specs(3),
            out_specs=vmem_specs(face_arrays(counts[0]) + 1),
            compiler_params=params(8),
        )(flags, answer, there)
        across = exchange(sent, AXES[0])
        correction = pl.pallas_call(
            functools.partial(last_near_kernel, faces),
            in_specs=vmem_specs(7 + len(theirs)),
            **result,
        )(flags, product, *inverses, spread, answer, there, *theirs)
    else:
        y, z = lax.axis_index("gy"), lax.axis_index("gz")
        member_of = group_of[y * planes + z]
        chosen = jnp.arange(groups, dtype=jnp.int32) == member_of
        total = lax.psum(jnp.where(chosen[:, None, None], payload[None], 0.0), ("gy", "gz"))
        total = lax.dynamic_index_in_dim(total, member_of, 0, keepdims=False)
        spread = spread_of(payload)
        answer = solve(
            [total[:first_rows]], [total[first_rows:message_rows]], [total[message_rows:]], []
        )

        def from_near(faces_of, axis):
            even, odd = faces_of
            if lax.axis_size(axis) == 2:
                return exchange([jnp.stack([even, odd])], axis)
            upward = is_even(axis)
            return exchange([jnp.where(upward, even, odd), jnp.where(upward, odd, even)], axis)

        blocks = answer.reshape(FACES, ncon, columns)
        near = [
            *from_near(product[4:6], AXES[2]),
            *from_near(blocks[2:4], AXES[1]),
            *from_near(blocks[4:6], AXES[2]),
        ]
        mine = answer[:size]
        across = from_near(blocks[:2], AXES[0])
        correction = pl.pallas_call(
            functools.partial(last_plain_kernel, faces),
            in_specs=vmem_specs(5 + len(near)),
            **result,
        )(product, *inverses, spread, answer, *near)
    correction = pl.pallas_call(
        functools.partial(last_far_kernel, ncon),
        in_specs=vmem_specs(2 + len(across)) + [main_memory],
        input_output_aliases={2 + len(across): 0},
        **result,
    )(spread, mine, *across, correction)
    return correction[None, None, None]


def solution(mesh):
    in_specs = (
        P("gx", "gy", "gz", None, None),
        P("gx", "gy", "gz", None, None, None),
        P("gx", "gy", "gz", None, None),
        P(),
    )
    out_specs = P("gx", "gy", "gz", None, None)
    return jax.shard_map(
        per_device, mesh=mesh, in_specs=in_specs, out_specs=out_specs, check_vma=False
    )
```
